32 devices in a mesh: dp: 16 (over z, x, core), mp: 2 (over y).
Axes of the slice: x: 2, y: 2, z: 4, core: 2. Of those that a mesh axis runs over, the one named last changes fastest.
Arguments:
- tokens: bfloat16 [4096, 768], P('dp'), may hold values from -8 to 8, as said below
- lengths: int32 [16], P('dp'), may hold values from 64 to 256, as said below
- cotangent: bfloat16 [4096, 768], P('dp'), may hold values from -6 to 6
- projection: bfloat16 [2, 768, 3, 768], P(None, None, None, 'mp'), may hold values from -0.21875 to 0.21875
- conv_taps: float32 [2, 12, 33], replicated, may hold values from -0.6 to 0.6
- output_weight: bfloat16 [2, 768, 768], P(None, 'mp'), may hold values from -0.21875 to 0.21875
- norm_gains: float32 [2, 2, 768], replicated, may hold values from 0.5 to 1.5
- norm_shifts: float32 [2, 2, 768], replicated, may hold values from -1.8 to 1.8
- up_weight: bfloat16 [2, 768, 3072], P(None, None, 'mp'), may hold values from -0.21875 to 0.21875
- down_weight: bfloat16 [2, 3072, 768], P(None, 'mp'), may hold values from -0.109375 to 0.109375
Outputs:
- activations: bfloat16 [4096, 768], P('dp')
- token_grad: float32 [4096, 768], P('dp')
- projection_grad: float32 [2, 768, 3, 768], P(None, None, None, 'mp')
- taps_grad: float32 [2, 12, 33], replicated
- output_grad: float32 [2, 768, 768], P(None, 'mp')
- gains_grad: float32 [2, 2, 768], replicated
- shifts_grad: float32 [2, 2, 768], replicated
- upward_grad: float32 [2, 768, 3072], P(None, None, 'mp')
- downward_grad: float32 [2, 3072, 768], P(None, 'mp')
The draws below stay inside these ranges and needn't reach their ends.
Inputs may be any that keep to these rules, and one draw needn't show every extreme that they name: The first lengths[i] rows of slot i hold sequence i, the rest of the slot is padding; some slot is full in every draw. `tokens`: activations of order one.
All inputs are finite; a program needn't handle non-finite values.
Results may differ from the reference program's by a relative error of at most 0.03.
Values may be sent and summed in bfloat16 or wider, within the bound.
A program may use at most 192 MiB of HBM per device.

```python
import jax
import jax.numpy as jnp
from jax import lax

D = 768
H = 12
FF = 3072
M = 64
KS = 33
NEWTON = 6
LAYERS = 2
TOK_DEV = 256
SEQS = 16
TOKENS = 4096


def draw_tokens(key, part):
    key = jax.random.fold_in(key, 11)
    first_key, second_key = jax.random.split(key)
    noise = jnp.clip(jax.random.normal(first_key, (TOKENS, D), jnp.float32), -4.0, 4.0)
    common = jnp.clip(jax.random.normal(second_key, (TOKENS // 16, D), jnp.float32), -4.0, 4.0)
    return (noise + jnp.repeat(common, 16, axis=0)).astype(jnp.bfloat16)


def draw_lengths(key, part):
    key = jax.random.fold_in(key, 23)
    short_key, full_key, pick_key = jax.random.split(key, 3)
    shorter = jax.random.randint(short_key, (SEQS,), TOK_DEV // 4, TOK_DEV // 2 + 1, dtype=jnp.int32)
    filled = jax.random.randint(full_key, (SEQS,), 0, 4, dtype=jnp.int32) == 0
    chosen = jax.random.randint(pick_key, (), 0, SEQS, dtype=jnp.int32)
    filled = filled | (jnp.arange(SEQS, dtype=jnp.int32) == chosen)
    return jnp.where(filled, TOK_DEV, shorter).astype(jnp.int32)


def block_levels(stream_key, extent, pieces, smallest, top_value):
    def one(axis_at, blocks):
        steps = jax.random.uniform(jax.random.fold_in(jax.random.fold_in(stream_key, 6), axis_at), (blocks,), jnp.float32, smallest / len(pieces), top_value / len(pieces))
        return jnp.repeat(jnp.exp(steps), extent[axis_at] // blocks).reshape((-1,) + (1,) * (len(extent) - axis_at - 1))

    level = one(*pieces[0])
    for cut in pieces[1:]:
        level = level * one(*cut)
    return level


def normal_values(own_key, dims, deviation, most, cuts=(), held_as=jnp.bfloat16):
    factor_of = block_levels(own_key, dims, cuts, -0.22, 0.18) if cuts else 1.0
    values = jax.random.normal(own_key, dims, jnp.float32) * deviation * factor_of
    return jnp.minimum(jnp.maximum(values, -most), most).astype(held_as)


def setup_inputs(seed: int = 0) -> dict:
    splits = jax.random.split(jax.random.key(seed), 11)
    tokens = draw_tokens(jax.random.fold_in(splits[10], 71), 0)
    lengths = draw_lengths(jax.random.fold_in(splits[10], 71), 0)
    cotangent = normal_values(splits[2], (TOKENS, D), 1.0, 6.0, ((0, 16),))
    projection = normal_values(splits[3], (LAYERS, D, 3, D), D ** -0.5, 0.21875, ((3, 2),))
    conv_taps = normal_values(splits[4], (LAYERS, H, KS), 0.1, 0.6, (), jnp.float32)
    output_weight = normal_values(splits[5], (LAYERS, D, D), D ** -0.5, 0.21875, ((1, 2),))
    norm_gains = jnp.clip(1.0 + 0.1 * jax.random.normal(splits[6], (LAYERS, 2, D), jnp.float32), 0.5, 1.5)
    norm_shifts = normal_values(splits[7], (LAYERS, 2, D), 0.3, 1.8, (), jnp.float32)
    up_weight = normal_values(splits[8], (LAYERS, D, FF), D ** -0.5, 0.21875, ((2, 2),))
    down_weight = normal_values(splits[9], (LAYERS, FF, D), FF ** -0.5, 0.109375, ((1, 2),))
    return dict(tokens=tokens, lengths=lengths, cotangent=cotangent, projection=projection, conv_taps=conv_taps, output_weight=output_weight, norm_gains=norm_gains, norm_shifts=norm_shifts, up_weight=up_weight, down_weight=down_weight)


@jax.custom_vjp
def low(v):
    return lax.optimization_barrier(v.astype(jnp.bfloat16)).astype(jnp.float32)

@jax.custom_vjp
def low_back(v):
    return v

def low_keep(v):
    return (low(v), None)

def low_pass(kept, grad):
    return (grad,)

def back_keep(v):
    return (v, None)

def back_low(kept, grad):
    return (low(grad),)
low.defvjp(low_keep, low_pass)
low_back.defvjp(back_keep, back_low)
highest_value = lax.Precision.HIGHEST

def softmax_row_block(scores):
    top = lax.optimization_barrier(jnp.max(scores, axis=-1, keepdims=True))
    matrix_powers = jnp.exp(scores - top)
    return matrix_powers / lax.optimization_barrier(jnp.sum(matrix_powers, axis=-1, keepdims=True))

def slot_masks(length, count, marks):
    position = jnp.arange(count, dtype=jnp.int32)
    inside = position < length
    segment = position * marks // length
    member = (segment[None, :] == jnp.arange(marks, dtype=jnp.int32)[:, None]) & inside[None, :]
    member = member.astype(jnp.float32)
    pooling = member / lax.optimization_barrier(jnp.sum(member, axis=1, keepdims=True))
    return (pooling, inside.astype(jnp.float32))

def nystrom(query_matrix, key_matrix, value_matrix, taps, pooling, valid):
    scale_factor = query_matrix.shape[-1] ** (-0.5)
    query_landmarks = jnp.dot(pooling, query_matrix, precision=highest_value)
    key_landmarks = jnp.dot(pooling, key_matrix, precision=highest_value)
    first_entry = softmax_row_block(jnp.dot(query_matrix, key_landmarks.T, precision=highest_value) * scale_factor)
    second = softmax_row_block(jnp.dot(query_landmarks, key_landmarks.T, precision=highest_value) * scale_factor)
    distant_scores = jnp.dot(query_landmarks, key_matrix.T, precision=highest_value) * scale_factor
    third = softmax_row_block(jnp.where(valid[None, :] > 0, distant_scores, -1e+30))
    identity = jnp.eye(second.shape[0], dtype=jnp.float32)
    inverse = second.T / jnp.sum(second * second)
    for sweep in range(NEWTON):
        product = jnp.dot(second, inverse, precision=highest_value)
        inner = 7.0 * identity - product
        inner = 15.0 * identity - jnp.dot(product, inner, precision=highest_value)
        inner = 13.0 * identity - jnp.dot(product, inner, precision=highest_value)
        inverse = 0.25 * jnp.dot(inverse, inner, precision=highest_value)
    summary = jnp.dot(third, value_matrix, precision=highest_value)
    mixed = jnp.dot(first_entry, jnp.dot(inverse, summary, precision=highest_value), precision=highest_value)
    masked = value_matrix * valid[:, None]
    reach = taps.shape[0] // 2
    padded = jnp.pad(masked, ((reach, reach), (0, 0)))
    length_rows = masked.shape[0]
    convolved = jnp.zeros_like(masked)
    for offset in range(taps.shape[0]):
        convolved = convolved + taps[offset] * padded[offset:offset + length_rows]
    return (mixed + convolved) * valid[:, None]

def heads_core(query_matrix, key_matrix, value_matrix, taps, pooling, valid):
    return jax.vmap(nystrom, in_axes=(1, 1, 1, 0, None, None), out_axes=1)(query_matrix, key_matrix, value_matrix, taps, pooling, valid)

def layer_norm(resid, gain, shift):
    centre = resid - lax.optimization_barrier(jnp.mean(resid, axis=-1, keepdims=True))
    spread = lax.rsqrt(lax.optimization_barrier(jnp.mean(centre * centre, axis=-1, keepdims=True)) + 1e-05)
    return centre * spread * gain + shift

def layer_forward(hidden, weights, pooling, valid):
    projection, taps, output_weight, gains, shifts, up_weight, down_weight = weights
    count, width = hidden.shape
    heads = taps.shape[0]
    entering = low(hidden)
    mixed = jnp.einsum('td,dsc->tsc', entering, projection, precision=highest_value)
    mixed = low(low_back(mixed))
    query_matrix = mixed[:, 0].reshape(count, heads, -1)
    key_matrix = mixed[:, 1].reshape(count, heads, -1)
    value_matrix = mixed[:, 2].reshape(count, heads, -1)
    attended = heads_core(query_matrix, key_matrix, value_matrix, taps, pooling, valid)
    joined = low(attended.reshape(count, -1))
    branch = low_back(jnp.dot(joined, output_weight, precision=highest_value))
    middle = layer_norm(hidden + branch, gains[0], shifts[0])
    upward = low_back(jnp.dot(low(middle), up_weight, precision=highest_value))
    active = low(jax.nn.gelu(upward, approximate=True))
    branch = low_back(jnp.dot(active, down_weight, precision=highest_value))
    return layer_norm(middle + branch, gains[1], shifts[1])

def block(hidden, weights, pooling, valid):
    for layer_index in range(LAYERS):
        hidden = layer_forward(hidden, tuple((item[layer_index] for item in weights)), pooling, valid)
    return hidden * valid[:, None]

def reference(tokens, lengths, cotangent, projection, conv_taps, output_weight, norm_gains, norm_shifts, up_weight, down_weight):
    weights = tuple((item.astype(jnp.float32) for item in (projection, conv_taps, output_weight, norm_gains, norm_shifts, up_weight, down_weight)))
    slot_tokens = tokens.astype(jnp.float32).reshape(SEQS, TOK_DEV, D)
    slot_cotangent = cotangent.astype(jnp.float32).reshape(SEQS, TOK_DEV, D)

    def one_slot(totals, item):
        hidden, length, upstream = item
        pooling, valid = slot_masks(length, TOK_DEV, M)
        output, backward = jax.vjp(lambda inputs, params: block(inputs, params, pooling, valid), hidden, weights)
        input_grad, weight_grads = backward(upstream)
        totals = jax.tree.map(lambda left, right: left + right, totals, weight_grads)
        return (totals, (output, input_grad))
    start = jax.tree.map(jnp.zeros_like, weights)
    totals, (outputs, input_grads) = lax.scan(one_slot, start, (slot_tokens, lengths, slot_cotangent))
    return (outputs.reshape(TOKENS, D).astype(jnp.bfloat16), input_grads.reshape(TOKENS, D), totals[0], totals[1], totals[2], totals[3], totals[4], totals[5], totals[6])
```

```python
import functools

import jax
import jax.numpy as jnp
from jax import lax
from jax.experimental import pallas as pl
from jax.experimental.pallas import tpu as pltpu
from jax.sharding import PartitionSpec as P

M = 64
NEWTON = 6
LAYERS = 2


highest_value = lax.Precision.HIGHEST


def merged(array, axis, join):
    gathered = jax.tree.map(
        lambda a, kind: lax.all_gather(a.astype(kind), axis),
        array,
        (jnp.bfloat16, jnp.bfloat16, jnp.bfloat16),
    )

    def take(source):
        return jax.tree.map(
            lambda a, own: lax.dynamic_index_in_dim(a, source, 0, False).astype(own.dtype),
            gathered,
            array,
        )

    return lax.fori_loop(
        1, lax.axis_size(axis), lambda source, state: join(state, take(source)), take(0)
    )


def for_sending(array):
    return jax.tree.map(lambda a: a.astype(jnp.bfloat16) if a.dtype == jnp.float32 else a, array)


def softmax_row_block(scores):
    top = jnp.max(scores, axis=-1, keepdims=True)
    matrix_powers = jnp.exp(scores - top)
    return matrix_powers / jnp.sum(matrix_powers, axis=-1, keepdims=True)


def slot_masks(length, count, marks):
    position = jnp.arange(count, dtype=jnp.int32)
    inside = position < length
    segment = position * marks // length
    member = (segment[None, :] == jnp.arange(marks, dtype=jnp.int32)[:, None]) & inside[None, :]
    member = member.astype(jnp.float32)
    pooling = member / jnp.sum(member, axis=1, keepdims=True)
    return (pooling, inside.astype(jnp.float32))


def inverse_head(query_landmarks, key_landmarks, summary):
    scale_factor = query_landmarks.shape[-1] ** (-0.5)
    second = softmax_row_block(
        jnp.dot(query_landmarks, key_landmarks.T, precision=highest_value) * scale_factor
    )
    identity = jnp.eye(second.shape[0], dtype=jnp.float32)
    inverse = second.T / jnp.sum(second * second)
    for sweep in range(NEWTON):
        product = jnp.dot(second, inverse, precision=highest_value)
        inner = 7.0 * identity - product
        inner = 15.0 * identity - jnp.dot(product, inner, precision=highest_value)
        inner = 13.0 * identity - jnp.dot(product, inner, precision=highest_value)
        inverse = 0.25 * jnp.dot(inverse, inner, precision=highest_value)
    return jnp.dot(inverse, summary, precision=highest_value)


def inverse_section(query_landmarks, key_landmarks, summary):
    return jax.vmap(inverse_head)(query_landmarks, key_landmarks, summary)


def near_section(query_matrix, key_landmarks, carried_over):
    scale_factor = query_matrix.shape[-1] ** (-0.5)
    first_entry = softmax_row_block(
        jnp.einsum("nlv,lgv->lng", query_matrix, key_landmarks, precision=highest_value)
        * scale_factor
    )
    return jnp.einsum("xtz,xzb->txb", first_entry, carried_over, precision=highest_value)


def far_scores(query_landmarks, key_matrix, valid_own):
    scale_factor = query_landmarks.shape[-1] ** (-0.5)
    distant_scores = (
        jnp.einsum("owz,toz->owt", query_landmarks, key_matrix, precision=highest_value)
        * scale_factor
    )
    live = valid_own[None, None, :] > 0
    return (jnp.where(live, distant_scores, -1e30), live)


def join_softmax(left, right):
    peak = jnp.maximum(left[0], right[0])
    left_factor = jnp.exp(left[0] - peak)
    right_factor = jnp.exp(right[0] - peak)
    return (
        peak,
        left[1] * left_factor + right[1] * right_factor,
        left[2] * left_factor[..., None] + right[2] * right_factor[..., None],
    )


def attend(query_matrix, key_matrix, value_matrix, pooled_local, valid_own):
    query_portion = jnp.einsum("ji,ilk->ljk", pooled_local, query_matrix, precision=highest_value)
    key_portion = jnp.einsum("ji,ilk->ljk", pooled_local, key_matrix, precision=highest_value)
    query_landmarks, key_landmarks = (
        lax.psum(query_portion.astype(jnp.bfloat16), "mp").astype(jnp.float32),
        lax.psum(key_portion.astype(jnp.bfloat16), "mp").astype(jnp.float32),
    )
    distant_scores, live = far_scores(query_landmarks, key_matrix, valid_own)
    peak = jnp.max(distant_scores, axis=-1)
    matrix_powers = jnp.where(live, jnp.exp(distant_scores - peak[..., None]), 0.0)
    totals = jnp.sum(matrix_powers, axis=-1)
    weighted_values = jnp.einsum(
        "naw,wno->nao", matrix_powers, value_matrix, precision=highest_value
    )
    peak, totals, weighted_values = merged((peak, totals, weighted_values), "mp", join_softmax)
    summary = weighted_values / totals[..., None]
    carried_over = inverse_section(query_landmarks, key_landmarks, summary)
    mixed = near_section(query_matrix, key_landmarks, carried_over)
    return (mixed, (query_landmarks, key_landmarks, peak, totals, summary))


def attend_back(
    grad_rows, query_matrix, key_matrix, value_matrix, pooled_local, valid_own, saved, tap_part
):
    query_landmarks, key_landmarks, peak, totals, summary = saved
    scale_factor = query_matrix.shape[-1] ** (-0.5)
    carried_over, inverse_back = jax.vjp(inverse_section, query_landmarks, key_landmarks, summary)
    unused, near_back = jax.vjp(near_section, query_matrix, key_landmarks, carried_over)
    query_grad, kland_part, carried_part = near_back(grad_rows)
    key_landmark_nearby, carried_grad, tap_grad = (
        lax.psum(kland_part.astype(jnp.bfloat16), "mp").astype(jnp.float32),
        lax.psum(carried_part.astype(jnp.bfloat16), "mp").astype(jnp.float32),
        lax.psum(tap_part.astype(jnp.bfloat16), "mp").astype(jnp.float32),
    )
    query_landmark_gradient, key_landmark_gradient, summary_gradient = inverse_back(carried_grad)
    distant_scores, live = far_scores(query_landmarks, key_matrix, valid_own)
    weight_spread = jnp.where(
        live, jnp.exp(distant_scores - peak[..., None]) / totals[..., None], 0.0
    )
    moving_along = jnp.einsum(
        "owz,toz->owt", summary_gradient, value_matrix, precision=highest_value
    )
    agreed = jnp.sum(summary_gradient * summary, axis=-1)
    slope_values = weight_spread * (moving_along - agreed[..., None])
    value_gradient = jnp.einsum(
        "ofq,ofn->qon", weight_spread, summary_gradient, precision=highest_value
    )
    query_landmark_remote = (
        jnp.einsum("naw,wno->nao", slope_values, key_matrix, precision=highest_value) * scale_factor
    )
    key_gradient = (
        jnp.einsum("ofq,ofn->qon", slope_values, query_landmarks, precision=highest_value)
        * scale_factor
    )
    query_landmark_remote = lax.psum(query_landmark_remote.astype(jnp.bfloat16), "mp").astype(
        jnp.float32
    )
    query_grad = query_grad + jnp.einsum(
        "ge,xgl->exl",
        pooled_local,
        query_landmark_gradient + query_landmark_remote,
        precision=highest_value,
    )
    key_gradient = key_gradient + jnp.einsum(
        "ge,xgl->exl",
        pooled_local,
        key_landmark_gradient + key_landmark_nearby,
        precision=highest_value,
    )
    return (query_grad, key_gradient, value_gradient, tap_grad)


def head_table(columns, heads, size_h):
    begin = lax.axis_index("mp") * columns
    owner = (begin + jnp.arange(columns, dtype=jnp.int32)) // size_h
    return (owner[None, :] == jnp.arange(heads, dtype=jnp.int32)[:, None]).astype(jnp.float32)


def convolve(value_cols, taps, table, valid):
    tap_cols = jnp.dot(taps.T, table, precision=highest_value)
    masked = value_cols * valid[:, None]
    reach = taps.shape[1] // 2
    padded = jnp.pad(masked, ((reach, reach), (0, 0)))
    length_rows = masked.shape[0]
    convolved = jnp.zeros_like(masked)
    for offset in range(taps.shape[1]):
        convolved = convolved + tap_cols[offset] * padded[offset : offset + length_rows]
    return convolved


def contract(left, right, left_dim, right_dim):
    return lax.dot_general(
        left, right, (((left_dim,), (right_dim,)), ((), ())), preferred_element_type=jnp.float32
    )


def normalize(resid, gain, shift):
    centre = resid - jnp.mean(resid, axis=-1, keepdims=True)
    spread = lax.rsqrt(jnp.mean(centre * centre, axis=-1, keepdims=True) + 1e-05)
    normed = centre * spread
    return (normed * gain + shift, normed, spread)


def normalize_back(upstream, normed, spread, gain):
    scaled = upstream * gain
    result = spread * (
        scaled
        - jnp.mean(scaled, axis=-1, keepdims=True)
        - normed * jnp.mean(scaled * normed, axis=-1, keepdims=True)
    )
    return (result, jnp.sum(upstream * normed, axis=0), jnp.sum(upstream, axis=0))


def own_rows(whole):
    count = whole.shape[0] // lax.axis_size("mp")
    return lax.dynamic_slice_in_dim(whole, lax.axis_index("mp") * count, count, 0)


def whole_rows(share):
    return lax.all_gather(share.astype(jnp.bfloat16), "mp", axis=0, tiled=True).astype(share.dtype)


def row_sums(partial_value):
    return lax.psum_scatter(
        partial_value.astype(jnp.bfloat16), "mp", scatter_dimension=0, tiled=True
    ).astype(jnp.float32)


def add_norm(partial_value, resid, gain, shift):
    summed = row_sums(partial_value)
    output, normed, spread = normalize(own_rows(resid) + summed, gain, shift)
    output = whole_rows(output)
    return (output, normed, spread)


def norm_step_back(upstream, normed, spread, gain):
    result, gain_part, shift_part = normalize_back(upstream, normed, spread, gain)
    whole = whole_rows(result)
    return (result, whole, gain_part, shift_part)


def add_input_grad(result, partial_value):
    total = result + row_sums(partial_value)
    return total


def forward_layer(hidden, weights, pooling_own, valid, valid_own):
    projection, taps, output_weight, gains, shifts, up_weight, down_weight = weights
    count, width = hidden.shape
    heads = taps.shape[0]
    size_h = width // heads
    columns = projection.shape[2]
    entering = hidden.astype(jnp.bfloat16)
    mixed = jnp.einsum(
        "td,dsc->tsc", entering, projection, preferred_element_type=jnp.float32
    ).astype(jnp.bfloat16)
    gathered = lax.all_to_all(mixed, "mp", split_axis=0, concat_axis=2, tiled=True)
    rows = gathered.shape[0]
    split_rows = gathered.astype(jnp.float32).reshape(rows, 3, heads, size_h)
    attended, saved = attend(
        split_rows[:, 0], split_rows[:, 1], split_rows[:, 2], pooling_own, valid_own
    )
    attended_cols = lax.all_to_all(
        for_sending(attended.reshape(rows, width)), "mp", split_axis=1, concat_axis=0, tiled=True
    )
    table = head_table(columns, heads, size_h)
    value_cols = mixed[:, 2].astype(jnp.float32)
    convolved = convolve(value_cols, taps, table, valid)
    joined = ((attended_cols + convolved) * valid[:, None]).astype(jnp.bfloat16)
    partial_value = jnp.dot(joined, output_weight, preferred_element_type=jnp.float32)
    middle, normed_first, spread_first = add_norm(partial_value, hidden, gains[0], shifts[0])
    entering_ffn = middle.astype(jnp.bfloat16)
    upward = jnp.dot(entering_ffn, up_weight, preferred_element_type=jnp.float32)
    active = jax.nn.gelu(upward, approximate=True).astype(jnp.bfloat16)
    partial_value = jnp.dot(active, down_weight, preferred_element_type=jnp.float32)
    output, normed_second, spread_second = add_norm(partial_value, middle, gains[1], shifts[1])
    kept = (
        entering,
        value_cols,
        split_rows,
        saved,
        joined,
        table,
        normed_first,
        spread_first,
        entering_ffn,
        upward,
        active,
        normed_second,
        spread_second,
    )
    return (output, kept)


def backward_layer(upstream, weights, kept, pooling_own, valid, valid_own):
    projection, taps, output_weight, gains, shifts, up_weight, down_weight = weights
    (
        entering,
        value_cols,
        split_rows,
        saved,
        joined,
        table,
        normed_first,
        spread_first,
        entering_ffn,
        upward,
        active,
        normed_second,
        spread_second,
    ) = kept
    count, width = entering.shape
    rows = split_rows.shape[0]
    heads = taps.shape[0]
    size_h = width // heads
    result_second, whole_second, gain_second, shift_second = norm_step_back(
        upstream, normed_second, spread_second, gains[1]
    )
    sent_second = whole_second.astype(jnp.bfloat16)
    down_grad = contract(active, sent_second, 0, 0)
    hidden_grad = contract(sent_second, down_weight, 1, 1)
    unused, gelu_back = jax.vjp(lambda value: jax.nn.gelu(value, approximate=True), upward)
    upward_sent = gelu_back(hidden_grad)[0].astype(jnp.bfloat16)
    up_grad = contract(entering_ffn, upward_sent, 0, 0)
    middle_grad = add_input_grad(result_second, contract(upward_sent, up_weight, 1, 1))
    result_first, whole_first, gain_first, shift_first = norm_step_back(
        middle_grad, normed_first, spread_first, gains[0]
    )
    sent_first = whole_first.astype(jnp.bfloat16)
    out_grad = contract(joined, sent_first, 0, 0)
    joined_grad = contract(sent_first, output_weight, 1, 1)
    masked_grad = joined_grad * valid[:, None]
    unused, conv_back = jax.vjp(
        lambda values, tap_rows: convolve(values, tap_rows, table, valid), value_cols, taps
    )
    conv_value_grad, tap_part = conv_back(masked_grad)
    row_grad = (
        lax.all_to_all(
            masked_grad.astype(jnp.bfloat16), "mp", split_axis=0, concat_axis=1, tiled=True
        )
        .astype(masked_grad.dtype)
        .reshape(rows, heads, size_h)
    )
    query_grad, key_gradient, value_gradient, tap_grad = attend_back(
        row_grad,
        split_rows[:, 0],
        split_rows[:, 1],
        split_rows[:, 2],
        pooling_own,
        valid_own,
        saved,
        tap_part,
    )
    stacked_rows = jnp.stack([query_grad, key_gradient, value_gradient], axis=1).reshape(
        rows, 3, width
    )
    column_grad = lax.all_to_all(
        for_sending(stacked_rows), "mp", split_axis=2, concat_axis=0, tiled=True
    ).astype(stacked_rows.dtype)
    column_grad = jnp.concatenate(
        [column_grad[:, :2], (column_grad[:, 2] + conv_value_grad)[:, None]], axis=1
    )
    mixed_sent = column_grad.astype(jnp.bfloat16)
    proj_grad = jnp.einsum("td,tsc->dsc", entering, mixed_sent, preferred_element_type=jnp.float32)
    below = add_input_grad(
        result_first,
        jnp.einsum("tsc,dsc->td", mixed_sent, projection, preferred_element_type=jnp.float32),
    )
    gain_grad = jnp.stack([gain_first, gain_second])
    shift_grad = jnp.stack([shift_first, shift_second])
    gain_grad, shift_grad = lax.psum((gain_grad, shift_grad), "mp")
    return (below, (proj_grad, tap_grad, out_grad, gain_grad, shift_grad, up_grad, down_grad))


def sum_layer(parts):
    return (
        lax.psum(parts[0].astype(jnp.bfloat16), "dp").astype(jnp.float32),
        lax.psum(parts[1].astype(jnp.bfloat16), "dp").astype(jnp.float32),
        lax.psum(parts[2].astype(jnp.bfloat16), "dp").astype(jnp.float32),
        lax.psum(parts[3].astype(jnp.bfloat16), "dp").astype(jnp.float32),
        lax.psum(parts[4].astype(jnp.bfloat16), "dp").astype(jnp.float32),
        lax.psum(parts[5].astype(jnp.bfloat16), "dp").astype(jnp.float32),
        lax.psum(parts[6].astype(jnp.bfloat16), "dp").astype(jnp.float32),
    )


def body(
    tokens,
    lengths,
    cotangent,
    projection,
    conv_taps,
    output_weight,
    norm_gains,
    norm_shifts,
    up_weight,
    down_weight,
):
    count = tokens.shape[0]
    pooling, valid = slot_masks(lengths[0], count, M)
    rows = count // lax.axis_size("mp")
    begin = lax.axis_index("mp") * rows
    pooling_own = lax.dynamic_slice_in_dim(pooling, begin, rows, 1)
    valid_own = lax.dynamic_slice_in_dim(valid, begin, rows, 0)
    weights = (
        projection,
        conv_taps,
        output_weight,
        norm_gains,
        norm_shifts,
        up_weight,
        down_weight,
    )
    hidden = tokens.astype(jnp.float32)
    keeping = []
    for layer_index in range(LAYERS):
        hidden, kept = forward_layer(
            hidden, tuple((item[layer_index] for item in weights)), pooling_own, valid, valid_own
        )
        keeping.append(kept)
    activations = (hidden * valid[:, None]).astype(jnp.bfloat16)
    upstream = cotangent.astype(jnp.float32) * valid[:, None]
    upstream = own_rows(upstream)
    collected = [None] * LAYERS
    for layer_index in reversed(range(LAYERS)):
        upstream, parts = backward_layer(
            upstream,
            tuple((item[layer_index] for item in weights)),
            keeping[layer_index],
            pooling_own,
            valid,
            valid_own,
        )
        collected[layer_index] = sum_layer(parts)
    stacked = tuple(
        (
            jnp.stack([collected[layer_index][member] for layer_index in range(LAYERS)])
            for member in range(7)
        )
    )
    upstream = whole_rows(upstream)
    return (
        activations,
        upstream,
        stacked[0],
        stacked[1],
        stacked[2],
        stacked[3],
        stacked[4],
        stacked[5],
        stacked[6],
    )


MESH = pl.DeviceIdType.MESH
F32 = jnp.float32
BF16 = jnp.bfloat16


def nn(a, b):
    return lax.dot_general(a, b, (((1,), (0,)), ((), ())), preferred_element_type=F32)


def nt(a, b):
    return lax.dot_general(a, b, (((1,), (1,)), ((), ())), preferred_element_type=F32)


def parts_of(x):
    high = x.astype(BF16)
    return high, (x - high.astype(F32)).astype(BF16)


def nn3(a, b):
    return nn(jnp.concatenate([a[0], a[1]], 1), jnp.concatenate([b[0], b[0]], 0)) + nn(a[0], b[1])


def nt3(a, b):
    return nt(jnp.concatenate([a[0], a[1]], 1), jnp.concatenate([b[0], b[0]], 1)) + nt(a[0], b[1])


def iota(shape, axis):
    return lax.broadcasted_iota(jnp.int32, shape, axis)


class Frame:
    def __init__(self, length, rows, size_h):
        self.length = length
        self.rows = rows
        self.lane0 = iota((1, 2 * size_h), 1) < size_h
        self.keep = [self.lane0.astype(F32).astype(BF16), (~self.lane0).astype(F32).astype(BF16)]
        self.diag = (iota((2 * M, 2 * M), 0) < M) == (iota((2 * M, 2 * M), 1) < M)
        self.ones = self.diag.astype(F32).astype(BF16)
        self.ones2 = jnp.concatenate([self.ones, self.ones], 0)
        j, t = iota((M, rows), 0), iota((M, rows), 1)
        member = (t * M >= j * length) & (t * M < (j + 1) * length)
        member = member.astype(F32)
        self.member = member.astype(BF16)
        self.inv = 1.0 / jnp.sum(member, axis=1, keepdims=True)
        t, j = iota((rows, M), 0), iota((rows, M), 1)
        self.member_t = ((t * M >= j * length) & (t * M < (j + 1) * length)).astype(F32).astype(BF16)
        self.valid = (iota((rows, 1), 0) < length).astype(F32)
        self.valid_lane = iota((1, rows), 1) < length
        self.band = jnp.abs(iota((rows, rows), 0) - iota((rows, rows), 1)) <= KREACH

    def stack(self, x):
        return jnp.where(self.diag, jnp.concatenate([x, x], 0), 0.0)

    def block(self, x):
        return jnp.where(self.diag, x, 0.0)

    def half_sums(self, x):
        high, low = parts_of(x)
        return nn(jnp.concatenate([high, low], 1), self.ones2)

    def toeplitz(self, row):
        spread = jnp.broadcast_to(row, (self.rows, self.rows))
        turned = pltpu.roll(spread, self.rows - KREACH, 1, stride=1, stride_axis=0)
        return jnp.where(self.band, turned, 0.0).astype(BF16)

    def conv(self, rows_pair, value):
        both = jnp.concatenate([self.toeplitz(rows_pair[0]), self.toeplitz(rows_pair[1])], 1)
        stacked = jnp.concatenate([value * self.keep[0], value * self.keep[1]], 0)
        return nn(both, stacked)

    def diagonals(self, product):
        banded = jnp.where(self.band, product, 0.0)
        total = banded[:8]
        for group in range(1, self.rows // 8):
            part = banded[8 * group : 8 * group + 8]
            total = total + pltpu.roll(part, self.rows - 8 * group, 1)
        total = pltpu.roll(total, KREACH, 1)
        result = total[:1]
        for row in range(1, 8):
            result = result + pltpu.roll(total[row : row + 1], self.rows - row, 1)
        return result


KREACH = 16


def softmax_masked(scores, live):
    scores = jnp.where(live, scores, -1e30)
    top = jnp.max(scores, axis=-1, keepdims=True)
    powers = jnp.where(live, jnp.exp(scores - top), 0.0)
    return powers / jnp.sum(powers, axis=-1, keepdims=True)


def attention(frame, qkv, taps, head0, size_h, keep, out_ref):
    scale = size_h ** (-0.5)
    pairs = qkv.shape[2] // (2 * size_h)
    ql = nn(frame.member, qkv[0]) * frame.inv
    kl = nn(frame.member, qkv[1]) * frame.inv
    keep["ql"][...] = ql
    keep["kl"][...] = kl
    cols = [slice(p * 2 * size_h, (p + 1) * 2 * size_h) for p in range(pairs)]
    qs = [parts_of(frame.stack(ql[:, c])) for c in cols]
    ks = [parts_of(frame.stack(kl[:, c])) for c in cols]
    second = [softmax_masked(nt3(qs[p], ks[p]) * scale, frame.diag) for p in range(pairs)]
    inverse = []
    halves = iota((2 * M, 1), 0) < M
    for p in range(pairs):
        keep["second"][p] = second[p]
        squares = jnp.sum(second[p] * second[p], axis=1, keepdims=True)
        first_total = jnp.sum(jnp.where(halves, squares, 0.0), axis=0, keepdims=True)
        other_total = jnp.sum(jnp.where(halves, 0.0, squares), axis=0, keepdims=True)
        inverse.append(second[p].T * (1.0 / jnp.where(halves, first_total, other_total)))
    second_parts = [parts_of(s) for s in second]
    for sweep in range(NEWTON):
        for p in range(pairs):
            keep["inverse"][sweep, p] = inverse[p]
        zp = [parts_of(z) for z in inverse]
        product = [nn3(second_parts[p], zp[p]) for p in range(pairs)]
        pp = [parts_of(x) for x in product]
        square = [nn3(pp[p], pp[p]) for p in range(pairs)]
        forward = [nn3(zp[p], pp[p]) for p in range(pairs)]
        last = [
            nn3(parts_of(forward[p]), parts_of(7.0 * product[p] - square[p])) for p in range(pairs)
        ]
        inverse = [
            0.25 * (13.0 * inverse[p] - 15.0 * forward[p] + last[p]) for p in range(pairs)
        ]
    for p in range(pairs):
        c = cols[p]
        keep["inverse"][NEWTON, p] = inverse[p]
        query, key, value = qkv[0, :, c], qkv[1, :, c], qkv[2, :, c]
        scores = nt(jnp.concatenate([query, query], 1), jnp.concatenate(ks[p], 1)) * scale
        top0 = jnp.max(jnp.where(frame.lane0, scores, -1e30), axis=-1, keepdims=True)
        top1 = jnp.max(jnp.where(frame.lane0, -1e30, scores), axis=-1, keepdims=True)
        powers = jnp.exp(scores - jnp.where(frame.lane0, top0, top1))
        first = (powers / frame.half_sums(powers)).astype(BF16)
        keep["first"][:, c] = first
        scores = nt(jnp.concatenate(qs[p], 1), jnp.concatenate([key, key], 1)) * scale
        third = softmax_masked(scores, frame.valid_lane).astype(BF16)
        keep["third"][p] = third
        summary = frame.block(nn(third, value))
        keep["summary"][p] = summary
        carried = nn3(parts_of(inverse[p]), parts_of(summary))
        keep["carried"][p] = carried
        mixed = nn(first, carried.astype(BF16))
        inside = (value.astype(F32) * frame.valid).astype(BF16)
        rows_pair = [taps[pl.ds(head0 + 2 * p + i, 1), :] for i in range(2)]
        mixed = (mixed + frame.conv(rows_pair, inside)) * frame.valid
        out_ref[:, c] = mixed.astype(BF16)


def attention_back(frame, grad, qkv, taps_turned, head0, size_h, keep, out_ref, taps_out):
    scale = size_h ** (-0.5)
    pairs = qkv.shape[2] // (2 * size_h)
    cols = [slice(p * 2 * size_h, (p + 1) * 2 * size_h) for p in range(pairs)]
    each = range(pairs)
    ql, kl = keep["ql"][...], keep["kl"][...]
    qs = [parts_of(frame.stack(ql[:, c])) for c in cols]
    ks = [parts_of(frame.stack(kl[:, c])) for c in cols]
    summary = [keep["summary"][p] for p in each]
    second = [keep["second"][p] for p in each]
    dq, dk_landmark, dcarried, grad_low = [], [], [], []
    for p in each:
        c = cols[p]
        g = grad[:, c].astype(BF16)
        grad_low.append(g)
        first = keep["first"][:, c].astype(F32)
        dfirst = nt(g, keep["carried"][p].astype(BF16))
        slope = first * dfirst
        slope = (slope - first * frame.half_sums(slope)) * scale
        dq.append(nn(slope.astype(BF16), ks[p][0]))
        dk_landmark.append(frame.block(nn(slope.T.astype(BF16), qkv[0, :, c])))
        dcarried.append(frame.block(nn(first.T.astype(BF16), g)))
    dcp = [parts_of(x) for x in dcarried]
    up = [nt3(dcp[p], parts_of(summary[p])) for p in each]
    dsummary = [nn3(parts_of(keep["inverse"][NEWTON, p].T), dcp[p]) for p in each]
    second_parts = [parts_of(s) for s in second]
    second_turned = [parts_of(s.T) for s in second]
    dsecond = [jnp.zeros_like(s) for s in second]
    for sweep in reversed(range(NEWTON)):
        inverse = [keep["inverse"][sweep, p] for p in each]
        zp = [parts_of(z) for z in inverse]
        product = [nn3(second_parts[p], zp[p]) for p in each]
        pp = [parts_of(x) for x in product]
        inner = [parts_of(7.0 * product[p] - nn3(pp[p], pp[p])) for p in each]
        forward_turned = [parts_of(nn3(zp[p], pp[p]).T) for p in each]
        product_turned = [parts_of(x.T) for x in product]
        inverse_turned = [parts_of(z.T) for z in inverse]
        upp = [parts_of(x) for x in up]
        dforward = [parts_of(0.25 * (nt3(upp[p], inner[p]) - 15.0 * up[p])) for p in each]
        dinner_full = [0.25 * nn3(forward_turned[p], upp[p]) for p in each]
        dinner = [parts_of(x) for x in dinner_full]
        dproduct = [
            parts_of(
                7.0 * dinner_full[p]
                - nt3(dinner[p], pp[p])
                - nn3(product_turned[p], dinner[p])
                + nn3(inverse_turned[p], dforward[p])
            )
            for p in each
        ]
        up = [
            3.25 * up[p] + nt3(dforward[p], pp[p]) + nn3(second_turned[p], dproduct[p])
            for p in each
        ]
        dsecond = [dsecond[p] + nt3(dproduct[p], zp[p]) for p in each]
    halves = iota((2 * M, 1), 0) < M
    for p in each:
        c = cols[p]
        query, key, value = qkv[0, :, c], qkv[1, :, c], qkv[2, :, c]
        squares = jnp.sum(second[p] * second[p], axis=1, keepdims=True)
        total0 = jnp.sum(jnp.where(halves, squares, 0.0), axis=0, keepdims=True)
        total1 = jnp.sum(jnp.where(halves, 0.0, squares), axis=0, keepdims=True)
        inverse_total = 1.0 / jnp.where(halves, total0, total1)
        start_agree = jnp.sum(up[p] * keep["inverse"][0, p], axis=1, keepdims=True)
        agree0 = jnp.sum(jnp.where(halves, start_agree, 0.0), axis=0, keepdims=True)
        agree1 = jnp.sum(jnp.where(halves, 0.0, start_agree), axis=0, keepdims=True)
        agree = jnp.where(halves, agree0, agree1)
        dsec = dsecond[p] + (up[p].T - 2.0 * agree * second[p]) * inverse_total
        slope = second[p] * dsec
        slope = (slope - second[p] * jnp.sum(slope, axis=-1, keepdims=True)) * scale
        dql = nn(slope.astype(BF16), ks[p][0])
        dkl = nn(slope.T.astype(BF16), qs[p][0]) + dk_landmark[p]
        third = keep["third"][p].astype(F32)
        ds = dsummary[p].astype(BF16)
        dthird = nt(ds, value)
        agreed = jnp.sum(dsummary[p] * summary[p], axis=-1, keepdims=True)
        slope = third * (dthird - agreed) * scale
        dv = nn(third.T.astype(BF16), ds)
        dql = dql + frame.block(nn(slope.astype(BF16), key))
        dk = nn(slope.T.astype(BF16), qs[p][0])
        dql = ((dql[:M] + dql[M:]) * frame.inv).astype(BF16)
        dkl = ((dkl[:M] + dkl[M:]) * frame.inv).astype(BF16)
        out_ref[0, :, c] = (dq[p] + nn(frame.member_t, dql)).astype(BF16)
        out_ref[1, :, c] = (dk + nn(frame.member_t, dkl)).astype(BF16)
        inside = (value.astype(F32) * frame.valid).astype(BF16)
        rows_pair = [taps_turned[pl.ds(head0 + 2 * p + i, 1), :] for i in range(2)]
        dv = dv + frame.valid * frame.conv(rows_pair, grad_low[p])
        out_ref[2, :, c] = dv.astype(BF16)
        for i in range(2):
            product = nt(grad_low[p] * frame.keep[i], inside)
            taps_out(2 * p + i, frame.diagonals(product))


def norm_rows(r, gain, shift):
    centre = r - jnp.mean(r, axis=-1, keepdims=True)
    spread = lax.rsqrt(jnp.mean(centre * centre, axis=-1, keepdims=True) + 1e-05)
    normed = centre * spread
    return normed * gain + shift, normed, spread


def norm_rows_back(dy, normed, spread, gain):
    scaled = dy * gain
    result = spread * (
        scaled
        - jnp.mean(scaled, axis=-1, keepdims=True)
        - normed * jnp.mean(scaled * normed, axis=-1, keepdims=True)
    )
    return (
        result,
        jnp.sum(dy * normed, axis=0, keepdims=True),
        jnp.sum(dy, axis=0, keepdims=True),
    )


GELU_A = 0.7978845608028654
GELU_B = 0.044715


def gelu_both(u):
    square = u * u
    t = jnp.tanh(GELU_A * (u + GELU_B * u * square))
    half = 0.5 * (1.0 + t)
    slope = half + 0.5 * u * (1.0 - t * t) * (GELU_A + (3.0 * GELU_A * GELU_B) * square)
    return u * half, slope


def whole_step(
    length_ref,
    tokens_ref,
    cotangent_ref,
    taps_ref,
    turned_ref,
    gains_ref,
    shifts_ref,
    projection_hbm,
    output_hbm,
    up_hbm,
    down_hbm,
    activations_ref,
    token_grad_ref,
    small_ref,
    down_grad_hbm,
    up_grad_hbm,
    other_grad_hbm,
    weights,
    kept,
    work,
    grads,
    wire,
    sems,
):
    rows, width = tokens_ref.shape
    columns = projection_hbm.shape[3]
    hidden = up_hbm.shape[2]
    heads = taps_ref.shape[1]
    size_h = width // heads
    half = rows // 2
    tile = 384
    dp, mp = lax.axis_index("dp"), lax.axis_index("mp")
    head0 = mp * (columns // size_h)
    partner = (dp, 1 - mp)

    loads = []
    order = [(projection_hbm, "projection"), (output_hbm, "output"), (up_hbm, "up"), (down_hbm, "down")]
    for layer in range(LAYERS):
        for index, (source, name) in enumerate(order):
            load = pltpu.make_async_copy(
                source.at[layer], weights[name].at[layer], sems["load"].at[layer * 4 + index]
            )
            load.start()
            loads.append(load)

    barrier = pltpu.get_barrier_semaphore()
    pl.semaphore_signal(barrier, inc=1, device_id=partner, device_id_type=MESH)
    pl.semaphore_wait(barrier, 1)

    frame = Frame(length_ref[0], rows, size_h)
    flights = {}

    def send(slot, piece, partial_value):
        span = pl.ds(piece * half, half)
        wire["send"][slot % 2, span, :] = partial_value.astype(BF16)
        copy = pltpu.make_async_remote_copy(
            src_ref=wire["send"].at[slot % 2, span],
            dst_ref=wire["receive"].at[slot, span],
            send_sem=sems["send"].at[slot * 2 + piece],
            recv_sem=sems["receive"].at[slot * 2 + piece],
            device_id=partner,
            device_id_type=MESH,
        )
        copy.start()
        flights[slot, piece] = copy

    def arrived(slot, piece):
        span = pl.ds(piece * half, half)
        flights[slot, piece].wait()
        return wire["send"][slot % 2, span, :].astype(F32) + wire["receive"][
            slot, span, :
        ].astype(F32)

    pieces = [slice(0, half), slice(half, rows)]
    valid = [frame.valid[c] for c in pieces]

    def project(layer, piece):
        c = pieces[piece]
        for i in range(3):
            kept["qkv"][layer, i, c, :] = nn(
                work["x_low"][c, :], weights["projection"][layer, i]
            ).astype(BF16)

    def keep_of(layer):
        names = ("ql", "kl", "second", "inverse", "first", "third", "summary", "carried")
        return {name: kept[name].at[layer] for name in names}

    work["x"][...] = tokens_ref[...].astype(F32)
    work["x_low"][...] = tokens_ref[...]
    loads[0].wait()
    for piece in range(2):
        project(0, piece)
    for layer in range(LAYERS):
        attention(
            frame,
            kept["qkv"].at[layer],
            taps_ref.at[layer],
            head0,
            size_h,
            keep_of(layer),
            work["mixed"],
        )
        loads[layer * 4 + 1].wait()
        slot = layer * 2
        for piece, c in enumerate(pieces):
            send(slot, piece, nn(work["mixed"][c, :], weights["output"][layer]))
        kept["mixed_t"][layer] = work["mixed"][...].T
        kept["x_t"][layer] = work["x_low"][...].T
        loads[layer * 4 + 2].wait()
        loads[layer * 4 + 3].wait()
        for piece, c in enumerate(pieces):
            summed = work["x"][c, :] + arrived(slot, piece)
            y, normed, spread = norm_rows(summed, gains_ref[layer, 0:1], shifts_ref[layer, 0:1])
            kept["normed"][layer, 0, c, :] = normed
            kept["spread"][layer, 0, c, :] = spread
            work["y"][c, :] = y
            work["y_low"][c, :] = y.astype(BF16)
            for j in range(hidden // tile):
                span = slice(j * tile, (j + 1) * tile)
                u = nn(work["y_low"][c, :], weights["up"][layer, :, span])
                active, slope = gelu_both(u)
                work["active"][c, span] = active.astype(BF16)
                kept["slope"][layer, c, span] = slope
            send(slot + 1, piece, nn(work["active"][c, :], weights["down"][layer]))
        kept["active_t"][layer] = work["active"][...].T
        kept["y_t"][layer] = work["y_low"][...].T
        if layer + 1 < LAYERS:
            loads[layer * 4 + 4].wait()
        for piece, c in enumerate(pieces):
            summed = work["y"][c, :] + arrived(slot + 1, piece)
            y, normed, spread = norm_rows(summed, gains_ref[layer, 1:2], shifts_ref[layer, 1:2])
            kept["normed"][layer, 1, c, :] = normed
            kept["spread"][layer, 1, c, :] = spread
            if layer + 1 < LAYERS:
                work["x"][c, :] = y
                work["x_low"][c, :] = y.astype(BF16)
                project(layer + 1, piece)
            else:
                activations_ref[c, :] = (y * valid[piece]).astype(BF16)

    stores = []

    def store(source, target, index):
        copy = pltpu.make_async_copy(source, target, sems["store"].at[index])
        copy.start()
        stores.append(copy)

    small_ref[...] = jnp.zeros_like(small_ref)
    for piece, c in enumerate(pieces):
        work["dy"][c, :] = cotangent_ref[c, :].astype(F32) * valid[piece]

    def norm_back(layer, which):
        gain = gains_ref[layer, which : which + 1]
        gain_sum = shift_sum = 0.0
        for c in pieces:
            result, gain_part, shift_part = norm_rows_back(
                work["dy"][c, :], kept["normed"][layer, which, c, :], kept["spread"][layer, which, c, :], gain
            )
            work["dr"][c, :] = result
            work["e"][c, :] = result.astype(BF16)
            gain_sum, shift_sum = gain_sum + gain_part, shift_sum + shift_part
        row = layer * 2 + which
        small_ref[row : row + 1, :] = gain_sum
        small_ref[row + 4 : row + 5, :] = shift_sum

    for layer in reversed(range(LAYERS)):
        slot = 4 + (LAYERS - 1 - layer) * 2
        norm_back(layer, 1)
        for j in range(hidden // tile):
            span = slice(j * tile, (j + 1) * tile)
            grads["down"][layer, span, :] = nn(kept["active_t"][layer, span, :], work["e"][...]).astype(BF16)
        store(grads["down"].at[layer], down_grad_hbm.at[layer], layer * 3)
        for j in range(hidden // tile):
            span = slice(j * tile, (j + 1) * tile)
            dh = nt(work["e"][...], weights["down"][layer, span, :])
            work["du"][:, span] = (dh * kept["slope"][layer, :, span]).astype(BF16)
        for piece, c in enumerate(pieces):
            send(slot, piece, nt(work["du"][c, :], weights["up"][layer]))
        for j in range(hidden // tile):
            span = slice(j * tile, (j + 1) * tile)
            grads["up"][layer, :, span] = nn(kept["y_t"][layer], work["du"][:, span]).astype(BF16)
        store(grads["up"].at[layer], up_grad_hbm.at[layer], layer * 3 + 1)
        for piece, c in enumerate(pieces):
            work["dy"][c, :] = work["dr"][c, :] + arrived(slot, piece)
        norm_back(layer, 0)
        for piece, c in enumerate(pieces):
            work["dmixed"][c, :] = nt(work["e"][c, :], weights["output"][layer]) * valid[piece]
        for j in range(2):
            span = slice(j * columns, (j + 1) * columns)
            grads["other"][layer, 0, span, :] = nn(kept["mixed_t"][layer], work["e"][:, span]).astype(BF16)

        def taps_out(head, row, layer=layer):
            small_ref[pl.ds(8 + layer * heads + head0 + head, 1), :rows] = row

        attention_back(
            frame,
            work["dmixed"],
            kept["qkv"].at[layer],
            turned_ref.at[layer],
            head0,
            size_h,
            keep_of(layer),
            work["dqkv"],
            taps_out,
        )
        for piece, c in enumerate(pieces):
            total = 0.0
            for i in range(3):
                total = total + nt(work["dqkv"][i, c, :], weights["projection"][layer, i])
            send(slot + 1, piece, total)
        for i in range(3):
            grads["other"][layer, 1 + i] = nn(kept["x_t"][layer], work["dqkv"][i]).astype(BF16)
        store(grads["other"].at[layer], other_grad_hbm.at[layer], layer * 3 + 2)
        target = work["dy"] if layer > 0 else token_grad_ref
        for piece, c in enumerate(pieces):
            target[c, :] = work["dr"][c, :] + arrived(slot + 1, piece)
    for copy in stores:
        copy.wait()


def fused_body(tokens, lengths, cotangent, projection, conv_taps, output_weight, norm_gains, norm_shifts, up_weight, down_weight):
    rows, width = tokens.shape
    columns, hidden = projection.shape[3], up_weight.shape[2]
    heads, reach = conv_taps.shape[1:]
    size_h = width // heads
    pairs = columns // (2 * size_h)
    by_kind = jnp.transpose(projection, (0, 2, 1, 3))
    room = ((0, 0), (0, 0), (0, rows - reach))
    taps = jnp.pad(conv_taps, room)
    turned = jnp.pad(conv_taps[:, :, ::-1], room)
    vmem = pl.BlockSpec(memory_space=pltpu.VMEM)
    hbm = pl.BlockSpec(memory_space=pl.ANY)
    two = 2 * M
    scratch = (
        dict(
            projection=pltpu.VMEM((LAYERS, 3, width, columns), BF16),
            output=pltpu.VMEM((LAYERS, columns, width), BF16),
            up=pltpu.VMEM((LAYERS, width, hidden), BF16),
            down=pltpu.VMEM((LAYERS, hidden, width), BF16),
        ),
        dict(
            qkv=pltpu.VMEM((LAYERS, 3, rows, columns), BF16),
            ql=pltpu.VMEM((LAYERS, M, columns), F32),
            kl=pltpu.VMEM((LAYERS, M, columns), F32),
            second=pltpu.VMEM((LAYERS, pairs, two, two), F32),
            inverse=pltpu.VMEM((LAYERS, NEWTON + 1, pairs, two, two), F32),
            first=pltpu.VMEM((LAYERS, rows, columns), BF16),
            third=pltpu.VMEM((LAYERS, pairs, two, rows), BF16),
            summary=pltpu.VMEM((LAYERS, pairs, two, two), F32),
            carried=pltpu.VMEM((LAYERS, pairs, two, two), F32),
            normed=pltpu.VMEM((LAYERS, 2, rows, width), F32),
            spread=pltpu.VMEM((LAYERS, 2, rows, 1), F32),
            slope=pltpu.VMEM((LAYERS, rows, hidden), F32),
            x_t=pltpu.VMEM((LAYERS, width, rows), BF16),
            mixed_t=pltpu.VMEM((LAYERS, columns, rows), BF16),
            y_t=pltpu.VMEM((LAYERS, width, rows), BF16),
            active_t=pltpu.VMEM((LAYERS, hidden, rows), BF16),
        ),
        dict(
            x=pltpu.VMEM((rows, width), F32),
            x_low=pltpu.VMEM((rows, width), BF16),
            y=pltpu.VMEM((rows, width), F32),
            y_low=pltpu.VMEM((rows, width), BF16),
            mixed=pltpu.VMEM((rows, columns), BF16),
            active=pltpu.VMEM((rows, hidden), BF16),
            dy=pltpu.VMEM((rows, width), F32),
            dr=pltpu.VMEM((rows, width), F32),
            e=pltpu.VMEM((rows, width), BF16),
            du=pltpu.VMEM((rows, hidden), BF16),
            dmixed=pltpu.VMEM((rows, columns), F32),
            dqkv=pltpu.VMEM((3, rows, columns), BF16),
        ),
        dict(
            down=pltpu.VMEM((LAYERS, hidden, width), BF16),
            up=pltpu.VMEM((LAYERS, width, hidden), BF16),
            other=pltpu.VMEM((LAYERS, 4, width, columns), BF16),
        ),
        dict(
            send=pltpu.VMEM((2, rows, width), BF16),
            receive=pltpu.VMEM((4 * LAYERS, rows, width), BF16),
        ),
        dict(
            load=pltpu.SemaphoreType.DMA((4 * LAYERS,)),
            store=pltpu.SemaphoreType.DMA((3 * LAYERS,)),
            send=pltpu.SemaphoreType.DMA((8 * LAYERS,)),
            receive=pltpu.SemaphoreType.DMA((8 * LAYERS,)),
        ),
    )
    shape = jax.ShapeDtypeStruct
    activations, token_grad, small, down_grad, up_grad, other_grad = pl.pallas_call(
        whole_step,
        out_shape=[
            shape((rows, width), BF16),
            shape((rows, width), F32),
            shape((8 + LAYERS * heads, width), F32),
            shape((LAYERS, hidden, width), BF16),
            shape((LAYERS, width, hidden), BF16),
            shape((LAYERS, 4, width, columns), BF16),
        ],
        in_specs=[pl.BlockSpec(memory_space=pltpu.SMEM)] + [vmem] * 6 + [hbm] * 4,
        out_specs=[vmem] * 3 + [hbm] * 3,
        scratch_shapes=scratch,
        compiler_params=pltpu.CompilerParams(
            collective_id=0, has_side_effects=True, vmem_limit_bytes=64 * 2**20
        ),
    )(lengths, tokens, cotangent, taps, turned, norm_gains, norm_shifts, by_kind, output_weight, up_weight, down_weight)
    small = lax.psum(small, "dp")
    down_grad = lax.psum(down_grad, "dp").astype(F32)
    up_grad = lax.psum(up_grad, "dp").astype(F32)
    other_grad = lax.psum(other_grad, "dp").astype(F32)
    projection_grad = jnp.transpose(other_grad[:, 1:], (0, 2, 1, 3))
    output_grad = jnp.concatenate([other_grad[:, 0, :columns], other_grad[:, 0, columns:]], axis=2)
    taps_grad = lax.psum(small[8:, :reach].reshape(LAYERS, heads, reach), "mp")
    gains_grad = small[0:4].reshape(LAYERS, 2, width)
    shifts_grad = small[4:8].reshape(LAYERS, 2, width)
    return (activations, token_grad, projection_grad, taps_grad, output_grad, gains_grad, shifts_grad, up_grad, down_grad)


def solution(mesh):
    fused = mesh.shape["mp"] == 2

    def step(*arrays):
        return (fused_body if fused else body)(*arrays)

    return jax.shard_map(
        step,
        mesh=mesh,
        in_specs=(
            P("dp", None),
            P("dp"),
            P("dp", None),
            P(None, None, None, "mp"),
            P(),
            P(None, "mp", None),
            P(),
            P(),
            P(None, None, "mp"),
            P(None, "mp", None),
        ),
        out_specs=(
            P("dp", None),
            P("dp", None),
            P(None, None, None, "mp"),
            P(),
            P(None, "mp", None),
            P(),
            P(),
            P(None, None, "mp"),
            P(None, "mp", None),
        ),
        check_vma=False,
    )
```

```python
import functools

import jax
import jax.numpy as jnp
from jax import lax
from jax.experimental import pallas as pl
from jax.experimental.pallas import tpu as pltpu
from jax.sharding import PartitionSpec as P

M = 64
NEWTON = 6
LAYERS = 2


highest_value = lax.Precision.HIGHEST


def merged(array, axis, join):
    gathered = jax.tree.map(
        lambda a, kind: lax.all_gather(a.astype(kind), axis),
        array,
        (jnp.bfloat16, jnp.bfloat16, jnp.bfloat16),
    )

    def take(source):
        return jax.tree.map(
            lambda a, own: lax.dynamic_index_in_dim(a, source, 0, False).astype(own.dtype),
            gathered,
            array,
        )

    return lax.fori_loop(
        1, lax.axis_size(axis), lambda source, state: join(state, take(source)), take(0)
    )


def for_sending(array):
    return jax.tree.map(lambda a: a.astype(jnp.bfloat16) if a.dtype == jnp.float32 else a, array)


def softmax_row_block(scores):
    top = jnp.max(scores, axis=-1, keepdims=True)
    matrix_powers = jnp.exp(scores - top)
    return matrix_powers / jnp.sum(matrix_powers, axis=-1, keepdims=True)


def slot_masks(length, count, marks):
    position = jnp.arange(count, dtype=jnp.int32)
    inside = position < length
    segment = position * marks // length
    member = (segment[None, :] == jnp.arange(marks, dtype=jnp.int32)[:, None]) & inside[None, :]
    member = member.astype(jnp.float32)
    pooling = member / jnp.sum(member, axis=1, keepdims=True)
    return (pooling, inside.astype(jnp.float32))


def inverse_head(query_landmarks, key_landmarks, summary):
    scale_factor = query_landmarks.shape[-1] ** (-0.5)
    second = softmax_row_block(
        jnp.dot(query_landmarks, key_landmarks.T, precision=highest_value) * scale_factor
    )
    identity = jnp.eye(second.shape[0], dtype=jnp.float32)
    inverse = second.T / jnp.sum(second * second)
    for sweep in range(NEWTON):
        product = jnp.dot(second, inverse, precision=highest_value)
        inner = 7.0 * identity - product
        inner = 15.0 * identity - jnp.dot(product, inner, precision=highest_value)
        inner = 13.0 * identity - jnp.dot(product, inner, precision=highest_value)
        inverse = 0.25 * jnp.dot(inverse, inner, precision=highest_value)
    return jnp.dot(inverse, summary, precision=highest_value)


def inverse_section(query_landmarks, key_landmarks, summary):
    return jax.vmap(inverse_head)(query_landmarks, key_landmarks, summary)


def near_section(query_matrix, key_landmarks, carried_over):
    scale_factor = query_matrix.shape[-1] ** (-0.5)
    first_entry = softmax_row_block(
        jnp.einsum("nlv,lgv->lng", query_matrix, key_landmarks, precision=highest_value)
        * scale_factor
    )
    return jnp.einsum("xtz,xzb->txb", first_entry, carried_over, precision=highest_value)


def far_scores(query_landmarks, key_matrix, valid_own):
    scale_factor = query_landmarks.shape[-1] ** (-0.5)
    distant_scores = (
        jnp.einsum("owz,toz->owt", query_landmarks, key_matrix, precision=highest_value)
        * scale_factor
    )
    live = valid_own[None, None, :] > 0
    return (jnp.where(live, distant_scores, -1e30), live)


def join_softmax(left, right):
    peak = jnp.maximum(left[0], right[0])
    left_factor = jnp.exp(left[0] - peak)
    right_factor = jnp.exp(right[0] - peak)
    return (
        peak,
        left[1] * left_factor + right[1] * right_factor,
        left[2] * left_factor[..., None] + right[2] * right_factor[..., None],
    )


def attend(query_matrix, key_matrix, value_matrix, pooled_local, valid_own):
    query_portion = jnp.einsum("ji,ilk->ljk", pooled_local, query_matrix, precision=highest_value)
    key_portion = jnp.einsum("ji,ilk->ljk", pooled_local, key_matrix, precision=highest_value)
    query_landmarks, key_landmarks = (
        lax.psum(query_portion.astype(jnp.bfloat16), "mp").astype(jnp.float32),
        lax.psum(key_portion.astype(jnp.bfloat16), "mp").astype(jnp.float32),
    )
    distant_scores, live = far_scores(query_landmarks, key_matrix, valid_own)
    peak = jnp.max(distant_scores, axis=-1)
    matrix_powers = jnp.where(live, jnp.exp(distant_scores - peak[..., None]), 0.0)
    totals = jnp.sum(matrix_powers, axis=-1)
    weighted_values = jnp.einsum(
        "naw,wno->nao", matrix_powers, value_matrix, precision=highest_value
    )
    peak, totals, weighted_values = merged((peak, totals, weighted_values), "mp", join_softmax)
    summary = weighted_values / totals[..., None]
    carried_over = inverse_section(query_landmarks, key_landmarks, summary)
    mixed = near_section(query_matrix, key_landmarks, carried_over)
    return (mixed, (query_landmarks, key_landmarks, peak, totals, summary))


def attend_back(
    grad_rows, query_matrix, key_matrix, value_matrix, pooled_local, valid_own, saved, tap_part
):
    query_landmarks, key_landmarks, peak, totals, summary = saved
    scale_factor = query_matrix.shape[-1] ** (-0.5)
    carried_over, inverse_back = jax.vjp(inverse_section, query_landmarks, key_landmarks, summary)
    unused, near_back = jax.vjp(near_section, query_matrix, key_landmarks, carried_over)
    query_grad, kland_part, carried_part = near_back(grad_rows)
    key_landmark_nearby, carried_grad, tap_grad = (
        lax.psum(kland_part.astype(jnp.bfloat16), "mp").astype(jnp.float32),
        lax.psum(carried_part.astype(jnp.bfloat16), "mp").astype(jnp.float32),
        lax.psum(tap_part.astype(jnp.bfloat16), "mp").astype(jnp.float32),
    )
    query_landmark_gradient, key_landmark_gradient, summary_gradient = inverse_back(carried_grad)
    distant_scores, live = far_scores(query_landmarks, key_matrix, valid_own)
    weight_spread = jnp.where(
        live, jnp.exp(distant_scores - peak[..., None]) / totals[..., None], 0.0
    )
    moving_along = jnp.einsum(
        "owz,toz->owt", summary_gradient, value_matrix, precision=highest_value
    )
    agreed = jnp.sum(summary_gradient * summary, axis=-1)
    slope_values = weight_spread * (moving_along - agreed[..., None])
    value_gradient = jnp.einsum(
        "ofq,ofn->qon", weight_spread, summary_gradient, precision=highest_value
    )
    query_landmark_remote = (
        jnp.einsum("naw,wno->nao", slope_values, key_matrix, precision=highest_value) * scale_factor
    )
    key_gradient = (
        jnp.einsum("ofq,ofn->qon", slope_values, query_landmarks, precision=highest_value)
        * scale_factor
    )
    query_landmark_remote = lax.psum(query_landmark_remote.astype(jnp.bfloat16), "mp").astype(
        jnp.float32
    )
    query_grad = query_grad + jnp.einsum(
        "ge,xgl->exl",
        pooled_local,
        query_landmark_gradient + query_landmark_remote,
        precision=highest_value,
    )
    key_gradient = key_gradient + jnp.einsum(
        "ge,xgl->exl",
        pooled_local,
        key_landmark_gradient + key_landmark_nearby,
        precision=highest_value,
    )
    return (query_grad, key_gradient, value_gradient, tap_grad)


def head_table(columns, heads, size_h):
    begin = lax.axis_index("mp") * columns
    owner = (begin + jnp.arange(columns, dtype=jnp.int32)) // size_h
    return (owner[None, :] == jnp.arange(heads, dtype=jnp.int32)[:, None]).astype(jnp.float32)


def convolve(value_cols, taps, table, valid):
    tap_cols = jnp.dot(taps.T, table, precision=highest_value)
    masked = value_cols * valid[:, None]
    reach = taps.shape[1] // 2
    padded = jnp.pad(masked, ((reach, reach), (0, 0)))
    length_rows = masked.shape[0]
    convolved = jnp.zeros_like(masked)
    for offset in range(taps.shape[1]):
        convolved = convolved + tap_cols[offset] * padded[offset : offset + length_rows]
    return convolved


def contract(left, right, left_dim, right_dim):
    return lax.dot_general(
        left, right, (((left_dim,), (right_dim,)), ((), ())), preferred_element_type=jnp.float32
    )


def normalize(resid, gain, shift):
    centre = resid - jnp.mean(resid, axis=-1, keepdims=True)
    spread = lax.rsqrt(jnp.mean(centre * centre, axis=-1, keepdims=True) + 1e-05)
    normed = centre * spread
    return (normed * gain + shift, normed, spread)


def normalize_back(upstream, normed, spread, gain):
    scaled = upstream * gain
    result = spread * (
        scaled
        - jnp.mean(scaled, axis=-1, keepdims=True)
        - normed * jnp.mean(scaled * normed, axis=-1, keepdims=True)
    )
    return (result, jnp.sum(upstream * normed, axis=0), jnp.sum(upstream, axis=0))


def own_rows(whole):
    count = whole.shape[0] // lax.axis_size("mp")
    return lax.dynamic_slice_in_dim(whole, lax.axis_index("mp") * count, count, 0)


def whole_rows(share):
    return lax.all_gather(share.astype(jnp.bfloat16), "mp", axis=0, tiled=True).astype(share.dtype)


def row_sums(partial_value):
    return lax.psum_scatter(
        partial_value.astype(jnp.bfloat16), "mp", scatter_dimension=0, tiled=True
    ).astype(jnp.float32)


def add_norm(partial_value, resid, gain, shift):
    summed = row_sums(partial_value)
    output, normed, spread = normalize(own_rows(resid) + summed, gain, shift)
    output = whole_rows(output)
    return (output, normed, spread)


def norm_step_back(upstream, normed, spread, gain):
    result, gain_part, shift_part = normalize_back(upstream, normed, spread, gain)
    whole = whole_rows(result)
    return (result, whole, gain_part, shift_part)


def add_input_grad(result, partial_value):
    total = result + row_sums(partial_value)
    return total


def forward_layer(hidden, weights, pooling_own, valid, valid_own):
    projection, taps, output_weight, gains, shifts, up_weight, down_weight = weights
    count, width = hidden.shape
    heads = taps.shape[0]
    size_h = width // heads
    columns = projection.shape[2]
    entering = hidden.astype(jnp.bfloat16)
    mixed = jnp.einsum(
        "td,dsc->tsc", entering, projection, preferred_element_type=jnp.float32
    ).astype(jnp.bfloat16)
    gathered = lax.all_to_all(mixed, "mp", split_axis=0, concat_axis=2, tiled=True)
    rows = gathered.shape[0]
    split_rows = gathered.astype(jnp.float32).reshape(rows, 3, heads, size_h)
    attended, saved = attend(
        split_rows[:, 0], split_rows[:, 1], split_rows[:, 2], pooling_own, valid_own
    )
    attended_cols = lax.all_to_all(
        for_sending(attended.reshape(rows, width)), "mp", split_axis=1, concat_axis=0, tiled=True
    )
    table = head_table(columns, heads, size_h)
    value_cols = mixed[:, 2].astype(jnp.float32)
    convolved = convolve(value_cols, taps, table, valid)
    joined = ((attended_cols + convolved) * valid[:, None]).astype(jnp.bfloat16)
    partial_value = jnp.dot(joined, output_weight, preferred_element_type=jnp.float32)
    middle, normed_first, spread_first = add_norm(partial_value, hidden, gains[0], shifts[0])
    entering_ffn = middle.astype(jnp.bfloat16)
    upward = jnp.dot(entering_ffn, up_weight, preferred_element_type=jnp.float32)
    active = jax.nn.gelu(upward, approximate=True).astype(jnp.bfloat16)
    partial_value = jnp.dot(active, down_weight, preferred_element_type=jnp.float32)
    output, normed_second, spread_second = add_norm(partial_value, middle, gains[1], shifts[1])
    kept = (
        entering,
        value_cols,
        split_rows,
        saved,
        joined,
        table,
        normed_first,
        spread_first,
        entering_ffn,
        upward,
        active,
        normed_second,
        spread_second,
    )
    return (output, kept)


def backward_layer(upstream, weights, kept, pooling_own, valid, valid_own):
    projection, taps, output_weight, gains, shifts, up_weight, down_weight = weights
    (
        entering,
        value_cols,
        split_rows,
        saved,
        joined,
        table,
        normed_first,
        spread_first,
        entering_ffn,
        upward,
        active,
        normed_second,
        spread_second,
    ) = kept
    count, width = entering.shape
    rows = split_rows.shape[0]
    heads = taps.shape[0]
    size_h = width // heads
    result_second, whole_second, gain_second, shift_second = norm_step_back(
        upstream, normed_second, spread_second, gains[1]
    )
    sent_second = whole_second.astype(jnp.bfloat16)
    down_grad = contract(active, sent_second, 0, 0)
    hidden_grad = contract(sent_second, down_weight, 1, 1)
    unused, gelu_back = jax.vjp(lambda value: jax.nn.gelu(value, approximate=True), upward)
    upward_sent = gelu_back(hidden_grad)[0].astype(jnp.bfloat16)
    up_grad = contract(entering_ffn, upward_sent, 0, 0)
    middle_grad = add_input_grad(result_second, contract(upward_sent, up_weight, 1, 1))
    result_first, whole_first, gain_first, shift_first = norm_step_back(
        middle_grad, normed_first, spread_first, gains[0]
    )
    sent_first = whole_first.astype(jnp.bfloat16)
    out_grad = contract(joined, sent_first, 0, 0)
    joined_grad = contract(sent_first, output_weight, 1, 1)
    masked_grad = joined_grad * valid[:, None]
    unused, conv_back = jax.vjp(
        lambda values, tap_rows: convolve(values, tap_rows, table, valid), value_cols, taps
    )
    conv_value_grad, tap_part = conv_back(masked_grad)
    row_grad = (
        lax.all_to_all(
            masked_grad.astype(jnp.bfloat16), "mp", split_axis=0, concat_axis=1, tiled=True
        )
        .astype(masked_grad.dtype)
        .reshape(rows, heads, size_h)
    )
    query_grad, key_gradient, value_gradient, tap_grad = attend_back(
        row_grad,
        split_rows[:, 0],
        split_rows[:, 1],
        split_rows[:, 2],
        pooling_own,
        valid_own,
        saved,
        tap_part,
    )
    stacked_rows = jnp.stack([query_grad, key_gradient, value_gradient], axis=1).reshape(
        rows, 3, width
    )
    column_grad = lax.all_to_all(
        for_sending(stacked_rows), "mp", split_axis=2, concat_axis=0, tiled=True
    ).astype(stacked_rows.dtype)
    column_grad = jnp.concatenate(
        [column_grad[:, :2], (column_grad[:, 2] + conv_value_grad)[:, None]], axis=1
    )
    mixed_sent = column_grad.astype(jnp.bfloat16)
    proj_grad = jnp.einsum("td,tsc->dsc", entering, mixed_sent, preferred_element_type=jnp.float32)
    below = add_input_grad(
        result_first,
        jnp.einsum("tsc,dsc->td", mixed_sent, projection, preferred_element_type=jnp.float32),
    )
    gain_grad = jnp.stack([gain_first, gain_second])
    shift_grad = jnp.stack([shift_first, shift_second])
    gain_grad, shift_grad = lax.psum((gain_grad, shift_grad), "mp")
    return (below, (proj_grad, tap_grad, out_grad, gain_grad, shift_grad, up_grad, down_grad))


def sum_layer(parts):
    return (
        lax.psum(parts[0].astype(jnp.bfloat16), "dp").astype(jnp.float32),
        lax.psum(parts[1].astype(jnp.bfloat16), "dp").astype(jnp.float32),
        lax.psum(parts[2].astype(jnp.bfloat16), "dp").astype(jnp.float32),
        lax.psum(parts[3].astype(jnp.bfloat16), "dp").astype(jnp.float32),
        lax.psum(parts[4].astype(jnp.bfloat16), "dp").astype(jnp.float32),
        lax.psum(parts[5].astype(jnp.bfloat16), "dp").astype(jnp.float32),
        lax.psum(parts[6].astype(jnp.bfloat16), "dp").astype(jnp.float32),
    )


def body(
    tokens,
    lengths,
    cotangent,
    projection,
    conv_taps,
    output_weight,
    norm_gains,
    norm_shifts,
    up_weight,
    down_weight,
):
    count = tokens.shape[0]
    pooling, valid = slot_masks(lengths[0], count, M)
    rows = count // lax.axis_size("mp")
    begin = lax.axis_index("mp") * rows
    pooling_own = lax.dynamic_slice_in_dim(pooling, begin, rows, 1)
    valid_own = lax.dynamic_slice_in_dim(valid, begin, rows, 0)
    weights = (
        projection,
        conv_taps,
        output_weight,
        norm_gains,
        norm_shifts,
        up_weight,
        down_weight,
    )
    hidden = tokens.astype(jnp.float32)
    keeping = []
    for layer_index in range(LAYERS):
        hidden, kept = forward_layer(
            hidden, tuple((item[layer_index] for item in weights)), pooling_own, valid, valid_own
        )
        keeping.append(kept)
    activations = (hidden * valid[:, None]).astype(jnp.bfloat16)
    upstream = cotangent.astype(jnp.float32) * valid[:, None]
    upstream = own_rows(upstream)
    collected = [None] * LAYERS
    for layer_index in reversed(range(LAYERS)):
        upstream, parts = backward_layer(
            upstream,
            tuple((item[layer_index] for item in weights)),
            keeping[layer_index],
            pooling_own,
            valid,
            valid_own,
        )
        collected[layer_index] = sum_layer(parts)
    stacked = tuple(
        (
            jnp.stack([collected[layer_index][member] for layer_index in range(LAYERS)])
            for member in range(7)
        )
    )
    upstream = whole_rows(upstream)
    return (
        activations,
        upstream,
        stacked[0],
        stacked[1],
        stacked[2],
        stacked[3],
        stacked[4],
        stacked[5],
        stacked[6],
    )


MESH = pl.DeviceIdType.MESH
F32 = jnp.float32
BF16 = jnp.bfloat16


def nn(a, b):
    return lax.dot_general(a, b, (((1,), (0,)), ((), ())), preferred_element_type=F32)


def nt(a, b):
    return lax.dot_general(a, b, (((1,), (1,)), ((), ())), preferred_element_type=F32)


def parts_of(x):
    high = x.astype(BF16)
    return high, (x - high.astype(F32)).astype(BF16)


def nn3(a, b):
    return nn(jnp.concatenate([a[0], a[1]], 1), jnp.concatenate([b[0], b[0]], 0)) + nn(a[0], b[1])


def nt3(a, b):
    return nt(jnp.concatenate([a[0], a[1]], 1), jnp.concatenate([b[0], b[0]], 1)) + nt(a[0], b[1])


def iota(shape, axis):
    return lax.broadcasted_iota(jnp.int32, shape, axis)


class Frame:
    def __init__(self, length, rows, size_h):
        self.length = length
        self.rows = rows
        self.lane0 = iota((1, 2 * size_h), 1) < size_h
        self.keep = [self.lane0.astype(F32).astype(BF16), (~self.lane0).astype(F32).astype(BF16)]
        self.diag = (iota((2 * M, 2 * M), 0) < M) == (iota((2 * M, 2 * M), 1) < M)
        self.ones = self.diag.astype(F32).astype(BF16)
        self.ones2 = jnp.concatenate([self.ones, self.ones], 0)
        j, t = iota((M, rows), 0), iota((M, rows), 1)
        member = (t * M >= j * length) & (t * M < (j + 1) * length)
        member = member.astype(F32)
        self.member = member.astype(BF16)
        self.inv = 1.0 / jnp.sum(member, axis=1, keepdims=True)
        t, j = iota((rows, M), 0), iota((rows, M), 1)
        self.member_t = ((t * M >= j * length) & (t * M < (j + 1) * length)).astype(F32).astype(BF16)
        self.valid = (iota((rows, 1), 0) < length).astype(F32)
        self.valid_lane = iota((1, rows), 1) < length
        self.band = jnp.abs(iota((rows, rows), 0) - iota((rows, rows), 1)) <= KREACH

    def stack(self, x):
        return jnp.where(self.diag, jnp.concatenate([x, x], 0), 0.0)

    def block(self, x):
        return jnp.where(self.diag, x, 0.0)

    def half_sums(self, x):
        high, low = parts_of(x)
        return nn(jnp.concatenate([high, low], 1), self.ones2)

    def toeplitz(self, row):
        spread = jnp.broadcast_to(row, (self.rows, self.rows))
        turned = pltpu.roll(spread, self.rows - KREACH, 1, stride=1, stride_axis=0)
        return jnp.where(self.band, turned, 0.0).astype(BF16)

    def conv(self, rows_pair, value):
        both = jnp.concatenate([self.toeplitz(rows_pair[0]), self.toeplitz(rows_pair[1])], 1)
        stacked = jnp.concatenate([value * self.keep[0], value * self.keep[1]], 0)
        return nn(both, stacked)

    def diagonals(self, product):
        banded = jnp.where(self.band, product, 0.0)
        total = banded[:8]
        for group in range(1, self.rows // 8):
            part = banded[8 * group : 8 * group + 8]
            total = total + pltpu.roll(part, self.rows - 8 * group, 1)
        total = pltpu.roll(total, KREACH, 1)
        result = total[:1]
        for row in range(1, 8):
            result = result + pltpu.roll(total[row : row + 1], self.rows - row, 1)
        return result


KREACH = 16


def softmax_masked(scores, live):
    scores = jnp.where(live, scores, -1e30)
    top = jnp.max(scores, axis=-1, keepdims=True)
    powers = jnp.where(live, jnp.exp(scores - top), 0.0)
    return powers / jnp.sum(powers, axis=-1, keepdims=True)


def attention(frame, qkv, taps, head0, size_h, keep, out_ref):
    scale = size_h ** (-0.5)
    pairs = qkv.shape[2] // (2 * size_h)
    ql = nn(frame.member, qkv[0]) * frame.inv
    kl = nn(frame.member, qkv[1]) * frame.inv
    keep["ql"][...] = ql
    keep["kl"][...] = kl
    cols = [slice(p * 2 * size_h, (p + 1) * 2 * size_h) for p in range(pairs)]
    qs = [parts_of(frame.stack(ql[:, c])) for c in cols]
    ks = [parts_of(frame.stack(kl[:, c])) for c in cols]
    second = [softmax_masked(nt3(qs[p], ks[p]) * scale, frame.diag) for p in range(pairs)]
    inverse = []
    halves = iota((2 * M, 1), 0) < M
    for p in range(pairs):
        keep["second"][p] = second[p]
        squares = jnp.sum(second[p] * second[p], axis=1, keepdims=True)
        first_total = jnp.sum(jnp.where(halves, squares, 0.0), axis=0, keepdims=True)
        other_total = jnp.sum(jnp.where(halves, 0.0, squares), axis=0, keepdims=True)
        inverse.append(second[p].T * (1.0 / jnp.where(halves, first_total, other_total)))
    second_parts = [parts_of(s) for s in second]
    for sweep in range(NEWTON):
        for p in range(pairs):
            keep["inverse"][sweep, p] = inverse[p]
        zp = [parts_of(z) for z in inverse]
        product = [nn3(second_parts[p], zp[p]) for p in range(pairs)]
        pp = [parts_of(x) for x in product]
        square = [nn3(pp[p], pp[p]) for p in range(pairs)]
        forward = [nn3(zp[p], pp[p]) for p in range(pairs)]
        last = [
            nn3(parts_of(forward[p]), parts_of(7.0 * product[p] - square[p])) for p in range(pairs)
        ]
        inverse = [
            0.25 * (13.0 * inverse[p] - 15.0 * forward[p] + last[p]) for p in range(pairs)
        ]
    for p in range(pairs):
        c = cols[p]
        keep["inverse"][NEWTON, p] = inverse[p]
        query, key, value = qkv[0, :, c], qkv[1, :, c], qkv[2, :, c]
        scores = nt(jnp.concatenate([query, query], 1), jnp.concatenate(ks[p], 1)) * scale
        top0 = jnp.max(jnp.where(frame.lane0, scores, -1e30), axis=-1, keepdims=True)
        top1 = jnp.max(jnp.where(frame.lane0, -1e30, scores), axis=-1, keepdims=True)
        powers = jnp.exp(scores - jnp.where(frame.lane0, top0, top1))
        first = (powers / frame.half_sums(powers)).astype(BF16)
        keep["first"][:, c] = first
        scores = nt(jnp.concatenate(qs[p], 1), jnp.concatenate([key, key], 1)) * scale
        third = softmax_masked(scores, frame.valid_lane).astype(BF16)
        keep["third"][p] = third
        summary = frame.block(nn(third, value))
        keep["summary"][p] = summary
        carried = nn3(parts_of(inverse[p]), parts_of(summary))
        keep["carried"][p] = carried
        mixed = nn(first, carried.astype(BF16))
        inside = (value.astype(F32) * frame.valid).astype(BF16)
        rows_pair = [taps[pl.ds(head0 + 2 * p + i, 1), :] for i in range(2)]
        mixed = (mixed + frame.conv(rows_pair, inside)) * frame.valid
        out_ref[:, c] = mixed.astype(BF16)


def attention_back(frame, grad, qkv, taps_turned, head0, size_h, keep, out_ref, taps_out):
    scale = size_h ** (-0.5)
    pairs = qkv.shape[2] // (2 * size_h)
    cols = [slice(p * 2 * size_h, (p + 1) * 2 * size_h) for p in range(pairs)]
    each = range(pairs)
    ql, kl = keep["ql"][...], keep["kl"][...]
    qs = [parts_of(frame.stack(ql[:, c])) for c in cols]
    ks = [parts_of(frame.stack(kl[:, c])) for c in cols]
    summary = [keep["summary"][p] for p in each]
    second = [keep["second"][p] for p in each]
    dq, dk_landmark, dcarried, grad_low = [], [], [], []
    for p in each:
        c = cols[p]
        g = grad[:, c].astype(BF16)
        grad_low.append(g)
        first = keep["first"][:, c].astype(F32)
        dfirst = nt(g, keep["carried"][p].astype(BF16))
        slope = first * dfirst
        slope = (slope - first * frame.half_sums(slope)) * scale
        dq.append(nn(slope.astype(BF16), ks[p][0]))
        dk_landmark.append(frame.block(nn(slope.T.astype(BF16), qkv[0, :, c])))
        dcarried.append(frame.block(nn(first.T.astype(BF16), g)))
    yield
    dcp = [parts_of(x) for x in dcarried]
    up = [nt3(dcp[p], parts_of(summary[p])) for p in each]
    dsummary = [nn3(parts_of(keep["inverse"][NEWTON, p].T), dcp[p]) for p in each]
    second_parts = [parts_of(s) for s in second]
    second_turned = [parts_of(s.T) for s in second]
    dsecond = [jnp.zeros_like(s) for s in second]
    for sweep in reversed(range(NEWTON)):
        inverse = [keep["inverse"][sweep, p] for p in each]
        zp = [parts_of(z) for z in inverse]
        product = [nn3(second_parts[p], zp[p]) for p in each]
        pp = [parts_of(x) for x in product]
        inner = [parts_of(7.0 * product[p] - nn3(pp[p], pp[p])) for p in each]
        forward_turned = [parts_of(nn3(zp[p], pp[p]).T) for p in each]
        product_turned = [parts_of(x.T) for x in product]
        inverse_turned = [parts_of(z.T) for z in inverse]
        upp = [parts_of(x) for x in up]
        dforward = [parts_of(0.25 * (nt3(upp[p], inner[p]) - 15.0 * up[p])) for p in each]
        dinner_full = [0.25 * nn3(forward_turned[p], upp[p]) for p in each]
        dinner = [parts_of(x) for x in dinner_full]
        dproduct = [
            parts_of(
                7.0 * dinner_full[p]
                - nt3(dinner[p], pp[p])
                - nn3(product_turned[p], dinner[p])
                + nn3(inverse_turned[p], dforward[p])
            )
            for p in each
        ]
        up = [
            3.25 * up[p] + nt3(dforward[p], pp[p]) + nn3(second_turned[p], dproduct[p])
            for p in each
        ]
        dsecond = [dsecond[p] + nt3(dproduct[p], zp[p]) for p in each]
        yield
    halves = iota((2 * M, 1), 0) < M
    for p in each:
        c = cols[p]
        query, key, value = qkv[0, :, c], qkv[1, :, c], qkv[2, :, c]
        squares = jnp.sum(second[p] * second[p], axis=1, keepdims=True)
        total0 = jnp.sum(jnp.where(halves, squares, 0.0), axis=0, keepdims=True)
        total1 = jnp.sum(jnp.where(halves, 0.0, squares), axis=0, keepdims=True)
        inverse_total = 1.0 / jnp.where(halves, total0, total1)
        start_agree = jnp.sum(up[p] * keep["inverse"][0, p], axis=1, keepdims=True)
        agree0 = jnp.sum(jnp.where(halves, start_agree, 0.0), axis=0, keepdims=True)
        agree1 = jnp.sum(jnp.where(halves, 0.0, start_agree), axis=0, keepdims=True)
        agree = jnp.where(halves, agree0, agree1)
        dsec = dsecond[p] + (up[p].T - 2.0 * agree * second[p]) * inverse_total
        slope = second[p] * dsec
        slope = (slope - second[p] * jnp.sum(slope, axis=-1, keepdims=True)) * scale
        dql = nn(slope.astype(BF16), ks[p][0])
        dkl = nn(slope.T.astype(BF16), qs[p][0]) + dk_landmark[p]
        third = keep["third"][p].astype(F32)
        ds = dsummary[p].astype(BF16)
        dthird = nt(ds, value)
        agreed = jnp.sum(dsummary[p] * summary[p], axis=-1, keepdims=True)
        slope = third * (dthird - agreed) * scale
        dv = nn(third.T.astype(BF16), ds)
        dql = dql + frame.block(nn(slope.astype(BF16), key))
        dk = nn(slope.T.astype(BF16), qs[p][0])
        dql = ((dql[:M] + dql[M:]) * frame.inv).astype(BF16)
        dkl = ((dkl[:M] + dkl[M:]) * frame.inv).astype(BF16)
        out_ref[0, :, c] = (dq[p] + nn(frame.member_t, dql)).astype(BF16)
        out_ref[1, :, c] = (dk + nn(frame.member_t, dkl)).astype(BF16)
        inside = (value.astype(F32) * frame.valid).astype(BF16)
        rows_pair = [taps_turned[pl.ds(head0 + 2 * p + i, 1), :] for i in range(2)]
        dv = dv + frame.valid * frame.conv(rows_pair, grad_low[p])
        out_ref[2, :, c] = dv.astype(BF16)
        for i in range(2):
            product = nt(grad_low[p] * frame.keep[i], inside)
            taps_out(2 * p + i, frame.diagonals(product))
        yield


def norm_rows(r, gain, shift):
    centre = r - jnp.mean(r, axis=-1, keepdims=True)
    spread = lax.rsqrt(jnp.mean(centre * centre, axis=-1, keepdims=True) + 1e-05)
    normed = centre * spread
    return normed * gain + shift, normed, spread


def norm_rows_back(dy, normed, spread, gain):
    scaled = dy * gain
    result = spread * (
        scaled
        - jnp.mean(scaled, axis=-1, keepdims=True)
        - normed * jnp.mean(scaled * normed, axis=-1, keepdims=True)
    )
    return (
        result,
        jnp.sum(dy * normed, axis=0, keepdims=True),
        jnp.sum(dy, axis=0, keepdims=True),
    )


GELU_A = 0.7978845608028654
GELU_B = 0.044715


def gelu_both(u):
    square = u * u
    t = jnp.tanh(GELU_A * (u + GELU_B * u * square))
    half = 0.5 * (1.0 + t)
    slope = half + 0.5 * u * (1.0 - t * t) * (GELU_A + (3.0 * GELU_A * GELU_B) * square)
    return u * half, slope


class Reduction:
    def __init__(self, sems):
        dp, self.mp = lax.axis_index("dp"), lax.axis_index("mp")
        z = dp // 4
        self.x = (dp // 2) % 2
        self.core = dp % 2
        self.upper = z // 2
        self.inner = (z == 1) | (z == 2)
        self.outer = (z == 0) | (z == 3)
        self.to_core = dp + 1 - 2 * self.core
        self.to_x = dp + 2 - 4 * self.x
        self.to_near = dp + 4 - 8 * (z % 2)
        self.to_mid = (3 - z) * 4 + dp % 4
        self.sems = sems
        self.pieces = []

    def greet(self, barrier):
        for other in (self.to_core, self.to_x, self.to_near, self.to_mid):
            pl.semaphore_signal(barrier, inc=1, device_id=(other, self.mp), device_id_type=MESH)

    def add(self, rows, kind, view, target, slots, credit, gives, takes):
        self.pieces.append((rows // 4, kind, view, target, slots, credit, gives, takes))

    def copy(self, index, slot, source, target, to, sent=None):
        sent = slot if sent is None else sent
        return pltpu.make_async_remote_copy(
            src_ref=source,
            dst_ref=target,
            send_sem=self.sems["ring_send"].at[index * 8 + sent],
            recv_sem=self.sems["ring_receive"].at[index * 8 + slot],
            device_id=(to, self.mp),
            device_id_type=MESH,
        )

    def event(self, index, step):
        quarter, kind, view, target, slots, credit, gives, takes = self.pieces[index]
        x, core, upper = self.x, self.core, self.upper
        side = x if kind == 0 else upper

        def region(half, which, count=1):
            start = (half * 2 + which) * quarter
            return view(start, count * quarter)

        def arrived(slot, ref):
            self.copy(index, slot, ref, ref, self.to_core).wait_recv()

        def sent(slot, ref):
            self.copy(index, slot, ref, ref, self.to_core).wait_send()

        def send(slot, source, destination, to, sem=None, need=None):
            if takes and need is not None:
                pl.semaphore_wait(self.sems["credit"].at[credit * 4 + need], 1)
            self.copy(index, slot, source, destination, to, sem).start()

        def free(which, to):
            if gives:
                pl.semaphore_signal(
                    self.sems["credit"].at[credit * 4 + which],
                    inc=1,
                    device_id=(to, self.mp),
                    device_id_type=MESH,
                )

        def ready(which, slot, ref, to):
            sent(slot, ref)
            pl.semaphore_signal(
                self.sems["ready"].at[index * 4 + which],
                inc=1,
                device_id=(to, self.mp),
                device_id_type=MESH,
            )

        def await_ready(which):
            pl.semaphore_wait(self.sems["ready"].at[index * 4 + which], 1)

        def slot_part(name, which):
            return slots[name].at[pl.ds(pl.multiple_of(which * quarter, 16), quarter)]

        def sum_into(ref, others):
            block = 48 if quarter % 48 == 0 else 16

            def step_rows(i, unused):
                span = pl.ds(pl.multiple_of(i * block, 16), block)
                total = ref[span, :].astype(F32)
                for other in others:
                    total = total + other[span, :].astype(F32)
                ref[span, :] = total.astype(BF16)
                return unused

            lax.fori_loop(0, quarter // block, step_rows, 0)

        def store(half, which):
            start = (half * 2 + which) * quarter
            pltpu.make_async_copy(
                view(start, quarter), target(start, quarter), self.sems["store"].at[index]
            ).start()

        mine, other = region(core, side), region(core, 1 - side)
        if step == 0:
            send(0, region(1 - core, 0, 2), slots["core"], self.to_core, need=0)
        elif step == 7:
            for slot, which in ((6, side), (7, 1 - side)):
                arrived(slot, region(1 - core, which))
                store(1 - core, which)
            sent(6, mine)
            sent(7, other)
            if kind == 0:
                sent(5, mine)

                @pl.when(self.inner)
                def _():
                    sent(4, mine)

            else:

                @pl.when(self.inner)
                def _():
                    for slot in (2, 4, 5):
                        sent(slot, mine)

        elif kind == 0:
            if step == 1:
                arrived(0, slots["core"])
                sum_into(other, [slot_part("core", 1 - x)])
                send(1, other, slots["x"], self.to_x, need=1)
                ready(0, 0, region(1 - core, 0, 2), self.to_core)
            elif step == 2:

                @pl.when(self.outer)
                def _():
                    arrived(1, slots["x"])
                    sum_into(mine, [slot_part("core", x), slots["x"]])
                    free(0, self.to_core)
                    free(1, self.to_x)
                    send(2, mine, slots["near"], self.to_near, need=2)
                    ready(1, 1, other, self.to_x)

            elif step == 3:

                @pl.when(self.inner)
                def _():
                    arrived(1, slots["x"])
                    arrived(2, slots["near"])
                    sum_into(mine, [slot_part("core", x), slots["x"], slots["near"]])
                    free(0, self.to_core)
                    free(1, self.to_x)
                    free(2, self.to_near)
                    send(3, mine, slots["mid"], self.to_mid, need=3)
                    ready(1, 1, other, self.to_x)

                @pl.when(self.outer)
                def _():
                    ready(2, 2, mine, self.to_near)

            elif step == 4:

                @pl.when(self.inner)
                def _():
                    arrived(3, slots["mid"])
                    sent(3, mine)
                    sum_into(mine, [slots["mid"]])
                    free(3, self.to_mid)
                    await_ready(2)
                    send(4, mine, mine, self.to_near)
                    await_ready(1)
                    send(5, mine, mine, self.to_x)
                    await_ready(0)
                    send(6, mine, mine, self.to_core)
                    store(core, side)

            elif step == 5:

                @pl.when(self.outer)
                def _():
                    arrived(4, mine)
                    await_ready(1)
                    send(5, mine, mine, self.to_x)
                    await_ready(0)
                    send(6, mine, mine, self.to_core)
                    store(core, side)

            elif step == 6:
                arrived(5, other)
                send(7, other, other, self.to_core)
                store(core, 1 - side)
        else:
            if step == 1:

                @pl.when(self.outer)
                def _():
                    arrived(0, slots["core"])
                    sum_into(region(core, 0), [slot_part("core", 0)])
                    sum_into(region(core, 1), [slot_part("core", 1)])
                    free(0, self.to_core)
                    send(2, region(core, 0, 2), slots["near"], self.to_near, need=2)
                    ready(0, 0, region(1 - core, 0, 2), self.to_core)

            elif step == 2:

                @pl.when(self.outer)
                def _():
                    ready(2, 2, region(core, 0, 2), self.to_near)

                @pl.when(self.inner)
                def _():
                    arrived(0, slots["core"])
                    arrived(2, slots["near"])
                    sum_into(other, [slot_part("core", 1 - side), slot_part("near", 1 - side)])
                    send(3, other, slots["mid"], self.to_mid, need=3)
                    ready(0, 0, region(1 - core, 0, 2), self.to_core)

            elif step == 3:

                @pl.when(self.inner)
                def _():
                    arrived(3, slots["mid"])
                    sum_into(mine, [slot_part("core", side), slot_part("near", side), slots["mid"]])
                    free(0, self.to_core)
                    free(2, self.to_near)
                    free(3, self.to_mid)
                    send(1, mine, slots["x"], self.to_x, need=1)
                    ready(3, 3, other, self.to_mid)

            elif step == 4:

                @pl.when(self.inner)
                def _():
                    arrived(1, slots["x"])
                    sent(1, mine)
                    sum_into(mine, [slots["x"]])
                    free(1, self.to_x)
                    await_ready(3)
                    send(4, mine, mine, self.to_mid)
                    await_ready(2)
                    send(4, mine, mine, self.to_near, sem=2)
                    await_ready(0)
                    send(6, mine, mine, self.to_core)
                    store(core, side)

            elif step == 5:

                @pl.when(self.inner)
                def _():
                    arrived(4, other)
                    send(5, other, other, self.to_near)
                    send(7, other, other, self.to_core)
                    store(core, 1 - side)

                @pl.when(self.outer)
                def _():
                    arrived(4, mine)
                    await_ready(0)
                    send(6, mine, mine, self.to_core)
                    store(core, side)

            elif step == 6:

                @pl.when(self.outer)
                def _():
                    arrived(5, other)
                    send(7, other, other, self.to_core)
                    store(core, 1 - side)

    def finish(self):
        for index, piece in enumerate(self.pieces):
            whole = piece[2](0, 4 * piece[0])
            pltpu.make_async_copy(whole, whole, self.sems["store"].at[index]).wait()


class SmallSum:
    def __init__(self, ring, total, slots, sems, first_tap):
        self.ring, self.total, self.slots, self.sems, self.first_tap = ring, total, slots, sems, first_tap

    def copy(self, slot, target, to, mp):
        return pltpu.make_async_remote_copy(
            src_ref=self.total,
            dst_ref=target,
            send_sem=self.sems["small_send"].at[slot],
            recv_sem=self.sems["small_receive"].at[slot],
            device_id=(to, mp),
            device_id_type=MESH,
        )

    def event(self, step):
        ring, total, slots = self.ring, self.total, self.slots
        dp = ring.to_core + 2 * ring.core - 1

        def start(slot, to, mp=None):
            self.copy(slot, slots.at[slot], to, ring.mp if mp is None else mp).start()

        def take(slot):
            self.copy(slot, slots.at[slot], dp, ring.mp).wait_recv()

        def sent(slot):
            self.copy(slot, slots.at[slot], dp, ring.mp).wait_send()

        if step == 0:
            start(0, dp, 1 - ring.mp)
        elif step == 1:
            take(0)
            sent(0)
            total[self.first_tap :, :] += slots[0, self.first_tap :, :]
            start(1, ring.to_core)
        elif step == 2:
            take(1)
            sent(1)
            total[...] += slots[1]
            start(2, ring.to_x)
        elif step == 3:
            take(2)
            sent(2)
            total[...] += slots[2]

            @pl.when(ring.outer)
            def _():
                start(3, ring.to_near)

        elif step == 4:

            @pl.when(ring.inner)
            def _():
                take(3)
                total[...] += slots[3]
                start(4, ring.to_mid)

        elif step == 5:

            @pl.when(ring.inner)
            def _():
                take(4)
                sent(4)
                total[...] += slots[4]
                start(5, ring.to_near)

        elif step == 6:

            @pl.when(ring.outer)
            def _():
                take(5)
                sent(3)
                total[...] = slots[5]

            @pl.when(ring.inner)
            def _():
                sent(5)


def whole_step(
    length_ref,
    tokens_ref,
    cotangent_ref,
    taps_ref,
    turned_ref,
    gains_ref,
    shifts_ref,
    projection_hbm,
    output_hbm,
    up_hbm,
    down_hbm,
    activations_ref,
    token_grad_ref,
    small_ref,
    down_grad_hbm,
    up_grad_hbm,
    projection_grad_hbm,
    output_grad_hbm,
    weights,
    kept,
    work,
    grads,
    wire,
    slots,
    sems,
):
    rows, width = tokens_ref.shape
    columns = projection_hbm.shape[3]
    hidden = up_hbm.shape[2]
    heads = taps_ref.shape[1]
    size_h = width // heads
    half = rows // 2
    tile = 384
    dp, mp = lax.axis_index("dp"), lax.axis_index("mp")
    head0 = mp * (columns // size_h)
    partner = (dp, 1 - mp)

    loads = []
    order = [(projection_hbm, "projection"), (output_hbm, "output"), (up_hbm, "up"), (down_hbm, "down")]
    for layer in range(LAYERS):
        for index, (source, name) in enumerate(order):
            load = pltpu.make_async_copy(
                source.at[layer], weights[name].at[layer], sems["load"].at[layer * 4 + index]
            )
            load.start()
            loads.append(load)

    barrier = pltpu.get_barrier_semaphore()
    pl.semaphore_signal(barrier, inc=1, device_id=partner, device_id_type=MESH)
    ring = Reduction(sems)
    ring.greet(barrier)
    pl.semaphore_wait(barrier, 5)

    frame = Frame(length_ref[0], rows, size_h)
    flights = {}

    def send(slot, piece, partial_value):
        span = pl.ds(piece * half, half)
        wire["send"][slot % 2, span, :] = partial_value.astype(BF16)
        copy = pltpu.make_async_remote_copy(
            src_ref=wire["send"].at[slot % 2, span],
            dst_ref=wire["receive"].at[slot % 2, span],
            send_sem=sems["send"].at[slot * 2 + piece],
            recv_sem=sems["receive"].at[slot * 2 + piece],
            device_id=partner,
            device_id_type=MESH,
        )
        copy.start()
        flights[slot, piece] = copy

    def arrived(slot, piece):
        span = pl.ds(piece * half, half)
        flights[slot, piece].wait()
        return wire["send"][slot % 2, span, :].astype(F32) + wire["receive"][
            slot % 2, span, :
        ].astype(F32)

    pieces = [slice(0, half), slice(half, rows)]
    valid = [frame.valid[c] for c in pieces]

    def project(layer, piece):
        c = pieces[piece]
        for i in range(3):
            kept["qkv"][layer, i, c, :] = nn(
                work["x_low"][c, :], weights["projection"][layer, i]
            ).astype(BF16)

    def keep_of(layer):
        names = ("ql", "kl", "second", "inverse", "first", "third", "summary", "carried")
        return {name: kept[name].at[layer] for name in names}

    work["x"][...] = tokens_ref[...].astype(F32)
    work["x_low"][...] = tokens_ref[...]
    loads[0].wait()
    for piece in range(2):
        project(0, piece)
    for layer in range(LAYERS):
        attention(
            frame,
            kept["qkv"].at[layer],
            taps_ref.at[layer],
            head0,
            size_h,
            keep_of(layer),
            work["mixed"],
        )
        loads[layer * 4 + 1].wait()
        slot = layer * 2
        for piece, c in enumerate(pieces):
            send(slot, piece, nn(work["mixed"][c, :], weights["output"][layer]))
        kept["mixed_t"][layer] = work["mixed"][...].T
        kept["x_t"][layer] = work["x_low"][...].T
        loads[layer * 4 + 2].wait()
        loads[layer * 4 + 3].wait()
        for piece, c in enumerate(pieces):
            summed = work["x"][c, :] + arrived(slot, piece)
            y, normed, spread = norm_rows(summed, gains_ref[layer, 0:1], shifts_ref[layer, 0:1])
            kept["normed"][layer, 0, c, :] = normed.astype(BF16)
            kept["spread"][layer, 0, c, :] = spread
            work["y"][c, :] = y
            work["y_low"][c, :] = y.astype(BF16)
            for j in range(hidden // tile):
                span = slice(j * tile, (j + 1) * tile)
                u = nn(work["y_low"][c, :], weights["up"][layer, :, span])
                active, slope = gelu_both(u)
                work["active"][c, span] = active.astype(BF16)
                kept["slope"][layer, c, span] = slope.astype(BF16)
            send(slot + 1, piece, nn(work["active"][c, :], weights["down"][layer]))
        kept["active_t"][layer] = work["active"][...].T
        kept["y_t"][layer] = work["y_low"][...].T
        if layer + 1 < LAYERS:
            loads[layer * 4 + 4].wait()
        for piece, c in enumerate(pieces):
            summed = work["y"][c, :] + arrived(slot + 1, piece)
            y, normed, spread = norm_rows(summed, gains_ref[layer, 1:2], shifts_ref[layer, 1:2])
            kept["normed"][layer, 1, c, :] = normed.astype(BF16)
            kept["spread"][layer, 1, c, :] = spread
            if layer + 1 < LAYERS:
                work["x"][c, :] = y
                work["x_low"][c, :] = y.astype(BF16)
                project(layer + 1, piece)
            else:
                activations_ref[c, :] = (y * valid[piece]).astype(BF16)

    def add_pieces(layer):
        for k, (name, rows_of, kind) in enumerate(pieces_of(width, columns, hidden)):
            index = 0 if name != "projection" else 1 + sum(
                1 for item in pieces_of(width, columns, hidden)[:k] if item[0] == name
            )
            before = sum(
                item[1] for item in pieces_of(width, columns, hidden)[:k] if item[0] == name
            )

            def span(start, count, before=before):
                return pl.ds(pl.multiple_of(before + start, 16), count)

            if name in ("down", "up"):
                hbm = down_grad_hbm if name == "down" else up_grad_hbm

                def view(start, count, span=span, name=name):
                    return grads[name].at[layer, span(start, count)]

                def target(start, count, span=span, hbm=hbm):
                    return hbm.at[layer, span(start, count)]

            elif name == "projection":

                def view(start, count, index=index):
                    return grads["other"].at[layer, index, pl.ds(pl.multiple_of(start, 16), count)]

                def target(start, count, index=index):
                    return projection_grad_hbm.at[
                        layer, index - 1, pl.ds(pl.multiple_of(start, 16), count)
                    ]

            else:

                def view(start, count):
                    return grads["other"].at[layer, 0, pl.ds(pl.multiple_of(start, 16), count)]

                def target(start, count):
                    return output_grad_hbm.at[
                        layer,
                        pl.ds(pl.multiple_of(start % columns, 16), count),
                        pl.ds(pl.multiple_of(start // columns * columns, 128), columns),
                    ]

            ring.add(rows_of, kind, view, target, slots[k], k, layer > 0, layer + 1 < LAYERS)

    for layer in reversed(range(LAYERS)):
        add_pieces(layer)
    small = SmallSum(ring, small_ref, wire["small"], sems, 8)
    dy_ref, dr_ref, e_ref, du_ref = work["x"], work["y"], work["y_low"], work["active"]

    def norm_back(layer, which):
        gain = gains_ref[layer, which : which + 1]
        gain_sum = shift_sum = 0.0
        for c in pieces:
            result, gain_part, shift_part = norm_rows_back(
                dy_ref[c, :],
                kept["normed"][layer, which, c, :].astype(F32),
                kept["spread"][layer, which, c, :],
                gain,
            )
            dr_ref[c, :] = result
            e_ref[c, :] = result.astype(BF16)
            gain_sum, shift_sum = gain_sum + gain_part, shift_sum + shift_part
        row = layer * 2 + which
        small_ref[row : row + 1, :] = gain_sum
        small_ref[row + 4 : row + 5, :] = shift_sum

    def backward():
        small_ref[...] = jnp.zeros_like(small_ref)
        for piece, c in enumerate(pieces):
            dy_ref[c, :] = cotangent_ref[c, :].astype(F32) * valid[piece]
        for layer in reversed(range(LAYERS)):
            slot = 4 + (LAYERS - 1 - layer) * 2
            norm_back(layer, 1)
            yield
            block = hidden // DOWN_PIECES
            for j in range(DOWN_PIECES):
                span = slice(j * block, (j + 1) * block)
                grads["down"][layer, span, :] = nn(
                    kept["active_t"][layer, span, :], e_ref[...]
                ).astype(BF16)
                yield
            for j in range(hidden // tile):
                span = slice(j * tile, (j + 1) * tile)
                dh = nt(e_ref[...], weights["down"][layer, span, :])
                du_ref[:, span] = (dh * kept["slope"][layer, :, span].astype(F32)).astype(BF16)
            yield
            for piece, c in enumerate(pieces):
                send(slot, piece, nt(du_ref[c, :], weights["up"][layer]))
                yield
            block = width // UP_PIECES
            for j in range(UP_PIECES):
                span = slice(j * block, (j + 1) * block)
                grads["up"][layer, span, :] = nn(kept["y_t"][layer, span, :], du_ref[...]).astype(
                    BF16
                )
                yield
            for piece, c in enumerate(pieces):
                dy_ref[c, :] = dr_ref[c, :] + arrived(slot, piece)
            norm_back(layer, 0)
            yield
            for piece, c in enumerate(pieces):
                work["dmixed"][c, :] = nt(e_ref[c, :], weights["output"][layer]) * valid[piece]
            yield
            for j in range(2):
                span = slice(j * columns, (j + 1) * columns)
                grads["other"][layer, 0, span, :] = nn(
                    kept["mixed_t"][layer], e_ref[:, span]
                ).astype(BF16)
            yield

            def taps_out(head, row, layer=layer):
                small_ref[pl.ds(8 + layer * heads + head0 + head, 1), :rows] = row

            yield from attention_back(
                frame,
                work["dmixed"],
                kept["qkv"].at[layer],
                turned_ref.at[layer],
                head0,
                size_h,
                keep_of(layer),
                work["dqkv"],
                taps_out,
            )
            for piece, c in enumerate(pieces):
                total = 0.0
                for i in range(3):
                    total = total + nt(work["dqkv"][i, c, :], weights["projection"][layer, i])
                send(slot + 1, piece, total)
                yield
            for i in range(3):
                grads["other"][layer, 1 + i] = nn(kept["x_t"][layer], work["dqkv"][i]).astype(BF16)
                yield
            target = dy_ref if layer > 0 else token_grad_ref
            for piece, c in enumerate(pieces):
                target[c, :] = dr_ref[c, :] + arrived(slot + 1, piece)
        yield

    items = backward()
    for code in ORDER:
        if code < 0:
            next(items)
        elif code >= 1000:
            small.event(code - 1000)
        else:
            ring.event(code // 8, code % 8)
    ring.finish()


DOWN_PIECES = 2
UP_PIECES = 2
PIECE_KINDS = (1, 0, 0, 0, 0, 0, 1, 0)
ORDER = (
    -1, -1, 0, -1, 8, -1, 1, -1, -1, -1, 9, 16, -1, 24, 17, 25, 10, -1, -1, -1, 32, -1, 2, -1, 33, -1, 18, -1,
    -1, -1, -1, 11, -1, -1, 3, 26, -1, -1, -1, 19, 34, -1, 40, -1, 48, -1, 56, 41, 49, 12, 57, 27, 4, 35, 20,
    -1, 42, 58, -1, 13, 64, -1, 72, -1, -1, 65, -1, 28, 50, -1, 73, 80, -1, 43, 88, 81, 14, 59, 5, 89, 15, 21,
    -1, 36, 74, -1, 51, -1, 96, -1, -1, 29, 44, 97, -1, -1, 66, 60, 82, -1, -1, -1, 6, -1, -1, 7, 75, 90, 37,
    -1, 1000, -1, -1, 67, -1, 45, 104, -1, 112, -1, 120, 83, 105, 22, 113, 61, 1001, 121, 23, 1002, 76, 91,
    -1, 30, 98, 52, 84, 31, 38, 77, 39, 114, 46, 47, 99, 92, 106, 53, 62, 85, 63, 115, 122, 68, 100, 107, 123,
    1003, 1004, 93, 54, 55, 108, 78, 124, 79, 1005, 69, 101, 109, 125, 1006, 86, 87, 70, 71, 94, 95, 116, 102,
    103, 117, 110, 111, 126, 127, 118, 119,
)


def pieces_of(width, columns, hidden):
    names = ["down"] * DOWN_PIECES + ["up"] * UP_PIECES + ["output"] + ["projection"] * 3
    rows = {"down": hidden // DOWN_PIECES, "up": width // UP_PIECES, "output": width, "projection": width}
    return [(name, rows[name], kind) for name, kind in zip(names, PIECE_KINDS)]


def slots_of(name, rows, kind, width, columns, hidden):
    across = {"down": width, "up": hidden, "output": columns, "projection": columns}[name]

    def room(count):
        return pltpu.VMEM((count, across), BF16)

    return dict(
        core=room(rows // 2),
        x=room(rows // 4),
        near=room(rows // 4 if kind == 0 else rows // 2),
        mid=room(rows // 4),
    )


def fused_body(tokens, lengths, cotangent, projection, conv_taps, output_weight, norm_gains, norm_shifts, up_weight, down_weight):
    rows, width = tokens.shape
    columns, hidden = projection.shape[3], up_weight.shape[2]
    heads, reach = conv_taps.shape[1:]
    size_h = width // heads
    pairs = columns // (2 * size_h)
    by_kind = jnp.transpose(projection, (0, 2, 1, 3))
    room = ((0, 0), (0, 0), (0, rows - reach))
    taps = jnp.pad(conv_taps, room)
    turned = jnp.pad(conv_taps[:, :, ::-1], room)
    vmem = pl.BlockSpec(memory_space=pltpu.VMEM)
    hbm = pl.BlockSpec(memory_space=pl.ANY)
    two = 2 * M
    pieces = pieces_of(width, columns, hidden)
    scratch = (
        dict(
            projection=pltpu.VMEM((LAYERS, 3, width, columns), BF16),
            output=pltpu.VMEM((LAYERS, columns, width), BF16),
            up=pltpu.VMEM((LAYERS, width, hidden), BF16),
            down=pltpu.VMEM((LAYERS, hidden, width), BF16),
        ),
        dict(
            qkv=pltpu.VMEM((LAYERS, 3, rows, columns), BF16),
            ql=pltpu.VMEM((LAYERS, M, columns), F32),
            kl=pltpu.VMEM((LAYERS, M, columns), F32),
            second=pltpu.VMEM((LAYERS, pairs, two, two), F32),
            inverse=pltpu.VMEM((LAYERS, NEWTON + 1, pairs, two, two), F32),
            first=pltpu.VMEM((LAYERS, rows, columns), BF16),
            third=pltpu.VMEM((LAYERS, pairs, two, rows), BF16),
            summary=pltpu.VMEM((LAYERS, pairs, two, two), F32),
            carried=pltpu.VMEM((LAYERS, pairs, two, two), F32),
            normed=pltpu.VMEM((LAYERS, 2, rows, width), BF16),
            spread=pltpu.VMEM((LAYERS, 2, rows, 1), F32),
            slope=pltpu.VMEM((LAYERS, rows, hidden), BF16),
            x_t=pltpu.VMEM((LAYERS, width, rows), BF16),
            mixed_t=pltpu.VMEM((LAYERS, columns, rows), BF16),
            y_t=pltpu.VMEM((LAYERS, width, rows), BF16),
            active_t=pltpu.VMEM((LAYERS, hidden, rows), BF16),
        ),
        dict(
            x=pltpu.VMEM((rows, width), F32),
            x_low=pltpu.VMEM((rows, width), BF16),
            y=pltpu.VMEM((rows, width), F32),
            y_low=pltpu.VMEM((rows, width), BF16),
            mixed=pltpu.VMEM((rows, columns), BF16),
            active=pltpu.VMEM((rows, hidden), BF16),
            dmixed=pltpu.VMEM((rows, columns), F32),
            dqkv=pltpu.VMEM((3, rows, columns), BF16),
        ),
        dict(
            down=pltpu.VMEM((LAYERS, hidden, width), BF16),
            up=pltpu.VMEM((LAYERS, width, hidden), BF16),
            other=pltpu.VMEM((LAYERS, 4, width, columns), BF16),
        ),
        dict(
            send=pltpu.VMEM((2, rows, width), BF16),
            receive=pltpu.VMEM((2, rows, width), BF16),
            small=pltpu.VMEM((6, 8 + LAYERS * heads, width), F32),
        ),
        [slots_of(*item, width, columns, hidden) for item in pieces],
        dict(
            load=pltpu.SemaphoreType.DMA((4 * LAYERS,)),
            store=pltpu.SemaphoreType.DMA((len(pieces) * LAYERS,)),
            ring_send=pltpu.SemaphoreType.DMA((8 * len(pieces) * LAYERS,)),
            ring_receive=pltpu.SemaphoreType.DMA((8 * len(pieces) * LAYERS,)),
            small_send=pltpu.SemaphoreType.DMA((6,)),
            small_receive=pltpu.SemaphoreType.DMA((6,)),
            credit=pltpu.SemaphoreType.REGULAR((4 * len(pieces),)),
            ready=pltpu.SemaphoreType.REGULAR((4 * len(pieces) * LAYERS,)),
            send=pltpu.SemaphoreType.DMA((8 * LAYERS,)),
            receive=pltpu.SemaphoreType.DMA((8 * LAYERS,)),
        ),
    )
    shape = jax.ShapeDtypeStruct
    activations, token_grad, small, down_grad, up_grad, projection_grad, output_grad = pl.pallas_call(
        whole_step,
        out_shape=[
            shape((rows, width), BF16),
            shape((rows, width), F32),
            shape((8 + LAYERS * heads, width), F32),
            shape((LAYERS, hidden, width), BF16),
            shape((LAYERS, width, hidden), BF16),
            shape((LAYERS, 3, width, columns), BF16),
            shape((LAYERS, columns, width), BF16),
        ],
        in_specs=[pl.BlockSpec(memory_space=pltpu.SMEM)] + [vmem] * 6 + [hbm] * 4,
        out_specs=[vmem] * 3 + [hbm] * 4,
        scratch_shapes=scratch,
        compiler_params=pltpu.CompilerParams(
            collective_id=0, has_side_effects=True, vmem_limit_bytes=64 * 2**20
        ),
    )(lengths, tokens, cotangent, taps, turned, norm_gains, norm_shifts, by_kind, output_weight, up_weight, down_weight)
    projection_grad = jnp.transpose(projection_grad.astype(F32), (0, 2, 1, 3))
    taps_grad = small[8:, :reach].reshape(LAYERS, heads, reach)
    gains_grad = small[0:4].reshape(LAYERS, 2, width)
    shifts_grad = small[4:8].reshape(LAYERS, 2, width)
    return (
        activations,
        token_grad,
        projection_grad,
        taps_grad,
        output_grad.astype(F32),
        gains_grad,
        shifts_grad,
        up_grad.astype(F32),
        down_grad.astype(F32),
    )


def solution(mesh):
    fused = mesh.shape["mp"] == 2 and mesh.shape["dp"] == 16

    def step(*arrays):
        return (fused_body if fused else body)(*arrays)

    return jax.shard_map(
        step,
        mesh=mesh,
        in_specs=(
            P("dp", None),
            P("dp"),
            P("dp", None),
            P(None, None, None, "mp"),
            P(),
            P(None, "mp", None),
            P(),
            P(),
            P(None, None, "mp"),
            P(None, "mp", None),
        ),
        out_specs=(
            P("dp", None),
            P("dp", None),
            P(None, None, None, "mp"),
            P(),
            P(None, "mp", None),
            P(),
            P(),
            P(None, None, "mp"),
            P(None, "mp", None),
        ),
        check_vma=False,
    )
```

```python
import functools

import jax
import jax.numpy as jnp
from jax import lax
from jax.experimental import pallas as pl
from jax.experimental.pallas import tpu as pltpu
from jax.sharding import PartitionSpec as P

M = 64
NEWTON = 6
LAYERS = 2


highest_value = lax.Precision.HIGHEST


def merged(array, axis, join):
    gathered = jax.tree.map(
        lambda a, kind: lax.all_gather(a.astype(kind), axis),
        array,
        (jnp.bfloat16, jnp.bfloat16, jnp.bfloat16),
    )

    def take(source):
        return jax.tree.map(
            lambda a, own: lax.dynamic_index_in_dim(a, source, 0, False).astype(own.dtype),
            gathered,
            array,
        )

    return lax.fori_loop(
        1, lax.axis_size(axis), lambda source, state: join(state, take(source)), take(0)
    )


def for_sending(array):
    return jax.tree.map(lambda a: a.astype(jnp.bfloat16) if a.dtype == jnp.float32 else a, array)


def softmax_row_block(scores):
    top = jnp.max(scores, axis=-1, keepdims=True)
    matrix_powers = jnp.exp(scores - top)
    return matrix_powers / jnp.sum(matrix_powers, axis=-1, keepdims=True)


def slot_masks(length, count, marks):
    position = jnp.arange(count, dtype=jnp.int32)
    inside = position < length
    segment = position * marks // length
    member = (segment[None, :] == jnp.arange(marks, dtype=jnp.int32)[:, None]) & inside[None, :]
    member = member.astype(jnp.float32)
    pooling = member / jnp.sum(member, axis=1, keepdims=True)
    return (pooling, inside.astype(jnp.float32))


def inverse_head(query_landmarks, key_landmarks, summary):
    scale_factor = query_landmarks.shape[-1] ** (-0.5)
    second = softmax_row_block(
        jnp.dot(query_landmarks, key_landmarks.T, precision=highest_value) * scale_factor
    )
    identity = jnp.eye(second.shape[0], dtype=jnp.float32)
    inverse = second.T / jnp.sum(second * second)
    for sweep in range(NEWTON):
        product = jnp.dot(second, inverse, precision=highest_value)
        inner = 7.0 * identity - product
        inner = 15.0 * identity - jnp.dot(product, inner, precision=highest_value)
        inner = 13.0 * identity - jnp.dot(product, inner, precision=highest_value)
        inverse = 0.25 * jnp.dot(inverse, inner, precision=highest_value)
    return jnp.dot(inverse, summary, precision=highest_value)


def inverse_section(query_landmarks, key_landmarks, summary):
    return jax.vmap(inverse_head)(query_landmarks, key_landmarks, summary)


def near_section(query_matrix, key_landmarks, carried_over):
    scale_factor = query_matrix.shape[-1] ** (-0.5)
    first_entry = softmax_row_block(
        jnp.einsum("nlv,lgv->lng", query_matrix, key_landmarks, precision=highest_value)
        * scale_factor
    )
    return jnp.einsum("xtz,xzb->txb", first_entry, carried_over, precision=highest_value)


def far_scores(query_landmarks, key_matrix, valid_own):
    scale_factor = query_landmarks.shape[-1] ** (-0.5)
    distant_scores = (
        jnp.einsum("owz,toz->owt", query_landmarks, key_matrix, precision=highest_value)
        * scale_factor
    )
    live = valid_own[None, None, :] > 0
    return (jnp.where(live, distant_scores, -1e30), live)


def join_softmax(left, right):
    peak = jnp.maximum(left[0], right[0])
    left_factor = jnp.exp(left[0] - peak)
    right_factor = jnp.exp(right[0] - peak)
    return (
        peak,
        left[1] * left_factor + right[1] * right_factor,
        left[2] * left_factor[..., None] + right[2] * right_factor[..., None],
    )


def attend(query_matrix, key_matrix, value_matrix, pooled_local, valid_own):
    query_portion = jnp.einsum("ji,ilk->ljk", pooled_local, query_matrix, precision=highest_value)
    key_portion = jnp.einsum("ji,ilk->ljk", pooled_local, key_matrix, precision=highest_value)
    query_landmarks, key_landmarks = (
        lax.psum(query_portion.astype(jnp.bfloat16), "mp").astype(jnp.float32),
        lax.psum(key_portion.astype(jnp.bfloat16), "mp").astype(jnp.float32),
    )
    distant_scores, live = far_scores(query_landmarks, key_matrix, valid_own)
    peak = jnp.max(distant_scores, axis=-1)
    matrix_powers = jnp.where(live, jnp.exp(distant_scores - peak[..., None]), 0.0)
    totals = jnp.sum(matrix_powers, axis=-1)
    weighted_values = jnp.einsum(
        "naw,wno->nao", matrix_powers, value_matrix, precision=highest_value
    )
    peak, totals, weighted_values = merged((peak, totals, weighted_values), "mp", join_softmax)
    summary = weighted_values / totals[..., None]
    carried_over = inverse_section(query_landmarks, key_landmarks, summary)
    mixed = near_section(query_matrix, key_landmarks, carried_over)
    return (mixed, (query_landmarks, key_landmarks, peak, totals, summary))


def attend_back(
    grad_rows, query_matrix, key_matrix, value_matrix, pooled_local, valid_own, saved, tap_part
):
    query_landmarks, key_landmarks, peak, totals, summary = saved
    scale_factor = query_matrix.shape[-1] ** (-0.5)
    carried_over, inverse_back = jax.vjp(inverse_section, query_landmarks, key_landmarks, summary)
    unused, near_back = jax.vjp(near_section, query_matrix, key_landmarks, carried_over)
    query_grad, kland_part, carried_part = near_back(grad_rows)
    key_landmark_nearby, carried_grad, tap_grad = (
        lax.psum(kland_part.astype(jnp.bfloat16), "mp").astype(jnp.float32),
        lax.psum(carried_part.astype(jnp.bfloat16), "mp").astype(jnp.float32),
        lax.psum(tap_part.astype(jnp.bfloat16), "mp").astype(jnp.float32),
    )
    query_landmark_gradient, key_landmark_gradient, summary_gradient = inverse_back(carried_grad)
    distant_scores, live = far_scores(query_landmarks, key_matrix, valid_own)
    weight_spread = jnp.where(
        live, jnp.exp(distant_scores - peak[..., None]) / totals[..., None], 0.0
    )
    moving_along = jnp.einsum(
        "owz,toz->owt", summary_gradient, value_matrix, precision=highest_value
    )
    agreed = jnp.sum(summary_gradient * summary, axis=-1)
    slope_values = weight_spread * (moving_along - agreed[..., None])
    value_gradient = jnp.einsum(
        "ofq,ofn->qon", weight_spread, summary_gradient, precision=highest_value
    )
    query_landmark_remote = (
        jnp.einsum("naw,wno->nao", slope_values, key_matrix, precision=highest_value) * scale_factor
    )
    key_gradient = (
        jnp.einsum("ofq,ofn->qon", slope_values, query_landmarks, precision=highest_value)
        * scale_factor
    )
    query_landmark_remote = lax.psum(query_landmark_remote.astype(jnp.bfloat16), "mp").astype(
        jnp.float32
    )
    query_grad = query_grad + jnp.einsum(
        "ge,xgl->exl",
        pooled_local,
        query_landmark_gradient + query_landmark_remote,
        precision=highest_value,
    )
    key_gradient = key_gradient + jnp.einsum(
        "ge,xgl->exl",
        pooled_local,
        key_landmark_gradient + key_landmark_nearby,
        precision=highest_value,
    )
    return (query_grad, key_gradient, value_gradient, tap_grad)


def head_table(columns, heads, size_h):
    begin = lax.axis_index("mp") * columns
    owner = (begin + jnp.arange(columns, dtype=jnp.int32)) // size_h
    return (owner[None, :] == jnp.arange(heads, dtype=jnp.int32)[:, None]).astype(jnp.float32)


def convolve(value_cols, taps, table, valid):
    tap_cols = jnp.dot(taps.T, table, precision=highest_value)
    masked = value_cols * valid[:, None]
    reach = taps.shape[1] // 2
    padded = jnp.pad(masked, ((reach, reach), (0, 0)))
    length_rows = masked.shape[0]
    convolved = jnp.zeros_like(masked)
    for offset in range(taps.shape[1]):
        convolved = convolved + tap_cols[offset] * padded[offset : offset + length_rows]
    return convolved


def contract(left, right, left_dim, right_dim):
    return lax.dot_general(
        left, right, (((left_dim,), (right_dim,)), ((), ())), preferred_element_type=jnp.float32
    )


def normalize(resid, gain, shift):
    centre = resid - jnp.mean(resid, axis=-1, keepdims=True)
    spread = lax.rsqrt(jnp.mean(centre * centre, axis=-1, keepdims=True) + 1e-05)
    normed = centre * spread
    return (normed * gain + shift, normed, spread)


def normalize_back(upstream, normed, spread, gain):
    scaled = upstream * gain
    result = spread * (
        scaled
        - jnp.mean(scaled, axis=-1, keepdims=True)
        - normed * jnp.mean(scaled * normed, axis=-1, keepdims=True)
    )
    return (result, jnp.sum(upstream * normed, axis=0), jnp.sum(upstream, axis=0))


def own_rows(whole):
    count = whole.shape[0] // lax.axis_size("mp")
    return lax.dynamic_slice_in_dim(whole, lax.axis_index("mp") * count, count, 0)


def whole_rows(share):
    return lax.all_gather(share.astype(jnp.bfloat16), "mp", axis=0, tiled=True).astype(share.dtype)


def row_sums(partial_value):
    return lax.psum_scatter(
        partial_value.astype(jnp.bfloat16), "mp", scatter_dimension=0, tiled=True
    ).astype(jnp.float32)


def add_norm(partial_value, resid, gain, shift):
    summed = row_sums(partial_value)
    output, normed, spread = normalize(own_rows(resid) + summed, gain, shift)
    output = whole_rows(output)
    return (output, normed, spread)


def norm_step_back(upstream, normed, spread, gain):
    result, gain_part, shift_part = normalize_back(upstream, normed, spread, gain)
    whole = whole_rows(result)
    return (result, whole, gain_part, shift_part)


def add_input_grad(result, partial_value):
    total = result + row_sums(partial_value)
    return total


def forward_layer(hidden, weights, pooling_own, valid, valid_own):
    projection, taps, output_weight, gains, shifts, up_weight, down_weight = weights
    count, width = hidden.shape
    heads = taps.shape[0]
    size_h = width // heads
    columns = projection.shape[2]
    entering = hidden.astype(jnp.bfloat16)
    mixed = jnp.einsum(
        "td,dsc->tsc", entering, projection, preferred_element_type=jnp.float32
    ).astype(jnp.bfloat16)
    gathered = lax.all_to_all(mixed, "mp", split_axis=0, concat_axis=2, tiled=True)
    rows = gathered.shape[0]
    split_rows = gathered.astype(jnp.float32).reshape(rows, 3, heads, size_h)
    attended, saved = attend(
        split_rows[:, 0], split_rows[:, 1], split_rows[:, 2], pooling_own, valid_own
    )
    attended_cols = lax.all_to_all(
        for_sending(attended.reshape(rows, width)), "mp", split_axis=1, concat_axis=0, tiled=True
    )
    table = head_table(columns, heads, size_h)
    value_cols = mixed[:, 2].astype(jnp.float32)
    convolved = convolve(value_cols, taps, table, valid)
    joined = ((attended_cols + convolved) * valid[:, None]).astype(jnp.bfloat16)
    partial_value = jnp.dot(joined, output_weight, preferred_element_type=jnp.float32)
    middle, normed_first, spread_first = add_norm(partial_value, hidden, gains[0], shifts[0])
    entering_ffn = middle.astype(jnp.bfloat16)
    upward = jnp.dot(entering_ffn, up_weight, preferred_element_type=jnp.float32)
    active = jax.nn.gelu(upward, approximate=True).astype(jnp.bfloat16)
    partial_value = jnp.dot(active, down_weight, preferred_element_type=jnp.float32)
    output, normed_second, spread_second = add_norm(partial_value, middle, gains[1], shifts[1])
    kept = (
        entering,
        value_cols,
        split_rows,
        saved,
        joined,
        table,
        normed_first,
        spread_first,
        entering_ffn,
        upward,
        active,
        normed_second,
        spread_second,
    )
    return (output, kept)


def backward_layer(upstream, weights, kept, pooling_own, valid, valid_own):
    projection, taps, output_weight, gains, shifts, up_weight, down_weight = weights
    (
        entering,
        value_cols,
        split_rows,
        saved,
        joined,
        table,
        normed_first,
        spread_first,
        entering_ffn,
        upward,
        active,
        normed_second,
        spread_second,
    ) = kept
    count, width = entering.shape
    rows = split_rows.shape[0]
    heads = taps.shape[0]
    size_h = width // heads
    result_second, whole_second, gain_second, shift_second = norm_step_back(
        upstream, normed_second, spread_second, gains[1]
    )
    sent_second = whole_second.astype(jnp.bfloat16)
    down_grad = contract(active, sent_second, 0, 0)
    hidden_grad = contract(sent_second, down_weight, 1, 1)
    unused, gelu_back = jax.vjp(lambda value: jax.nn.gelu(value, approximate=True), upward)
    upward_sent = gelu_back(hidden_grad)[0].astype(jnp.bfloat16)
    up_grad = contract(entering_ffn, upward_sent, 0, 0)
    middle_grad = add_input_grad(result_second, contract(upward_sent, up_weight, 1, 1))
    result_first, whole_first, gain_first, shift_first = norm_step_back(
        middle_grad, normed_first, spread_first, gains[0]
    )
    sent_first = whole_first.astype(jnp.bfloat16)
    out_grad = contract(joined, sent_first, 0, 0)
    joined_grad = contract(sent_first, output_weight, 1, 1)
    masked_grad = joined_grad * valid[:, None]
    unused, conv_back = jax.vjp(
        lambda values, tap_rows: convolve(values, tap_rows, table, valid), value_cols, taps
    )
    conv_value_grad, tap_part = conv_back(masked_grad)
    row_grad = (
        lax.all_to_all(
            masked_grad.astype(jnp.bfloat16), "mp", split_axis=0, concat_axis=1, tiled=True
        )
        .astype(masked_grad.dtype)
        .reshape(rows, heads, size_h)
    )
    query_grad, key_gradient, value_gradient, tap_grad = attend_back(
        row_grad,
        split_rows[:, 0],
        split_rows[:, 1],
        split_rows[:, 2],
        pooling_own,
        valid_own,
        saved,
        tap_part,
    )
    stacked_rows = jnp.stack([query_grad, key_gradient, value_gradient], axis=1).reshape(
        rows, 3, width
    )
    column_grad = lax.all_to_all(
        for_sending(stacked_rows), "mp", split_axis=2, concat_axis=0, tiled=True
    ).astype(stacked_rows.dtype)
    column_grad = jnp.concatenate(
        [column_grad[:, :2], (column_grad[:, 2] + conv_value_grad)[:, None]], axis=1
    )
    mixed_sent = column_grad.astype(jnp.bfloat16)
    proj_grad = jnp.einsum("td,tsc->dsc", entering, mixed_sent, preferred_element_type=jnp.float32)
    below = add_input_grad(
        result_first,
        jnp.einsum("tsc,dsc->td", mixed_sent, projection, preferred_element_type=jnp.float32),
    )
    gain_grad = jnp.stack([gain_first, gain_second])
    shift_grad = jnp.stack([shift_first, shift_second])
    gain_grad, shift_grad = lax.psum((gain_grad, shift_grad), "mp")
    return (below, (proj_grad, tap_grad, out_grad, gain_grad, shift_grad, up_grad, down_grad))


def sum_layer(parts):
    return (
        lax.psum(parts[0].astype(jnp.bfloat16), "dp").astype(jnp.float32),
        lax.psum(parts[1].astype(jnp.bfloat16), "dp").astype(jnp.float32),
        lax.psum(parts[2].astype(jnp.bfloat16), "dp").astype(jnp.float32),
        lax.psum(parts[3].astype(jnp.bfloat16), "dp").astype(jnp.float32),
        lax.psum(parts[4].astype(jnp.bfloat16), "dp").astype(jnp.float32),
        lax.psum(parts[5].astype(jnp.bfloat16), "dp").astype(jnp.float32),
        lax.psum(parts[6].astype(jnp.bfloat16), "dp").astype(jnp.float32),
    )


def body(
    tokens,
    lengths,
    cotangent,
    projection,
    conv_taps,
    output_weight,
    norm_gains,
    norm_shifts,
    up_weight,
    down_weight,
):
    count = tokens.shape[0]
    pooling, valid = slot_masks(lengths[0], count, M)
    rows = count // lax.axis_size("mp")
    begin = lax.axis_index("mp") * rows
    pooling_own = lax.dynamic_slice_in_dim(pooling, begin, rows, 1)
    valid_own = lax.dynamic_slice_in_dim(valid, begin, rows, 0)
    weights = (
        projection,
        conv_taps,
        output_weight,
        norm_gains,
        norm_shifts,
        up_weight,
        down_weight,
    )
    hidden = tokens.astype(jnp.float32)
    keeping = []
    for layer_index in range(LAYERS):
        hidden, kept = forward_layer(
            hidden, tuple((item[layer_index] for item in weights)), pooling_own, valid, valid_own
        )
        keeping.append(kept)
    activations = (hidden * valid[:, None]).astype(jnp.bfloat16)
    upstream = cotangent.astype(jnp.float32) * valid[:, None]
    upstream = own_rows(upstream)
    collected = [None] * LAYERS
    for layer_index in reversed(range(LAYERS)):
        upstream, parts = backward_layer(
            upstream,
            tuple((item[layer_index] for item in weights)),
            keeping[layer_index],
            pooling_own,
            valid,
            valid_own,
        )
        collected[layer_index] = sum_layer(parts)
    stacked = tuple(
        (
            jnp.stack([collected[layer_index][member] for layer_index in range(LAYERS)])
            for member in range(7)
        )
    )
    upstream = whole_rows(upstream)
    return (
        activations,
        upstream,
        stacked[0],
        stacked[1],
        stacked[2],
        stacked[3],
        stacked[4],
        stacked[5],
        stacked[6],
    )


MESH = pl.DeviceIdType.MESH
F32 = jnp.float32
BF16 = jnp.bfloat16


def nn(a, b):
    return lax.dot_general(a, b, (((1,), (0,)), ((), ())), preferred_element_type=F32)


def nt(a, b):
    return lax.dot_general(a, b, (((1,), (1,)), ((), ())), preferred_element_type=F32)


def parts_of(x):
    high = x.astype(BF16)
    return high, (x - high.astype(F32)).astype(BF16)


def nn3(a, b):
    return nn(jnp.concatenate([a[0], a[1]], 1), jnp.concatenate([b[0], b[0]], 0)) + nn(a[0], b[1])


def nt3(a, b):
    return nt(jnp.concatenate([a[0], a[1]], 1), jnp.concatenate([b[0], b[0]], 1)) + nt(a[0], b[1])


def iota(shape, axis):
    return lax.broadcasted_iota(jnp.int32, shape, axis)


class Frame:
    def __init__(self, length, rows, size_h):
        self.length = length
        self.rows = rows
        self.lane0 = iota((1, 2 * size_h), 1) < size_h
        self.keep = [self.lane0.astype(F32).astype(BF16), (~self.lane0).astype(F32).astype(BF16)]
        self.diag = (iota((2 * M, 2 * M), 0) < M) == (iota((2 * M, 2 * M), 1) < M)
        self.ones = self.diag.astype(F32).astype(BF16)
        self.ones2 = jnp.concatenate([self.ones, self.ones], 0)
        j, t = iota((M, rows), 0), iota((M, rows), 1)
        member = (t * M >= j * length) & (t * M < (j + 1) * length)
        member = member.astype(F32)
        self.member = member.astype(BF16)
        self.inv = 1.0 / jnp.sum(member, axis=1, keepdims=True)
        t, j = iota((rows, M), 0), iota((rows, M), 1)
        self.member_t = ((t * M >= j * length) & (t * M < (j + 1) * length)).astype(F32).astype(BF16)
        self.valid = (iota((rows, 1), 0) < length).astype(F32)
        self.valid_lane = iota((1, rows), 1) < length
        self.band = jnp.abs(iota((rows, rows), 0) - iota((rows, rows), 1)) <= KREACH

    def stack(self, x):
        return jnp.where(self.diag, jnp.concatenate([x, x], 0), 0.0)

    def block(self, x):
        return jnp.where(self.diag, x, 0.0)

    def half_sums(self, x):
        high, low = parts_of(x)
        return nn(jnp.concatenate([high, low], 1), self.ones2)

    def toeplitz(self, row):
        spread = jnp.broadcast_to(row, (self.rows, self.rows))
        turned = pltpu.roll(spread, self.rows - KREACH, 1, stride=1, stride_axis=0)
        return jnp.where(self.band, turned, 0.0).astype(BF16)

    def conv(self, rows_pair, value):
        both = jnp.concatenate([self.toeplitz(rows_pair[0]), self.toeplitz(rows_pair[1])], 1)
        stacked = jnp.concatenate([value * self.keep[0], value * self.keep[1]], 0)
        return nn(both, stacked)

    def diagonals(self, product):
        banded = jnp.where(self.band, product, 0.0)
        total = banded[:8]
        for group in range(1, self.rows // 8):
            part = banded[8 * group : 8 * group + 8]
            total = total + pltpu.roll(part, self.rows - 8 * group, 1)
        total = pltpu.roll(total, KREACH, 1)
        result = total[:1]
        for row in range(1, 8):
            result = result + pltpu.roll(total[row : row + 1], self.rows - row, 1)
        return result


KREACH = 16


def softmax_masked(scores, live):
    scores = jnp.where(live, scores, -1e30)
    top = jnp.max(scores, axis=-1, keepdims=True)
    powers = jnp.where(live, jnp.exp(scores - top), 0.0)
    return powers / jnp.sum(powers, axis=-1, keepdims=True)


def attention(frame, qkv, taps, head0, size_h, keep, out_ref):
    scale = size_h ** (-0.5)
    pairs = qkv.shape[2] // (2 * size_h)
    ql = nn(frame.member, qkv[0]) * frame.inv
    kl = nn(frame.member, qkv[1]) * frame.inv
    keep["ql"][...] = ql
    keep["kl"][...] = kl
    cols = [slice(p * 2 * size_h, (p + 1) * 2 * size_h) for p in range(pairs)]
    qs = [parts_of(frame.stack(ql[:, c])) for c in cols]
    ks = [parts_of(frame.stack(kl[:, c])) for c in cols]
    second = [softmax_masked(nt3(qs[p], ks[p]) * scale, frame.diag) for p in range(pairs)]
    inverse = []
    halves = iota((2 * M, 1), 0) < M
    for p in range(pairs):
        keep["second"][p] = second[p]
        squares = jnp.sum(second[p] * second[p], axis=1, keepdims=True)
        first_total = jnp.sum(jnp.where(halves, squares, 0.0), axis=0, keepdims=True)
        other_total = jnp.sum(jnp.where(halves, 0.0, squares), axis=0, keepdims=True)
        inverse.append(second[p].T * (1.0 / jnp.where(halves, first_total, other_total)))
    second_parts = [parts_of(s) for s in second]
    for sweep in range(NEWTON):
        for p in range(pairs):
            keep["inverse"][sweep, p] = inverse[p]
        zp = [parts_of(z) for z in inverse]
        product = [nn3(second_parts[p], zp[p]) for p in range(pairs)]
        pp = [parts_of(x) for x in product]
        square = [nn3(pp[p], pp[p]) for p in range(pairs)]
        forward = [nn3(zp[p], pp[p]) for p in range(pairs)]
        last = [
            nn3(parts_of(forward[p]), parts_of(7.0 * product[p] - square[p])) for p in range(pairs)
        ]
        inverse = [
            0.25 * (13.0 * inverse[p] - 15.0 * forward[p] + last[p]) for p in range(pairs)
        ]
    for p in range(pairs):
        c = cols[p]
        keep["inverse"][NEWTON, p] = inverse[p]
        query, key, value = qkv[0, :, c], qkv[1, :, c], qkv[2, :, c]
        scores = nt(jnp.concatenate([query, query], 1), jnp.concatenate(ks[p], 1)) * scale
        top0 = jnp.max(jnp.where(frame.lane0, scores, -1e30), axis=-1, keepdims=True)
        top1 = jnp.max(jnp.where(frame.lane0, -1e30, scores), axis=-1, keepdims=True)
        powers = jnp.exp(scores - jnp.where(frame.lane0, top0, top1))
        first = (powers / frame.half_sums(powers)).astype(BF16)
        keep["first"][:, c] = first
        scores = nt(jnp.concatenate(qs[p], 1), jnp.concatenate([key, key], 1)) * scale
        third = softmax_masked(scores, frame.valid_lane).astype(BF16)
        keep["third"][p] = third
        summary = frame.block(nn(third, value))
        keep["summary"][p] = summary
        carried = nn3(parts_of(inverse[p]), parts_of(summary))
        keep["carried"][p] = carried
        mixed = nn(first, carried.astype(BF16))
        inside = (value.astype(F32) * frame.valid).astype(BF16)
        rows_pair = [taps[pl.ds(head0 + 2 * p + i, 1), :] for i in range(2)]
        mixed = (mixed + frame.conv(rows_pair, inside)) * frame.valid
        out_ref[:, c] = mixed.astype(BF16)


def attention_back(frame, grad, qkv, taps_turned, head0, size_h, keep, out_ref, taps_out):
    scale = size_h ** (-0.5)
    pairs = qkv.shape[2] // (2 * size_h)
    cols = [slice(p * 2 * size_h, (p + 1) * 2 * size_h) for p in range(pairs)]
    each = range(pairs)
    ql, kl = keep["ql"][...], keep["kl"][...]
    qs = [parts_of(frame.stack(ql[:, c])) for c in cols]
    ks = [parts_of(frame.stack(kl[:, c])) for c in cols]
    summary = [keep["summary"][p] for p in each]
    second = [keep["second"][p] for p in each]
    dq, dk_landmark, dcarried, grad_low = [], [], [], []
    for p in each:
        c = cols[p]
        g = grad[:, c].astype(BF16)
        grad_low.append(g)
        first = keep["first"][:, c].astype(F32)
        dfirst = nt(g, keep["carried"][p].astype(BF16))
        slope = first * dfirst
        slope = (slope - first * frame.half_sums(slope)) * scale
        dq.append(nn(slope.astype(BF16), ks[p][0]))
        dk_landmark.append(frame.block(nn(slope.T.astype(BF16), qkv[0, :, c])))
        dcarried.append(frame.block(nn(first.T.astype(BF16), g)))
    yield
    dcp = [parts_of(x) for x in dcarried]
    up = [nt3(dcp[p], parts_of(summary[p])) for p in each]
    dsummary = [nn3(parts_of(keep["inverse"][NEWTON, p].T), dcp[p]) for p in each]
    second_parts = [parts_of(s) for s in second]
    second_turned = [parts_of(s.T) for s in second]
    dsecond = [jnp.zeros_like(s) for s in second]
    for sweep in reversed(range(NEWTON)):
        inverse = [keep["inverse"][sweep, p] for p in each]
        zp = [parts_of(z) for z in inverse]
        product = [nn3(second_parts[p], zp[p]) for p in each]
        pp = [parts_of(x) for x in product]
        inner = [parts_of(7.0 * product[p] - nn3(pp[p], pp[p])) for p in each]
        forward_turned = [parts_of(nn3(zp[p], pp[p]).T) for p in each]
        product_turned = [parts_of(x.T) for x in product]
        inverse_turned = [parts_of(z.T) for z in inverse]
        upp = [parts_of(x) for x in up]
        dforward = [parts_of(0.25 * (nt3(upp[p], inner[p]) - 15.0 * up[p])) for p in each]
        dinner_full = [0.25 * nn3(forward_turned[p], upp[p]) for p in each]
        dinner = [parts_of(x) for x in dinner_full]
        dproduct = [
            parts_of(
                7.0 * dinner_full[p]
                - nt3(dinner[p], pp[p])
                - nn3(product_turned[p], dinner[p])
                + nn3(inverse_turned[p], dforward[p])
            )
            for p in each
        ]
        up = [
            3.25 * up[p] + nt3(dforward[p], pp[p]) + nn3(second_turned[p], dproduct[p])
            for p in each
        ]
        dsecond = [dsecond[p] + nt3(dproduct[p], zp[p]) for p in each]
        yield
    halves = iota((2 * M, 1), 0) < M
    for p in each:
        c = cols[p]
        query, key, value = qkv[0, :, c], qkv[1, :, c], qkv[2, :, c]
        squares = jnp.sum(second[p] * second[p], axis=1, keepdims=True)
        total0 = jnp.sum(jnp.where(halves, squares, 0.0), axis=0, keepdims=True)
        total1 = jnp.sum(jnp.where(halves, 0.0, squares), axis=0, keepdims=True)
        inverse_total = 1.0 / jnp.where(halves, total0, total1)
        start_agree = jnp.sum(up[p] * keep["inverse"][0, p], axis=1, keepdims=True)
        agree0 = jnp.sum(jnp.where(halves, start_agree, 0.0), axis=0, keepdims=True)
        agree1 = jnp.sum(jnp.where(halves, 0.0, start_agree), axis=0, keepdims=True)
        agree = jnp.where(halves, agree0, agree1)
        dsec = dsecond[p] + (up[p].T - 2.0 * agree * second[p]) * inverse_total
        slope = second[p] * dsec
        slope = (slope - second[p] * jnp.sum(slope, axis=-1, keepdims=True)) * scale
        dql = nn(slope.astype(BF16), ks[p][0])
        dkl = nn(slope.T.astype(BF16), qs[p][0]) + dk_landmark[p]
        third = keep["third"][p].astype(F32)
        ds = dsummary[p].astype(BF16)
        dthird = nt(ds, value)
        agreed = jnp.sum(dsummary[p] * summary[p], axis=-1, keepdims=True)
        slope = third * (dthird - agreed) * scale
        dv = nn(third.T.astype(BF16), ds)
        dql = dql + frame.block(nn(slope.astype(BF16), key))
        dk = nn(slope.T.astype(BF16), qs[p][0])
        dql = ((dql[:M] + dql[M:]) * frame.inv).astype(BF16)
        dkl = ((dkl[:M] + dkl[M:]) * frame.inv).astype(BF16)
        out_ref[0, :, c] = (dq[p] + nn(frame.member_t, dql)).astype(BF16)
        out_ref[1, :, c] = (dk + nn(frame.member_t, dkl)).astype(BF16)
        inside = (value.astype(F32) * frame.valid).astype(BF16)
        rows_pair = [taps_turned[pl.ds(head0 + 2 * p + i, 1), :] for i in range(2)]
        dv = dv + frame.valid * frame.conv(rows_pair, grad_low[p])
        out_ref[2, :, c] = dv.astype(BF16)
        for i in range(2):
            product = nt(grad_low[p] * frame.keep[i], inside)
            taps_out(2 * p + i, frame.diagonals(product))
        yield


def norm_rows(r, gain, shift):
    centre = r - jnp.mean(r, axis=-1, keepdims=True)
    spread = lax.rsqrt(jnp.mean(centre * centre, axis=-1, keepdims=True) + 1e-05)
    normed = centre * spread
    return normed * gain + shift, normed, spread


def norm_rows_back(dy, normed, spread, gain):
    scaled = dy * gain
    result = spread * (
        scaled
        - jnp.mean(scaled, axis=-1, keepdims=True)
        - normed * jnp.mean(scaled * normed, axis=-1, keepdims=True)
    )
    return (
        result,
        jnp.sum(dy * normed, axis=0, keepdims=True),
        jnp.sum(dy, axis=0, keepdims=True),
    )


GELU_A = 0.7978845608028654
GELU_B = 0.044715


def gelu_both(u):
    square = u * u
    t = jnp.tanh(GELU_A * (u + GELU_B * u * square))
    half = 0.5 * (1.0 + t)
    slope = half + 0.5 * u * (1.0 - t * t) * (GELU_A + (3.0 * GELU_A * GELU_B) * square)
    return u * half, slope


class Reduction:
    def __init__(self, sems):
        dp, self.mp = lax.axis_index("dp"), lax.axis_index("mp")
        z = dp // 4
        self.x = (dp // 2) % 2
        self.core = dp % 2
        self.upper = z // 2
        self.inner = (z == 1) | (z == 2)
        self.outer = (z == 0) | (z == 3)
        self.to_core = dp + 1 - 2 * self.core
        self.to_x = dp + 2 - 4 * self.x
        self.to_near = dp + 4 - 8 * (z % 2)
        self.to_mid = (3 - z) * 4 + dp % 4
        self.sems = sems
        self.pieces = []

    def greet(self, barrier):
        for other in (self.to_core, self.to_x, self.to_near, self.to_mid):
            pl.semaphore_signal(barrier, inc=1, device_id=(other, self.mp), device_id_type=MESH)

    def add(self, rows, kind, view, slots, credit, gives, takes):
        self.pieces.append((rows // 4, kind, view, slots, credit, gives, takes))

    def copy(self, index, slot, source, target, to, sent=None):
        sent = slot if sent is None else sent
        return pltpu.make_async_remote_copy(
            src_ref=source,
            dst_ref=target,
            send_sem=self.sems["ring_send"].at[index * 8 + sent],
            recv_sem=self.sems["ring_receive"].at[index * 8 + slot],
            device_id=(to, self.mp),
            device_id_type=MESH,
        )

    def event(self, index, step):
        quarter, kind, view, slots, credit, gives, takes = self.pieces[index]
        x, core, upper = self.x, self.core, self.upper
        side = x if kind == 0 else upper

        def region(half, which, count=1):
            start = (half * 2 + which) * quarter
            return view(start, count * quarter)

        def arrived(slot, ref):
            self.copy(index, slot, ref, ref, self.to_core).wait_recv()

        def sent(slot, ref):
            self.copy(index, slot, ref, ref, self.to_core).wait_send()

        def send(slot, source, destination, to, sem=None, need=None):
            if takes and need is not None:
                pl.semaphore_wait(self.sems["credit"].at[credit * 4 + need], 1)
            self.copy(index, slot, source, destination, to, sem).start()

        def free(which, to):
            if gives:
                pl.semaphore_signal(
                    self.sems["credit"].at[credit * 4 + which],
                    inc=1,
                    device_id=(to, self.mp),
                    device_id_type=MESH,
                )

        def ready(which, slot, ref, to):
            sent(slot, ref)
            pl.semaphore_signal(
                self.sems["ready"].at[index * 4 + which],
                inc=1,
                device_id=(to, self.mp),
                device_id_type=MESH,
            )

        def await_ready(which):
            pl.semaphore_wait(self.sems["ready"].at[index * 4 + which], 1)

        def slot_part(name, which):
            return slots[name].at[pl.ds(pl.multiple_of(which * quarter, 16), quarter)]

        def sum_into(ref, others):
            block = 48 if quarter % 48 == 0 else 16

            def step_rows(i, unused):
                span = pl.ds(pl.multiple_of(i * block, 16), block)
                total = ref[span, :].astype(F32)
                for other in others:
                    total = total + other[span, :].astype(F32)
                ref[span, :] = total.astype(BF16)
                return unused

            lax.fori_loop(0, quarter // block, step_rows, 0)

        mine, other = region(core, side), region(core, 1 - side)
        if step == 0:
            send(0, region(1 - core, 0, 2), slots["core"], self.to_core, need=0)
        elif step == 7:
            for slot, which in ((6, side), (7, 1 - side)):
                arrived(slot, region(1 - core, which))
            sent(6, mine)
            sent(7, other)
            if kind == 0:
                sent(5, mine)

                @pl.when(self.inner)
                def _():
                    sent(4, mine)

            else:

                @pl.when(self.inner)
                def _():
                    for slot in (2, 4, 5):
                        sent(slot, mine)

        elif kind == 0:
            if step == 1:
                arrived(0, slots["core"])
                sum_into(other, [slot_part("core", 1 - x)])
                send(1, other, slots["x"], self.to_x, need=1)
                ready(0, 0, region(1 - core, 0, 2), self.to_core)
            elif step == 2:

                @pl.when(self.outer)
                def _():
                    arrived(1, slots["x"])
                    sum_into(mine, [slot_part("core", x), slots["x"]])
                    free(0, self.to_core)
                    free(1, self.to_x)
                    send(2, mine, slots["near"], self.to_near, need=2)
                    ready(1, 1, other, self.to_x)

            elif step == 3:

                @pl.when(self.inner)
                def _():
                    arrived(1, slots["x"])
                    arrived(2, slots["near"])
                    sum_into(mine, [slot_part("core", x), slots["x"], slots["near"]])
                    free(0, self.to_core)
                    free(1, self.to_x)
                    free(2, self.to_near)
                    send(3, mine, slots["mid"], self.to_mid, need=3)
                    ready(1, 1, other, self.to_x)

                @pl.when(self.outer)
                def _():
                    ready(2, 2, mine, self.to_near)

            elif step == 4:

                @pl.when(self.inner)
                def _():
                    arrived(3, slots["mid"])
                    sent(3, mine)
                    sum_into(mine, [slots["mid"]])
                    free(3, self.to_mid)
                    await_ready(2)
                    send(4, mine, mine, self.to_near)
                    await_ready(1)
                    send(5, mine, mine, self.to_x)
                    await_ready(0)
                    send(6, mine, mine, self.to_core)

            elif step == 5:

                @pl.when(self.outer)
                def _():
                    arrived(4, mine)
                    await_ready(1)
                    send(5, mine, mine, self.to_x)
                    await_ready(0)
                    send(6, mine, mine, self.to_core)

            elif step == 6:
                arrived(5, other)
                send(7, other, other, self.to_core)
        else:
            if step == 1:

                @pl.when(self.outer)
                def _():
                    arrived(0, slots["core"])
                    sum_into(region(core, 0), [slot_part("core", 0)])
                    sum_into(region(core, 1), [slot_part("core", 1)])
                    free(0, self.to_core)
                    send(2, region(core, 0, 2), slots["near"], self.to_near, need=2)
                    ready(0, 0, region(1 - core, 0, 2), self.to_core)

            elif step == 2:

                @pl.when(self.outer)
                def _():
                    ready(2, 2, region(core, 0, 2), self.to_near)

                @pl.when(self.inner)
                def _():
                    arrived(0, slots["core"])
                    arrived(2, slots["near"])
                    sum_into(other, [slot_part("core", 1 - side), slot_part("near", 1 - side)])
                    send(3, other, slots["mid"], self.to_mid, need=3)
                    ready(0, 0, region(1 - core, 0, 2), self.to_core)

            elif step == 3:

                @pl.when(self.inner)
                def _():
                    arrived(3, slots["mid"])
                    sum_into(mine, [slot_part("core", side), slot_part("near", side), slots["mid"]])
                    free(0, self.to_core)
                    free(2, self.to_near)
                    free(3, self.to_mid)
                    send(1, mine, slots["x"], self.to_x, need=1)
                    ready(3, 3, other, self.to_mid)

            elif step == 4:

                @pl.when(self.inner)
                def _():
                    arrived(1, slots["x"])
                    sent(1, mine)
                    sum_into(mine, [slots["x"]])
                    free(1, self.to_x)
                    await_ready(3)
                    send(4, mine, mine, self.to_mid)
                    await_ready(2)
                    send(4, mine, mine, self.to_near, sem=2)
                    await_ready(0)
                    send(6, mine, mine, self.to_core)

            elif step == 5:

                @pl.when(self.inner)
                def _():
                    arrived(4, other)
                    send(5, other, other, self.to_near)
                    send(7, other, other, self.to_core)

                @pl.when(self.outer)
                def _():
                    arrived(4, mine)
                    await_ready(0)
                    send(6, mine, mine, self.to_core)

            elif step == 6:

                @pl.when(self.outer)
                def _():
                    arrived(5, other)
                    send(7, other, other, self.to_core)


class SmallSum:
    def __init__(self, ring, total, slots, sems, first_tap):
        self.ring, self.total, self.slots, self.sems, self.first_tap = ring, total, slots, sems, first_tap

    def copy(self, slot, target, to, mp):
        return pltpu.make_async_remote_copy(
            src_ref=self.total,
            dst_ref=target,
            send_sem=self.sems["small_send"].at[slot],
            recv_sem=self.sems["small_receive"].at[slot],
            device_id=(to, mp),
            device_id_type=MESH,
        )

    def event(self, step):
        ring, total, slots = self.ring, self.total, self.slots
        dp = ring.to_core + 2 * ring.core - 1

        def start(slot, to, mp=None):
            self.copy(slot, slots.at[slot], to, ring.mp if mp is None else mp).start()

        def take(slot):
            self.copy(slot, slots.at[slot], dp, ring.mp).wait_recv()

        def sent(slot):
            self.copy(slot, slots.at[slot], dp, ring.mp).wait_send()

        if step == 0:
            start(0, dp, 1 - ring.mp)
        elif step == 1:
            take(0)
            sent(0)
            total[self.first_tap :, :] += slots[0, self.first_tap :, :]
            start(1, ring.to_core)
        elif step == 2:
            take(1)
            sent(1)
            total[...] += slots[1]
            start(2, ring.to_x)
        elif step == 3:
            take(2)
            sent(2)
            total[...] += slots[2]

            @pl.when(ring.outer)
            def _():
                start(3, ring.to_near)

        elif step == 4:

            @pl.when(ring.inner)
            def _():
                take(3)
                total[...] += slots[3]
                start(4, ring.to_mid)

        elif step == 5:

            @pl.when(ring.inner)
            def _():
                take(4)
                sent(4)
                total[...] += slots[4]
                start(5, ring.to_near)

        elif step == 6:

            @pl.when(ring.outer)
            def _():
                take(5)
                sent(3)
                total[...] = slots[5]

            @pl.when(ring.inner)
            def _():
                sent(5)


def whole_step(
    length_ref,
    tokens_ref,
    cotangent_ref,
    raw_taps_ref,
    gains_ref,
    shifts_ref,
    projection_hbm,
    output_hbm,
    up_hbm,
    down_hbm,
    activations_ref,
    token_grad_ref,
    small_ref,
    down_grad_ref,
    up_grad_ref,
    other_grad_ref,
    weights,
    kept,
    work,
    wire,
    slots,
    sems,
):
    rows, width = tokens_ref.shape
    columns = projection_hbm.shape[3]
    hidden = up_hbm.shape[2]
    heads, _, reach = raw_taps_ref.shape
    grads = dict(down=down_grad_ref, up=up_grad_ref, other=other_grad_ref)
    size_h = width // heads
    half = rows // 2
    tile = 384
    dp, mp = lax.axis_index("dp"), lax.axis_index("mp")
    head0 = mp * (columns // size_h)
    partner = (dp, 1 - mp)

    loads = []
    order = [(projection_hbm, "projection"), (output_hbm, "output"), (up_hbm, "up"), (down_hbm, "down")]
    for layer in range(LAYERS):
        for index, (source, name) in enumerate(order):
            load = pltpu.make_async_copy(
                source.at[layer], weights[name].at[layer], sems["load"].at[layer * 4 + index]
            )
            load.start()
            loads.append(load)

    barrier = pltpu.get_barrier_semaphore()
    pl.semaphore_signal(barrier, inc=1, device_id=partner, device_id_type=MESH)
    ring = Reduction(sems)
    ring.greet(barrier)
    pl.semaphore_wait(barrier, 5)

    frame = Frame(length_ref[0], rows, size_h)
    taps_ref, turned_ref = work["taps"], work["turned"]
    taps_ref[...] = jnp.zeros_like(taps_ref)
    mirror = iota((rows, rows), 0) + iota((rows, rows), 1) == reach - 1
    mirror = mirror.astype(F32).astype(BF16)
    for layer in range(LAYERS):
        taps_ref[layer, :heads, :reach] = raw_taps_ref[:, layer, :]
        turned_ref[layer] = nn(taps_ref[layer].astype(BF16), mirror)
    flights = {}

    def send(slot, piece, partial_value):
        span = pl.ds(piece * half, half)
        wire["send"][slot % 2, span, :] = partial_value.astype(BF16)
        copy = pltpu.make_async_remote_copy(
            src_ref=wire["send"].at[slot % 2, span],
            dst_ref=wire["receive"].at[slot % 2, span],
            send_sem=sems["send"].at[slot * 2 + piece],
            recv_sem=sems["receive"].at[slot * 2 + piece],
            device_id=partner,
            device_id_type=MESH,
        )
        copy.start()
        flights[slot, piece] = copy

    def arrived(slot, piece):
        span = pl.ds(piece * half, half)
        flights[slot, piece].wait()
        return wire["send"][slot % 2, span, :].astype(F32) + wire["receive"][
            slot % 2, span, :
        ].astype(F32)

    pieces = [slice(0, half), slice(half, rows)]
    valid = [frame.valid[c] for c in pieces]

    def project(layer, piece):
        c = pieces[piece]
        for i in range(3):
            kept["qkv"][layer, i, c, :] = nn(
                work["x_low"][c, :], weights["projection"][layer, i]
            ).astype(BF16)

    def keep_of(layer):
        names = ("ql", "kl", "second", "inverse", "first", "third", "summary", "carried")
        return {name: kept[name].at[layer] for name in names}

    work["x"][...] = tokens_ref[...].astype(F32)
    work["x_low"][...] = tokens_ref[...]
    loads[0].wait()
    for piece in range(2):
        project(0, piece)
    for layer in range(LAYERS):
        attention(
            frame,
            kept["qkv"].at[layer],
            taps_ref.at[layer],
            head0,
            size_h,
            keep_of(layer),
            work["mixed"],
        )
        loads[layer * 4 + 1].wait()
        slot = layer * 2
        for piece, c in enumerate(pieces):
            send(slot, piece, nn(work["mixed"][c, :], weights["output"][layer]))
        kept["mixed_t"][layer] = work["mixed"][...].T
        kept["x_t"][layer] = work["x_low"][...].T
        loads[layer * 4 + 2].wait()
        loads[layer * 4 + 3].wait()
        for piece, c in enumerate(pieces):
            summed = work["x"][c, :] + arrived(slot, piece)
            y, normed, spread = norm_rows(summed, gains_ref[layer, 0:1], shifts_ref[layer, 0:1])
            kept["normed"][layer, 0, c, :] = normed.astype(BF16)
            kept["spread"][layer, 0, c, :] = spread
            work["y"][c, :] = y
            work["y_low"][c, :] = y.astype(BF16)
            for j in range(hidden // tile):
                span = slice(j * tile, (j + 1) * tile)
                u = nn(work["y_low"][c, :], weights["up"][layer, :, span])
                active, slope = gelu_both(u)
                work["active"][c, span] = active.astype(BF16)
                kept["slope"][layer, c, span] = slope.astype(BF16)
            send(slot + 1, piece, nn(work["active"][c, :], weights["down"][layer]))
        kept["active_t"][layer] = work["active"][...].T
        kept["y_t"][layer] = work["y_low"][...].T
        if layer + 1 < LAYERS:
            loads[layer * 4 + 4].wait()
        for piece, c in enumerate(pieces):
            summed = work["y"][c, :] + arrived(slot + 1, piece)
            y, normed, spread = norm_rows(summed, gains_ref[layer, 1:2], shifts_ref[layer, 1:2])
            kept["normed"][layer, 1, c, :] = normed.astype(BF16)
            kept["spread"][layer, 1, c, :] = spread
            if layer + 1 < LAYERS:
                work["x"][c, :] = y
                work["x_low"][c, :] = y.astype(BF16)
                project(layer + 1, piece)
            else:
                activations_ref[c, :] = (y * valid[piece]).astype(BF16)

    def add_pieces(layer):
        for k, (name, rows_of, kind) in enumerate(pieces_of(width, columns, hidden)):
            index = 0 if name != "projection" else 1 + sum(
                1 for item in pieces_of(width, columns, hidden)[:k] if item[0] == name
            )
            before = sum(
                item[1] for item in pieces_of(width, columns, hidden)[:k] if item[0] == name
            )

            def span(start, count, before=before):
                return pl.ds(pl.multiple_of(before + start, 16), count)

            if name in ("down", "up"):

                def view(start, count, span=span, name=name):
                    return grads[name].at[layer, span(start, count)]

            else:

                def view(start, count, index=index):
                    return grads["other"].at[layer, index, pl.ds(pl.multiple_of(start, 16), count)]

            ring.add(rows_of, kind, view, slots[k], k, layer > 0, layer + 1 < LAYERS)

    for layer in reversed(range(LAYERS)):
        add_pieces(layer)
    small = SmallSum(ring, small_ref, wire["small"], sems, 8)
    dy_ref, dr_ref, e_ref, du_ref = work["x"], work["y"], work["y_low"], work["active"]

    def norm_back(layer, which):
        gain = gains_ref[layer, which : which + 1]
        gain_sum = shift_sum = 0.0
        for c in pieces:
            result, gain_part, shift_part = norm_rows_back(
                dy_ref[c, :],
                kept["normed"][layer, which, c, :].astype(F32),
                kept["spread"][layer, which, c, :],
                gain,
            )
            dr_ref[c, :] = result
            e_ref[c, :] = result.astype(BF16)
            gain_sum, shift_sum = gain_sum + gain_part, shift_sum + shift_part
        row = layer * 2 + which
        small_ref[row : row + 1, :] = gain_sum
        small_ref[row + 4 : row + 5, :] = shift_sum

    def backward():
        small_ref[...] = jnp.zeros_like(small_ref)
        for piece, c in enumerate(pieces):
            dy_ref[c, :] = cotangent_ref[c, :].astype(F32) * valid[piece]
        for layer in reversed(range(LAYERS)):
            slot = 4 + (LAYERS - 1 - layer) * 2
            norm_back(layer, 1)
            yield
            block = hidden // DOWN_PIECES
            for j in range(DOWN_PIECES):
                span = slice(j * block, (j + 1) * block)
                grads["down"][layer, span, :] = nn(
                    kept["active_t"][layer, span, :], e_ref[...]
                ).astype(BF16)
                yield
            for j in range(hidden // tile):
                span = slice(j * tile, (j + 1) * tile)
                dh = nt(e_ref[...], weights["down"][layer, span, :])
                du_ref[:, span] = (dh * kept["slope"][layer, :, span].astype(F32)).astype(BF16)
            yield
            for piece, c in enumerate(pieces):
                send(slot, piece, nt(du_ref[c, :], weights["up"][layer]))
                yield
            block = width // UP_PIECES
            for j in range(UP_PIECES):
                span = slice(j * block, (j + 1) * block)
                grads["up"][layer, span, :] = nn(kept["y_t"][layer, span, :], du_ref[...]).astype(
                    BF16
                )
                yield
            for piece, c in enumerate(pieces):
                dy_ref[c, :] = dr_ref[c, :] + arrived(slot, piece)
            norm_back(layer, 0)
            yield
            for piece, c in enumerate(pieces):
                work["dmixed"][c, :] = nt(e_ref[c, :], weights["output"][layer]) * valid[piece]
            yield
            for j in range(2):
                span = slice(j * columns, (j + 1) * columns)
                grads["other"][layer, 0, span, :] = nn(
                    kept["mixed_t"][layer], e_ref[:, span]
                ).astype(BF16)
            yield

            def taps_out(head, row, layer=layer):
                small_ref[pl.ds(8 + layer * heads + head0 + head, 1), :rows] = row

            yield from attention_back(
                frame,
                work["dmixed"],
                kept["qkv"].at[layer],
                turned_ref.at[layer],
                head0,
                size_h,
                keep_of(layer),
                work["dqkv"],
                taps_out,
            )
            for piece, c in enumerate(pieces):
                total = 0.0
                for i in range(3):
                    total = total + nt(work["dqkv"][i, c, :], weights["projection"][layer, i])
                send(slot + 1, piece, total)
                yield
            for i in range(3):
                grads["other"][layer, 1 + i] = nn(kept["x_t"][layer], work["dqkv"][i]).astype(BF16)
                yield
            target = dy_ref if layer > 0 else token_grad_ref
            for piece, c in enumerate(pieces):
                target[c, :] = dr_ref[c, :] + arrived(slot + 1, piece)
        yield

    items = backward()
    for code in ORDER:
        if code < 0:
            next(items)
        elif code >= 1000:
            small.event(code - 1000)
        else:
            ring.event(code // 8, code % 8)


DOWN_PIECES = 4
UP_PIECES = 4
PIECE_KINDS = (1, 0, 0, 0, 1, 0, 0, 0, 1, 0, 1, 0)
ORDER = (
    -1, -1, 0, -1, 8, -1, 16, -1, 24, 1, -1, 17, 9, 25, -1, -1, -1, 32, -1, 40, -1, 48, -1, 56, 33, 41, 49,
    18, 57, 2, 10, 26, -1, 34, 3, -1, -1, 64, -1, 42, 19, 65, -1, -1, 50, -1, 35, 11, -1, -1, 58, 20, 27, -1,
    4, -1, -1, 43, 12, 36, -1, -1, 28, -1, -1, 72, 21, -1, 80, -1, 88, 66, 73, 81, 5, 89, 51, 44, 22, 13, 59,
    -1, 74, 90, 37, 29, -1, 96, 67, -1, 104, -1, 112, 14, 6, -1, 120, 97, -1, 113, 105, 121, 82, 45, 52, 30,
    -1, 75, 60, -1, 68, -1, 128, -1, 136, 38, -1, 91, 144, -1, 152, 129, 137, 83, 114, 145, 53, 153, 76, 98,
    106, 61, -1, 122, 69, -1, -1, 160, 46, -1, 161, 77, 92, 130, -1, 138, -1, 99, 70, -1, 115, -1, 146, -1,
    107, 131, 93, -1, 84, -1, 123, 54, 116, -1, -1, 1000, 154, -1, 108, -1, -1, 168, -1, 176, -1, 184, 62,
    162, 85, 169, 177, 1001, 117, 185, 78, 1002, 139, 124, 109, 94, 147, 163, 100, 155, 140, -1, 170, 86, 125,
    132, 148, 118, 178, 101, 186, 141, 110, 156, 171, 133, 187, 179, 1003, 1004, 172, 126, 149, 188, 164,
    1005, 142, 102, 127, 157, 150, 134, 103, 173, 158, 189, 63, 165, 1006, 180, 174, 166, 47, 181, 190, 167,
    79, 55, 39, 23, 71, 175, 159, 7, 119, 191, 111, 87, 95, 151, 182, 31, 15, 135, 143, 183,
)


def pieces_of(width, columns, hidden):
    names = ["down"] * DOWN_PIECES + ["up"] * UP_PIECES + ["output"] + ["projection"] * 3
    rows = {"down": hidden // DOWN_PIECES, "up": width // UP_PIECES, "output": width, "projection": width}
    return [(name, rows[name], kind) for name, kind in zip(names, PIECE_KINDS)]


def slots_of(name, rows, kind, width, columns, hidden):
    across = {"down": width, "up": hidden, "output": columns, "projection": columns}[name]

    def room(count):
        return pltpu.VMEM((count, across), BF16)

    return dict(
        core=room(rows // 2),
        x=room(rows // 4),
        near=room(rows // 4 if kind == 0 else rows // 2),
        mid=room(rows // 4),
    )


def fused_body(tokens, lengths, cotangent, projection, conv_taps, output_weight, norm_gains, norm_shifts, up_weight, down_weight):
    rows, width = tokens.shape
    columns, hidden = projection.shape[3], up_weight.shape[2]
    heads, reach = conv_taps.shape[1:]
    size_h = width // heads
    pairs = columns // (2 * size_h)
    by_kind = jnp.transpose(projection, (0, 2, 1, 3))
    by_head = jnp.transpose(conv_taps, (1, 0, 2))
    vmem = pl.BlockSpec(memory_space=pltpu.VMEM)
    hbm = pl.BlockSpec(memory_space=pl.ANY)
    two = 2 * M
    pieces = pieces_of(width, columns, hidden)
    scratch = (
        dict(
            projection=pltpu.VMEM((LAYERS, 3, width, columns), BF16),
            output=pltpu.VMEM((LAYERS, columns, width), BF16),
            up=pltpu.VMEM((LAYERS, width, hidden), BF16),
            down=pltpu.VMEM((LAYERS, hidden, width), BF16),
        ),
        dict(
            qkv=pltpu.VMEM((LAYERS, 3, rows, columns), BF16),
            ql=pltpu.VMEM((LAYERS, M, columns), F32),
            kl=pltpu.VMEM((LAYERS, M, columns), F32),
            second=pltpu.VMEM((LAYERS, pairs, two, two), F32),
            inverse=pltpu.VMEM((LAYERS, NEWTON + 1, pairs, two, two), F32),
            first=pltpu.VMEM((LAYERS, rows, columns), BF16),
            third=pltpu.VMEM((LAYERS, pairs, two, rows), BF16),
            summary=pltpu.VMEM((LAYERS, pairs, two, two), F32),
            carried=pltpu.VMEM((LAYERS, pairs, two, two), F32),
            normed=pltpu.VMEM((LAYERS, 2, rows, width), BF16),
            spread=pltpu.VMEM((LAYERS, 2, rows, 1), F32),
            slope=pltpu.VMEM((LAYERS, rows, hidden), BF16),
            x_t=pltpu.VMEM((LAYERS, width, rows), BF16),
            mixed_t=pltpu.VMEM((LAYERS, columns, rows), BF16),
            y_t=pltpu.VMEM((LAYERS, width, rows), BF16),
            active_t=pltpu.VMEM((LAYERS, hidden, rows), BF16),
        ),
        dict(
            x=pltpu.VMEM((rows, width), F32),
            x_low=pltpu.VMEM((rows, width), BF16),
            y=pltpu.VMEM((rows, width), F32),
            y_low=pltpu.VMEM((rows, width), BF16),
            mixed=pltpu.VMEM((rows, columns), BF16),
            active=pltpu.VMEM((rows, hidden), BF16),
            dmixed=pltpu.VMEM((rows, columns), F32),
            dqkv=pltpu.VMEM((3, rows, columns), BF16),
            taps=pltpu.VMEM((LAYERS, 16, rows), F32),
            turned=pltpu.VMEM((LAYERS, 16, rows), F32),
        ),
        dict(
            send=pltpu.VMEM((2, rows, width), BF16),
            receive=pltpu.VMEM((2, rows, width), BF16),
            small=pltpu.VMEM((6, 8 + LAYERS * heads, width), F32),
        ),
        [slots_of(*item, width, columns, hidden) for item in pieces],
        dict(
            load=pltpu.SemaphoreType.DMA((4 * LAYERS,)),
            ring_send=pltpu.SemaphoreType.DMA((8 * len(pieces) * LAYERS,)),
            ring_receive=pltpu.SemaphoreType.DMA((8 * len(pieces) * LAYERS,)),
            small_send=pltpu.SemaphoreType.DMA((6,)),
            small_receive=pltpu.SemaphoreType.DMA((6,)),
            credit=pltpu.SemaphoreType.REGULAR((4 * len(pieces),)),
            ready=pltpu.SemaphoreType.REGULAR((4 * len(pieces) * LAYERS,)),
            send=pltpu.SemaphoreType.DMA((8 * LAYERS,)),
            receive=pltpu.SemaphoreType.DMA((8 * LAYERS,)),
        ),
    )
    own = pltpu.VMEM
    results = pl.pallas_call(
        whole_step,
        out_shape=[
            own((rows, width), BF16),
            own((rows, width), F32),
            own((8 + LAYERS * heads, width), F32),
            own((LAYERS, hidden, width), BF16),
            own((LAYERS, width, hidden), BF16),
            own((LAYERS, 4, width, columns), BF16),
        ],
        in_specs=[pl.BlockSpec(memory_space=pltpu.SMEM)] + [vmem] * 5 + [hbm] * 4,
        out_specs=[vmem] * 6,
        scratch_shapes=scratch,
        compiler_params=pltpu.CompilerParams(
            collective_id=0, has_side_effects=True, vmem_limit_bytes=VMEM_ROOM
        ),
    )(
        lengths,
        tokens,
        cotangent,
        by_head,
        norm_gains,
        norm_shifts,
        by_kind,
        output_weight,
        up_weight,
        down_weight,
    )
    shape = jax.ShapeDtypeStruct
    held = [pltpu.with_memory_space_constraint(result, pltpu.VMEM) for result in results]
    wide = [
        (LAYERS, hidden, width),
        (LAYERS, width, hidden),
        (LAYERS, 3, width, columns),
        (LAYERS, columns, width),
    ]
    outputs = pl.pallas_call(
        widen,
        out_shape=[shape(size, F32) for size in wide]
        + [
            shape((rows, width), BF16),
            shape((rows, width), F32),
            shape((heads, LAYERS, reach), F32),
            shape((LAYERS, 2, width), F32),
            shape((LAYERS, 2, width), F32),
        ],
        in_specs=[vmem] * 6,
        out_specs=[hbm] * 4 + [vmem] * 5,
        scratch_shapes=[pltpu.VMEM(size, F32) for size in wide] + [pltpu.SemaphoreType.DMA((LAYERS * (2 * WIDE_PARTS + 4),))],
        compiler_params=pltpu.CompilerParams(vmem_limit_bytes=WIDE_ROOM),
    )(*held)
    down_grad, up_grad, projection_grad, output_grad = outputs[:4]
    activations, token_grad, taps_grad, gains_grad, shifts_grad = outputs[4:]
    return (
        activations,
        token_grad,
        jnp.transpose(projection_grad, (0, 2, 1, 3)),
        jnp.transpose(taps_grad, (1, 0, 2)),
        output_grad,
        gains_grad,
        shifts_grad,
        up_grad,
        down_grad,
    )


VMEM_ROOM = 47 * 2**20
WIDE_ROOM = 32 * 2**20
WIDE_PARTS = 4


def widen(
    activations_ref,
    token_grad_ref,
    small_ref,
    down_ref,
    up_ref,
    other_ref,
    down_hbm,
    up_hbm,
    projection_hbm,
    output_hbm,
    activations_out,
    token_grad_out,
    taps_out,
    gains_out,
    shifts_out,
    down_wide,
    up_wide,
    projection_wide,
    output_wide,
    sems,
):
    heads, _, reach = taps_out.shape
    columns = output_wide.shape[1]
    copies = []

    def send(source, target):
        copies.append(pltpu.make_async_copy(source, target, sems.at[len(copies)]))
        copies[-1].start()

    def cast(target, source, start, count):
        def step(i, unused):
            span = pl.ds(pl.multiple_of(start + i * 32, 32), 32)
            target[span, :] = source[span, :].astype(F32)
            return unused

        lax.fori_loop(0, count // 32, step, 0)

    for layer in range(LAYERS):
        for wide, source, hbm in ((down_wide, down_ref, down_hbm), (up_wide, up_ref, up_hbm)):
            count = source.shape[1] // WIDE_PARTS
            for part in range(WIDE_PARTS):
                cast(wide.at[layer], source.at[layer], part * count, count)
                span = pl.ds(part * count, count)
                send(wide.at[layer, span], hbm.at[layer, span])
        for i in range(3):
            cast(projection_wide.at[layer, i], other_ref.at[layer, 1 + i], 0, other_ref.shape[2])
            send(projection_wide.at[layer, i], projection_hbm.at[layer, i])
        for i in range(2):
            side = slice(i * columns, (i + 1) * columns)
            output_wide[layer, :, side] = other_ref[layer, 0, side, :].astype(F32)
        send(output_wide.at[layer], output_hbm.at[layer])
    activations_out[...] = activations_ref[...]
    token_grad_out[...] = token_grad_ref[...]
    for layer in range(LAYERS):
        gains_out[layer] = small_ref[2 * layer : 2 * layer + 2, :]
        shifts_out[layer] = small_ref[4 + 2 * layer : 6 + 2 * layer, :]
        first = 8 + layer * heads
        taps_out[:, layer, :] = small_ref[first : first + heads, :reach]
    for copy in copies:
        copy.wait()


def solution(mesh):
    fused = mesh.shape["mp"] == 2 and mesh.shape["dp"] == 16

    def step(*arrays):
        return (fused_body if fused else body)(*arrays)

    return jax.shard_map(
        step,
        mesh=mesh,
        in_specs=(
            P("dp", None),
            P("dp"),
            P("dp", None),
            P(None, None, None, "mp"),
            P(),
            P(None, "mp", None),
            P(),
            P(),
            P(None, None, "mp"),
            P(None, "mp", None),
        ),
        out_specs=(
            P("dp", None),
            P("dp", None),
            P(None, None, None, "mp"),
            P(),
            P(None, "mp", None),
            P(),
            P(),
            P(None, None, "mp"),
            P(None, "mp", None),
        ),
        check_vma=False,
    )
```

```python
import functools

import jax
import jax.numpy as jnp
from jax import lax
from jax.experimental import pallas as pl
from jax.experimental.pallas import tpu as pltpu
from jax.sharding import PartitionSpec as P

M = 64
NEWTON = 6
LAYERS = 2


highest_value = lax.Precision.HIGHEST


def merged(array, axis, join):
    gathered = jax.tree.map(
        lambda a, kind: lax.all_gather(a.astype(kind), axis),
        array,
        (jnp.bfloat16, jnp.bfloat16, jnp.bfloat16),
    )

    def take(source):
        return jax.tree.map(
            lambda a, own: lax.dynamic_index_in_dim(a, source, 0, False).astype(own.dtype),
            gathered,
            array,
        )

    return lax.fori_loop(
        1, lax.axis_size(axis), lambda source, state: join(state, take(source)), take(0)
    )


def for_sending(array):
    return jax.tree.map(lambda a: a.astype(jnp.bfloat16) if a.dtype == jnp.float32 else a, array)


def softmax_row_block(scores):
    top = jnp.max(scores, axis=-1, keepdims=True)
    matrix_powers = jnp.exp(scores - top)
    return matrix_powers / jnp.sum(matrix_powers, axis=-1, keepdims=True)


def slot_masks(length, count, marks):
    position = jnp.arange(count, dtype=jnp.int32)
    inside = position < length
    segment = position * marks // length
    member = (segment[None, :] == jnp.arange(marks, dtype=jnp.int32)[:, None]) & inside[None, :]
    member = member.astype(jnp.float32)
    pooling = member / jnp.sum(member, axis=1, keepdims=True)
    return (pooling, inside.astype(jnp.float32))


def inverse_head(query_landmarks, key_landmarks, summary):
    scale_factor = query_landmarks.shape[-1] ** (-0.5)
    second = softmax_row_block(
        jnp.dot(query_landmarks, key_landmarks.T, precision=highest_value) * scale_factor
    )
    identity = jnp.eye(second.shape[0], dtype=jnp.float32)
    inverse = second.T / jnp.sum(second * second)
    for sweep in range(NEWTON):
        product = jnp.dot(second, inverse, precision=highest_value)
        inner = 7.0 * identity - product
        inner = 15.0 * identity - jnp.dot(product, inner, precision=highest_value)
        inner = 13.0 * identity - jnp.dot(product, inner, precision=highest_value)
        inverse = 0.25 * jnp.dot(inverse, inner, precision=highest_value)
    return jnp.dot(inverse, summary, precision=highest_value)


def inverse_section(query_landmarks, key_landmarks, summary):
    return jax.vmap(inverse_head)(query_landmarks, key_landmarks, summary)


def near_section(query_matrix, key_landmarks, carried_over):
    scale_factor = query_matrix.shape[-1] ** (-0.5)
    first_entry = softmax_row_block(
        jnp.einsum("nlv,lgv->lng", query_matrix, key_landmarks, precision=highest_value)
        * scale_factor
    )
    return jnp.einsum("xtz,xzb->txb", first_entry, carried_over, precision=highest_value)


def far_scores(query_landmarks, key_matrix, valid_own):
    scale_factor = query_landmarks.shape[-1] ** (-0.5)
    distant_scores = (
        jnp.einsum("owz,toz->owt", query_landmarks, key_matrix, precision=highest_value)
        * scale_factor
    )
    live = valid_own[None, None, :] > 0
    return (jnp.where(live, distant_scores, -1e30), live)


def join_softmax(left, right):
    peak = jnp.maximum(left[0], right[0])
    left_factor = jnp.exp(left[0] - peak)
    right_factor = jnp.exp(right[0] - peak)
    return (
        peak,
        left[1] * left_factor + right[1] * right_factor,
        left[2] * left_factor[..., None] + right[2] * right_factor[..., None],
    )


def attend(query_matrix, key_matrix, value_matrix, pooled_local, valid_own):
    query_portion = jnp.einsum("ji,ilk->ljk", pooled_local, query_matrix, precision=highest_value)
    key_portion = jnp.einsum("ji,ilk->ljk", pooled_local, key_matrix, precision=highest_value)
    query_landmarks, key_landmarks = (
        lax.psum(query_portion.astype(jnp.bfloat16), "mp").astype(jnp.float32),
        lax.psum(key_portion.astype(jnp.bfloat16), "mp").astype(jnp.float32),
    )
    distant_scores, live = far_scores(query_landmarks, key_matrix, valid_own)
    peak = jnp.max(distant_scores, axis=-1)
    matrix_powers = jnp.where(live, jnp.exp(distant_scores - peak[..., None]), 0.0)
    totals = jnp.sum(matrix_powers, axis=-1)
    weighted_values = jnp.einsum(
        "naw,wno->nao", matrix_powers, value_matrix, precision=highest_value
    )
    peak, totals, weighted_values = merged((peak, totals, weighted_values), "mp", join_softmax)
    summary = weighted_values / totals[..., None]
    carried_over = inverse_section(query_landmarks, key_landmarks, summary)
    mixed = near_section(query_matrix, key_landmarks, carried_over)
    return (mixed, (query_landmarks, key_landmarks, peak, totals, summary))


def attend_back(
    grad_rows, query_matrix, key_matrix, value_matrix, pooled_local, valid_own, saved, tap_part
):
    query_landmarks, key_landmarks, peak, totals, summary = saved
    scale_factor = query_matrix.shape[-1] ** (-0.5)
    carried_over, inverse_back = jax.vjp(inverse_section, query_landmarks, key_landmarks, summary)
    unused, near_back = jax.vjp(near_section, query_matrix, key_landmarks, carried_over)
    query_grad, kland_part, carried_part = near_back(grad_rows)
    key_landmark_nearby, carried_grad, tap_grad = (
        lax.psum(kland_part.astype(jnp.bfloat16), "mp").astype(jnp.float32),
        lax.psum(carried_part.astype(jnp.bfloat16), "mp").astype(jnp.float32),
        lax.psum(tap_part.astype(jnp.bfloat16), "mp").astype(jnp.float32),
    )
    query_landmark_gradient, key_landmark_gradient, summary_gradient = inverse_back(carried_grad)
    distant_scores, live = far_scores(query_landmarks, key_matrix, valid_own)
    weight_spread = jnp.where(
        live, jnp.exp(distant_scores - peak[..., None]) / totals[..., None], 0.0
    )
    moving_along = jnp.einsum(
        "owz,toz->owt", summary_gradient, value_matrix, precision=highest_value
    )
    agreed = jnp.sum(summary_gradient * summary, axis=-1)
    slope_values = weight_spread * (moving_along - agreed[..., None])
    value_gradient = jnp.einsum(
        "ofq,ofn->qon", weight_spread, summary_gradient, precision=highest_value
    )
    query_landmark_remote = (
        jnp.einsum("naw,wno->nao", slope_values, key_matrix, precision=highest_value) * scale_factor
    )
    key_gradient = (
        jnp.einsum("ofq,ofn->qon", slope_values, query_landmarks, precision=highest_value)
        * scale_factor
    )
    query_landmark_remote = lax.psum(query_landmark_remote.astype(jnp.bfloat16), "mp").astype(
        jnp.float32
    )
    query_grad = query_grad + jnp.einsum(
        "ge,xgl->exl",
        pooled_local,
        query_landmark_gradient + query_landmark_remote,
        precision=highest_value,
    )
    key_gradient = key_gradient + jnp.einsum(
        "ge,xgl->exl",
        pooled_local,
        key_landmark_gradient + key_landmark_nearby,
        precision=highest_value,
    )
    return (query_grad, key_gradient, value_gradient, tap_grad)


def head_table(columns, heads, size_h):
    begin = lax.axis_index("mp") * columns
    owner = (begin + jnp.arange(columns, dtype=jnp.int32)) // size_h
    return (owner[None, :] == jnp.arange(heads, dtype=jnp.int32)[:, None]).astype(jnp.float32)


def convolve(value_cols, taps, table, valid):
    tap_cols = jnp.dot(taps.T, table, precision=highest_value)
    masked = value_cols * valid[:, None]
    reach = taps.shape[1] // 2
    padded = jnp.pad(masked, ((reach, reach), (0, 0)))
    length_rows = masked.shape[0]
    convolved = jnp.zeros_like(masked)
    for offset in range(taps.shape[1]):
        convolved = convolved + tap_cols[offset] * padded[offset : offset + length_rows]
    return convolved


def contract(left, right, left_dim, right_dim):
    return lax.dot_general(
        left, right, (((left_dim,), (right_dim,)), ((), ())), preferred_element_type=jnp.float32
    )


def normalize(resid, gain, shift):
    centre = resid - jnp.mean(resid, axis=-1, keepdims=True)
    spread = lax.rsqrt(jnp.mean(centre * centre, axis=-1, keepdims=True) + 1e-05)
    normed = centre * spread
    return (normed * gain + shift, normed, spread)


def normalize_back(upstream, normed, spread, gain):
    scaled = upstream * gain
    result = spread * (
        scaled
        - jnp.mean(scaled, axis=-1, keepdims=True)
        - normed * jnp.mean(scaled * normed, axis=-1, keepdims=True)
    )
    return (result, jnp.sum(upstream * normed, axis=0), jnp.sum(upstream, axis=0))


def own_rows(whole):
    count = whole.shape[0] // lax.axis_size("mp")
    return lax.dynamic_slice_in_dim(whole, lax.axis_index("mp") * count, count, 0)


def whole_rows(share):
    return lax.all_gather(share.astype(jnp.bfloat16), "mp", axis=0, tiled=True).astype(share.dtype)


def row_sums(partial_value):
    return lax.psum_scatter(
        partial_value.astype(jnp.bfloat16), "mp", scatter_dimension=0, tiled=True
    ).astype(jnp.float32)


def add_norm(partial_value, resid, gain, shift):
    summed = row_sums(partial_value)
    output, normed, spread = normalize(own_rows(resid) + summed, gain, shift)
    output = whole_rows(output)
    return (output, normed, spread)


def norm_step_back(upstream, normed, spread, gain):
    result, gain_part, shift_part = normalize_back(upstream, normed, spread, gain)
    whole = whole_rows(result)
    return (result, whole, gain_part, shift_part)


def add_input_grad(result, partial_value):
    total = result + row_sums(partial_value)
    return total


def forward_layer(hidden, weights, pooling_own, valid, valid_own):
    projection, taps, output_weight, gains, shifts, up_weight, down_weight = weights
    count, width = hidden.shape
    heads = taps.shape[0]
    size_h = width // heads
    columns = projection.shape[2]
    entering = hidden.astype(jnp.bfloat16)
    mixed = jnp.einsum(
        "td,dsc->tsc", entering, projection, preferred_element_type=jnp.float32
    ).astype(jnp.bfloat16)
    gathered = lax.all_to_all(mixed, "mp", split_axis=0, concat_axis=2, tiled=True)
    rows = gathered.shape[0]
    split_rows = gathered.astype(jnp.float32).reshape(rows, 3, heads, size_h)
    attended, saved = attend(
        split_rows[:, 0], split_rows[:, 1], split_rows[:, 2], pooling_own, valid_own
    )
    attended_cols = lax.all_to_all(
        for_sending(attended.reshape(rows, width)), "mp", split_axis=1, concat_axis=0, tiled=True
    )
    table = head_table(columns, heads, size_h)
    value_cols = mixed[:, 2].astype(jnp.float32)
    convolved = convolve(value_cols, taps, table, valid)
    joined = ((attended_cols + convolved) * valid[:, None]).astype(jnp.bfloat16)
    partial_value = jnp.dot(joined, output_weight, preferred_element_type=jnp.float32)
    middle, normed_first, spread_first = add_norm(partial_value, hidden, gains[0], shifts[0])
    entering_ffn = middle.astype(jnp.bfloat16)
    upward = jnp.dot(entering_ffn, up_weight, preferred_element_type=jnp.float32)
    active = jax.nn.gelu(upward, approximate=True).astype(jnp.bfloat16)
    partial_value = jnp.dot(active, down_weight, preferred_element_type=jnp.float32)
    output, normed_second, spread_second = add_norm(partial_value, middle, gains[1], shifts[1])
    kept = (
        entering,
        value_cols,
        split_rows,
        saved,
        joined,
        table,
        normed_first,
        spread_first,
        entering_ffn,
        upward,
        active,
        normed_second,
        spread_second,
    )
    return (output, kept)


def backward_layer(upstream, weights, kept, pooling_own, valid, valid_own):
    projection, taps, output_weight, gains, shifts, up_weight, down_weight = weights
    (
        entering,
        value_cols,
        split_rows,
        saved,
        joined,
        table,
        normed_first,
        spread_first,
        entering_ffn,
        upward,
        active,
        normed_second,
        spread_second,
    ) = kept
    count, width = entering.shape
    rows = split_rows.shape[0]
    heads = taps.shape[0]
    size_h = width // heads
    result_second, whole_second, gain_second, shift_second = norm_step_back(
        upstream, normed_second, spread_second, gains[1]
    )
    sent_second = whole_second.astype(jnp.bfloat16)
    down_grad = contract(active, sent_second, 0, 0)
    hidden_grad = contract(sent_second, down_weight, 1, 1)
    unused, gelu_back = jax.vjp(lambda value: jax.nn.gelu(value, approximate=True), upward)
    upward_sent = gelu_back(hidden_grad)[0].astype(jnp.bfloat16)
    up_grad = contract(entering_ffn, upward_sent, 0, 0)
    middle_grad = add_input_grad(result_second, contract(upward_sent, up_weight, 1, 1))
    result_first, whole_first, gain_first, shift_first = norm_step_back(
        middle_grad, normed_first, spread_first, gains[0]
    )
    sent_first = whole_first.astype(jnp.bfloat16)
    out_grad = contract(joined, sent_first, 0, 0)
    joined_grad = contract(sent_first, output_weight, 1, 1)
    masked_grad = joined_grad * valid[:, None]
    unused, conv_back = jax.vjp(
        lambda values, tap_rows: convolve(values, tap_rows, table, valid), value_cols, taps
    )
    conv_value_grad, tap_part = conv_back(masked_grad)
    row_grad = (
        lax.all_to_all(
            masked_grad.astype(jnp.bfloat16), "mp", split_axis=0, concat_axis=1, tiled=True
        )
        .astype(masked_grad.dtype)
        .reshape(rows, heads, size_h)
    )
    query_grad, key_gradient, value_gradient, tap_grad = attend_back(
        row_grad,
        split_rows[:, 0],
        split_rows[:, 1],
        split_rows[:, 2],
        pooling_own,
        valid_own,
        saved,
        tap_part,
    )
    stacked_rows = jnp.stack([query_grad, key_gradient, value_gradient], axis=1).reshape(
        rows, 3, width
    )
    column_grad = lax.all_to_all(
        for_sending(stacked_rows), "mp", split_axis=2, concat_axis=0, tiled=True
    ).astype(stacked_rows.dtype)
    column_grad = jnp.concatenate(
        [column_grad[:, :2], (column_grad[:, 2] + conv_value_grad)[:, None]], axis=1
    )
    mixed_sent = column_grad.astype(jnp.bfloat16)
    proj_grad = jnp.einsum("td,tsc->dsc", entering, mixed_sent, preferred_element_type=jnp.float32)
    below = add_input_grad(
        result_first,
        jnp.einsum("tsc,dsc->td", mixed_sent, projection, preferred_element_type=jnp.float32),
    )
    gain_grad = jnp.stack([gain_first, gain_second])
    shift_grad = jnp.stack([shift_first, shift_second])
    gain_grad, shift_grad = lax.psum((gain_grad, shift_grad), "mp")
    return (below, (proj_grad, tap_grad, out_grad, gain_grad, shift_grad, up_grad, down_grad))


def sum_layer(parts):
    return (
        lax.psum(parts[0].astype(jnp.bfloat16), "dp").astype(jnp.float32),
        lax.psum(parts[1].astype(jnp.bfloat16), "dp").astype(jnp.float32),
        lax.psum(parts[2].astype(jnp.bfloat16), "dp").astype(jnp.float32),
        lax.psum(parts[3].astype(jnp.bfloat16), "dp").astype(jnp.float32),
        lax.psum(parts[4].astype(jnp.bfloat16), "dp").astype(jnp.float32),
        lax.psum(parts[5].astype(jnp.bfloat16), "dp").astype(jnp.float32),
        lax.psum(parts[6].astype(jnp.bfloat16), "dp").astype(jnp.float32),
    )


def body(
    tokens,
    lengths,
    cotangent,
    projection,
    conv_taps,
    output_weight,
    norm_gains,
    norm_shifts,
    up_weight,
    down_weight,
):
    count = tokens.shape[0]
    pooling, valid = slot_masks(lengths[0], count, M)
    rows = count // lax.axis_size("mp")
    begin = lax.axis_index("mp") * rows
    pooling_own = lax.dynamic_slice_in_dim(pooling, begin, rows, 1)
    valid_own = lax.dynamic_slice_in_dim(valid, begin, rows, 0)
    weights = (
        projection,
        conv_taps,
        output_weight,
        norm_gains,
        norm_shifts,
        up_weight,
        down_weight,
    )
    hidden = tokens.astype(jnp.float32)
    keeping = []
    for layer_index in range(LAYERS):
        hidden, kept = forward_layer(
            hidden, tuple((item[layer_index] for item in weights)), pooling_own, valid, valid_own
        )
        keeping.append(kept)
    activations = (hidden * valid[:, None]).astype(jnp.bfloat16)
    upstream = cotangent.astype(jnp.float32) * valid[:, None]
    upstream = own_rows(upstream)
    collected = [None] * LAYERS
    for layer_index in reversed(range(LAYERS)):
        upstream, parts = backward_layer(
            upstream,
            tuple((item[layer_index] for item in weights)),
            keeping[layer_index],
            pooling_own,
            valid,
            valid_own,
        )
        collected[layer_index] = sum_layer(parts)
    stacked = tuple(
        (
            jnp.stack([collected[layer_index][member] for layer_index in range(LAYERS)])
            for member in range(7)
        )
    )
    upstream = whole_rows(upstream)
    return (
        activations,
        upstream,
        stacked[0],
        stacked[1],
        stacked[2],
        stacked[3],
        stacked[4],
        stacked[5],
        stacked[6],
    )


MESH = pl.DeviceIdType.MESH
F32 = jnp.float32
BF16 = jnp.bfloat16


def nn(a, b):
    return lax.dot_general(a, b, (((1,), (0,)), ((), ())), preferred_element_type=F32)


def nt(a, b):
    return lax.dot_general(a, b, (((1,), (1,)), ((), ())), preferred_element_type=F32)


def parts_of(x):
    high = x.astype(BF16)
    return high, (x - high.astype(F32)).astype(BF16)


def nn3(a, b):
    return nn(jnp.concatenate([a[0], a[1]], 1), jnp.concatenate([b[0], b[0]], 0)) + nn(a[0], b[1])


def nt3(a, b):
    return nt(jnp.concatenate([a[0], a[1]], 1), jnp.concatenate([b[0], b[0]], 1)) + nt(a[0], b[1])


def iota(shape, axis):
    return lax.broadcasted_iota(jnp.int32, shape, axis)


class Frame:
    def __init__(self, length, rows, size_h):
        self.length = length
        self.rows = rows
        self.lane0 = iota((1, 2 * size_h), 1) < size_h
        self.keep = [self.lane0.astype(F32).astype(BF16), (~self.lane0).astype(F32).astype(BF16)]
        self.diag = (iota((2 * M, 2 * M), 0) < M) == (iota((2 * M, 2 * M), 1) < M)
        self.ones = self.diag.astype(F32).astype(BF16)
        self.ones2 = jnp.concatenate([self.ones, self.ones], 0)
        j, t = iota((M, rows), 0), iota((M, rows), 1)
        member = (t * M >= j * length) & (t * M < (j + 1) * length)
        member = member.astype(F32)
        self.member = member.astype(BF16)
        self.inv = 1.0 / jnp.sum(member, axis=1, keepdims=True)
        t, j = iota((rows, M), 0), iota((rows, M), 1)
        self.member_t = ((t * M >= j * length) & (t * M < (j + 1) * length)).astype(F32).astype(BF16)
        self.valid = (iota((rows, 1), 0) < length).astype(F32)
        self.valid_lane = iota((1, rows), 1) < length
        self.band = jnp.abs(iota((rows, rows), 0) - iota((rows, rows), 1)) <= KREACH

    def stack(self, x):
        return jnp.where(self.diag, jnp.concatenate([x, x], 0), 0.0)

    def block(self, x):
        return jnp.where(self.diag, x, 0.0)

    def half_sums(self, x):
        high, low = parts_of(x)
        return nn(jnp.concatenate([high, low], 1), self.ones2)

    def toeplitz(self, row):
        spread = jnp.broadcast_to(row, (self.rows, self.rows))
        turned = pltpu.roll(spread, self.rows - KREACH, 1, stride=1, stride_axis=0)
        return jnp.where(self.band, turned, 0.0).astype(BF16)

    def conv(self, rows_pair, value):
        both = jnp.concatenate([self.toeplitz(rows_pair[0]), self.toeplitz(rows_pair[1])], 1)
        stacked = jnp.concatenate([value * self.keep[0], value * self.keep[1]], 0)
        return nn(both, stacked)

    def diagonals(self, product):
        banded = jnp.where(self.band, product, 0.0)
        total = banded[:8]
        for group in range(1, self.rows // 8):
            part = banded[8 * group : 8 * group + 8]
            total = total + pltpu.roll(part, self.rows - 8 * group, 1)
        total = pltpu.roll(total, KREACH, 1)
        result = total[:1]
        for row in range(1, 8):
            result = result + pltpu.roll(total[row : row + 1], self.rows - row, 1)
        return result


KREACH = 16


def softmax_masked(scores, live):
    scores = jnp.where(live, scores, -1e30)
    top = jnp.max(scores, axis=-1, keepdims=True)
    powers = jnp.where(live, jnp.exp(scores - top), 0.0)
    return powers / jnp.sum(powers, axis=-1, keepdims=True)


def attention(frame, qkv, taps, head0, size_h, keep, out_ref):
    scale = size_h ** (-0.5)
    pairs = qkv.shape[2] // (2 * size_h)
    ql = nn(frame.member, qkv[0]) * frame.inv
    kl = nn(frame.member, qkv[1]) * frame.inv
    keep["ql"][...] = ql
    keep["kl"][...] = kl
    cols = [slice(p * 2 * size_h, (p + 1) * 2 * size_h) for p in range(pairs)]
    qs = [parts_of(frame.stack(ql[:, c])) for c in cols]
    ks = [parts_of(frame.stack(kl[:, c])) for c in cols]
    second = [softmax_masked(nt3(qs[p], ks[p]) * scale, frame.diag) for p in range(pairs)]
    inverse = []
    halves = iota((2 * M, 1), 0) < M
    for p in range(pairs):
        keep["second"][p] = second[p]
        squares = jnp.sum(second[p] * second[p], axis=1, keepdims=True)
        first_total = jnp.sum(jnp.where(halves, squares, 0.0), axis=0, keepdims=True)
        other_total = jnp.sum(jnp.where(halves, 0.0, squares), axis=0, keepdims=True)
        inverse.append(second[p].T * (1.0 / jnp.where(halves, first_total, other_total)))
    second_parts = [parts_of(s) for s in second]
    for sweep in range(NEWTON):
        for p in range(pairs):
            keep["inverse"][sweep, p] = inverse[p]
        zp = [parts_of(z) for z in inverse]
        product = [nn3(second_parts[p], zp[p]) for p in range(pairs)]
        pp = [parts_of(x) for x in product]
        square = [nn3(pp[p], pp[p]) for p in range(pairs)]
        forward = [nn3(zp[p], pp[p]) for p in range(pairs)]
        last = [
            nn3(parts_of(forward[p]), parts_of(7.0 * product[p] - square[p])) for p in range(pairs)
        ]
        inverse = [
            0.25 * (13.0 * inverse[p] - 15.0 * forward[p] + last[p]) for p in range(pairs)
        ]
    for p in range(pairs):
        c = cols[p]
        keep["inverse"][NEWTON, p] = inverse[p]
        query, key, value = qkv[0, :, c], qkv[1, :, c], qkv[2, :, c]
        scores = nt(jnp.concatenate([query, query], 1), jnp.concatenate(ks[p], 1)) * scale
        top0 = jnp.max(jnp.where(frame.lane0, scores, -1e30), axis=-1, keepdims=True)
        top1 = jnp.max(jnp.where(frame.lane0, -1e30, scores), axis=-1, keepdims=True)
        powers = jnp.exp(scores - jnp.where(frame.lane0, top0, top1))
        first = (powers / frame.half_sums(powers)).astype(BF16)
        keep["first"][:, c] = first
        scores = nt(jnp.concatenate(qs[p], 1), jnp.concatenate([key, key], 1)) * scale
        third = softmax_masked(scores, frame.valid_lane).astype(BF16)
        keep["third"][p] = third
        summary = frame.block(nn(third, value))
        keep["summary"][p] = summary
        carried = nn3(parts_of(inverse[p]), parts_of(summary))
        keep["carried"][p] = carried
        mixed = nn(first, carried.astype(BF16))
        inside = (value.astype(F32) * frame.valid).astype(BF16)
        rows_pair = [taps[pl.ds(head0 + 2 * p + i, 1), :] for i in range(2)]
        mixed = (mixed + frame.conv(rows_pair, inside)) * frame.valid
        out_ref[:, c] = mixed.astype(BF16)


def attention_back(frame, grad, qkv, taps_turned, head0, size_h, keep, out_ref, taps_out):
    scale = size_h ** (-0.5)
    pairs = qkv.shape[2] // (2 * size_h)
    cols = [slice(p * 2 * size_h, (p + 1) * 2 * size_h) for p in range(pairs)]
    each = range(pairs)
    ql, kl = keep["ql"][...], keep["kl"][...]
    qs = [parts_of(frame.stack(ql[:, c])) for c in cols]
    ks = [parts_of(frame.stack(kl[:, c])) for c in cols]
    summary = [keep["summary"][p] for p in each]
    second = [keep["second"][p] for p in each]
    dq, dk_landmark, dcarried, grad_low = [], [], [], []
    for p in each:
        c = cols[p]
        g = grad[:, c].astype(BF16)
        grad_low.append(g)
        first = keep["first"][:, c].astype(F32)
        dfirst = nt(g, keep["carried"][p].astype(BF16))
        slope = first * dfirst
        slope = (slope - first * frame.half_sums(slope)) * scale
        dq.append(nn(slope.astype(BF16), ks[p][0]))
        dk_landmark.append(frame.block(nn(slope.T.astype(BF16), qkv[0, :, c])))
        dcarried.append(frame.block(nn(first.T.astype(BF16), g)))
    yield
    dcp = [parts_of(x) for x in dcarried]
    up = [nt3(dcp[p], parts_of(summary[p])) for p in each]
    dsummary = [nn3(parts_of(keep["inverse"][NEWTON, p].T), dcp[p]) for p in each]
    second_parts = [parts_of(s) for s in second]
    second_turned = [parts_of(s.T) for s in second]
    dsecond = [jnp.zeros_like(s) for s in second]
    for sweep in reversed(range(NEWTON)):
        inverse = [keep["inverse"][sweep, p] for p in each]
        zp = [parts_of(z) for z in inverse]
        product = [nn3(second_parts[p], zp[p]) for p in each]
        pp = [parts_of(x) for x in product]
        inner = [parts_of(7.0 * product[p] - nn3(pp[p], pp[p])) for p in each]
        forward_turned = [parts_of(nn3(zp[p], pp[p]).T) for p in each]
        product_turned = [parts_of(x.T) for x in product]
        inverse_turned = [parts_of(z.T) for z in inverse]
        upp = [parts_of(x) for x in up]
        dforward = [parts_of(0.25 * (nt3(upp[p], inner[p]) - 15.0 * up[p])) for p in each]
        dinner_full = [0.25 * nn3(forward_turned[p], upp[p]) for p in each]
        dinner = [parts_of(x) for x in dinner_full]
        dproduct = [
            parts_of(
                7.0 * dinner_full[p]
                - nt3(dinner[p], pp[p])
                - nn3(product_turned[p], dinner[p])
                + nn3(inverse_turned[p], dforward[p])
            )
            for p in each
        ]
        up = [
            3.25 * up[p] + nt3(dforward[p], pp[p]) + nn3(second_turned[p], dproduct[p])
            for p in each
        ]
        dsecond = [dsecond[p] + nt3(dproduct[p], zp[p]) for p in each]
        yield
    halves = iota((2 * M, 1), 0) < M
    for p in each:
        c = cols[p]
        query, key, value = qkv[0, :, c], qkv[1, :, c], qkv[2, :, c]
        squares = jnp.sum(second[p] * second[p], axis=1, keepdims=True)
        total0 = jnp.sum(jnp.where(halves, squares, 0.0), axis=0, keepdims=True)
        total1 = jnp.sum(jnp.where(halves, 0.0, squares), axis=0, keepdims=True)
        inverse_total = 1.0 / jnp.where(halves, total0, total1)
        start_agree = jnp.sum(up[p] * keep["inverse"][0, p], axis=1, keepdims=True)
        agree0 = jnp.sum(jnp.where(halves, start_agree, 0.0), axis=0, keepdims=True)
        agree1 = jnp.sum(jnp.where(halves, 0.0, start_agree), axis=0, keepdims=True)
        agree = jnp.where(halves, agree0, agree1)
        dsec = dsecond[p] + (up[p].T - 2.0 * agree * second[p]) * inverse_total
        slope = second[p] * dsec
        slope = (slope - second[p] * jnp.sum(slope, axis=-1, keepdims=True)) * scale
        dql = nn(slope.astype(BF16), ks[p][0])
        dkl = nn(slope.T.astype(BF16), qs[p][0]) + dk_landmark[p]
        third = keep["third"][p].astype(F32)
        ds = dsummary[p].astype(BF16)
        dthird = nt(ds, value)
        agreed = jnp.sum(dsummary[p] * summary[p], axis=-1, keepdims=True)
        slope = third * (dthird - agreed) * scale
        dv = nn(third.T.astype(BF16), ds)
        dql = dql + frame.block(nn(slope.astype(BF16), key))
        dk = nn(slope.T.astype(BF16), qs[p][0])
        dql = ((dql[:M] + dql[M:]) * frame.inv).astype(BF16)
        dkl = ((dkl[:M] + dkl[M:]) * frame.inv).astype(BF16)
        out_ref[0, :, c] = (dq[p] + nn(frame.member_t, dql)).astype(BF16)
        out_ref[1, :, c] = (dk + nn(frame.member_t, dkl)).astype(BF16)
        inside = (value.astype(F32) * frame.valid).astype(BF16)
        rows_pair = [taps_turned[pl.ds(head0 + 2 * p + i, 1), :] for i in range(2)]
        dv = dv + frame.valid * frame.conv(rows_pair, grad_low[p])
        out_ref[2, :, c] = dv.astype(BF16)
        for i in range(2):
            product = nt(grad_low[p] * frame.keep[i], inside)
            taps_out(2 * p + i, frame.diagonals(product))
        yield


def norm_rows(r, gain, shift):
    centre = r - jnp.mean(r, axis=-1, keepdims=True)
    spread = lax.rsqrt(jnp.mean(centre * centre, axis=-1, keepdims=True) + 1e-05)
    normed = centre * spread
    return normed * gain + shift, normed, spread


def norm_rows_back(dy, normed, spread, gain):
    scaled = dy * gain
    result = spread * (
        scaled
        - jnp.mean(scaled, axis=-1, keepdims=True)
        - normed * jnp.mean(scaled * normed, axis=-1, keepdims=True)
    )
    return (
        result,
        jnp.sum(dy * normed, axis=0, keepdims=True),
        jnp.sum(dy, axis=0, keepdims=True),
    )


GELU_A = 0.7978845608028654
GELU_B = 0.044715


def gelu_both(u):
    square = u * u
    t = jnp.tanh(GELU_A * (u + GELU_B * u * square))
    half = 0.5 * (1.0 + t)
    slope = half + 0.5 * u * (1.0 - t * t) * (GELU_A + (3.0 * GELU_A * GELU_B) * square)
    return u * half, slope


class Reduction:
    def __init__(self, sems):
        dp, self.mp = lax.axis_index("dp"), lax.axis_index("mp")
        z = dp // 4
        self.x = (dp // 2) % 2
        self.core = dp % 2
        self.upper = z // 2
        self.inner = (z == 1) | (z == 2)
        self.outer = (z == 0) | (z == 3)
        self.to_core = dp + 1 - 2 * self.core
        self.to_x = dp + 2 - 4 * self.x
        self.to_near = dp + 4 - 8 * (z % 2)
        self.to_mid = (3 - z) * 4 + dp % 4
        self.sems = sems
        self.pieces = []

    def greet(self, barrier):
        for other in (self.to_core, self.to_x, self.to_near, self.to_mid):
            pl.semaphore_signal(barrier, inc=1, device_id=(other, self.mp), device_id_type=MESH)

    def add(self, rows, kind, view, slots, credit, gives, takes, other_kind):
        self.pieces.append((rows // 4, kind, view, slots, credit, gives, takes, other_kind))

    def copy(self, index, slot, source, target, to, sent=None):
        sent = slot if sent is None else sent
        return pltpu.make_async_remote_copy(
            src_ref=source,
            dst_ref=target,
            send_sem=self.sems["ring_send"].at[index * 8 + sent],
            recv_sem=self.sems["ring_receive"].at[index * 8 + slot],
            device_id=(to, self.mp),
            device_id_type=MESH,
        )

    def event(self, index, step):
        quarter, kind, view, slots, credit, gives, takes, other_kind = self.pieces[index]
        x, core, upper = self.x, self.core, self.upper
        side = x if kind == 0 else upper

        def region(half, which, count=1):
            start = (half * 2 + which) * quarter
            return view(start, count * quarter)

        def arrived(slot, ref):
            self.copy(index, slot, ref, ref, self.to_core).wait_recv()

        def sent(slot, ref):
            self.copy(index, slot, ref, ref, self.to_core).wait_send()

        def send(slot, source, destination, to, sem=None, need=None):
            if takes and need is not None:
                pl.semaphore_wait(self.sems["credit"].at[credit * 4 + need], 1)
            self.copy(index, slot, source, destination, to, sem).start()

        def free(which, to):
            if gives:
                pl.semaphore_signal(
                    self.sems["credit"].at[credit * 4 + which],
                    inc=1,
                    device_id=(to, self.mp),
                    device_id_type=MESH,
                )

        def ready(which, slot, ref, to):
            sent(slot, ref)
            pl.semaphore_signal(
                self.sems["ready"].at[index * 4 + which],
                inc=1,
                device_id=(to, self.mp),
                device_id_type=MESH,
            )

        def await_ready(which):
            pl.semaphore_wait(self.sems["ready"].at[index * 4 + which], 1)

        def slot_part(name, which):
            return slots[name].at[pl.ds(pl.multiple_of(which * quarter, 16), quarter)]

        def sum_into(ref, others):
            block = 48 if quarter % 48 == 0 else 16

            def step_rows(i, unused):
                span = pl.ds(pl.multiple_of(i * block, 16), block)
                total = ref[span, :].astype(F32)
                for other in others:
                    total = total + other[span, :].astype(F32)
                ref[span, :] = total.astype(BF16)
                return unused

            lax.fori_loop(0, quarter // block, step_rows, 0)

        mine, other = region(core, side), region(core, 1 - side)
        if step == 0:
            send(0, region(1 - core, 0, 2), slots["core"], self.to_core, need=0)
        elif step == 7:
            for slot, which in ((6, side), (7, 1 - side)):
                arrived(slot, region(1 - core, which))
            sent(6, mine)
            sent(7, other)
            if kind == 0:
                sent(5, mine)

                @pl.when(self.inner)
                def _():
                    sent(4, mine)

            else:

                @pl.when(self.inner)
                def _():
                    for slot in (2, 4, 5):
                        sent(slot, mine)

        elif kind == 0:
            if step == 1:
                arrived(0, slots["core"])
                sum_into(other, [slot_part("core", 1 - x)])
                if other_kind == 0:
                    send(1, other, slots["x"], self.to_x, need=1)
                else:
                    if takes:

                        @pl.when(self.inner)
                        def _():
                            pl.semaphore_wait(self.sems["credit"].at[credit * 4 + 1], 1)

                    send(1, other, slots["x"], self.to_x)
                ready(0, 0, region(1 - core, 0, 2), self.to_core)
            elif step == 2:

                @pl.when(self.outer)
                def _():
                    arrived(1, slots["x"])
                    sum_into(mine, [slot_part("core", x), slots["x"]])
                    free(0, self.to_core)
                    if other_kind == 0:
                        free(1, self.to_x)
                    send(2, mine, slot_part("near", 0), self.to_near, need=2)
                    ready(1, 1, other, self.to_x)

            elif step == 3:

                @pl.when(self.inner)
                def _():
                    arrived(1, slots["x"])
                    arrived(2, slot_part("near", 0))
                    sum_into(mine, [slot_part("core", x), slots["x"], slot_part("near", 0)])
                    free(0, self.to_core)
                    free(1, self.to_x)
                    free(2, self.to_near)
                    send(3, mine, slots["mid"], self.to_mid, need=3)
                    ready(1, 1, other, self.to_x)

                @pl.when(self.outer)
                def _():
                    ready(2, 2, mine, self.to_near)

            elif step == 4:

                @pl.when(self.inner)
                def _():
                    arrived(3, slots["mid"])
                    sent(3, mine)
                    sum_into(mine, [slots["mid"]])
                    free(3, self.to_mid)
                    await_ready(2)
                    send(4, mine, mine, self.to_near)
                    await_ready(1)
                    send(5, mine, mine, self.to_x)
                    await_ready(0)
                    send(6, mine, mine, self.to_core)

            elif step == 5:

                @pl.when(self.outer)
                def _():
                    arrived(4, mine)
                    await_ready(1)
                    send(5, mine, mine, self.to_x)
                    await_ready(0)
                    send(6, mine, mine, self.to_core)

            elif step == 6:
                arrived(5, other)
                send(7, other, other, self.to_core)
        else:
            if step == 1:

                @pl.when(self.outer)
                def _():
                    arrived(0, slots["core"])
                    sum_into(region(core, 0), [slot_part("core", 0)])
                    sum_into(region(core, 1), [slot_part("core", 1)])
                    free(0, self.to_core)
                    send(2, region(core, 0, 2), slots["near"], self.to_near, need=2)
                    ready(0, 0, region(1 - core, 0, 2), self.to_core)

            elif step == 2:

                @pl.when(self.outer)
                def _():
                    ready(2, 2, region(core, 0, 2), self.to_near)

                @pl.when(self.inner)
                def _():
                    arrived(0, slots["core"])
                    arrived(2, slots["near"])
                    sum_into(other, [slot_part("core", 1 - side), slot_part("near", 1 - side)])
                    send(3, other, slots["mid"], self.to_mid, need=3)
                    ready(0, 0, region(1 - core, 0, 2), self.to_core)

            elif step == 3:

                @pl.when(self.inner)
                def _():
                    arrived(3, slots["mid"])
                    sum_into(mine, [slot_part("core", side), slot_part("near", side), slots["mid"]])
                    free(0, self.to_core)
                    free(2, self.to_near)
                    free(3, self.to_mid)
                    send(1, mine, slots["x"], self.to_x, need=1)
                    ready(3, 3, other, self.to_mid)

            elif step == 4:

                @pl.when(self.inner)
                def _():
                    arrived(1, slots["x"])
                    sent(1, mine)
                    sum_into(mine, [slots["x"]])
                    free(1, self.to_x)
                    await_ready(3)
                    send(4, mine, mine, self.to_mid)
                    await_ready(2)
                    send(4, mine, mine, self.to_near, sem=2)
                    await_ready(0)
                    send(6, mine, mine, self.to_core)

            elif step == 5:

                @pl.when(self.inner)
                def _():
                    arrived(4, other)
                    send(5, other, other, self.to_near)
                    send(7, other, other, self.to_core)

                @pl.when(self.outer)
                def _():
                    arrived(4, mine)
                    await_ready(0)
                    send(6, mine, mine, self.to_core)

            elif step == 6:

                @pl.when(self.outer)
                def _():
                    arrived(5, other)
                    send(7, other, other, self.to_core)


class SmallSum:
    def __init__(self, ring, total, slots, sems, first_tap):
        self.ring, self.total, self.slots, self.sems, self.first_tap = ring, total, slots, sems, first_tap

    def copy(self, slot, target, to, mp):
        return pltpu.make_async_remote_copy(
            src_ref=self.total,
            dst_ref=target,
            send_sem=self.sems["small_send"].at[slot],
            recv_sem=self.sems["small_receive"].at[slot],
            device_id=(to, mp),
            device_id_type=MESH,
        )

    def event(self, step):
        ring, total, slots = self.ring, self.total, self.slots
        dp = ring.to_core + 2 * ring.core - 1

        def start(slot, to, mp=None):
            self.copy(slot, slots.at[slot], to, ring.mp if mp is None else mp).start()

        def take(slot):
            self.copy(slot, slots.at[slot], dp, ring.mp).wait_recv()

        def sent(slot):
            self.copy(slot, slots.at[slot], dp, ring.mp).wait_send()

        if step == 0:
            start(0, dp, 1 - ring.mp)
        elif step == 1:
            take(0)
            sent(0)
            total[self.first_tap :, :] += slots[0, self.first_tap :, :]
            start(1, ring.to_core)
        elif step == 2:
            take(1)
            sent(1)
            total[...] += slots[1]
            start(2, ring.to_x)
        elif step == 3:
            take(2)
            sent(2)
            total[...] += slots[2]

            @pl.when(ring.outer)
            def _():
                start(3, ring.to_near)

        elif step == 4:

            @pl.when(ring.inner)
            def _():
                take(3)
                total[...] += slots[3]
                start(4, ring.to_mid)

        elif step == 5:

            @pl.when(ring.inner)
            def _():
                take(4)
                sent(4)
                total[...] += slots[4]
                start(5, ring.to_near)

        elif step == 6:

            @pl.when(ring.outer)
            def _():
                take(5)
                sent(3)
                total[...] = slots[5]

            @pl.when(ring.inner)
            def _():
                sent(5)


def whole_step(
    length_ref,
    tokens_ref,
    cotangent_ref,
    raw_taps_ref,
    gains_ref,
    shifts_ref,
    projection_hbm,
    output_hbm,
    up_hbm,
    down_hbm,
    activations_ref,
    token_grad_ref,
    small_ref,
    down_grad_ref,
    up_grad_ref,
    other_grad_ref,
    weights,
    kept,
    work,
    wire,
    slots,
    sems,
):
    rows, width = tokens_ref.shape
    columns = projection_hbm.shape[3]
    hidden = up_hbm.shape[2]
    heads, _, reach = raw_taps_ref.shape
    grads = dict(down=down_grad_ref, up=up_grad_ref, other=other_grad_ref)
    size_h = width // heads
    half = rows // 2
    tile = 384
    dp, mp = lax.axis_index("dp"), lax.axis_index("mp")
    head0 = mp * (columns // size_h)
    partner = (dp, 1 - mp)

    def own_half(layer):
        return weights["output"].at[layer, mp]

    loads = []
    order = [(projection_hbm, "projection"), (output_hbm, "output"), (up_hbm, "up"), (down_hbm, "down")]
    for layer in range(LAYERS):
        for index, (source, name) in enumerate(order):
            load = pltpu.make_async_copy(
                source.at[layer],
                own_half(layer) if name == "output" else weights[name].at[layer],
                sems["load"].at[layer * 4 + index],
            )
            load.start()
            loads.append(load)

    barrier = pltpu.get_barrier_semaphore()
    pl.semaphore_signal(barrier, inc=1, device_id=partner, device_id_type=MESH)
    ring = Reduction(sems)
    ring.greet(barrier)
    pl.semaphore_wait(barrier, 5)

    frame = Frame(length_ref[0], rows, size_h)
    taps_ref, turned_ref = work["taps"], work["turned"]
    taps_ref[...] = jnp.zeros_like(taps_ref)
    mirror = iota((rows, rows), 0) + iota((rows, rows), 1) == reach - 1
    mirror = mirror.astype(F32).astype(BF16)
    for layer in range(LAYERS):
        taps_ref[layer, :heads, :reach] = raw_taps_ref[:, layer, :]
        turned_ref[layer] = nn(taps_ref[layer].astype(BF16), mirror)
    flights = {}

    def send(slot, piece, partial_value):
        span = pl.ds(piece * half, half)
        wire["send"][slot % 2, span, :] = partial_value.astype(BF16)
        copy = pltpu.make_async_remote_copy(
            src_ref=wire["send"].at[slot % 2, span],
            dst_ref=wire["receive"].at[slot % 2, span],
            send_sem=sems["send"].at[slot * 2 + piece],
            recv_sem=sems["receive"].at[slot * 2 + piece],
            device_id=partner,
            device_id_type=MESH,
        )
        copy.start()
        flights[slot, piece] = copy

    def arrived(slot, piece):
        span = pl.ds(piece * half, half)
        flights[slot, piece].wait()
        return wire["send"][slot % 2, span, :].astype(F32) + wire["receive"][
            slot % 2, span, :
        ].astype(F32)

    def share_copy(layer, hop):
        part = columns // 2
        which, first = (mp, ring.core) if hop == 0 else (1 - mp, ring.core)
        place = weights["output"].at[layer, which, pl.ds(pl.multiple_of(first * part, 16), part)]
        return pltpu.make_async_remote_copy(
            src_ref=place,
            dst_ref=place,
            send_sem=sems["share_send"].at[layer * 2 + hop],
            recv_sem=sems["share_receive"].at[layer * 2 + hop],
            device_id=partner if hop == 0 else (ring.to_core, mp),
            device_id_type=MESH,
        )

    def gather_copy(layer, piece):
        place = work["mixed"].at[mp, pl.ds(piece * half, half)]
        return pltpu.make_async_remote_copy(
            src_ref=place,
            dst_ref=place,
            send_sem=sems["gather_send"].at[layer * 2 + piece],
            recv_sem=sems["gather_receive"].at[layer * 2 + piece],
            device_id=partner,
            device_id_type=MESH,
        )

    pieces = [slice(0, half), slice(half, rows)]
    valid = [frame.valid[c] for c in pieces]

    def project(layer, piece):
        c = pieces[piece]
        for i in range(3):
            kept["qkv"][layer, i, c, :] = nn(
                work["x_low"][c, :], weights["projection"][layer, i]
            ).astype(BF16)

    def keep_of(layer):
        names = ("ql", "kl", "second", "inverse", "first", "third", "summary", "carried")
        return {name: kept[name].at[layer] for name in names}

    work["x"][...] = tokens_ref[...].astype(F32)
    work["x_low"][...] = tokens_ref[...]
    loads[0].wait()
    for piece in range(2):
        project(0, piece)
    for layer in range(LAYERS):
        loads[layer * 4 + 1].wait()
        share_copy(layer, 0).start()
        attention(
            frame,
            kept["qkv"].at[layer],
            taps_ref.at[layer],
            head0,
            size_h,
            keep_of(layer),
            work["mixed"].at[mp],
        )
        slot = layer * 2
        for piece in range(2):
            gather_copy(layer, piece).start()
        share_copy(layer, 0).wait()
        share_copy(layer, 1).start()
        kept["mixed_t"][layer] = work["mixed"][mp].T
        kept["x_t"][layer] = work["x_low"][...].T
        loads[layer * 4 + 2].wait()
        loads[layer * 4 + 3].wait()
        share_copy(layer, 1).wait()
        for piece, c in enumerate(pieces):
            gather_copy(layer, piece).wait()
            summed = work["x"][c, :]
            for side in range(2):
                summed = summed + nn(work["mixed"][side, c, :], weights["output"][layer, side])
            y, normed, spread = norm_rows(summed, gains_ref[layer, 0:1], shifts_ref[layer, 0:1])
            kept["normed"][layer, 0, c, :] = normed.astype(BF16)
            kept["spread"][layer, 0, c, :] = spread
            work["y"][c, :] = y
            work["y_low"][c, :] = y.astype(BF16)
            for j in range(hidden // tile):
                span = slice(j * tile, (j + 1) * tile)
                u = nn(work["y_low"][c, :], weights["up"][layer, :, span])
                active, slope = gelu_both(u)
                work["active"][c, span] = active.astype(BF16)
                kept["slope"][layer, c, span] = slope.astype(BF16)
            send(slot + 1, piece, nn(work["active"][c, :], weights["down"][layer]))
        kept["active_t"][layer] = work["active"][...].T
        kept["y_t"][layer] = work["y_low"][...].T
        if layer + 1 < LAYERS:
            loads[layer * 4 + 4].wait()
        for piece, c in enumerate(pieces):
            summed = work["y"][c, :] + arrived(slot + 1, piece)
            y, normed, spread = norm_rows(summed, gains_ref[layer, 1:2], shifts_ref[layer, 1:2])
            kept["normed"][layer, 1, c, :] = normed.astype(BF16)
            kept["spread"][layer, 1, c, :] = spread
            if layer + 1 < LAYERS:
                work["x"][c, :] = y
                work["x_low"][c, :] = y.astype(BF16)
                project(layer + 1, piece)
            else:
                activations_ref[c, :] = (y * valid[piece]).astype(BF16)

    def add_pieces(layer):
        for k, (name, rows_of, kind) in enumerate(pieces_of(width, columns, hidden, layer)):
            index = 0 if name != "projection" else 1 + sum(
                1 for item in pieces_of(width, columns, hidden, layer)[:k] if item[0] == name
            )
            before = sum(
                item[1] for item in pieces_of(width, columns, hidden, layer)[:k] if item[0] == name
            )

            def span(start, count, before=before):
                return pl.ds(pl.multiple_of(before + start, 16), count)

            if name in ("down", "up"):

                def view(start, count, span=span, name=name):
                    return grads[name].at[layer, span(start, count)]

            else:

                def view(start, count, index=index):
                    return grads["other"].at[layer, index, pl.ds(pl.multiple_of(start, 16), count)]

            ring.add(rows_of, kind, view, slots[k], k, layer > 0, layer + 1 < LAYERS, PIECE_KINDS[1 - layer][k])

    for layer in reversed(range(LAYERS)):
        add_pieces(layer)
    small = SmallSum(ring, small_ref, wire["small"], sems, 8)
    dy_ref, dr_ref, e_ref, du_ref = work["x"], work["y"], work["y_low"], work["active"]

    def norm_back(layer, which):
        gain = gains_ref[layer, which : which + 1]
        gain_sum = shift_sum = 0.0
        for c in pieces:
            result, gain_part, shift_part = norm_rows_back(
                dy_ref[c, :],
                kept["normed"][layer, which, c, :].astype(F32),
                kept["spread"][layer, which, c, :],
                gain,
            )
            dr_ref[c, :] = result
            e_ref[c, :] = result.astype(BF16)
            gain_sum, shift_sum = gain_sum + gain_part, shift_sum + shift_part
        row = layer * 2 + which
        small_ref[row : row + 1, :] = gain_sum
        small_ref[row + 4 : row + 5, :] = shift_sum

    def backward():
        small_ref[...] = jnp.zeros_like(small_ref)
        for piece, c in enumerate(pieces):
            dy_ref[c, :] = cotangent_ref[c, :].astype(F32) * valid[piece]
        for layer in reversed(range(LAYERS)):
            slot = 4 + (LAYERS - 1 - layer) * 2
            norm_back(layer, 1)
            yield
            block = hidden // DOWN_PIECES
            for j in range(DOWN_PIECES):
                span = slice(j * block, (j + 1) * block)
                grads["down"][layer, span, :] = nn(
                    kept["active_t"][layer, span, :], e_ref[...]
                ).astype(BF16)
                yield
            for j in range(hidden // tile):
                span = slice(j * tile, (j + 1) * tile)
                dh = nt(e_ref[...], weights["down"][layer, span, :])
                du_ref[:, span] = (dh * kept["slope"][layer, :, span].astype(F32)).astype(BF16)
            yield
            for piece, c in enumerate(pieces):
                send(slot, piece, nt(du_ref[c, :], weights["up"][layer]))
                yield
            block = width // UP_PIECES
            for j in range(UP_PIECES):
                span = slice(j * block, (j + 1) * block)
                grads["up"][layer, span, :] = nn(kept["y_t"][layer, span, :], du_ref[...]).astype(
                    BF16
                )
                yield
            for piece, c in enumerate(pieces):
                dy_ref[c, :] = dr_ref[c, :] + arrived(slot, piece)
            norm_back(layer, 0)
            yield
            for piece, c in enumerate(pieces):
                work["dmixed"][c, :] = nt(e_ref[c, :], weights["output"][layer, mp]) * valid[piece]
            yield
            for j in range(2):
                span = slice(j * columns, (j + 1) * columns)
                grads["other"][layer, 0, span, :] = nn(
                    kept["mixed_t"][layer], e_ref[:, span]
                ).astype(BF16)
            yield

            def taps_out(head, row, layer=layer):
                small_ref[pl.ds(8 + layer * heads + head0 + head, 1), :rows] = row

            yield from attention_back(
                frame,
                work["dmixed"],
                kept["qkv"].at[layer],
                turned_ref.at[layer],
                head0,
                size_h,
                keep_of(layer),
                work["dqkv"],
                taps_out,
            )
            for piece, c in enumerate(pieces):
                total = 0.0
                for i in range(3):
                    total = total + nt(work["dqkv"][i, c, :], weights["projection"][layer, i])
                send(slot + 1, piece, total)
                yield
            for i in range(3):
                grads["other"][layer, 1 + i] = nn(kept["x_t"][layer], work["dqkv"][i]).astype(BF16)
                yield
            target = dy_ref if layer > 0 else token_grad_ref
            for piece, c in enumerate(pieces):
                target[c, :] = dr_ref[c, :] + arrived(slot + 1, piece)
        yield

    items = backward()
    for code in ORDER:
        if code < 0:
            next(items)
        elif code >= 1000:
            small.event(code - 1000)
        else:
            ring.event(code // 8, code % 8)


DOWN_PIECES = 4
UP_PIECES = 4
PIECE_KINDS = (
    (0, 0, 1, 0, 0, 0, 1, 1, 0, 0, 0, 0),
    (1, 1, 0, 0, 0, 0, 0, 0, 1, 1, 0, 1),
)
ORDER = (
    -1, -1, 0, -1, 8, -1, 16, -1, 24, 1, -1, 9, 17, -1, 25, -1, -1, 32, -1, 40, -1, 48, -1, 56, 33, 41, 49,
    18, 57, 2, 26, -1, 34, 10, 3, -1, -1, 64, -1, 42, 65, 19, -1, -1, 50, -1, 27, 11, -1, -1, 20, 35, 58, -1,
    -1, 4, 28, 43, -1, 12, -1, 36, -1, -1, -1, 21, 72, -1, 80, -1, 88, 66, 73, 5, 81, 89, 22, 29, 44, 51, 82,
    13, 59, -1, 37, 30, 67, -1, 96, -1, 104, -1, 112, -1, 6, 120, 97, 52, 74, -1, 113, 105, 38, 68, 45, 60,
    121, -1, -1, -1, 128, -1, 136, -1, 14, 75, 98, 144, 90, -1, 152, 129, 137, 145, 53, 106, 153, 83, 69, 46,
    91, -1, 61, 84, 114, 122, -1, -1, 160, -1, 70, 99, 130, 161, -1, -1, 76, 85, 138, 115, -1, -1, -1, 100,
    54, 146, -1, -1, 62, 77, 107, -1, -1, 92, 147, 1000, -1, 162, -1, 101, -1, 168, -1, 176, 154, -1, 108,
    184, 86, 169, 78, 177, 1001, 123, 185, 1002, 93, 116, 131, 155, 102, 139, 124, -1, 109, 94, 178, 170, 186,
    148, 163, 117, 79, 132, 140, 171, 179, 187, 164, 1003, 1004, 125, 110, 172, 156, 149, 180, 126, 118, 188,
    1005, 39, 133, 31, 141, 134, 165, 142, 173, 15, 157, 166, 150, 143, 181, 174, 189, 1006, 71, 182, 158, 47,
    190, 183, 63, 103, 23, 135, 151, 119, 159, 7, 191, 167, 175, 111, 127, 55, 95, 87,
)


def pieces_of(width, columns, hidden, layer):
    names = ["down"] * DOWN_PIECES + ["up"] * UP_PIECES + ["output"] + ["projection"] * 3
    rows = {"down": hidden // DOWN_PIECES, "up": width // UP_PIECES, "output": width, "projection": width}
    return [(name, rows[name], kind) for name, kind in zip(names, PIECE_KINDS[layer])]


def slots_of(name, rows, kind, width, columns, hidden):
    across = {"down": width, "up": hidden, "output": columns, "projection": columns}[name]

    def room(count):
        return pltpu.VMEM((count, across), BF16)

    return dict(
        core=room(rows // 2),
        x=room(rows // 4),
        near=room(rows // 4 if kind == 0 else rows // 2),
        mid=room(rows // 4),
    )


def fused_body(tokens, lengths, cotangent, projection, conv_taps, output_weight, norm_gains, norm_shifts, up_weight, down_weight):
    rows, width = tokens.shape
    columns, hidden = projection.shape[3], up_weight.shape[2]
    heads, reach = conv_taps.shape[1:]
    size_h = width // heads
    pairs = columns // (2 * size_h)
    by_kind = jnp.transpose(projection, (0, 2, 1, 3))
    by_head = jnp.transpose(conv_taps, (1, 0, 2))
    vmem = pl.BlockSpec(memory_space=pltpu.VMEM)
    hbm = pl.BlockSpec(memory_space=pl.ANY)
    two = 2 * M
    pieces = pieces_of(width, columns, hidden, 0)
    scratch = (
        dict(
            projection=pltpu.VMEM((LAYERS, 3, width, columns), BF16),
            output=pltpu.VMEM((LAYERS, 2, columns, width), BF16),
            up=pltpu.VMEM((LAYERS, width, hidden), BF16),
            down=pltpu.VMEM((LAYERS, hidden, width), BF16),
        ),
        dict(
            qkv=pltpu.VMEM((LAYERS, 3, rows, columns), BF16),
            ql=pltpu.VMEM((LAYERS, M, columns), F32),
            kl=pltpu.VMEM((LAYERS, M, columns), F32),
            second=pltpu.VMEM((LAYERS, pairs, two, two), F32),
            inverse=pltpu.VMEM((LAYERS, NEWTON + 1, pairs, two, two), F32),
            first=pltpu.VMEM((LAYERS, rows, columns), BF16),
            third=pltpu.VMEM((LAYERS, pairs, two, rows), BF16),
            summary=pltpu.VMEM((LAYERS, pairs, two, two), F32),
            carried=pltpu.VMEM((LAYERS, pairs, two, two), F32),
            normed=pltpu.VMEM((LAYERS, 2, rows, width), BF16),
            spread=pltpu.VMEM((LAYERS, 2, rows, 1), F32),
            slope=pltpu.VMEM((LAYERS, rows, hidden), BF16),
            x_t=pltpu.VMEM((LAYERS, width, rows), BF16),
            mixed_t=pltpu.VMEM((LAYERS, columns, rows), BF16),
            y_t=pltpu.VMEM((LAYERS, width, rows), BF16),
            active_t=pltpu.VMEM((LAYERS, hidden, rows), BF16),
        ),
        dict(
            x=pltpu.VMEM((rows, width), F32),
            x_low=pltpu.VMEM((rows, width), BF16),
            y=pltpu.VMEM((rows, width), F32),
            y_low=pltpu.VMEM((rows, width), BF16),
            mixed=pltpu.VMEM((2, rows, columns), BF16),
            active=pltpu.VMEM((rows, hidden), BF16),
            dmixed=pltpu.VMEM((rows, columns), F32),
            dqkv=pltpu.VMEM((3, rows, columns), BF16),
            taps=pltpu.VMEM((LAYERS, 16, rows), F32),
            turned=pltpu.VMEM((LAYERS, 16, rows), F32),
        ),
        dict(
            send=pltpu.VMEM((2, rows, width), BF16),
            receive=pltpu.VMEM((2, rows, width), BF16),
            small=pltpu.VMEM((6, 8 + LAYERS * heads, width), F32),
        ),
        [
            slots_of(name, count, max(kinds), width, columns, hidden)
            for (name, count, _), kinds in zip(pieces, zip(*PIECE_KINDS))
        ],
        dict(
            load=pltpu.SemaphoreType.DMA((4 * LAYERS,)),
            ring_send=pltpu.SemaphoreType.DMA((8 * len(pieces) * LAYERS,)),
            ring_receive=pltpu.SemaphoreType.DMA((8 * len(pieces) * LAYERS,)),
            small_send=pltpu.SemaphoreType.DMA((6,)),
            small_receive=pltpu.SemaphoreType.DMA((6,)),
            credit=pltpu.SemaphoreType.REGULAR((4 * len(pieces),)),
            ready=pltpu.SemaphoreType.REGULAR((4 * len(pieces) * LAYERS,)),
            share_send=pltpu.SemaphoreType.DMA((2 * LAYERS,)),
            share_receive=pltpu.SemaphoreType.DMA((2 * LAYERS,)),
            gather_send=pltpu.SemaphoreType.DMA((2 * LAYERS,)),
            gather_receive=pltpu.SemaphoreType.DMA((2 * LAYERS,)),
            send=pltpu.SemaphoreType.DMA((8 * LAYERS,)),
            receive=pltpu.SemaphoreType.DMA((8 * LAYERS,)),
        ),
    )
    own = pltpu.VMEM
    results = pl.pallas_call(
        whole_step,
        out_shape=[
            own((rows, width), BF16),
            own((rows, width), F32),
            own((8 + LAYERS * heads, width), F32),
            own((LAYERS, hidden, width), BF16),
            own((LAYERS, width, hidden), BF16),
            own((LAYERS, 4, width, columns), BF16),
        ],
        in_specs=[pl.BlockSpec(memory_space=pltpu.SMEM)] + [vmem] * 5 + [hbm] * 4,
        out_specs=[vmem] * 6,
        scratch_shapes=scratch,
        compiler_params=pltpu.CompilerParams(
            collective_id=0, has_side_effects=True, vmem_limit_bytes=VMEM_ROOM
        ),
    )(
        lengths,
        tokens,
        cotangent,
        by_head,
        norm_gains,
        norm_shifts,
        by_kind,
        output_weight,
        up_weight,
        down_weight,
    )
    shape = jax.ShapeDtypeStruct
    held = [pltpu.with_memory_space_constraint(result, pltpu.VMEM) for result in results]
    wide = [
        (LAYERS, hidden, width),
        (LAYERS, width, hidden),
        (LAYERS, 3, width, columns),
        (LAYERS, columns, width),
    ]
    outputs = pl.pallas_call(
        widen,
        out_shape=[shape(size, F32) for size in wide]
        + [
            shape((rows, width), BF16),
            shape((rows, width), F32),
            shape((heads, LAYERS, reach), F32),
            shape((LAYERS, 2, width), F32),
            shape((LAYERS, 2, width), F32),
        ],
        in_specs=[vmem] * 6,
        out_specs=[hbm] * 4 + [vmem] * 5,
        scratch_shapes=[pltpu.VMEM(size, F32) for size in wide] + [pltpu.SemaphoreType.DMA((LAYERS * (2 * WIDE_PARTS + 4),))],
        compiler_params=pltpu.CompilerParams(vmem_limit_bytes=WIDE_ROOM),
    )(*held)
    down_grad, up_grad, projection_grad, output_grad = outputs[:4]
    activations, token_grad, taps_grad, gains_grad, shifts_grad = outputs[4:]
    return (
        activations,
        token_grad,
        jnp.transpose(projection_grad, (0, 2, 1, 3)),
        jnp.transpose(taps_grad, (1, 0, 2)),
        output_grad,
        gains_grad,
        shifts_grad,
        up_grad,
        down_grad,
    )


VMEM_ROOM = 97 * 2**19
WIDE_ROOM = 32 * 2**20
WIDE_PARTS = 4


def widen(
    activations_ref,
    token_grad_ref,
    small_ref,
    down_ref,
    up_ref,
    other_ref,
    down_hbm,
    up_hbm,
    projection_hbm,
    output_hbm,
    activations_out,
    token_grad_out,
    taps_out,
    gains_out,
    shifts_out,
    down_wide,
    up_wide,
    projection_wide,
    output_wide,
    sems,
):
    heads, _, reach = taps_out.shape
    columns = output_wide.shape[1]
    copies = []

    def send(source, target):
        copies.append(pltpu.make_async_copy(source, target, sems.at[len(copies)]))
        copies[-1].start()

    def cast(target, source, start, count):
        def step(i, unused):
            span = pl.ds(pl.multiple_of(start + i * 32, 32), 32)
            target[span, :] = source[span, :].astype(F32)
            return unused

        lax.fori_loop(0, count // 32, step, 0)

    for layer in range(LAYERS):
        for wide, source, hbm in ((down_wide, down_ref, down_hbm), (up_wide, up_ref, up_hbm)):
            count = source.shape[1] // WIDE_PARTS
            for part in range(WIDE_PARTS):
                cast(wide.at[layer], source.at[layer], part * count, count)
                span = pl.ds(part * count, count)
                send(wide.at[layer, span], hbm.at[layer, span])
        for i in range(3):
            cast(projection_wide.at[layer, i], other_ref.at[layer, 1 + i], 0, other_ref.shape[2])
            send(projection_wide.at[layer, i], projection_hbm.at[layer, i])
        for i in range(2):
            side = slice(i * columns, (i + 1) * columns)
            output_wide[layer, :, side] = other_ref[layer, 0, side, :].astype(F32)
        send(output_wide.at[layer], output_hbm.at[layer])
    activations_out[...] = activations_ref[...]
    token_grad_out[...] = token_grad_ref[...]
    for layer in range(LAYERS):
        gains_out[layer] = small_ref[2 * layer : 2 * layer + 2, :]
        shifts_out[layer] = small_ref[4 + 2 * layer : 6 + 2 * layer, :]
        first = 8 + layer * heads
        taps_out[:, layer, :] = small_ref[first : first + heads, :reach]
    for copy in copies:
        copy.wait()


def solution(mesh):
    fused = mesh.shape["mp"] == 2 and mesh.shape["dp"] == 16

    def step(*arrays):
        return (fused_body if fused else body)(*arrays)

    return jax.shard_map(
        step,
        mesh=mesh,
        in_specs=(
            P("dp", None),
            P("dp"),
            P("dp", None),
            P(None, None, None, "mp"),
            P(),
            P(None, "mp", None),
            P(),
            P(),
            P(None, None, "mp"),
            P(None, "mp", None),
        ),
        out_specs=(
            P("dp", None),
            P("dp", None),
            P(None, None, None, "mp"),
            P(),
            P(None, "mp", None),
            P(),
            P(),
            P(None, None, "mp"),
            P(None, "mp", None),
        ),
        check_vma=False,
    )
```

```python
from typing import Any, NamedTuple

import jax
import jax.numpy as jnp
from jax import lax
from jax.experimental import pallas as pl
from jax.experimental.pallas import tpu as pltpu
from jax.sharding import PartitionSpec as P

M = 64
NEWTON = 6
LAYERS = 2


highest_value = lax.Precision.HIGHEST


def merged(array, axis, join):
    gathered = jax.tree.map(
        lambda a, kind: lax.all_gather(a.astype(kind), axis),
        array,
        (jnp.bfloat16, jnp.bfloat16, jnp.bfloat16),
    )

    def take(source):
        return jax.tree.map(
            lambda a, own: lax.dynamic_index_in_dim(a, source, 0, False).astype(own.dtype),
            gathered,
            array,
        )

    return lax.fori_loop(
        1, lax.axis_size(axis), lambda source, state: join(state, take(source)), take(0)
    )


def for_sending(array):
    return jax.tree.map(lambda a: a.astype(jnp.bfloat16) if a.dtype == jnp.float32 else a, array)


def softmax_row_block(scores):
    top = jnp.max(scores, axis=-1, keepdims=True)
    matrix_powers = jnp.exp(scores - top)
    return matrix_powers / jnp.sum(matrix_powers, axis=-1, keepdims=True)


def slot_masks(length, count, marks):
    position = jnp.arange(count, dtype=jnp.int32)
    inside = position < length
    segment = position * marks // length
    member = (segment[None, :] == jnp.arange(marks, dtype=jnp.int32)[:, None]) & inside[None, :]
    member = member.astype(jnp.float32)
    pooling = member / jnp.sum(member, axis=1, keepdims=True)
    return (pooling, inside.astype(jnp.float32))


def inverse_head(query_landmarks, key_landmarks, summary):
    scale_factor = query_landmarks.shape[-1] ** (-0.5)
    second = softmax_row_block(
        jnp.dot(query_landmarks, key_landmarks.T, precision=highest_value) * scale_factor
    )
    identity = jnp.eye(second.shape[0], dtype=jnp.float32)
    inverse = second.T / jnp.sum(second * second)
    for sweep in range(NEWTON):
        product = jnp.dot(second, inverse, precision=highest_value)
        inner = 7.0 * identity - product
        inner = 15.0 * identity - jnp.dot(product, inner, precision=highest_value)
        inner = 13.0 * identity - jnp.dot(product, inner, precision=highest_value)
        inverse = 0.25 * jnp.dot(inverse, inner, precision=highest_value)
    return jnp.dot(inverse, summary, precision=highest_value)


def inverse_section(query_landmarks, key_landmarks, summary):
    return jax.vmap(inverse_head)(query_landmarks, key_landmarks, summary)


def near_section(query_matrix, key_landmarks, carried_over):
    scale_factor = query_matrix.shape[-1] ** (-0.5)
    first_entry = softmax_row_block(
        jnp.einsum("nlv,lgv->lng", query_matrix, key_landmarks, precision=highest_value)
        * scale_factor
    )
    return jnp.einsum("xtz,xzb->txb", first_entry, carried_over, precision=highest_value)


def far_scores(query_landmarks, key_matrix, valid_own):
    scale_factor = query_landmarks.shape[-1] ** (-0.5)
    distant_scores = (
        jnp.einsum("owz,toz->owt", query_landmarks, key_matrix, precision=highest_value)
        * scale_factor
    )
    live = valid_own[None, None, :] > 0
    return (jnp.where(live, distant_scores, -1e30), live)


def join_softmax(left, right):
    peak = jnp.maximum(left[0], right[0])
    left_factor = jnp.exp(left[0] - peak)
    right_factor = jnp.exp(right[0] - peak)
    return (
        peak,
        left[1] * left_factor + right[1] * right_factor,
        left[2] * left_factor[..., None] + right[2] * right_factor[..., None],
    )


def attend(query_matrix, key_matrix, value_matrix, pooled_local, valid_own):
    query_portion = jnp.einsum("ji,ilk->ljk", pooled_local, query_matrix, precision=highest_value)
    key_portion = jnp.einsum("ji,ilk->ljk", pooled_local, key_matrix, precision=highest_value)
    query_landmarks, key_landmarks = (
        lax.psum(query_portion.astype(jnp.bfloat16), "mp").astype(jnp.float32),
        lax.psum(key_portion.astype(jnp.bfloat16), "mp").astype(jnp.float32),
    )
    distant_scores, live = far_scores(query_landmarks, key_matrix, valid_own)
    peak = jnp.max(distant_scores, axis=-1)
    matrix_powers = jnp.where(live, jnp.exp(distant_scores - peak[..., None]), 0.0)
    totals = jnp.sum(matrix_powers, axis=-1)
    weighted_values = jnp.einsum(
        "naw,wno->nao", matrix_powers, value_matrix, precision=highest_value
    )
    peak, totals, weighted_values = merged((peak, totals, weighted_values), "mp", join_softmax)
    summary = weighted_values / totals[..., None]
    carried_over = inverse_section(query_landmarks, key_landmarks, summary)
    mixed = near_section(query_matrix, key_landmarks, carried_over)
    return (mixed, (query_landmarks, key_landmarks, peak, totals, summary))


def attend_back(
    grad_rows, query_matrix, key_matrix, value_matrix, pooled_local, valid_own, saved, tap_part
):
    query_landmarks, key_landmarks, peak, totals, summary = saved
    scale_factor = query_matrix.shape[-1] ** (-0.5)
    carried_over, inverse_back = jax.vjp(inverse_section, query_landmarks, key_landmarks, summary)
    unused, near_back = jax.vjp(near_section, query_matrix, key_landmarks, carried_over)
    query_grad, kland_part, carried_part = near_back(grad_rows)
    key_landmark_nearby, carried_grad, tap_grad = (
        lax.psum(kland_part.astype(jnp.bfloat16), "mp").astype(jnp.float32),
        lax.psum(carried_part.astype(jnp.bfloat16), "mp").astype(jnp.float32),
        lax.psum(tap_part.astype(jnp.bfloat16), "mp").astype(jnp.float32),
    )
    query_landmark_gradient, key_landmark_gradient, summary_gradient = inverse_back(carried_grad)
    distant_scores, live = far_scores(query_landmarks, key_matrix, valid_own)
    weight_spread = jnp.where(
        live, jnp.exp(distant_scores - peak[..., None]) / totals[..., None], 0.0
    )
    moving_along = jnp.einsum(
        "owz,toz->owt", summary_gradient, value_matrix, precision=highest_value
    )
    agreed = jnp.sum(summary_gradient * summary, axis=-1)
    slope_values = weight_spread * (moving_along - agreed[..., None])
    value_gradient = jnp.einsum(
        "ofq,ofn->qon", weight_spread, summary_gradient, precision=highest_value
    )
    query_landmark_remote = (
        jnp.einsum("naw,wno->nao", slope_values, key_matrix, precision=highest_value) * scale_factor
    )
    key_gradient = (
        jnp.einsum("ofq,ofn->qon", slope_values, query_landmarks, precision=highest_value)
        * scale_factor
    )
    query_landmark_remote = lax.psum(query_landmark_remote.astype(jnp.bfloat16), "mp").astype(
        jnp.float32
    )
    query_grad = query_grad + jnp.einsum(
        "ge,xgl->exl",
        pooled_local,
        query_landmark_gradient + query_landmark_remote,
        precision=highest_value,
    )
    key_gradient = key_gradient + jnp.einsum(
        "ge,xgl->exl",
        pooled_local,
        key_landmark_gradient + key_landmark_nearby,
        precision=highest_value,
    )
    return (query_grad, key_gradient, value_gradient, tap_grad)


def head_table(columns, heads, size_h):
    begin = lax.axis_index("mp") * columns
    owner = (begin + jnp.arange(columns, dtype=jnp.int32)) // size_h
    return (owner[None, :] == jnp.arange(heads, dtype=jnp.int32)[:, None]).astype(jnp.float32)


def convolve(value_cols, taps, table, valid):
    tap_cols = jnp.dot(taps.T, table, precision=highest_value)
    masked = value_cols * valid[:, None]
    reach = taps.shape[1] // 2
    padded = jnp.pad(masked, ((reach, reach), (0, 0)))
    length_rows = masked.shape[0]
    convolved = jnp.zeros_like(masked)
    for offset in range(taps.shape[1]):
        convolved = convolved + tap_cols[offset] * padded[offset : offset + length_rows]
    return convolved


def contract(left, right, left_dim, right_dim):
    return lax.dot_general(
        left, right, (((left_dim,), (right_dim,)), ((), ())), preferred_element_type=jnp.float32
    )


def normalize(resid, gain, shift):
    centre = resid - jnp.mean(resid, axis=-1, keepdims=True)
    spread = lax.rsqrt(jnp.mean(centre * centre, axis=-1, keepdims=True) + 1e-05)
    normed = centre * spread
    return (normed * gain + shift, normed, spread)


def normalize_back(upstream, normed, spread, gain):
    scaled = upstream * gain
    result = spread * (
        scaled
        - jnp.mean(scaled, axis=-1, keepdims=True)
        - normed * jnp.mean(scaled * normed, axis=-1, keepdims=True)
    )
    return (result, jnp.sum(upstream * normed, axis=0), jnp.sum(upstream, axis=0))


def own_rows(whole):
    count = whole.shape[0] // lax.axis_size("mp")
    return lax.dynamic_slice_in_dim(whole, lax.axis_index("mp") * count, count, 0)


def whole_rows(share):
    return lax.all_gather(share.astype(jnp.bfloat16), "mp", axis=0, tiled=True).astype(share.dtype)


def row_sums(partial_value):
    return lax.psum_scatter(
        partial_value.astype(jnp.bfloat16), "mp", scatter_dimension=0, tiled=True
    ).astype(jnp.float32)


def add_norm(partial_value, resid, gain, shift):
    summed = row_sums(partial_value)
    output, normed, spread = normalize(own_rows(resid) + summed, gain, shift)
    output = whole_rows(output)
    return (output, normed, spread)


def norm_step_back(upstream, normed, spread, gain):
    result, gain_part, shift_part = normalize_back(upstream, normed, spread, gain)
    whole = whole_rows(result)
    return (result, whole, gain_part, shift_part)


def add_input_grad(result, partial_value):
    total = result + row_sums(partial_value)
    return total


def forward_layer(hidden, weights, pooling_own, valid, valid_own):
    projection, taps, output_weight, gains, shifts, up_weight, down_weight = weights
    count, width = hidden.shape
    heads = taps.shape[0]
    size_h = width // heads
    columns = projection.shape[2]
    entering = hidden.astype(jnp.bfloat16)
    mixed = jnp.einsum(
        "td,dsc->tsc", entering, projection, preferred_element_type=jnp.float32
    ).astype(jnp.bfloat16)
    gathered = lax.all_to_all(mixed, "mp", split_axis=0, concat_axis=2, tiled=True)
    rows = gathered.shape[0]
    split_rows = gathered.astype(jnp.float32).reshape(rows, 3, heads, size_h)
    attended, saved = attend(
        split_rows[:, 0], split_rows[:, 1], split_rows[:, 2], pooling_own, valid_own
    )
    attended_cols = lax.all_to_all(
        for_sending(attended.reshape(rows, width)), "mp", split_axis=1, concat_axis=0, tiled=True
    )
    table = head_table(columns, heads, size_h)
    value_cols = mixed[:, 2].astype(jnp.float32)
    convolved = convolve(value_cols, taps, table, valid)
    joined = ((attended_cols + convolved) * valid[:, None]).astype(jnp.bfloat16)
    partial_value = jnp.dot(joined, output_weight, preferred_element_type=jnp.float32)
    middle, normed_first, spread_first = add_norm(partial_value, hidden, gains[0], shifts[0])
    entering_ffn = middle.astype(jnp.bfloat16)
    upward = jnp.dot(entering_ffn, up_weight, preferred_element_type=jnp.float32)
    active = jax.nn.gelu(upward, approximate=True).astype(jnp.bfloat16)
    partial_value = jnp.dot(active, down_weight, preferred_element_type=jnp.float32)
    output, normed_second, spread_second = add_norm(partial_value, middle, gains[1], shifts[1])
    kept = (
        entering,
        value_cols,
        split_rows,
        saved,
        joined,
        table,
        normed_first,
        spread_first,
        entering_ffn,
        upward,
        active,
        normed_second,
        spread_second,
    )
    return (output, kept)


def backward_layer(upstream, weights, kept, pooling_own, valid, valid_own):
    projection, taps, output_weight, gains, shifts, up_weight, down_weight = weights
    (
        entering,
        value_cols,
        split_rows,
        saved,
        joined,
        table,
        normed_first,
        spread_first,
        entering_ffn,
        upward,
        active,
        normed_second,
        spread_second,
    ) = kept
    count, width = entering.shape
    rows = split_rows.shape[0]
    heads = taps.shape[0]
    size_h = width // heads
    result_second, whole_second, gain_second, shift_second = norm_step_back(
        upstream, normed_second, spread_second, gains[1]
    )
    sent_second = whole_second.astype(jnp.bfloat16)
    down_grad = contract(active, sent_second, 0, 0)
    hidden_grad = contract(sent_second, down_weight, 1, 1)
    unused, gelu_back = jax.vjp(lambda value: jax.nn.gelu(value, approximate=True), upward)
    upward_sent = gelu_back(hidden_grad)[0].astype(jnp.bfloat16)
    up_grad = contract(entering_ffn, upward_sent, 0, 0)
    middle_grad = add_input_grad(result_second, contract(upward_sent, up_weight, 1, 1))
    result_first, whole_first, gain_first, shift_first = norm_step_back(
        middle_grad, normed_first, spread_first, gains[0]
    )
    sent_first = whole_first.astype(jnp.bfloat16)
    out_grad = contract(joined, sent_first, 0, 0)
    joined_grad = contract(sent_first, output_weight, 1, 1)
    masked_grad = joined_grad * valid[:, None]
    unused, conv_back = jax.vjp(
        lambda values, tap_rows: convolve(values, tap_rows, table, valid), value_cols, taps
    )
    conv_value_grad, tap_part = conv_back(masked_grad)
    row_grad = (
        lax.all_to_all(
            masked_grad.astype(jnp.bfloat16), "mp", split_axis=0, concat_axis=1, tiled=True
        )
        .astype(masked_grad.dtype)
        .reshape(rows, heads, size_h)
    )
    query_grad, key_gradient, value_gradient, tap_grad = attend_back(
        row_grad,
        split_rows[:, 0],
        split_rows[:, 1],
        split_rows[:, 2],
        pooling_own,
        valid_own,
        saved,
        tap_part,
    )
    stacked_rows = jnp.stack([query_grad, key_gradient, value_gradient], axis=1).reshape(
        rows, 3, width
    )
    column_grad = lax.all_to_all(
        for_sending(stacked_rows), "mp", split_axis=2, concat_axis=0, tiled=True
    ).astype(stacked_rows.dtype)
    column_grad = jnp.concatenate(
        [column_grad[:, :2], (column_grad[:, 2] + conv_value_grad)[:, None]], axis=1
    )
    mixed_sent = column_grad.astype(jnp.bfloat16)
    proj_grad = jnp.einsum("td,tsc->dsc", entering, mixed_sent, preferred_element_type=jnp.float32)
    below = add_input_grad(
        result_first,
        jnp.einsum("tsc,dsc->td", mixed_sent, projection, preferred_element_type=jnp.float32),
    )
    gain_grad = jnp.stack([gain_first, gain_second])
    shift_grad = jnp.stack([shift_first, shift_second])
    gain_grad, shift_grad = lax.psum((gain_grad, shift_grad), "mp")
    return (below, (proj_grad, tap_grad, out_grad, gain_grad, shift_grad, up_grad, down_grad))


def sum_layer(parts):
    return (
        lax.psum(parts[0].astype(jnp.bfloat16), "dp").astype(jnp.float32),
        lax.psum(parts[1].astype(jnp.bfloat16), "dp").astype(jnp.float32),
        lax.psum(parts[2].astype(jnp.bfloat16), "dp").astype(jnp.float32),
        lax.psum(parts[3].astype(jnp.bfloat16), "dp").astype(jnp.float32),
        lax.psum(parts[4].astype(jnp.bfloat16), "dp").astype(jnp.float32),
        lax.psum(parts[5].astype(jnp.bfloat16), "dp").astype(jnp.float32),
        lax.psum(parts[6].astype(jnp.bfloat16), "dp").astype(jnp.float32),
    )


def body(
    tokens,
    lengths,
    cotangent,
    projection,
    conv_taps,
    output_weight,
    norm_gains,
    norm_shifts,
    up_weight,
    down_weight,
):
    count = tokens.shape[0]
    pooling, valid = slot_masks(lengths[0], count, M)
    rows = count // lax.axis_size("mp")
    begin = lax.axis_index("mp") * rows
    pooling_own = lax.dynamic_slice_in_dim(pooling, begin, rows, 1)
    valid_own = lax.dynamic_slice_in_dim(valid, begin, rows, 0)
    weights = (
        projection,
        conv_taps,
        output_weight,
        norm_gains,
        norm_shifts,
        up_weight,
        down_weight,
    )
    hidden = tokens.astype(jnp.float32)
    keeping = []
    for layer_index in range(LAYERS):
        hidden, kept = forward_layer(
            hidden, tuple((item[layer_index] for item in weights)), pooling_own, valid, valid_own
        )
        keeping.append(kept)
    activations = (hidden * valid[:, None]).astype(jnp.bfloat16)
    upstream = cotangent.astype(jnp.float32) * valid[:, None]
    upstream = own_rows(upstream)
    collected = [None] * LAYERS
    for layer_index in reversed(range(LAYERS)):
        upstream, parts = backward_layer(
            upstream,
            tuple((item[layer_index] for item in weights)),
            keeping[layer_index],
            pooling_own,
            valid,
            valid_own,
        )
        collected[layer_index] = sum_layer(parts)
    stacked = tuple(
        (
            jnp.stack([collected[layer_index][member] for layer_index in range(LAYERS)])
            for member in range(7)
        )
    )
    upstream = whole_rows(upstream)
    return (
        activations,
        upstream,
        stacked[0],
        stacked[1],
        stacked[2],
        stacked[3],
        stacked[4],
        stacked[5],
        stacked[6],
    )


class Weights(NamedTuple):
    projection: Any
    output: Any
    up: Any
    down: Any


class Kept(NamedTuple):
    ql: Any
    kl: Any
    second: Any
    inverse: Any
    first: Any
    third: Any
    summary: Any
    carried: Any


class Stored(NamedTuple):
    attention: Any
    qkv: Any
    normed: Any
    spread: Any
    slope: Any
    x_t: Any
    mixed_t: Any
    y_t: Any
    active_t: Any


class Work(NamedTuple):
    x: Any
    x_low: Any
    y: Any
    y_low: Any
    mixed: Any
    active: Any
    dmixed: Any
    dqkv: Any
    taps: Any
    turned: Any


class Wire(NamedTuple):
    send: Any
    receive: Any
    small: Any


class Sems(NamedTuple):
    load: Any
    ring_send: Any
    ring_receive: Any
    small_send: Any
    small_receive: Any
    credit: Any
    ready: Any
    share_send: Any
    share_receive: Any
    gather_send: Any
    gather_receive: Any
    send: Any
    receive: Any


class Slots(NamedTuple):
    core: Any
    x: Any
    near: Any
    mid: Any


class Grads(NamedTuple):
    down: Any
    up: Any
    other: Any


DOWN, UP, OUTPUT, PROJECTION = range(4)


MESH = pl.DeviceIdType.MESH
F32 = jnp.float32
BF16 = jnp.bfloat16


def nn(a, b):
    return lax.dot_general(a, b, (((1,), (0,)), ((), ())), preferred_element_type=F32)


def nt(a, b):
    return lax.dot_general(a, b, (((1,), (1,)), ((), ())), preferred_element_type=F32)


def parts_of(x):
    high = x.astype(BF16)
    return high, (x - high.astype(F32)).astype(BF16)


def nn3(a, b):
    return nn(jnp.concatenate([a[0], a[1]], 1), jnp.concatenate([b[0], b[0]], 0)) + nn(a[0], b[1])


def nt3(a, b):
    return nt(jnp.concatenate([a[0], a[1]], 1), jnp.concatenate([b[0], b[0]], 1)) + nt(a[0], b[1])


def iota(shape, axis):
    return lax.broadcasted_iota(jnp.int32, shape, axis)


class Frame:
    def __init__(self, length, rows, size_h):
        self.length = length
        self.rows = rows
        self.lane0 = iota((1, 2 * size_h), 1) < size_h
        self.keep = [self.lane0.astype(F32).astype(BF16), (~self.lane0).astype(F32).astype(BF16)]
        self.diag = (iota((2 * M, 2 * M), 0) < M) == (iota((2 * M, 2 * M), 1) < M)
        self.ones = self.diag.astype(F32).astype(BF16)
        self.ones2 = jnp.concatenate([self.ones, self.ones], 0)
        j, t = iota((M, rows), 0), iota((M, rows), 1)
        member = (t * M >= j * length) & (t * M < (j + 1) * length)
        member = member.astype(F32)
        self.member = member.astype(BF16)
        self.inv = 1.0 / jnp.sum(member, axis=1, keepdims=True)
        t, j = iota((rows, M), 0), iota((rows, M), 1)
        self.member_t = ((t * M >= j * length) & (t * M < (j + 1) * length)).astype(F32).astype(BF16)
        self.valid = (iota((rows, 1), 0) < length).astype(F32)
        self.valid_lane = iota((1, rows), 1) < length
        self.band = jnp.abs(iota((rows, rows), 0) - iota((rows, rows), 1)) <= KREACH

    def stack(self, x):
        return jnp.where(self.diag, jnp.concatenate([x, x], 0), 0.0)

    def block(self, x):
        return jnp.where(self.diag, x, 0.0)

    def pack(self, x):
        return x[:M] + x[M:]

    def spread(self, x):
        return jnp.concatenate([x * self.keep[0], x * self.keep[1]], 0)

    def times(self, a, b):
        high, low = b
        left = jnp.concatenate([a[0], a[1]], 1)
        return nn(left, jnp.concatenate([high, high], 0)) + nn(a[0], low)

    def spread_parts(self, x):
        return tuple(self.spread(half) for half in parts_of(x))

    def half_sums(self, x):
        high, low = parts_of(x)
        return nn(jnp.concatenate([high, low], 1), self.ones2)

    def toeplitz(self, row):
        spread = jnp.broadcast_to(row, (self.rows, self.rows))
        turned = pltpu.roll(spread, self.rows - KREACH, 1, stride=1, stride_axis=0)
        return jnp.where(self.band, turned, 0.0).astype(BF16)

    def conv(self, rows_pair, value):
        both = jnp.concatenate([self.toeplitz(rows_pair[0]), self.toeplitz(rows_pair[1])], 1)
        stacked = jnp.concatenate([value * self.keep[0], value * self.keep[1]], 0)
        return nn(both, stacked)

    def diagonals(self, product):
        banded = jnp.where(self.band, product, 0.0)
        total = banded[:8]
        for group in range(1, self.rows // 8):
            part = banded[8 * group : 8 * group + 8]
            total = total + pltpu.roll(part, self.rows - 8 * group, 1)
        total = pltpu.roll(total, KREACH, 1)
        result = total[:1]
        for row in range(1, 8):
            result = result + pltpu.roll(total[row : row + 1], self.rows - row, 1)
        return result


KREACH = 16


def softmax_masked(scores, live):
    scores = jnp.where(live, scores, -1e30)
    top = jnp.max(scores, axis=-1, keepdims=True)
    powers = jnp.where(live, jnp.exp(scores - top), 0.0)
    return powers / jnp.sum(powers, axis=-1, keepdims=True)


def attention(frame, qkv, taps, head0, size_h, keep, out_ref):
    scale = size_h ** (-0.5)
    pairs = qkv.shape[2] // (2 * size_h)
    ql = nn(frame.member, qkv[0]) * frame.inv
    kl = nn(frame.member, qkv[1]) * frame.inv
    keep.ql[...] = ql
    keep.kl[...] = kl
    cols = [slice(p * 2 * size_h, (p + 1) * 2 * size_h) for p in range(pairs)]
    qs = [parts_of(frame.stack(ql[:, c])) for c in cols]
    ks = [parts_of(frame.stack(kl[:, c])) for c in cols]
    second = [softmax_masked(nt3(qs[p], ks[p]) * scale, frame.diag) for p in range(pairs)]
    inverse = []
    halves = iota((2 * M, 1), 0) < M
    for p in range(pairs):
        keep.second[p] = second[p]
        squares = jnp.sum(second[p] * second[p], axis=1, keepdims=True)
        first_total = jnp.sum(jnp.where(halves, squares, 0.0), axis=0, keepdims=True)
        other_total = jnp.sum(jnp.where(halves, 0.0, squares), axis=0, keepdims=True)
        inverse.append(second[p].T * (1.0 / jnp.where(halves, first_total, other_total)))
    second_parts = [parts_of(frame.pack(s)) for s in second]
    summaries, firsts, convolved = [None] * pairs, [None] * pairs, [None] * pairs

    def far(p):
        key, value = qkv[1, :, cols[p]], qkv[2, :, cols[p]]
        scores = nt(jnp.concatenate(qs[p], 1), jnp.concatenate([key, key], 1)) * scale
        third = softmax_masked(scores, frame.valid_lane).astype(BF16)
        keep.third[p] = third
        summaries[p] = frame.block(nn(third, value))
        keep.summary[p] = summaries[p]

    def near(p):
        query = qkv[0, :, cols[p]]
        scores = nt(jnp.concatenate([query, query], 1), jnp.concatenate(ks[p], 1)) * scale
        top0 = jnp.max(jnp.where(frame.lane0, scores, -1e30), axis=-1, keepdims=True)
        top1 = jnp.max(jnp.where(frame.lane0, -1e30, scores), axis=-1, keepdims=True)
        powers = jnp.exp(scores - jnp.where(frame.lane0, top0, top1))
        firsts[p] = (powers / frame.half_sums(powers)).astype(BF16)
        keep.first[:, cols[p]] = firsts[p]

    def local(p):
        inside = (qkv[2, :, cols[p]].astype(F32) * frame.valid).astype(BF16)
        rows_pair = [taps[pl.ds(head0 + 2 * p + i, 1), :] for i in range(2)]
        convolved[p] = frame.conv(rows_pair, inside)

    beside = [(task, p) for p in range(pairs) for task in (far, near, local)]
    inverse = [frame.pack(z) for z in inverse]
    product = [frame.times(second_parts[p], frame.spread_parts(inverse[p])) for p in range(pairs)]
    for sweep in range(NEWTON):
        for p in range(pairs):
            keep.inverse[sweep, p] = inverse[p]
        zp = [parts_of(z) for z in inverse]
        pp = [parts_of(x) for x in product]
        right = [tuple(frame.spread(half) for half in pp[p]) for p in range(pairs)]
        square = [frame.times(pp[p], right[p]) for p in range(pairs)]
        forward = [frame.times(zp[p], right[p]) for p in range(pairs)]
        for task, p in beside[sweep * len(beside) // NEWTON : (sweep + 1) * len(beside) // NEWTON]:
            task(p)
        inner = [frame.spread_parts(7.0 * product[p] - square[p]) for p in range(pairs)]
        if sweep + 1 < NEWTON:
            product = [0.25 * (13.0 * product[p] - 15.0 * square[p] + frame.times(parts_of(square[p]), inner[p])) for p in range(pairs)]
        inverse = [0.25 * (13.0 * inverse[p] - 15.0 * forward[p] + frame.times(parts_of(forward[p]), inner[p])) for p in range(pairs)]
    for p in range(pairs):
        keep.inverse[NEWTON, p] = inverse[p]
        carried = frame.stack(frame.times(parts_of(inverse[p]), parts_of(summaries[p])))
        keep.carried[p] = carried
        mixed = nn(firsts[p], carried.astype(BF16))
        out_ref[:, cols[p]] = ((mixed + convolved[p]) * frame.valid).astype(BF16)


def attention_back(frame, grad, qkv, taps_turned, head0, size_h, keep, out_ref, taps_out):
    scale = size_h ** (-0.5)
    pairs = qkv.shape[2] // (2 * size_h)
    cols = [slice(p * 2 * size_h, (p + 1) * 2 * size_h) for p in range(pairs)]
    each = range(pairs)
    ql, kl = keep.ql[...], keep.kl[...]
    qs = [parts_of(frame.stack(ql[:, c])) for c in cols]
    ks = [parts_of(frame.stack(kl[:, c])) for c in cols]
    summary = [keep.summary[p] for p in each]
    second = [keep.second[p] for p in each]
    dq, dk_landmark, dcarried, grad_low = [], [], [], []
    for p in each:
        c = cols[p]
        g = grad[:, c].astype(BF16)
        grad_low.append(g)
        first = keep.first[:, c].astype(F32)
        dfirst = nt(g, keep.carried[p].astype(BF16))
        slope = first * dfirst
        slope = (slope - first * frame.half_sums(slope)) * scale
        dq.append(nn(slope.astype(BF16), ks[p][0]))
        dk_landmark.append(frame.block(nn(slope.T.astype(BF16), qkv[0, :, c])))
        dcarried.append(frame.block(nn(first.T.astype(BF16), g)))
    yield
    dcp = [parts_of(x) for x in dcarried]
    up = [nt3(dcp[p], parts_of(summary[p])) for p in each]
    dsummary = [nn3(parts_of(frame.stack(keep.inverse[NEWTON, p]).T), dcp[p]) for p in each]
    second_parts = [parts_of(s) for s in second]
    second_turned = [parts_of(s.T) for s in second]
    dsecond = [jnp.zeros_like(s) for s in second]
    for sweep in reversed(range(NEWTON)):
        inverse = [frame.stack(keep.inverse[sweep, p]) for p in each]
        zp = [parts_of(z) for z in inverse]
        product = [nn3(second_parts[p], zp[p]) for p in each]
        pp = [parts_of(x) for x in product]
        inner = [parts_of(7.0 * product[p] - nn3(pp[p], pp[p])) for p in each]
        forward_turned = [parts_of(nn3(zp[p], pp[p]).T) for p in each]
        product_turned = [parts_of(x.T) for x in product]
        inverse_turned = [parts_of(z.T) for z in inverse]
        upp = [parts_of(x) for x in up]
        dforward = [parts_of(0.25 * (nt3(upp[p], inner[p]) - 15.0 * up[p])) for p in each]
        dinner_full = [0.25 * nn3(forward_turned[p], upp[p]) for p in each]
        dinner = [parts_of(x) for x in dinner_full]
        dproduct = [
            parts_of(
                7.0 * dinner_full[p]
                - nt3(dinner[p], pp[p])
                - nn3(product_turned[p], dinner[p])
                + nn3(inverse_turned[p], dforward[p])
            )
            for p in each
        ]
        up = [
            3.25 * up[p] + nt3(dforward[p], pp[p]) + nn3(second_turned[p], dproduct[p])
            for p in each
        ]
        dsecond = [dsecond[p] + nt3(dproduct[p], zp[p]) for p in each]
        yield
    halves = iota((2 * M, 1), 0) < M
    for p in each:
        c = cols[p]
        query, key, value = qkv[0, :, c], qkv[1, :, c], qkv[2, :, c]
        squares = jnp.sum(second[p] * second[p], axis=1, keepdims=True)
        total0 = jnp.sum(jnp.where(halves, squares, 0.0), axis=0, keepdims=True)
        total1 = jnp.sum(jnp.where(halves, 0.0, squares), axis=0, keepdims=True)
        inverse_total = 1.0 / jnp.where(halves, total0, total1)
        start_agree = jnp.sum(up[p] * frame.stack(keep.inverse[0, p]), axis=1, keepdims=True)
        agree0 = jnp.sum(jnp.where(halves, start_agree, 0.0), axis=0, keepdims=True)
        agree1 = jnp.sum(jnp.where(halves, 0.0, start_agree), axis=0, keepdims=True)
        agree = jnp.where(halves, agree0, agree1)
        dsec = dsecond[p] + (up[p].T - 2.0 * agree * second[p]) * inverse_total
        slope = second[p] * dsec
        slope = (slope - second[p] * jnp.sum(slope, axis=-1, keepdims=True)) * scale
        dql = nn(slope.astype(BF16), ks[p][0])
        dkl = nn(slope.T.astype(BF16), qs[p][0]) + dk_landmark[p]
        third = keep.third[p].astype(F32)
        ds = dsummary[p].astype(BF16)
        dthird = nt(ds, value)
        agreed = jnp.sum(dsummary[p] * summary[p], axis=-1, keepdims=True)
        slope = third * (dthird - agreed) * scale
        dv = nn(third.T.astype(BF16), ds)
        dql = dql + frame.block(nn(slope.astype(BF16), key))
        dk = nn(slope.T.astype(BF16), qs[p][0])
        dql = ((dql[:M] + dql[M:]) * frame.inv).astype(BF16)
        dkl = ((dkl[:M] + dkl[M:]) * frame.inv).astype(BF16)
        out_ref[0, :, c] = (dq[p] + nn(frame.member_t, dql)).astype(BF16)
        out_ref[1, :, c] = (dk + nn(frame.member_t, dkl)).astype(BF16)
        inside = (value.astype(F32) * frame.valid).astype(BF16)
        rows_pair = [taps_turned[pl.ds(head0 + 2 * p + i, 1), :] for i in range(2)]
        dv = dv + frame.valid * frame.conv(rows_pair, grad_low[p])
        out_ref[2, :, c] = dv.astype(BF16)
        for i in range(2):
            product = nt(grad_low[p] * frame.keep[i], inside)
            taps_out(2 * p + i, frame.diagonals(product))
        yield


def norm_rows(r, gain, shift):
    centre = r - jnp.mean(r, axis=-1, keepdims=True)
    spread = lax.rsqrt(jnp.mean(centre * centre, axis=-1, keepdims=True) + 1e-05)
    normed = centre * spread
    return normed * gain + shift, normed, spread


def norm_rows_back(dy, normed, spread, gain):
    scaled = dy * gain
    result = spread * (
        scaled
        - jnp.mean(scaled, axis=-1, keepdims=True)
        - normed * jnp.mean(scaled * normed, axis=-1, keepdims=True)
    )
    return (
        result,
        jnp.sum(dy * normed, axis=0, keepdims=True),
        jnp.sum(dy, axis=0, keepdims=True),
    )


GELU_A = 0.7978845608028654
GELU_B = 0.044715


def gelu_both(u):
    square = u * u
    t = jnp.tanh(GELU_A * (u + GELU_B * u * square))
    half = 0.5 * (1.0 + t)
    slope = half + 0.5 * u * (1.0 - t * t) * (GELU_A + (3.0 * GELU_A * GELU_B) * square)
    return u * half, slope


SEND_SEM = ((0, 1, 2, 2, 0, 1, 2, 3), (0, 1, 2, 2, 0, 3, 2, 4, 1))
RECEIVE_SEM = ((0, 1, 2, 3, 2, 6, 5, 4), (0, 1, 2, 3, 6, 6, 5, 4, 2))
SENDS, RECEIVES = 5, 7


class Reduction:
    def __init__(self, sems):
        dp, self.mp = lax.axis_index("dp"), lax.axis_index("mp")
        z = dp // 4
        self.x = (dp // 2) % 2
        self.core = dp % 2
        self.upper = z // 2
        self.inner = (z == 1) | (z == 2)
        self.outer = (z == 0) | (z == 3)
        self.to_core = dp + 1 - 2 * self.core
        self.to_x = dp + 2 - 4 * self.x
        self.to_near = dp + 4 - 8 * (z % 2)
        self.to_mid = (3 - z) * 4 + dp % 4
        self.sems = sems
        self.pieces = []

    def greet(self, barrier):
        for other in (self.to_core, self.to_x, self.to_near, self.to_mid):
            pl.semaphore_signal(barrier, inc=1, device_id=(other, self.mp), device_id_type=MESH)

    def add(self, rows, kind, view, slots, credit, gives, takes, other_kind):
        self.pieces.append((rows // 4, kind, view, slots, credit, gives, takes, other_kind))

    def copy(self, index, slot, source, target, to):
        kind, place = self.pieces[index][1], self.pieces[index][4]
        return pltpu.make_async_remote_copy(
            src_ref=source,
            dst_ref=target,
            send_sem=self.sems.ring_send.at[place * SENDS + SEND_SEM[kind][slot]],
            recv_sem=self.sems.ring_receive.at[place * RECEIVES + RECEIVE_SEM[kind][slot]],
            device_id=(to, self.mp),
            device_id_type=MESH,
        )

    def event(self, index, step):
        quarter, kind, view, slots, credit, gives, takes, other_kind = self.pieces[index]
        x, core, upper = self.x, self.core, self.upper
        side = x if kind == 0 else upper

        def region(half, which, count=1):
            start = (half * 2 + which) * quarter
            return view(start, count * quarter)

        def arrived(slot, ref):
            self.copy(index, slot, ref, ref, self.to_core).wait_recv()

        def sent(slot, ref):
            self.copy(index, slot, ref, ref, self.to_core).wait_send()

        def send(slot, source, destination, to, need=None):
            if takes and need is not None:
                pl.semaphore_wait(self.sems.credit.at[credit * 4 + need], 1)
            self.copy(index, slot, source, destination, to).start()

        def free(which, to):
            if gives:
                pl.semaphore_signal(
                    self.sems.credit.at[credit * 4 + which],
                    inc=1,
                    device_id=(to, self.mp),
                    device_id_type=MESH,
                )

        def ready(which, slot, ref, to):
            sent(slot, ref)
            pl.semaphore_signal(
                self.sems.ready.at[credit * 4 + which],
                inc=1,
                device_id=(to, self.mp),
                device_id_type=MESH,
            )

        def await_ready(which):
            pl.semaphore_wait(self.sems.ready.at[credit * 4 + which], 1)

        def slot_part(ref, which):
            return ref.at[pl.ds(pl.multiple_of(which * quarter, 16), quarter)]

        def sum_into(ref, others):
            block = 48 if quarter % 48 == 0 else 16

            def step_rows(i, unused):
                span = pl.ds(pl.multiple_of(i * block, 16), block)
                total = ref[span, :].astype(F32)
                for other in others:
                    total = total + other[span, :].astype(F32)
                ref[span, :] = total.astype(BF16)
                return unused

            lax.fori_loop(0, quarter // block, step_rows, 0)

        mine, other = region(core, side), region(core, 1 - side)
        if step == 0:
            send(0, region(1 - core, 0, 2), slots.core, self.to_core, need=0)
        elif step == 7:
            for slot, which in ((6, side), (7, 1 - side)):
                arrived(slot, region(1 - core, which))
            sent(6, mine)
            sent(7, other)
            if kind == 0:
                sent(5, mine)

                @pl.when(self.inner)
                def _():
                    sent(4, mine)

            else:

                @pl.when(self.inner)
                def _():
                    for slot in (4, 5, 8):
                        sent(slot, mine)

        elif kind == 0:
            if step == 1:
                arrived(0, slots.core)
                sum_into(other, [slot_part(slots.core, 1 - x)])
                if other_kind == 0:
                    send(1, other, slots.x, self.to_x, need=1)
                else:
                    if takes:

                        @pl.when(self.inner)
                        def _():
                            pl.semaphore_wait(self.sems.credit.at[credit * 4 + 1], 1)

                    send(1, other, slots.x, self.to_x)
                ready(0, 0, region(1 - core, 0, 2), self.to_core)
            elif step == 2:

                @pl.when(self.outer)
                def _():
                    arrived(1, slots.x)
                    sum_into(mine, [slot_part(slots.core, x), slots.x])
                    free(0, self.to_core)
                    if other_kind == 0:
                        free(1, self.to_x)
                    send(2, mine, slot_part(slots.near, 0), self.to_near, need=2)
                    ready(1, 1, other, self.to_x)

            elif step == 3:

                @pl.when(self.inner)
                def _():
                    arrived(1, slots.x)
                    arrived(2, slot_part(slots.near, 0))
                    sum_into(mine, [slot_part(slots.core, x), slots.x, slot_part(slots.near, 0)])
                    free(0, self.to_core)
                    free(1, self.to_x)
                    free(2, self.to_near)
                    send(3, mine, slots.mid, self.to_mid, need=3)
                    ready(1, 1, other, self.to_x)

                @pl.when(self.outer)
                def _():
                    ready(2, 2, mine, self.to_near)

            elif step == 4:

                @pl.when(self.inner)
                def _():
                    arrived(3, slots.mid)
                    sent(3, mine)
                    sum_into(mine, [slots.mid])
                    free(3, self.to_mid)
                    await_ready(2)
                    send(4, mine, mine, self.to_near)
                    await_ready(1)
                    send(5, mine, mine, self.to_x)
                    await_ready(0)
                    send(6, mine, mine, self.to_core)

            elif step == 5:

                @pl.when(self.outer)
                def _():
                    arrived(4, mine)
                    await_ready(1)
                    send(5, mine, mine, self.to_x)
                    await_ready(0)
                    send(6, mine, mine, self.to_core)

            elif step == 6:
                arrived(5, other)
                send(7, other, other, self.to_core)
        else:
            if step == 1:

                @pl.when(self.outer)
                def _():
                    arrived(0, slots.core)
                    sum_into(region(core, 0), [slot_part(slots.core, 0)])
                    sum_into(region(core, 1), [slot_part(slots.core, 1)])
                    free(0, self.to_core)
                    send(2, region(core, 0, 2), slots.near, self.to_near, need=2)
                    ready(0, 0, region(1 - core, 0, 2), self.to_core)

            elif step == 2:

                @pl.when(self.outer)
                def _():
                    ready(2, 2, region(core, 0, 2), self.to_near)

                @pl.when(self.inner)
                def _():
                    arrived(0, slots.core)
                    arrived(2, slots.near)
                    sum_into(other, [slot_part(slots.core, 1 - side), slot_part(slots.near, 1 - side)])
                    send(3, other, slots.mid, self.to_mid, need=3)
                    ready(0, 0, region(1 - core, 0, 2), self.to_core)

            elif step == 3:

                @pl.when(self.inner)
                def _():
                    arrived(3, slots.mid)
                    sum_into(mine, [slot_part(slots.core, side), slot_part(slots.near, side), slots.mid])
                    free(0, self.to_core)
                    free(2, self.to_near)
                    free(3, self.to_mid)
                    send(1, mine, slots.x, self.to_x, need=1)
                    ready(3, 3, other, self.to_mid)

            elif step == 4:

                @pl.when(self.inner)
                def _():
                    arrived(1, slots.x)
                    sent(1, mine)
                    sum_into(mine, [slots.x])
                    free(1, self.to_x)
                    await_ready(3)
                    send(4, mine, mine, self.to_mid)
                    await_ready(2)
                    send(8, mine, mine, self.to_near)
                    await_ready(0)
                    send(6, mine, mine, self.to_core)

            elif step == 5:

                @pl.when(self.inner)
                def _():
                    arrived(4, other)
                    send(5, other, other, self.to_near)
                    send(7, other, other, self.to_core)

                @pl.when(self.outer)
                def _():
                    arrived(8, mine)
                    await_ready(0)
                    send(6, mine, mine, self.to_core)

            elif step == 6:

                @pl.when(self.outer)
                def _():
                    arrived(5, other)
                    send(7, other, other, self.to_core)


class SmallSum:
    def __init__(self, ring, total, slots, sems, first_tap):
        self.ring, self.total, self.slots, self.sems, self.first_tap = ring, total, slots, sems, first_tap

    def copy(self, slot, target, to, mp):
        return pltpu.make_async_remote_copy(
            src_ref=self.total,
            dst_ref=target,
            send_sem=self.sems.small_send.at[slot],
            recv_sem=self.sems.small_receive.at[slot],
            device_id=(to, mp),
            device_id_type=MESH,
        )

    def event(self, step):
        ring, total, slots = self.ring, self.total, self.slots
        dp = ring.to_core + 2 * ring.core - 1

        def start(slot, to, mp=None):
            self.copy(slot, slots.at[slot], to, ring.mp if mp is None else mp).start()

        def take(slot):
            self.copy(slot, slots.at[slot], dp, ring.mp).wait_recv()

        def sent(slot):
            self.copy(slot, slots.at[slot], dp, ring.mp).wait_send()

        if step == 0:
            start(0, dp, 1 - ring.mp)
        elif step == 1:
            take(0)
            sent(0)
            total[self.first_tap :, :] += slots[0, self.first_tap :, :]
            start(1, ring.to_core)
        elif step == 2:
            take(1)
            sent(1)
            total[...] += slots[1]
            start(2, ring.to_x)
        elif step == 3:
            take(2)
            sent(2)
            total[...] += slots[2]

            @pl.when(ring.outer)
            def _():
                start(3, ring.to_near)

        elif step == 4:

            @pl.when(ring.inner)
            def _():
                take(3)
                total[...] += slots[3]
                start(4, ring.to_mid)

        elif step == 5:

            @pl.when(ring.inner)
            def _():
                take(4)
                sent(4)
                total[...] += slots[4]
                start(5, ring.to_near)

        elif step == 6:

            @pl.when(ring.outer)
            def _():
                take(5)
                sent(3)
                total[...] = slots[5]

            @pl.when(ring.inner)
            def _():
                sent(5)


def whole_step(
    length_ref,
    tokens_ref,
    cotangent_ref,
    raw_taps_ref,
    gains_ref,
    shifts_ref,
    projection_hbm,
    output_hbm,
    up_hbm,
    down_hbm,
    activations_ref,
    token_grad_ref,
    small_ref,
    down_grad_ref,
    up_grad_ref,
    other_grad_ref,
    weights,
    kept,
    work,
    wire,
    slots,
    sems,
):
    rows, width = tokens_ref.shape
    columns = projection_hbm.shape[3]
    hidden = up_hbm.shape[2]
    heads, _, reach = raw_taps_ref.shape
    grads = Grads(down_grad_ref, up_grad_ref, other_grad_ref)
    size_h = width // heads
    half = rows // 2
    tile = 384
    dp, mp = lax.axis_index("dp"), lax.axis_index("mp")
    head0 = mp * (columns // size_h)
    partner = (dp, 1 - mp)

    def own_half(layer):
        return weights.output.at[layer, mp]

    loads = []
    order = [
        (projection_hbm, weights.projection),
        (output_hbm, weights.output),
        (up_hbm, weights.up),
        (down_hbm, weights.down),
    ]
    for layer in range(LAYERS):
        for index, (source, place) in enumerate(order):
            load = pltpu.make_async_copy(
                source.at[layer],
                own_half(layer) if index == 1 else place.at[layer],
                sems.load.at[layer * 4 + index],
            )
            load.start()
            loads.append(load)

    barrier = pltpu.get_barrier_semaphore()
    pl.semaphore_signal(barrier, inc=1, device_id=partner, device_id_type=MESH)
    ring = Reduction(sems)
    ring.greet(barrier)

    frame = Frame(length_ref[0], rows, size_h)
    taps_ref, turned_ref = work.taps, work.turned
    taps_ref[...] = jnp.zeros_like(taps_ref)
    mirror = iota((rows, rows), 0) + iota((rows, rows), 1) == reach - 1
    mirror = mirror.astype(F32).astype(BF16)
    for layer in range(LAYERS):
        taps_ref[layer, :heads, :reach] = raw_taps_ref[:, layer, :]
        turned_ref[layer] = nn(taps_ref[layer].astype(BF16), mirror)
    flights = {}

    def send(slot, piece, partial_value):
        span = pl.ds(piece * half, half)
        wire.send[slot % 2, span, :] = partial_value.astype(BF16)
        copy = pltpu.make_async_remote_copy(
            src_ref=wire.send.at[slot % 2, span],
            dst_ref=wire.receive.at[slot % 2, span],
            send_sem=sems.send.at[slot % 2 * 2 + piece],
            recv_sem=sems.receive.at[slot % 2 * 2 + piece],
            device_id=partner,
            device_id_type=MESH,
        )
        copy.start()
        flights[slot, piece] = copy

    def arrived(slot, piece):
        span = pl.ds(piece * half, half)
        flights[slot, piece].wait()
        return wire.send[slot % 2, span, :].astype(F32) + wire.receive[
            slot % 2, span, :
        ].astype(F32)

    def share_copy(layer, hop):
        part = columns // 2
        which, first = (mp, ring.core) if hop == 0 else (1 - mp, ring.core)
        place = weights.output.at[layer, which, pl.ds(pl.multiple_of(first * part, 16), part)]
        return pltpu.make_async_remote_copy(
            src_ref=place,
            dst_ref=place,
            send_sem=sems.share_send.at[layer * 2 + hop],
            recv_sem=sems.share_receive.at[layer * 2 + hop],
            device_id=partner if hop == 0 else (ring.to_core, mp),
            device_id_type=MESH,
        )

    def gather_copy(layer, piece):
        place = work.mixed.at[mp, pl.ds(piece * half, half)]
        return pltpu.make_async_remote_copy(
            src_ref=place,
            dst_ref=place,
            send_sem=sems.gather_send.at[piece],
            recv_sem=sems.gather_receive.at[piece],
            device_id=partner,
            device_id_type=MESH,
        )

    halves = [slice(0, half), slice(half, rows)]

    def project(layer, c):
        for i in range(3):
            kept.qkv[layer, i, c, :] = nn(
                work.x_low[c, :], weights.projection[layer, i]
            ).astype(BF16)

    def keep_of(layer):
        return Kept(*(ref.at[layer] for ref in kept.attention))

    work.x[...] = tokens_ref[...].astype(F32)
    work.x_low[...] = tokens_ref[...]
    loads[0].wait()
    for c in halves:
        project(0, c)
    pl.semaphore_wait(barrier, 5)
    for layer in range(LAYERS):
        loads[layer * 4 + 1].wait()
        share_copy(layer, 0).start()
        attention(
            frame,
            kept.qkv.at[layer],
            taps_ref.at[layer],
            head0,
            size_h,
            keep_of(layer),
            work.mixed.at[mp],
        )
        slot = layer * 2
        for piece in range(len(halves)):
            gather_copy(layer, piece).start()
        share_copy(layer, 0).wait()
        share_copy(layer, 1).start()
        kept.mixed_t[layer] = work.mixed[mp].T
        kept.x_t[layer] = work.x_low[...].T
        loads[layer * 4 + 2].wait()
        loads[layer * 4 + 3].wait()
        share_copy(layer, 1).wait()
        for piece, c in enumerate(halves):
            gather_copy(layer, piece).wait()
            summed = work.x[c, :]
            for side in range(2):
                summed = summed + nn(work.mixed[side, c, :], weights.output[layer, side])
            y, normed, spread = norm_rows(summed, gains_ref[layer, 0:1], shifts_ref[layer, 0:1])
            kept.normed[layer, 0, c, :] = normed.astype(BF16)
            kept.spread[layer, 0, c, :] = spread
            work.y[c, :] = y
            work.y_low[c, :] = y.astype(BF16)
            for j in range(hidden // tile):
                span = slice(j * tile, (j + 1) * tile)
                u = nn(work.y_low[c, :], weights.up[layer, :, span])
                active, slope = gelu_both(u)
                work.active[c, span] = active.astype(BF16)
                kept.slope[layer, c, span] = slope.astype(BF16)
            send(slot + 1, piece, nn(work.active[c, :], weights.down[layer]))
        kept.active_t[layer] = work.active[...].T
        kept.y_t[layer] = work.y_low[...].T
        if layer + 1 < LAYERS:
            loads[layer * 4 + 4].wait()
        for piece, c in enumerate(halves):
            summed = work.y[c, :] + arrived(slot + 1, piece)
            y, normed, spread = norm_rows(summed, gains_ref[layer, 1:2], shifts_ref[layer, 1:2])
            kept.normed[layer, 1, c, :] = normed.astype(BF16)
            kept.spread[layer, 1, c, :] = spread
            if layer + 1 < LAYERS:
                work.x[c, :] = y
                work.x_low[c, :] = y.astype(BF16)
                project(layer + 1, c)
            else:
                activations_ref[c, :] = (y * frame.valid[c]).astype(BF16)

    def add_pieces(layer):
        listed = pieces_of(width, columns, hidden, layer)
        for k, (name, rows_of, kind) in enumerate(listed):
            before = sum(item[1] for item in listed[:k] if item[0] == name)
            index = sum(1 for item in listed[:k] if item[0] == name)

            def span(start, count, before=before):
                return pl.ds(pl.multiple_of(before + start, 16), count)

            if name in (DOWN, UP):

                def view(start, count, span=span, ref=grads.down if name == DOWN else grads.up):
                    return ref.at[layer, span(start, count)]

            else:

                def view(start, count, slab=0 if name == OUTPUT else 1 + index):
                    return grads.other.at[layer, slab, pl.ds(pl.multiple_of(start, 16), count)]

            ring.add(rows_of, kind, view, slots[k], k, layer > 0, layer + 1 < LAYERS, PIECE_KINDS[1 - layer][k])

    for layer in reversed(range(LAYERS)):
        add_pieces(layer)
    small = SmallSum(ring, small_ref, wire.small, sems, 8)
    dy_ref, dr_ref, e_ref, du_ref = work.x, work.y, work.y_low, work.active

    def norm_back(layer, which):
        gain = gains_ref[layer, which : which + 1]
        gain_sum = shift_sum = 0.0
        for c in halves:
            result, gain_part, shift_part = norm_rows_back(
                dy_ref[c, :],
                kept.normed[layer, which, c, :].astype(F32),
                kept.spread[layer, which, c, :],
                gain,
            )
            dr_ref[c, :] = result
            e_ref[c, :] = result.astype(BF16)
            gain_sum, shift_sum = gain_sum + gain_part, shift_sum + shift_part
        row = layer * 2 + which
        small_ref[row : row + 1, :] = gain_sum
        small_ref[row + 4 : row + 5, :] = shift_sum

    def backward():
        small_ref[...] = jnp.zeros_like(small_ref)
        for piece, c in enumerate(halves):
            dy_ref[c, :] = cotangent_ref[c, :].astype(F32) * frame.valid[c]
        for layer in reversed(range(LAYERS)):
            slot = 4 + (LAYERS - 1 - layer) * 2
            norm_back(layer, 1)
            yield
            block = hidden // DOWN_PIECES
            for j in range(DOWN_PIECES):
                span = slice(j * block, (j + 1) * block)
                grads.down[layer, span, :] = nn(
                    kept.active_t[layer, span, :], e_ref[...]
                ).astype(BF16)
                yield
            for j in range(hidden // tile):
                span = slice(j * tile, (j + 1) * tile)
                dh = nt(e_ref[...], weights.down[layer, span, :])
                du_ref[:, span] = (dh * kept.slope[layer, :, span].astype(F32)).astype(BF16)
            yield
            for piece, c in enumerate(halves):
                send(slot, piece, nt(du_ref[c, :], weights.up[layer]))
                yield
            block = width // UP_PIECES
            for j in range(UP_PIECES):
                span = slice(j * block, (j + 1) * block)
                grads.up[layer, span, :] = nn(kept.y_t[layer, span, :], du_ref[...]).astype(
                    BF16
                )
                yield
            for piece, c in enumerate(halves):
                dy_ref[c, :] = dr_ref[c, :] + arrived(slot, piece)
            norm_back(layer, 0)
            yield
            for piece, c in enumerate(halves):
                work.dmixed[c, :] = nt(e_ref[c, :], weights.output[layer, mp]) * frame.valid[c]
            yield
            for j in range(2):
                span = slice(j * columns, (j + 1) * columns)
                grads.other[layer, 0, span, :] = nn(
                    kept.mixed_t[layer], e_ref[:, span]
                ).astype(BF16)
            yield

            def taps_out(head, row, layer=layer):
                small_ref[pl.ds(8 + layer * heads + head0 + head, 1), :rows] = row

            yield from attention_back(
                frame,
                work.dmixed,
                kept.qkv.at[layer],
                turned_ref.at[layer],
                head0,
                size_h,
                keep_of(layer),
                work.dqkv,
                taps_out,
            )
            for piece, c in enumerate(halves):
                total = 0.0
                for i in range(3):
                    total = total + nt(work.dqkv[i, c, :], weights.projection[layer, i])
                send(slot + 1, piece, total)
                yield
            for i in range(3):
                grads.other[layer, 1 + i] = nn(kept.x_t[layer], work.dqkv[i]).astype(BF16)
                yield
            target = dy_ref if layer > 0 else token_grad_ref
            for piece, c in enumerate(halves):
                target[c, :] = dr_ref[c, :] + arrived(slot + 1, piece)
        yield

    items = backward()
    for code in ORDER:
        if code < 0:
            next(items)
        elif code >= 1000:
            small.event(code - 1000)
        else:
            ring.event(code // 8, code % 8)


DOWN_PIECES = 4
UP_PIECES = 4
PIECE_KINDS = (
    (0, 1, 1, 0, 0, 1, 0, 0, 1, 0, 0, 0),
    (1, 0, 1, 0, 0, 0, 0, 0, 1, 0, 0, 1),
)
ORDER = (
    -1, -1, 0, -1, 8, -1, 16, -1, 24, 1, -1, 9, 17, -1, 25, -1, -1, 32, -1, 40, -1, 48, -1, 56, 33, 41, 10,
    49, 57, 2, 26, -1, 34, 3, 18, -1, -1, 64, -1, 11, 42, 65, -1, -1, 50, -1, 19, 27, -1, -1, 58, -1, 12, 35,
    -1, 4, -1, 28, 43, 20, -1, -1, -1, 36, -1, 72, -1, 80, -1, 13, 88, 66, 73, 81, 89, 5, 51, 44, 14, 29, 59,
    -1, 21, 82, 74, 37, -1, -1, 15, 67, 104, -1, -1, -1, 6, 52, 30, 90, 105, -1, -1, 38, 7, 31, 45, 83, 96,
    120, 60, -1, -1, 39, 68, 128, -1, -1, 97, 75, 91, 121, 22, 129, 23, 112, 46, 53, 113, 98, 61, -1, 84, 47,
    136, 106, -1, -1, 122, -1, 92, 69, 76, 137, -1, 130, 114, -1, 85, 107, -1, 99, -1, 54, -1, 93, -1, 55, 62,
    144, 123, -1, 63, 152, 115, -1, 70, 86, 145, 153, 100, -1, 71, 77, 1000, 138, 160, -1, 108, 124, -1, -1,
    -1, 87, 176, 131, 161, 94, -1, 116, 146, 95, 1001, 184, 177, 1002, 101, 139, 185, 154, 109, 162, 78, 79,
    168, 125, 178, 132, 147, -1, 169, 117, 155, 163, 179, 148, 1003, 1004, 156, 140, 102, 110, 111, 186, 133,
    103, 180, 187, 1005, 126, 118, 127, 119, 170, 149, 134, 135, 157, 171, 188, 164, 172, 150, 141, 151, 158,
    181, 159, 1006, 189, 182, 183, 165, 190, 173, 191, 142, 143, 174, 166, 175, 167,
)


def pieces_of(width, columns, hidden, layer):
    names = [DOWN] * DOWN_PIECES + [UP] * UP_PIECES + [OUTPUT] + [PROJECTION] * 3
    rows = {DOWN: hidden // DOWN_PIECES, UP: width // UP_PIECES, OUTPUT: width, PROJECTION: width}
    return [(name, rows[name], kind) for name, kind in zip(names, PIECE_KINDS[layer])]


def slots_of(name, rows, kind, width, columns, hidden):
    across = {DOWN: width, UP: hidden, OUTPUT: columns, PROJECTION: columns}[name]

    def room(count):
        return pltpu.VMEM((count, across), BF16)

    return Slots(
        core=room(rows // 2),
        x=room(rows // 4),
        near=room(rows // 4 if kind == 0 else rows // 2),
        mid=room(rows // 4),
    )


def fused_body(tokens, lengths, cotangent, projection, conv_taps, output_weight, norm_gains, norm_shifts, up_weight, down_weight):
    rows, width = tokens.shape
    columns, hidden = projection.shape[3], up_weight.shape[2]
    heads, reach = conv_taps.shape[1:]
    size_h = width // heads
    pairs = columns // (2 * size_h)
    by_kind = jnp.transpose(projection, (0, 2, 1, 3))
    by_head = jnp.transpose(conv_taps, (1, 0, 2))
    vmem = pl.BlockSpec(memory_space=pltpu.VMEM)
    hbm = pl.BlockSpec(memory_space=pl.ANY)
    two = 2 * M
    pieces = pieces_of(width, columns, hidden, 0)
    scratch = (
        Weights(
            projection=pltpu.VMEM((LAYERS, 3, width, columns), BF16),
            output=pltpu.VMEM((LAYERS, 2, columns, width), BF16),
            up=pltpu.VMEM((LAYERS, width, hidden), BF16),
            down=pltpu.VMEM((LAYERS, hidden, width), BF16),
        ),
        Stored(
            attention=Kept(
                ql=pltpu.VMEM((LAYERS, M, columns), F32),
                kl=pltpu.VMEM((LAYERS, M, columns), F32),
                second=pltpu.VMEM((LAYERS, pairs, two, two), F32),
                inverse=pltpu.VMEM((LAYERS, NEWTON + 1, pairs, M, two), F32),
                first=pltpu.VMEM((LAYERS, rows, columns), BF16),
                third=pltpu.VMEM((LAYERS, pairs, two, rows), BF16),
                summary=pltpu.VMEM((LAYERS, pairs, two, two), F32),
                carried=pltpu.VMEM((LAYERS, pairs, two, two), F32),
            ),
            qkv=pltpu.VMEM((LAYERS, 3, rows, columns), BF16),
            normed=pltpu.VMEM((LAYERS, 2, rows, width), BF16),
            spread=pltpu.VMEM((LAYERS, 2, rows, 1), F32),
            slope=pltpu.VMEM((LAYERS, rows, hidden), BF16),
            x_t=pltpu.VMEM((LAYERS, width, rows), BF16),
            mixed_t=pltpu.VMEM((LAYERS, columns, rows), BF16),
            y_t=pltpu.VMEM((LAYERS, width, rows), BF16),
            active_t=pltpu.VMEM((LAYERS, hidden, rows), BF16),
        ),
        Work(
            x=pltpu.VMEM((rows, width), F32),
            x_low=pltpu.VMEM((rows, width), BF16),
            y=pltpu.VMEM((rows, width), F32),
            y_low=pltpu.VMEM((rows, width), BF16),
            mixed=pltpu.VMEM((2, rows, columns), BF16),
            active=pltpu.VMEM((rows, hidden), BF16),
            dmixed=pltpu.VMEM((rows, columns), F32),
            dqkv=pltpu.VMEM((3, rows, columns), BF16),
            taps=pltpu.VMEM((LAYERS, 16, rows), F32),
            turned=pltpu.VMEM((LAYERS, 16, rows), F32),
        ),
        Wire(
            send=pltpu.VMEM((2, rows, width), BF16),
            receive=pltpu.VMEM((2, rows, width), BF16),
            small=pltpu.VMEM((6, 8 + LAYERS * heads, width), F32),
        ),
        [
            slots_of(name, count, max(kinds), width, columns, hidden)
            for (name, count, _), kinds in zip(pieces, zip(*PIECE_KINDS))
        ],
        Sems(
            load=pltpu.SemaphoreType.DMA((4 * LAYERS,)),
            ring_send=pltpu.SemaphoreType.DMA((SENDS * len(pieces),)),
            ring_receive=pltpu.SemaphoreType.DMA((RECEIVES * len(pieces),)),
            small_send=pltpu.SemaphoreType.DMA((6,)),
            small_receive=pltpu.SemaphoreType.DMA((6,)),
            credit=pltpu.SemaphoreType.REGULAR((4 * len(pieces),)),
            ready=pltpu.SemaphoreType.REGULAR((4 * len(pieces),)),
            share_send=pltpu.SemaphoreType.DMA((2 * LAYERS,)),
            share_receive=pltpu.SemaphoreType.DMA((2 * LAYERS,)),
            gather_send=pltpu.SemaphoreType.DMA((2,)),
            gather_receive=pltpu.SemaphoreType.DMA((2,)),
            send=pltpu.SemaphoreType.DMA((4,)),
            receive=pltpu.SemaphoreType.DMA((4,)),
        ),
    )
    own = pltpu.VMEM
    results = pl.pallas_call(
        whole_step,
        out_shape=[
            own((rows, width), BF16),
            own((rows, width), F32),
            own((8 + LAYERS * heads, width), F32),
            own((LAYERS, hidden, width), BF16),
            own((LAYERS, width, hidden), BF16),
            own((LAYERS, 4, width, columns), BF16),
        ],
        in_specs=[pl.BlockSpec(memory_space=pltpu.SMEM)] + [vmem] * 5 + [hbm] * 4,
        out_specs=[vmem] * 6,
        scratch_shapes=scratch,
        compiler_params=pltpu.CompilerParams(
            collective_id=0, has_side_effects=True, vmem_limit_bytes=VMEM_ROOM
        ),
    )(
        lengths,
        tokens,
        cotangent,
        by_head,
        norm_gains,
        norm_shifts,
        by_kind,
        output_weight,
        up_weight,
        down_weight,
    )
    shape = jax.ShapeDtypeStruct
    held = [pltpu.with_memory_space_constraint(result, pltpu.VMEM) for result in results]
    wide = [
        (LAYERS, hidden, width),
        (LAYERS, width, hidden),
        (LAYERS, 3, width, columns),
        (LAYERS, columns, width),
    ]
    outputs = pl.pallas_call(
        widen,
        out_shape=[shape(size, F32) for size in wide]
        + [
            shape((rows, width), BF16),
            shape((rows, width), F32),
            shape((heads, LAYERS, reach), F32),
            shape((LAYERS, 2, width), F32),
            shape((LAYERS, 2, width), F32),
        ],
        in_specs=[vmem] * 6,
        out_specs=[hbm] * 4 + [vmem] * 5,
        scratch_shapes=[pltpu.VMEM(size, F32) for size in wide] + [pltpu.SemaphoreType.DMA((LAYERS * (2 * WIDE_PARTS + 4),))],
        compiler_params=pltpu.CompilerParams(vmem_limit_bytes=WIDE_ROOM),
    )(*held)
    down_grad, up_grad, projection_grad, output_grad = outputs[:4]
    activations, token_grad, taps_grad, gains_grad, shifts_grad = outputs[4:]
    return (
        activations,
        token_grad,
        jnp.transpose(projection_grad, (0, 2, 1, 3)),
        jnp.transpose(taps_grad, (1, 0, 2)),
        output_grad,
        gains_grad,
        shifts_grad,
        up_grad,
        down_grad,
    )


VMEM_ROOM = 97 * 2**19
WIDE_ROOM = 32 * 2**20
WIDE_PARTS = 4


def widen(
    activations_ref,
    token_grad_ref,
    small_ref,
    down_ref,
    up_ref,
    other_ref,
    down_hbm,
    up_hbm,
    projection_hbm,
    output_hbm,
    activations_out,
    token_grad_out,
    taps_out,
    gains_out,
    shifts_out,
    down_wide,
    up_wide,
    projection_wide,
    output_wide,
    sems,
):
    heads, _, reach = taps_out.shape
    columns = output_wide.shape[1]
    copies = []

    def send(source, target):
        copies.append(pltpu.make_async_copy(source, target, sems.at[len(copies)]))
        copies[-1].start()

    def cast(target, source, start, count):
        def step(i, unused):
            span = pl.ds(pl.multiple_of(start + i * 32, 32), 32)
            target[span, :] = source[span, :].astype(F32)
            return unused

        lax.fori_loop(0, count // 32, step, 0)

    for layer in range(LAYERS):
        for wide, source, hbm in ((down_wide, down_ref, down_hbm), (up_wide, up_ref, up_hbm)):
            count = source.shape[1] // WIDE_PARTS
            for part in range(WIDE_PARTS):
                cast(wide.at[layer], source.at[layer], part * count, count)
                span = pl.ds(part * count, count)
                send(wide.at[layer, span], hbm.at[layer, span])
        for i in range(3):
            cast(projection_wide.at[layer, i], other_ref.at[layer, 1 + i], 0, other_ref.shape[2])
            send(projection_wide.at[layer, i], projection_hbm.at[layer, i])
        for i in range(2):
            side = slice(i * columns, (i + 1) * columns)
            output_wide[layer, :, side] = other_ref[layer, 0, side, :].astype(F32)
        send(output_wide.at[layer], output_hbm.at[layer])
    activations_out[...] = activations_ref[...]
    token_grad_out[...] = token_grad_ref[...]
    for layer in range(LAYERS):
        gains_out[layer] = small_ref[2 * layer : 2 * layer + 2, :]
        shifts_out[layer] = small_ref[4 + 2 * layer : 6 + 2 * layer, :]
        first = 8 + layer * heads
        taps_out[:, layer, :] = small_ref[first : first + heads, :reach]
    for copy in copies:
        copy.wait()


def solution(mesh):
    fused = mesh.shape["mp"] == 2 and mesh.shape["dp"] == 16

    def step(*arrays):
        return (fused_body if fused else body)(*arrays)

    return jax.shard_map(
        step,
        mesh=mesh,
        in_specs=(
            P("dp", None),
            P("dp"),
            P("dp", None),
            P(None, None, None, "mp"),
            P(),
            P(None, "mp", None),
            P(),
            P(),
            P(None, None, "mp"),
            P(None, "mp", None),
        ),
        out_specs=(
            P("dp", None),
            P("dp", None),
            P(None, None, None, "mp"),
            P(),
            P(None, "mp", None),
            P(),
            P(),
            P(None, None, "mp"),
            P(None, "mp", None),
        ),
        check_vma=False,
    )
```

```python
from typing import Any, NamedTuple

import jax
import jax.numpy as jnp
from jax import lax
from jax.experimental import pallas as pl
from jax.experimental.pallas import tpu as pltpu
from jax.sharding import PartitionSpec as P

M = 64
NEWTON = 6
LAYERS = 2


highest_value = lax.Precision.HIGHEST


def merged(array, axis, join):
    gathered = jax.tree.map(
        lambda a, kind: lax.all_gather(a.astype(kind), axis),
        array,
        (jnp.bfloat16, jnp.bfloat16, jnp.bfloat16),
    )

    def take(source):
        return jax.tree.map(
            lambda a, own: lax.dynamic_index_in_dim(a, source, 0, False).astype(own.dtype),
            gathered,
            array,
        )

    return lax.fori_loop(
        1, lax.axis_size(axis), lambda source, state: join(state, take(source)), take(0)
    )


def for_sending(array):
    return jax.tree.map(lambda a: a.astype(jnp.bfloat16) if a.dtype == jnp.float32 else a, array)


def softmax_row_block(scores):
    top = jnp.max(scores, axis=-1, keepdims=True)
    matrix_powers = jnp.exp(scores - top)
    return matrix_powers / jnp.sum(matrix_powers, axis=-1, keepdims=True)


def slot_masks(length, count, marks):
    position = jnp.arange(count, dtype=jnp.int32)
    inside = position < length
    segment = position * marks // length
    member = (segment[None, :] == jnp.arange(marks, dtype=jnp.int32)[:, None]) & inside[None, :]
    member = member.astype(jnp.float32)
    pooling = member / jnp.sum(member, axis=1, keepdims=True)
    return (pooling, inside.astype(jnp.float32))


def inverse_head(query_landmarks, key_landmarks, summary):
    scale_factor = query_landmarks.shape[-1] ** (-0.5)
    second = softmax_row_block(
        jnp.dot(query_landmarks, key_landmarks.T, precision=highest_value) * scale_factor
    )
    identity = jnp.eye(second.shape[0], dtype=jnp.float32)
    inverse = second.T / jnp.sum(second * second)
    for sweep in range(NEWTON):
        product = jnp.dot(second, inverse, precision=highest_value)
        inner = 7.0 * identity - product
        inner = 15.0 * identity - jnp.dot(product, inner, precision=highest_value)
        inner = 13.0 * identity - jnp.dot(product, inner, precision=highest_value)
        inverse = 0.25 * jnp.dot(inverse, inner, precision=highest_value)
    return jnp.dot(inverse, summary, precision=highest_value)


def inverse_section(query_landmarks, key_landmarks, summary):
    return jax.vmap(inverse_head)(query_landmarks, key_landmarks, summary)


def near_section(query_matrix, key_landmarks, carried_over):
    scale_factor = query_matrix.shape[-1] ** (-0.5)
    first_entry = softmax_row_block(
        jnp.einsum("nlv,lgv->lng", query_matrix, key_landmarks, precision=highest_value)
        * scale_factor
    )
    return jnp.einsum("xtz,xzb->txb", first_entry, carried_over, precision=highest_value)


def far_scores(query_landmarks, key_matrix, valid_own):
    scale_factor = query_landmarks.shape[-1] ** (-0.5)
    distant_scores = (
        jnp.einsum("owz,toz->owt", query_landmarks, key_matrix, precision=highest_value)
        * scale_factor
    )
    live = valid_own[None, None, :] > 0
    return (jnp.where(live, distant_scores, -1e30), live)


def join_softmax(left, right):
    peak = jnp.maximum(left[0], right[0])
    left_factor = jnp.exp(left[0] - peak)
    right_factor = jnp.exp(right[0] - peak)
    return (
        peak,
        left[1] * left_factor + right[1] * right_factor,
        left[2] * left_factor[..., None] + right[2] * right_factor[..., None],
    )


def attend(query_matrix, key_matrix, value_matrix, pooled_local, valid_own):
    query_portion = jnp.einsum("ji,ilk->ljk", pooled_local, query_matrix, precision=highest_value)
    key_portion = jnp.einsum("ji,ilk->ljk", pooled_local, key_matrix, precision=highest_value)
    query_landmarks, key_landmarks = (
        lax.psum(query_portion.astype(jnp.bfloat16), "mp").astype(jnp.float32),
        lax.psum(key_portion.astype(jnp.bfloat16), "mp").astype(jnp.float32),
    )
    distant_scores, live = far_scores(query_landmarks, key_matrix, valid_own)
    peak = jnp.max(distant_scores, axis=-1)
    matrix_powers = jnp.where(live, jnp.exp(distant_scores - peak[..., None]), 0.0)
    totals = jnp.sum(matrix_powers, axis=-1)
    weighted_values = jnp.einsum(
        "naw,wno->nao", matrix_powers, value_matrix, precision=highest_value
    )
    peak, totals, weighted_values = merged((peak, totals, weighted_values), "mp", join_softmax)
    summary = weighted_values / totals[..., None]
    carried_over = inverse_section(query_landmarks, key_landmarks, summary)
    mixed = near_section(query_matrix, key_landmarks, carried_over)
    return (mixed, (query_landmarks, key_landmarks, peak, totals, summary))


def attend_back(
    grad_rows, query_matrix, key_matrix, value_matrix, pooled_local, valid_own, saved, tap_part
):
    query_landmarks, key_landmarks, peak, totals, summary = saved
    scale_factor = query_matrix.shape[-1] ** (-0.5)
    carried_over, inverse_back = jax.vjp(inverse_section, query_landmarks, key_landmarks, summary)
    unused, near_back = jax.vjp(near_section, query_matrix, key_landmarks, carried_over)
    query_grad, kland_part, carried_part = near_back(grad_rows)
    key_landmark_nearby, carried_grad, tap_grad = (
        lax.psum(kland_part.astype(jnp.bfloat16), "mp").astype(jnp.float32),
        lax.psum(carried_part.astype(jnp.bfloat16), "mp").astype(jnp.float32),
        lax.psum(tap_part.astype(jnp.bfloat16), "mp").astype(jnp.float32),
    )
    query_landmark_gradient, key_landmark_gradient, summary_gradient = inverse_back(carried_grad)
    distant_scores, live = far_scores(query_landmarks, key_matrix, valid_own)
    weight_spread = jnp.where(
        live, jnp.exp(distant_scores - peak[..., None]) / totals[..., None], 0.0
    )
    moving_along = jnp.einsum(
        "owz,toz->owt", summary_gradient, value_matrix, precision=highest_value
    )
    agreed = jnp.sum(summary_gradient * summary, axis=-1)
    slope_values = weight_spread * (moving_along - agreed[..., None])
    value_gradient = jnp.einsum(
        "ofq,ofn->qon", weight_spread, summary_gradient, precision=highest_value
    )
    query_landmark_remote = (
        jnp.einsum("naw,wno->nao", slope_values, key_matrix, precision=highest_value) * scale_factor
    )
    key_gradient = (
        jnp.einsum("ofq,ofn->qon", slope_values, query_landmarks, precision=highest_value)
        * scale_factor
    )
    query_landmark_remote = lax.psum(query_landmark_remote.astype(jnp.bfloat16), "mp").astype(
        jnp.float32
    )
    query_grad = query_grad + jnp.einsum(
        "ge,xgl->exl",
        pooled_local,
        query_landmark_gradient + query_landmark_remote,
        precision=highest_value,
    )
    key_gradient = key_gradient + jnp.einsum(
        "ge,xgl->exl",
        pooled_local,
        key_landmark_gradient + key_landmark_nearby,
        precision=highest_value,
    )
    return (query_grad, key_gradient, value_gradient, tap_grad)


def head_table(columns, heads, size_h):
    begin = lax.axis_index("mp") * columns
    owner = (begin + jnp.arange(columns, dtype=jnp.int32)) // size_h
    return (owner[None, :] == jnp.arange(heads, dtype=jnp.int32)[:, None]).astype(jnp.float32)


def convolve(value_cols, taps, table, valid):
    tap_cols = jnp.dot(taps.T, table, precision=highest_value)
    masked = value_cols * valid[:, None]
    reach = taps.shape[1] // 2
    padded = jnp.pad(masked, ((reach, reach), (0, 0)))
    length_rows = masked.shape[0]
    convolved = jnp.zeros_like(masked)
    for offset in range(taps.shape[1]):
        convolved = convolved + tap_cols[offset] * padded[offset : offset + length_rows]
    return convolved


def contract(left, right, left_dim, right_dim):
    return lax.dot_general(
        left, right, (((left_dim,), (right_dim,)), ((), ())), preferred_element_type=jnp.float32
    )


def normalize(resid, gain, shift):
    centre = resid - jnp.mean(resid, axis=-1, keepdims=True)
    spread = lax.rsqrt(jnp.mean(centre * centre, axis=-1, keepdims=True) + 1e-05)
    normed = centre * spread
    return (normed * gain + shift, normed, spread)


def normalize_back(upstream, normed, spread, gain):
    scaled = upstream * gain
    result = spread * (
        scaled
        - jnp.mean(scaled, axis=-1, keepdims=True)
        - normed * jnp.mean(scaled * normed, axis=-1, keepdims=True)
    )
    return (result, jnp.sum(upstream * normed, axis=0), jnp.sum(upstream, axis=0))


def own_rows(whole):
    count = whole.shape[0] // lax.axis_size("mp")
    return lax.dynamic_slice_in_dim(whole, lax.axis_index("mp") * count, count, 0)


def whole_rows(share):
    return lax.all_gather(share.astype(jnp.bfloat16), "mp", axis=0, tiled=True).astype(share.dtype)


def row_sums(partial_value):
    return lax.psum_scatter(
        partial_value.astype(jnp.bfloat16), "mp", scatter_dimension=0, tiled=True
    ).astype(jnp.float32)


def add_norm(partial_value, resid, gain, shift):
    summed = row_sums(partial_value)
    output, normed, spread = normalize(own_rows(resid) + summed, gain, shift)
    output = whole_rows(output)
    return (output, normed, spread)


def norm_step_back(upstream, normed, spread, gain):
    result, gain_part, shift_part = normalize_back(upstream, normed, spread, gain)
    whole = whole_rows(result)
    return (result, whole, gain_part, shift_part)


def add_input_grad(result, partial_value):
    total = result + row_sums(partial_value)
    return total


def forward_layer(hidden, weights, pooling_own, valid, valid_own):
    projection, taps, output_weight, gains, shifts, up_weight, down_weight = weights
    count, width = hidden.shape
    heads = taps.shape[0]
    size_h = width // heads
    columns = projection.shape[2]
    entering = hidden.astype(jnp.bfloat16)
    mixed = jnp.einsum(
        "td,dsc->tsc", entering, projection, preferred_element_type=jnp.float32
    ).astype(jnp.bfloat16)
    gathered = lax.all_to_all(mixed, "mp", split_axis=0, concat_axis=2, tiled=True)
    rows = gathered.shape[0]
    split_rows = gathered.astype(jnp.float32).reshape(rows, 3, heads, size_h)
    attended, saved = attend(
        split_rows[:, 0], split_rows[:, 1], split_rows[:, 2], pooling_own, valid_own
    )
    attended_cols = lax.all_to_all(
        for_sending(attended.reshape(rows, width)), "mp", split_axis=1, concat_axis=0, tiled=True
    )
    table = head_table(columns, heads, size_h)
    value_cols = mixed[:, 2].astype(jnp.float32)
    convolved = convolve(value_cols, taps, table, valid)
    joined = ((attended_cols + convolved) * valid[:, None]).astype(jnp.bfloat16)
    partial_value = jnp.dot(joined, output_weight, preferred_element_type=jnp.float32)
    middle, normed_first, spread_first = add_norm(partial_value, hidden, gains[0], shifts[0])
    entering_ffn = middle.astype(jnp.bfloat16)
    upward = jnp.dot(entering_ffn, up_weight, preferred_element_type=jnp.float32)
    active = jax.nn.gelu(upward, approximate=True).astype(jnp.bfloat16)
    partial_value = jnp.dot(active, down_weight, preferred_element_type=jnp.float32)
    output, normed_second, spread_second = add_norm(partial_value, middle, gains[1], shifts[1])
    kept = (
        entering,
        value_cols,
        split_rows,
        saved,
        joined,
        table,
        normed_first,
        spread_first,
        entering_ffn,
        upward,
        active,
        normed_second,
        spread_second,
    )
    return (output, kept)


def backward_layer(upstream, weights, kept, pooling_own, valid, valid_own):
    projection, taps, output_weight, gains, shifts, up_weight, down_weight = weights
    (
        entering,
        value_cols,
        split_rows,
        saved,
        joined,
        table,
        normed_first,
        spread_first,
        entering_ffn,
        upward,
        active,
        normed_second,
        spread_second,
    ) = kept
    count, width = entering.shape
    rows = split_rows.shape[0]
    heads = taps.shape[0]
    size_h = width // heads
    result_second, whole_second, gain_second, shift_second = norm_step_back(
        upstream, normed_second, spread_second, gains[1]
    )
    sent_second = whole_second.astype(jnp.bfloat16)
    down_grad = contract(active, sent_second, 0, 0)
    hidden_grad = contract(sent_second, down_weight, 1, 1)
    unused, gelu_back = jax.vjp(lambda value: jax.nn.gelu(value, approximate=True), upward)
    upward_sent = gelu_back(hidden_grad)[0].astype(jnp.bfloat16)
    up_grad = contract(entering_ffn, upward_sent, 0, 0)
    middle_grad = add_input_grad(result_second, contract(upward_sent, up_weight, 1, 1))
    result_first, whole_first, gain_first, shift_first = norm_step_back(
        middle_grad, normed_first, spread_first, gains[0]
    )
    sent_first = whole_first.astype(jnp.bfloat16)
    out_grad = contract(joined, sent_first, 0, 0)
    joined_grad = contract(sent_first, output_weight, 1, 1)
    masked_grad = joined_grad * valid[:, None]
    unused, conv_back = jax.vjp(
        lambda values, tap_rows: convolve(values, tap_rows, table, valid), value_cols, taps
    )
    conv_value_grad, tap_part = conv_back(masked_grad)
    row_grad = (
        lax.all_to_all(
            masked_grad.astype(jnp.bfloat16), "mp", split_axis=0, concat_axis=1, tiled=True
        )
        .astype(masked_grad.dtype)
        .reshape(rows, heads, size_h)
    )
    query_grad, key_gradient, value_gradient, tap_grad = attend_back(
        row_grad,
        split_rows[:, 0],
        split_rows[:, 1],
        split_rows[:, 2],
        pooling_own,
        valid_own,
        saved,
        tap_part,
    )
    stacked_rows = jnp.stack([query_grad, key_gradient, value_gradient], axis=1).reshape(
        rows, 3, width
    )
    column_grad = lax.all_to_all(
        for_sending(stacked_rows), "mp", split_axis=2, concat_axis=0, tiled=True
    ).astype(stacked_rows.dtype)
    column_grad = jnp.concatenate(
        [column_grad[:, :2], (column_grad[:, 2] + conv_value_grad)[:, None]], axis=1
    )
    mixed_sent = column_grad.astype(jnp.bfloat16)
    proj_grad = jnp.einsum("td,tsc->dsc", entering, mixed_sent, preferred_element_type=jnp.float32)
    below = add_input_grad(
        result_first,
        jnp.einsum("tsc,dsc->td", mixed_sent, projection, preferred_element_type=jnp.float32),
    )
    gain_grad = jnp.stack([gain_first, gain_second])
    shift_grad = jnp.stack([shift_first, shift_second])
    gain_grad, shift_grad = lax.psum((gain_grad, shift_grad), "mp")
    return (below, (proj_grad, tap_grad, out_grad, gain_grad, shift_grad, up_grad, down_grad))


def sum_layer(parts):
    return (
        lax.psum(parts[0].astype(jnp.bfloat16), "dp").astype(jnp.float32),
        lax.psum(parts[1].astype(jnp.bfloat16), "dp").astype(jnp.float32),
        lax.psum(parts[2].astype(jnp.bfloat16), "dp").astype(jnp.float32),
        lax.psum(parts[3].astype(jnp.bfloat16), "dp").astype(jnp.float32),
        lax.psum(parts[4].astype(jnp.bfloat16), "dp").astype(jnp.float32),
        lax.psum(parts[5].astype(jnp.bfloat16), "dp").astype(jnp.float32),
        lax.psum(parts[6].astype(jnp.bfloat16), "dp").astype(jnp.float32),
    )


def body(
    tokens,
    lengths,
    cotangent,
    projection,
    conv_taps,
    output_weight,
    norm_gains,
    norm_shifts,
    up_weight,
    down_weight,
):
    count = tokens.shape[0]
    pooling, valid = slot_masks(lengths[0], count, M)
    rows = count // lax.axis_size("mp")
    begin = lax.axis_index("mp") * rows
    pooling_own = lax.dynamic_slice_in_dim(pooling, begin, rows, 1)
    valid_own = lax.dynamic_slice_in_dim(valid, begin, rows, 0)
    weights = (
        projection,
        conv_taps,
        output_weight,
        norm_gains,
        norm_shifts,
        up_weight,
        down_weight,
    )
    hidden = tokens.astype(jnp.float32)
    keeping = []
    for layer_index in range(LAYERS):
        hidden, kept = forward_layer(
            hidden, tuple((item[layer_index] for item in weights)), pooling_own, valid, valid_own
        )
        keeping.append(kept)
    activations = (hidden * valid[:, None]).astype(jnp.bfloat16)
    upstream = cotangent.astype(jnp.float32) * valid[:, None]
    upstream = own_rows(upstream)
    collected = [None] * LAYERS
    for layer_index in reversed(range(LAYERS)):
        upstream, parts = backward_layer(
            upstream,
            tuple((item[layer_index] for item in weights)),
            keeping[layer_index],
            pooling_own,
            valid,
            valid_own,
        )
        collected[layer_index] = sum_layer(parts)
    stacked = tuple(
        (
            jnp.stack([collected[layer_index][member] for layer_index in range(LAYERS)])
            for member in range(7)
        )
    )
    upstream = whole_rows(upstream)
    return (
        activations,
        upstream,
        stacked[0],
        stacked[1],
        stacked[2],
        stacked[3],
        stacked[4],
        stacked[5],
        stacked[6],
    )


class Weights(NamedTuple):
    projection: Any
    output: Any
    up: Any
    down: Any


class Kept(NamedTuple):
    ql: Any
    kl: Any
    second: Any
    inverse: Any
    first: Any
    third: Any
    summary: Any
    carried: Any


class Stored(NamedTuple):
    attention: Any
    qkv: Any
    normed: Any
    spread: Any
    slope: Any
    x_t: Any
    mixed_t: Any
    y_t: Any
    active_t: Any


class Work(NamedTuple):
    x: Any
    x_low: Any
    y: Any
    y_low: Any
    mixed: Any
    active: Any
    dmixed: Any
    dqkv: Any
    taps: Any
    turned: Any


class Shared(NamedTuple):
    active_t: Any
    slope: Any
    y_t: Any
    e: Any


class Wire(NamedTuple):
    send: Any
    receive: Any
    small: Any


class Sems(NamedTuple):
    load: Any
    ring_send: Any
    ring_receive: Any
    small_send: Any
    small_receive: Any
    credit: Any
    ready: Any
    factor_send: Any
    factor_receive: Any
    share_send: Any
    share_receive: Any
    gather_send: Any
    gather_receive: Any
    send: Any
    receive: Any


class Slots(NamedTuple):
    core: Any
    x: Any
    near: Any
    mid: Any


class Grads(NamedTuple):
    down: Any
    up: Any
    other: Any


DOWN, UP, OUTPUT, PROJECTION = range(4)


MESH = pl.DeviceIdType.MESH
F32 = jnp.float32
BF16 = jnp.bfloat16


def nn(a, b):
    return lax.dot_general(a, b, (((1,), (0,)), ((), ())), preferred_element_type=F32)


def nt(a, b):
    return lax.dot_general(a, b, (((1,), (1,)), ((), ())), preferred_element_type=F32)


def parts_of(x):
    high = x.astype(BF16)
    return high, (x - high.astype(F32)).astype(BF16)


def nn3(a, b):
    return nn(jnp.concatenate([a[0], a[1]], 1), jnp.concatenate([b[0], b[0]], 0)) + nn(a[0], b[1])


def nt3(a, b):
    return nt(jnp.concatenate([a[0], a[1]], 1), jnp.concatenate([b[0], b[0]], 1)) + nt(a[0], b[1])


def iota(shape, axis):
    return lax.broadcasted_iota(jnp.int32, shape, axis)


class Frame:
    def __init__(self, length, rows, size_h):
        self.length = length
        self.rows = rows
        self.lane0 = iota((1, 2 * size_h), 1) < size_h
        self.keep = [self.lane0.astype(F32).astype(BF16), (~self.lane0).astype(F32).astype(BF16)]
        self.diag = (iota((2 * M, 2 * M), 0) < M) == (iota((2 * M, 2 * M), 1) < M)
        self.ones = self.diag.astype(F32).astype(BF16)
        self.ones2 = jnp.concatenate([self.ones, self.ones], 0)
        j, t = iota((M, rows), 0), iota((M, rows), 1)
        member = (t * M >= j * length) & (t * M < (j + 1) * length)
        member = member.astype(F32)
        self.member = member.astype(BF16)
        self.inv = 1.0 / jnp.sum(member, axis=1, keepdims=True)
        t, j = iota((rows, M), 0), iota((rows, M), 1)
        self.member_t = ((t * M >= j * length) & (t * M < (j + 1) * length)).astype(F32).astype(BF16)
        self.valid = (iota((rows, 1), 0) < length).astype(F32)
        self.valid_lane = iota((1, rows), 1) < length
        self.band = jnp.abs(iota((rows, rows), 0) - iota((rows, rows), 1)) <= KREACH

    def stack(self, x):
        return jnp.where(self.diag, jnp.concatenate([x, x], 0), 0.0)

    def block(self, x):
        return jnp.where(self.diag, x, 0.0)

    def pack(self, x):
        return x[:M] + x[M:]

    def spread(self, x):
        return jnp.concatenate([x * self.keep[0], x * self.keep[1]], 0)

    def times(self, a, b):
        high, low = b
        left = jnp.concatenate([a[0], a[1]], 1)
        return nn(left, jnp.concatenate([high, high], 0)) + nn(a[0], low)

    def spread_parts(self, x):
        return tuple(self.spread(half) for half in parts_of(x))

    def half_sums(self, x):
        high, low = parts_of(x)
        return nn(jnp.concatenate([high, low], 1), self.ones2)

    def toeplitz(self, row):
        spread = jnp.broadcast_to(row, (self.rows, self.rows))
        turned = pltpu.roll(spread, self.rows - KREACH, 1, stride=1, stride_axis=0)
        return jnp.where(self.band, turned, 0.0).astype(BF16)

    def conv(self, rows_pair, value):
        both = jnp.concatenate([self.toeplitz(rows_pair[0]), self.toeplitz(rows_pair[1])], 1)
        stacked = jnp.concatenate([value * self.keep[0], value * self.keep[1]], 0)
        return nn(both, stacked)

    def diagonals(self, product):
        banded = jnp.where(self.band, product, 0.0)
        total = banded[:8]
        for group in range(1, self.rows // 8):
            part = banded[8 * group : 8 * group + 8]
            total = total + pltpu.roll(part, self.rows - 8 * group, 1)
        total = pltpu.roll(total, KREACH, 1)
        result = total[:1]
        for row in range(1, 8):
            result = result + pltpu.roll(total[row : row + 1], self.rows - row, 1)
        return result


KREACH = 16


def softmax_masked(scores, live):
    scores = jnp.where(live, scores, -1e30)
    top = jnp.max(scores, axis=-1, keepdims=True)
    powers = jnp.where(live, jnp.exp(scores - top), 0.0)
    return powers / jnp.sum(powers, axis=-1, keepdims=True)


def attention(frame, qkv, taps, head0, size_h, keep, out_ref):
    scale = size_h ** (-0.5)
    pairs = qkv.shape[2] // (2 * size_h)
    ql = nn(frame.member, qkv[0]) * frame.inv
    kl = nn(frame.member, qkv[1]) * frame.inv
    keep.ql[...] = ql
    keep.kl[...] = kl
    cols = [slice(p * 2 * size_h, (p + 1) * 2 * size_h) for p in range(pairs)]
    qs = [parts_of(frame.stack(ql[:, c])) for c in cols]
    ks = [parts_of(frame.stack(kl[:, c])) for c in cols]
    second = [softmax_masked(nt3(qs[p], ks[p]) * scale, frame.diag) for p in range(pairs)]
    inverse = []
    halves = iota((2 * M, 1), 0) < M
    for p in range(pairs):
        keep.second[p] = second[p]
        squares = jnp.sum(second[p] * second[p], axis=1, keepdims=True)
        first_total = jnp.sum(jnp.where(halves, squares, 0.0), axis=0, keepdims=True)
        other_total = jnp.sum(jnp.where(halves, 0.0, squares), axis=0, keepdims=True)
        inverse.append(second[p].T * (1.0 / jnp.where(halves, first_total, other_total)))
    second_parts = [parts_of(frame.pack(s)) for s in second]
    summaries, firsts, convolved = [None] * pairs, [None] * pairs, [None] * pairs

    def far(p):
        key, value = qkv[1, :, cols[p]], qkv[2, :, cols[p]]
        scores = nt(jnp.concatenate(qs[p], 1), jnp.concatenate([key, key], 1)) * scale
        third = softmax_masked(scores, frame.valid_lane).astype(BF16)
        keep.third[p] = third
        summaries[p] = frame.block(nn(third, value))
        keep.summary[p] = summaries[p]

    def near(p):
        query = qkv[0, :, cols[p]]
        scores = nt(jnp.concatenate([query, query], 1), jnp.concatenate(ks[p], 1)) * scale
        top0 = jnp.max(jnp.where(frame.lane0, scores, -1e30), axis=-1, keepdims=True)
        top1 = jnp.max(jnp.where(frame.lane0, -1e30, scores), axis=-1, keepdims=True)
        powers = jnp.exp(scores - jnp.where(frame.lane0, top0, top1))
        firsts[p] = (powers / frame.half_sums(powers)).astype(BF16)
        keep.first[:, cols[p]] = firsts[p]

    def local(p):
        inside = (qkv[2, :, cols[p]].astype(F32) * frame.valid).astype(BF16)
        rows_pair = [taps[pl.ds(head0 + 2 * p + i, 1), :] for i in range(2)]
        convolved[p] = frame.conv(rows_pair, inside)

    beside = [(task, p) for p in range(pairs) for task in (far, near, local)]
    inverse = [frame.pack(z) for z in inverse]
    product = [frame.times(second_parts[p], frame.spread_parts(inverse[p])) for p in range(pairs)]
    for sweep in range(NEWTON):
        for p in range(pairs):
            keep.inverse[sweep, p] = inverse[p]
        zp = [parts_of(z) for z in inverse]
        pp = [parts_of(x) for x in product]
        right = [tuple(frame.spread(half) for half in pp[p]) for p in range(pairs)]
        square = [frame.times(pp[p], right[p]) for p in range(pairs)]
        forward = [frame.times(zp[p], right[p]) for p in range(pairs)]
        for task, p in beside[sweep * len(beside) // NEWTON : (sweep + 1) * len(beside) // NEWTON]:
            task(p)
        inner = [frame.spread_parts(7.0 * product[p] - square[p]) for p in range(pairs)]
        if sweep + 1 < NEWTON:
            product = [0.25 * (13.0 * product[p] - 15.0 * square[p] + frame.times(parts_of(square[p]), inner[p])) for p in range(pairs)]
        inverse = [0.25 * (13.0 * inverse[p] - 15.0 * forward[p] + frame.times(parts_of(forward[p]), inner[p])) for p in range(pairs)]
    for p in range(pairs):
        keep.inverse[NEWTON, p] = inverse[p]
        carried = frame.stack(frame.times(parts_of(inverse[p]), parts_of(summaries[p])))
        keep.carried[p] = carried
        mixed = nn(firsts[p], carried.astype(BF16))
        out_ref[:, cols[p]] = ((mixed + convolved[p]) * frame.valid).astype(BF16)


def attention_back(frame, grad, qkv, taps_turned, head0, size_h, keep, out_ref, taps_out):
    scale = size_h ** (-0.5)
    pairs = qkv.shape[2] // (2 * size_h)
    cols = [slice(p * 2 * size_h, (p + 1) * 2 * size_h) for p in range(pairs)]
    each = range(pairs)
    ql, kl = keep.ql[...], keep.kl[...]
    qs = [parts_of(frame.stack(ql[:, c])) for c in cols]
    ks = [parts_of(frame.stack(kl[:, c])) for c in cols]
    summary = [keep.summary[p] for p in each]
    second = [keep.second[p] for p in each]
    dq, dk_landmark, dcarried, grad_low = [], [], [], []
    for p in each:
        c = cols[p]
        g = grad[:, c].astype(BF16)
        grad_low.append(g)
        first = keep.first[:, c].astype(F32)
        dfirst = nt(g, keep.carried[p].astype(BF16))
        slope = first * dfirst
        slope = (slope - first * frame.half_sums(slope)) * scale
        dq.append(nn(slope.astype(BF16), ks[p][0]))
        dk_landmark.append(frame.block(nn(slope.T.astype(BF16), qkv[0, :, c])))
        dcarried.append(frame.block(nn(first.T.astype(BF16), g)))
    yield
    dcp = [parts_of(x) for x in dcarried]
    up = [nt3(dcp[p], parts_of(summary[p])) for p in each]
    dsummary = [nn3(parts_of(frame.stack(keep.inverse[NEWTON, p]).T), dcp[p]) for p in each]
    second_parts = [parts_of(s) for s in second]
    second_turned = [parts_of(s.T) for s in second]
    dsecond = [jnp.zeros_like(s) for s in second]
    for sweep in reversed(range(NEWTON)):
        inverse = [frame.stack(keep.inverse[sweep, p]) for p in each]
        zp = [parts_of(z) for z in inverse]
        product = [nn3(second_parts[p], zp[p]) for p in each]
        pp = [parts_of(x) for x in product]
        inner = [parts_of(7.0 * product[p] - nn3(pp[p], pp[p])) for p in each]
        forward_turned = [parts_of(nn3(zp[p], pp[p]).T) for p in each]
        product_turned = [parts_of(x.T) for x in product]
        inverse_turned = [parts_of(z.T) for z in inverse]
        upp = [parts_of(x) for x in up]
        dforward = [parts_of(0.25 * (nt3(upp[p], inner[p]) - 15.0 * up[p])) for p in each]
        dinner_full = [0.25 * nn3(forward_turned[p], upp[p]) for p in each]
        dinner = [parts_of(x) for x in dinner_full]
        dproduct = [
            parts_of(
                7.0 * dinner_full[p]
                - nt3(dinner[p], pp[p])
                - nn3(product_turned[p], dinner[p])
                + nn3(inverse_turned[p], dforward[p])
            )
            for p in each
        ]
        up = [
            3.25 * up[p] + nt3(dforward[p], pp[p]) + nn3(second_turned[p], dproduct[p])
            for p in each
        ]
        dsecond = [dsecond[p] + nt3(dproduct[p], zp[p]) for p in each]
        yield
    halves = iota((2 * M, 1), 0) < M
    for p in each:
        c = cols[p]
        query, key, value = qkv[0, :, c], qkv[1, :, c], qkv[2, :, c]
        squares = jnp.sum(second[p] * second[p], axis=1, keepdims=True)
        total0 = jnp.sum(jnp.where(halves, squares, 0.0), axis=0, keepdims=True)
        total1 = jnp.sum(jnp.where(halves, 0.0, squares), axis=0, keepdims=True)
        inverse_total = 1.0 / jnp.where(halves, total0, total1)
        start_agree = jnp.sum(up[p] * frame.stack(keep.inverse[0, p]), axis=1, keepdims=True)
        agree0 = jnp.sum(jnp.where(halves, start_agree, 0.0), axis=0, keepdims=True)
        agree1 = jnp.sum(jnp.where(halves, 0.0, start_agree), axis=0, keepdims=True)
        agree = jnp.where(halves, agree0, agree1)
        dsec = dsecond[p] + (up[p].T - 2.0 * agree * second[p]) * inverse_total
        slope = second[p] * dsec
        slope = (slope - second[p] * jnp.sum(slope, axis=-1, keepdims=True)) * scale
        dql = nn(slope.astype(BF16), ks[p][0])
        dkl = nn(slope.T.astype(BF16), qs[p][0]) + dk_landmark[p]
        third = keep.third[p].astype(F32)
        ds = dsummary[p].astype(BF16)
        dthird = nt(ds, value)
        agreed = jnp.sum(dsummary[p] * summary[p], axis=-1, keepdims=True)
        slope = third * (dthird - agreed) * scale
        dv = nn(third.T.astype(BF16), ds)
        dql = dql + frame.block(nn(slope.astype(BF16), key))
        dk = nn(slope.T.astype(BF16), qs[p][0])
        dql = ((dql[:M] + dql[M:]) * frame.inv).astype(BF16)
        dkl = ((dkl[:M] + dkl[M:]) * frame.inv).astype(BF16)
        out_ref[0, :, c] = (dq[p] + nn(frame.member_t, dql)).astype(BF16)
        out_ref[1, :, c] = (dk + nn(frame.member_t, dkl)).astype(BF16)
        inside = (value.astype(F32) * frame.valid).astype(BF16)
        rows_pair = [taps_turned[pl.ds(head0 + 2 * p + i, 1), :] for i in range(2)]
        dv = dv + frame.valid * frame.conv(rows_pair, grad_low[p])
        out_ref[2, :, c] = dv.astype(BF16)
        for i in range(2):
            product = nt(grad_low[p] * frame.keep[i], inside)
            taps_out(2 * p + i, frame.diagonals(product))
        yield


def norm_rows(r, gain, shift):
    centre = r - jnp.mean(r, axis=-1, keepdims=True)
    spread = lax.rsqrt(jnp.mean(centre * centre, axis=-1, keepdims=True) + 1e-05)
    normed = centre * spread
    return normed * gain + shift, normed, spread


def norm_rows_back(dy, normed, spread, gain):
    scaled = dy * gain
    result = spread * (
        scaled
        - jnp.mean(scaled, axis=-1, keepdims=True)
        - normed * jnp.mean(scaled * normed, axis=-1, keepdims=True)
    )
    return (
        result,
        jnp.sum(dy * normed, axis=0, keepdims=True),
        jnp.sum(dy, axis=0, keepdims=True),
    )


GELU_A = 0.7978845608028654
GELU_B = 0.044715


def gelu_both(u):
    square = u * u
    t = jnp.tanh(GELU_A * (u + GELU_B * u * square))
    half = 0.5 * (1.0 + t)
    slope = half + 0.5 * u * (1.0 - t * t) * (GELU_A + (3.0 * GELU_A * GELU_B) * square)
    return u * half, slope


SEND_SEM = ((0, 1, 2, 2, 0, 1, 2, 3), (0, 1, 2, 2, 0, 3, 2, 4, 1), (0, 1, 2, 2, 0, 1, 2, 3))
RECEIVE_SEM = ((0, 1, 2, 3, 2, 6, 5, 4), (0, 1, 2, 3, 6, 6, 5, 4, 2), (0, 1, 2, 3, 2, 6, 5, 4))
SENDS, RECEIVES = 5, 7


class Reduction:
    def __init__(self, sems):
        dp, self.mp = lax.axis_index("dp"), lax.axis_index("mp")
        z = dp // 4
        self.x = (dp // 2) % 2
        self.core = dp % 2
        self.upper = z // 2
        self.inner = (z == 1) | (z == 2)
        self.outer = (z == 0) | (z == 3)
        self.to_core = dp + 1 - 2 * self.core
        self.to_x = dp + 2 - 4 * self.x
        self.to_near = dp + 4 - 8 * (z % 2)
        self.to_mid = (3 - z) * 4 + dp % 4
        self.sems = sems
        self.pieces = []

    def greet(self, barrier):
        for other in (self.to_core, self.to_x, self.to_near, self.to_mid):
            pl.semaphore_signal(barrier, inc=1, device_id=(other, self.mp), device_id_type=MESH)

    def add(self, rows, kind, view, slots, credit, gives, takes, other_kind):
        self.pieces.append((rows // 4, kind, view, slots, credit, gives, takes, other_kind))

    def copy(self, index, slot, source, target, to):
        kind, place = self.pieces[index][1], self.pieces[index][4]
        return pltpu.make_async_remote_copy(
            src_ref=source,
            dst_ref=target,
            send_sem=self.sems.ring_send.at[place * SENDS + SEND_SEM[kind][slot]],
            recv_sem=self.sems.ring_receive.at[place * RECEIVES + RECEIVE_SEM[kind][slot]],
            device_id=(to, self.mp),
            device_id_type=MESH,
        )

    def event(self, index, step):
        quarter, kind, view, slots, credit, gives, takes, other_kind = self.pieces[index]
        x, core, upper = self.x, self.core, self.upper
        side = upper if kind == 1 else x

        def region(half, which, count=1):
            return view(half, which, count * quarter)

        def arrived(slot, ref):
            self.copy(index, slot, ref, ref, self.to_core).wait_recv()

        def sent(slot, ref):
            self.copy(index, slot, ref, ref, self.to_core).wait_send()

        def send(slot, source, destination, to, need=None):
            if takes and need is not None:
                pl.semaphore_wait(self.sems.credit.at[credit * 4 + need], 1)
            self.copy(index, slot, source, destination, to).start()

        def free(which, to):
            if gives:
                pl.semaphore_signal(
                    self.sems.credit.at[credit * 4 + which],
                    inc=1,
                    device_id=(to, self.mp),
                    device_id_type=MESH,
                )

        def ready(which, slot, ref, to):
            sent(slot, ref)
            pl.semaphore_signal(
                self.sems.ready.at[credit * 4 + which],
                inc=1,
                device_id=(to, self.mp),
                device_id_type=MESH,
            )

        def await_ready(which):
            pl.semaphore_wait(self.sems.ready.at[credit * 4 + which], 1)

        def slot_part(ref, which):
            return ref.at[pl.ds(pl.multiple_of(which * quarter, 16), quarter)]

        def sum_into(ref, others):
            block = 48 if quarter % 48 == 0 else 16

            def step_rows(i, unused):
                span = pl.ds(pl.multiple_of(i * block, 16), block)
                total = ref[span, :].astype(F32)
                for other in others:
                    total = total + other[span, :].astype(F32)
                ref[span, :] = total.astype(BF16)
                return unused

            lax.fori_loop(0, quarter // block, step_rows, 0)

        mine, other = region(core, side), region(core, 1 - side)
        if step == 0:
            if kind == 2:
                send(0, region(1 - core, x), slot_part(slots.core, 0), self.to_core, need=0)
            else:
                send(0, region(1 - core, 0, 2), slots.core, self.to_core, need=0)
        elif step == 7:
            for slot, which in ((6, side), (7, 1 - side)):
                arrived(slot, region(1 - core, which))
            sent(6, mine)
            sent(7, other)
            if kind != 1:
                sent(5, mine)

                @pl.when(self.inner)
                def _():
                    sent(4, mine)

            else:

                @pl.when(self.inner)
                def _():
                    for slot in (4, 5, 8):
                        sent(slot, mine)

        elif kind == 2 and step < 4:
            if step > 1:

                @pl.when(self.outer if step == 2 else self.inner)
                def _():
                    arrived(0, slot_part(slots.core, 0))
                    if step == 2:
                        sum_into(mine, [slot_part(slots.core, 0)])
                        send(2, mine, slot_part(slots.near, 0), self.to_near, need=2)
                    else:
                        arrived(2, slot_part(slots.near, 0))
                        sum_into(mine, [slot_part(slots.core, 0), slot_part(slots.near, 0)])
                        send(3, mine, slots.mid, self.to_mid, need=3)
                    ready(0, 0, region(1 - core, x), self.to_core)

            if step == 3:

                @pl.when(self.outer)
                def _():
                    ready(2, 2, mine, self.to_near)

        elif kind != 1:
            if step == 1:
                arrived(0, slots.core)
                sum_into(other, [slot_part(slots.core, 1 - x)])
                if other_kind == 0:
                    send(1, other, slots.x, self.to_x, need=1)
                else:
                    if takes:

                        @pl.when(self.inner)
                        def _():
                            pl.semaphore_wait(self.sems.credit.at[credit * 4 + 1], 1)

                    send(1, other, slots.x, self.to_x)
                ready(0, 0, region(1 - core, 0, 2), self.to_core)
            elif step == 2:

                @pl.when(self.outer)
                def _():
                    arrived(1, slots.x)
                    sum_into(mine, [slot_part(slots.core, x), slots.x])
                    free(0, self.to_core)
                    if other_kind == 0:
                        free(1, self.to_x)
                    send(2, mine, slot_part(slots.near, 0), self.to_near, need=2)
                    ready(1, 1, other, self.to_x)

            elif step == 3:

                @pl.when(self.inner)
                def _():
                    arrived(1, slots.x)
                    arrived(2, slot_part(slots.near, 0))
                    sum_into(mine, [slot_part(slots.core, x), slots.x, slot_part(slots.near, 0)])
                    free(0, self.to_core)
                    if other_kind != 2:
                        free(1, self.to_x)
                    free(2, self.to_near)
                    send(3, mine, slots.mid, self.to_mid, need=3)
                    ready(1, 1, other, self.to_x)

                @pl.when(self.outer)
                def _():
                    ready(2, 2, mine, self.to_near)

            elif step == 4:

                @pl.when(self.inner)
                def _():
                    arrived(3, slots.mid)
                    sent(3, mine)
                    sum_into(mine, [slots.mid])
                    free(3, self.to_mid)
                    await_ready(2)
                    send(4, mine, mine, self.to_near)
                    if kind == 0:
                        await_ready(1)
                    send(5, mine, mine, self.to_x)
                    await_ready(0)
                    send(6, mine, mine, self.to_core)

            elif step == 5:

                @pl.when(self.outer)
                def _():
                    arrived(4, mine)
                    if kind == 0:
                        await_ready(1)
                    send(5, mine, mine, self.to_x)
                    await_ready(0)
                    send(6, mine, mine, self.to_core)

            elif step == 6:
                arrived(5, other)
                send(7, other, other, self.to_core)
        else:
            if step == 1:

                @pl.when(self.outer)
                def _():
                    arrived(0, slots.core)
                    sum_into(region(core, 0), [slot_part(slots.core, 0)])
                    sum_into(region(core, 1), [slot_part(slots.core, 1)])
                    free(0, self.to_core)
                    send(2, region(core, 0, 2), slots.near, self.to_near, need=2)
                    ready(0, 0, region(1 - core, 0, 2), self.to_core)

            elif step == 2:

                @pl.when(self.outer)
                def _():
                    ready(2, 2, region(core, 0, 2), self.to_near)

                @pl.when(self.inner)
                def _():
                    arrived(0, slots.core)
                    arrived(2, slots.near)
                    sum_into(other, [slot_part(slots.core, 1 - side), slot_part(slots.near, 1 - side)])
                    send(3, other, slots.mid, self.to_mid, need=3)
                    ready(0, 0, region(1 - core, 0, 2), self.to_core)

            elif step == 3:

                @pl.when(self.inner)
                def _():
                    arrived(3, slots.mid)
                    sum_into(mine, [slot_part(slots.core, side), slot_part(slots.near, side), slots.mid])
                    free(0, self.to_core)
                    free(2, self.to_near)
                    free(3, self.to_mid)
                    send(1, mine, slots.x, self.to_x, need=1)
                    ready(3, 3, other, self.to_mid)

            elif step == 4:

                @pl.when(self.inner)
                def _():
                    arrived(1, slots.x)
                    sent(1, mine)
                    sum_into(mine, [slots.x])
                    if other_kind != 2:
                        free(1, self.to_x)
                    await_ready(3)
                    send(4, mine, mine, self.to_mid)
                    await_ready(2)
                    send(8, mine, mine, self.to_near)
                    await_ready(0)
                    send(6, mine, mine, self.to_core)

            elif step == 5:

                @pl.when(self.inner)
                def _():
                    arrived(4, other)
                    send(5, other, other, self.to_near)
                    send(7, other, other, self.to_core)

                @pl.when(self.outer)
                def _():
                    arrived(8, mine)
                    await_ready(0)
                    send(6, mine, mine, self.to_core)

            elif step == 6:

                @pl.when(self.outer)
                def _():
                    arrived(5, other)
                    send(7, other, other, self.to_core)


class SmallSum:
    def __init__(self, ring, total, slots, sems, first_tap):
        self.ring, self.total, self.slots, self.sems, self.first_tap = ring, total, slots, sems, first_tap

    def copy(self, slot, target, to, mp):
        return pltpu.make_async_remote_copy(
            src_ref=self.total,
            dst_ref=target,
            send_sem=self.sems.small_send.at[slot],
            recv_sem=self.sems.small_receive.at[slot],
            device_id=(to, mp),
            device_id_type=MESH,
        )

    def event(self, step):
        ring, total, slots = self.ring, self.total, self.slots
        dp = ring.to_core + 2 * ring.core - 1

        def start(slot, to, mp=None):
            self.copy(slot, slots.at[slot], to, ring.mp if mp is None else mp).start()

        def take(slot):
            self.copy(slot, slots.at[slot], dp, ring.mp).wait_recv()

        def sent(slot):
            self.copy(slot, slots.at[slot], dp, ring.mp).wait_send()

        if step == 0:
            start(0, dp, 1 - ring.mp)
        elif step == 1:
            take(0)
            sent(0)
            total[self.first_tap :, :] += slots[0, self.first_tap :, :]
            start(1, ring.to_core)
        elif step == 2:
            take(1)
            sent(1)
            total[...] += slots[1]
            start(2, ring.to_x)
        elif step == 3:
            take(2)
            sent(2)
            total[...] += slots[2]

            @pl.when(ring.outer)
            def _():
                start(3, ring.to_near)

        elif step == 4:

            @pl.when(ring.inner)
            def _():
                take(3)
                total[...] += slots[3]
                start(4, ring.to_mid)

        elif step == 5:

            @pl.when(ring.inner)
            def _():
                take(4)
                sent(4)
                total[...] += slots[4]
                start(5, ring.to_near)

        elif step == 6:

            @pl.when(ring.outer)
            def _():
                take(5)
                sent(3)
                total[...] = slots[5]

            @pl.when(ring.inner)
            def _():
                sent(5)


def whole_step(
    length_ref,
    tokens_ref,
    cotangent_ref,
    raw_taps_ref,
    gains_ref,
    shifts_ref,
    projection_hbm,
    output_hbm,
    up_hbm,
    down_hbm,
    activations_ref,
    token_grad_ref,
    small_ref,
    down_grad_ref,
    up_grad_ref,
    other_grad_ref,
    weights,
    kept,
    work,
    shared,
    wire,
    slots,
    sems,
):
    rows, width = tokens_ref.shape
    columns = projection_hbm.shape[3]
    hidden = up_hbm.shape[2]
    heads, _, reach = raw_taps_ref.shape
    grads = Grads(down_grad_ref, up_grad_ref, other_grad_ref)
    size_h = width // heads
    half = rows // 2
    tile = 384
    dp, mp = lax.axis_index("dp"), lax.axis_index("mp")
    head0 = mp * (columns // size_h)
    partner = (dp, 1 - mp)

    def own_half(layer):
        return weights.output.at[layer, mp]

    loads = []
    order = [
        (projection_hbm, weights.projection),
        (output_hbm, weights.output),
        (up_hbm, weights.up),
        (down_hbm, weights.down),
    ]
    for layer in range(LAYERS):
        for index, (source, place) in enumerate(order):
            load = pltpu.make_async_copy(
                source.at[layer],
                own_half(layer) if index == 1 else place.at[layer],
                sems.load.at[layer * 4 + index],
            )
            load.start()
            loads.append(load)

    barrier = pltpu.get_barrier_semaphore()
    pl.semaphore_signal(barrier, inc=1, device_id=partner, device_id_type=MESH)
    ring = Reduction(sems)
    ring.greet(barrier)

    frame = Frame(length_ref[0], rows, size_h)
    taps_ref, turned_ref = work.taps, work.turned
    taps_ref[...] = jnp.zeros_like(taps_ref)
    mirror = iota((rows, rows), 0) + iota((rows, rows), 1) == reach - 1
    mirror = mirror.astype(F32).astype(BF16)
    for layer in range(LAYERS):
        taps_ref[layer, :heads, :reach] = raw_taps_ref[:, layer, :]
        turned_ref[layer] = nn(taps_ref[layer].astype(BF16), mirror)
    flights = {}

    def send(slot, piece, partial_value):
        span = pl.ds(piece * half, half)
        wire.send[span, :] = partial_value.astype(BF16)
        copy = pltpu.make_async_remote_copy(
            src_ref=wire.send.at[span],
            dst_ref=wire.receive.at[slot % 2, span],
            send_sem=sems.send.at[slot % 2 * 2 + piece],
            recv_sem=sems.receive.at[slot % 2 * 2 + piece],
            device_id=partner,
            device_id_type=MESH,
        )
        copy.start()
        flights[slot, piece] = copy

    def arrived(slot, piece):
        span = pl.ds(piece * half, half)
        flights[slot, piece].wait()
        return wire.send[span, :].astype(F32) + wire.receive[
            slot % 2, span, :
        ].astype(F32)

    def share_copy(layer, hop):
        part = columns // 2
        which, first = (mp, ring.core) if hop == 0 else (1 - mp, ring.core)
        place = weights.output.at[layer, which, pl.ds(pl.multiple_of(first * part, 16), part)]
        return pltpu.make_async_remote_copy(
            src_ref=place,
            dst_ref=place,
            send_sem=sems.share_send.at[layer * 2 + hop],
            recv_sem=sems.share_receive.at[layer * 2 + hop],
            device_id=partner if hop == 0 else (ring.to_core, mp),
            device_id_type=MESH,
        )

    def gather_copy(layer, piece):
        place = work.mixed.at[mp, pl.ds(piece * half, half)]
        return pltpu.make_async_remote_copy(
            src_ref=place,
            dst_ref=place,
            send_sem=sems.gather_send.at[piece],
            recv_sem=sems.gather_receive.at[piece],
            device_id=partner,
            device_id_type=MESH,
        )

    side = hidden // 2
    near_rows = pl.ds(pl.multiple_of(ring.x * side, 128), side)
    far_rows = pl.ds(pl.multiple_of((1 - ring.x) * side, 128), side)
    factors = []

    def factor_copy(index, source, target):
        return pltpu.make_async_remote_copy(
            src_ref=source,
            dst_ref=target,
            send_sem=sems.factor_send.at[index],
            recv_sem=sems.factor_receive.at[index],
            device_id=(ring.to_x, mp),
            device_id_type=MESH,
        )

    halves = [slice(0, half), slice(half, rows)]

    def project(layer, c):
        for i in range(3):
            kept.qkv[layer, i, c, :] = nn(
                work.x_low[c, :], weights.projection[layer, i]
            ).astype(BF16)

    def keep_of(layer):
        return Kept(*(ref.at[layer] for ref in kept.attention))

    work.x[...] = tokens_ref[...].astype(F32)
    work.x_low[...] = tokens_ref[...]
    loads[0].wait()
    for c in halves:
        project(0, c)
    pl.semaphore_wait(barrier, 5)
    for layer in range(LAYERS):
        loads[layer * 4 + 1].wait()
        share_copy(layer, 0).start()
        attention(
            frame,
            kept.qkv.at[layer],
            taps_ref.at[layer],
            head0,
            size_h,
            keep_of(layer),
            work.mixed.at[mp],
        )
        slot = layer * 2
        for piece in range(len(halves)):
            gather_copy(layer, piece).start()
        share_copy(layer, 0).wait()
        share_copy(layer, 1).start()
        kept.mixed_t[layer] = work.mixed[mp].T
        kept.x_t[layer] = work.x_low[...].T
        loads[layer * 4 + 2].wait()
        loads[layer * 4 + 3].wait()
        share_copy(layer, 1).wait()
        for piece, c in enumerate(halves):
            gather_copy(layer, piece).wait()
            summed = work.x[c, :]
            for part in range(2):
                summed = summed + nn(work.mixed[part, c, :], weights.output[layer, part])
            y, normed, spread = norm_rows(summed, gains_ref[layer, 0:1], shifts_ref[layer, 0:1])
            kept.normed[layer, 0, c, :] = normed.astype(BF16)
            kept.spread[layer, 0, c, :] = spread
            work.y[c, :] = y
            work.y_low[c, :] = y.astype(BF16)
            for j in range(hidden // tile):
                span = slice(j * tile, (j + 1) * tile)
                u = nn(work.y_low[c, :], weights.up[layer, :, span])
                active, slope = gelu_both(u)
                work.active[c, span] = active.astype(BF16)
                kept.slope[layer, c, span] = slope.astype(BF16)
            send(slot + 1, piece, nn(work.active[c, :], weights.down[layer]))
        kept.active_t[layer] = work.active[...].T
        kept.y_t[layer] = work.y_low[...].T
        if FACTORED[layer]:
            factors.append(factor_copy(0, kept.active_t.at[layer, far_rows], shared.active_t))
            factors.append(factor_copy(1, kept.slope.at[layer, :, far_rows], shared.slope))
            factors.append(factor_copy(2, kept.y_t.at[layer], shared.y_t))
            for copy in factors:
                copy.start()
        if layer + 1 < LAYERS:
            loads[layer * 4 + 4].wait()
        for piece, c in enumerate(halves):
            summed = work.y[c, :] + arrived(slot + 1, piece)
            y, normed, spread = norm_rows(summed, gains_ref[layer, 1:2], shifts_ref[layer, 1:2])
            kept.normed[layer, 1, c, :] = normed.astype(BF16)
            kept.spread[layer, 1, c, :] = spread
            if layer + 1 < LAYERS:
                work.x[c, :] = y
                work.x_low[c, :] = y.astype(BF16)
                project(layer + 1, c)
            else:
                activations_ref[c, :] = (y * frame.valid[c]).astype(BF16)

    def add_pieces(layer):
        listed = pieces_of(width, columns, hidden, layer)
        listed_rows = {DOWN: hidden, UP: 2 * width}
        for k, (name, rows_of, kind) in enumerate(listed):
            before = sum(item[1] for item in listed[:k] if item[0] == name)
            index = sum(1 for item in listed[:k] if item[0] == name)

            quarter = rows_of // 4
            if kind == 2:
                before, high, wide = before // 2, quarter, listed_rows[name] // 2
            else:
                high, wide = 2 * quarter, quarter
            if name in (DOWN, UP):
                ref = (grads.down if name == DOWN else grads.up).at[layer]
            else:
                ref = grads.other.at[layer, 0 if name == OUTPUT else 1 + index]
                before = 0

            def view(half, which, count, ref=ref, before=before, high=high, wide=wide):
                return ref.at[pl.ds(pl.multiple_of(before + half * high + which * wide, 16), count)]

            ring.add(rows_of, kind, view, slots[k], k, layer > 0, layer + 1 < LAYERS, PIECE_KINDS[1 - layer][k])

    for layer in reversed(range(LAYERS)):
        add_pieces(layer)
    small = SmallSum(ring, small_ref, wire.small, sems, 8)
    dy_ref, dr_ref, e_ref, du_ref = work.x, work.y, work.y_low, work.active

    def norm_back(layer, which):
        gain = gains_ref[layer, which : which + 1]
        gain_sum = shift_sum = 0.0
        for c in halves:
            result, gain_part, shift_part = norm_rows_back(
                dy_ref[c, :],
                kept.normed[layer, which, c, :].astype(F32),
                kept.spread[layer, which, c, :],
                gain,
            )
            dr_ref[c, :] = result
            e_ref[c, :] = result.astype(BF16)
            gain_sum, shift_sum = gain_sum + gain_part, shift_sum + shift_part
        row = layer * 2 + which
        small_ref[row : row + 1, :] = gain_sum
        small_ref[row + 4 : row + 5, :] = shift_sum

    du_other = work.x_low

    def down_grads(layer):
        block = hidden // DOWN_PIECES
        for j in range(DOWN_PIECES):
            if FACTORED[layer]:
                low = slice(j * block // 2, (j + 1) * block // 2)
                span = pl.ds(pl.multiple_of(ring.x * side + low.start, 16), block // 2)
                value = nn(kept.active_t[layer, span, :], e_ref[...]) + nn(
                    shared.active_t[low, :], shared.e[...]
                )
            else:
                span = slice(j * block, (j + 1) * block)
                value = nn(kept.active_t[layer, span, :], e_ref[...])
            grads.down[layer, span, :] = value.astype(BF16)
            yield

    def up_grads(layer):
        block = 2 * width // UP_PIECES
        for j in range(UP_PIECES):
            if FACTORED[layer]:
                low = slice(j * block // 2, (j + 1) * block // 2)
                span = pl.ds(pl.multiple_of(ring.x * width + low.start, 16), block // 2)
                value = nn(kept.y_t[layer, low, :], du_ref[:, near_rows]) + nn(
                    shared.y_t[low, :], du_other[...]
                )
            else:
                span = slice(j * block, (j + 1) * block)
                at, first = divmod(j * block, width)
                value = nn(
                    kept.y_t[layer, first : first + block, :],
                    du_ref[:, at * side : (at + 1) * side],
                )
            grads.up[layer, span, :] = value.astype(BF16)
            yield

    def backward():
        small_ref[...] = jnp.zeros_like(small_ref)
        for piece, c in enumerate(halves):
            dy_ref[c, :] = cotangent_ref[c, :].astype(F32) * frame.valid[c]
        for layer in reversed(range(LAYERS)):
            slot = 4 + (LAYERS - 1 - layer) * 2
            norm_back(layer, 1)
            if FACTORED[layer]:
                factors.append(factor_copy(3, e_ref, shared.e))
                factors[3].start()
            yield
            if not FACTORED[layer]:
                yield from down_grads(layer)
            for j in range(hidden // tile):
                span = slice(j * tile, (j + 1) * tile)
                dh = nt(e_ref[...], weights.down[layer, span, :])
                du_ref[:, span] = (dh * kept.slope[layer, :, span].astype(F32)).astype(BF16)
            yield
            for piece, c in enumerate(halves):
                send(slot, piece, nt(du_ref[c, :], weights.up[layer]))
                yield
            if FACTORED[layer]:
                for copy in factors:
                    copy.wait()
                for j in range(side // tile):
                    span = slice(j * tile, (j + 1) * tile)
                    near = pl.ds(pl.multiple_of(ring.x * side + j * tile, 128), tile)
                    dh = nt(shared.e[...], weights.down[layer, near, :])
                    du_other[:, span] = (dh * shared.slope[:, span].astype(F32)).astype(BF16)
                yield
                yield from down_grads(layer)
            yield from up_grads(layer)
            for piece, c in enumerate(halves):
                dy_ref[c, :] = dr_ref[c, :] + arrived(slot, piece)
            norm_back(layer, 0)
            yield
            for piece, c in enumerate(halves):
                work.dmixed[c, :] = nt(e_ref[c, :], weights.output[layer, mp]) * frame.valid[c]
            yield
            for j in range(2):
                span = slice(j * columns, (j + 1) * columns)
                grads.other[layer, 0, span, :] = nn(
                    kept.mixed_t[layer], e_ref[:, span]
                ).astype(BF16)
            yield

            def taps_out(head, row, layer=layer):
                small_ref[pl.ds(8 + layer * heads + head0 + head, 1), :rows] = row

            yield from attention_back(
                frame,
                work.dmixed,
                kept.qkv.at[layer],
                turned_ref.at[layer],
                head0,
                size_h,
                keep_of(layer),
                work.dqkv,
                taps_out,
            )
            for piece, c in enumerate(halves):
                total = 0.0
                for i in range(3):
                    total = total + nt(work.dqkv[i, c, :], weights.projection[layer, i])
                send(slot + 1, piece, total)
                yield
            for i in range(3):
                grads.other[layer, 1 + i] = nn(kept.x_t[layer], work.dqkv[i]).astype(BF16)
                yield
            target = dy_ref if layer > 0 else token_grad_ref
            for piece, c in enumerate(halves):
                target[c, :] = dr_ref[c, :] + arrived(slot + 1, piece)
        yield

    items = backward()
    for code in ORDER:
        if code < 0:
            next(items)
        elif code >= 1000:
            small.event(code - 1000)
        else:
            ring.event(code // 8, code % 8)


FACTORED = (True, False)
DOWN_PIECES = 4
UP_PIECES = 4
PIECE_KINDS = (
    (2, 2, 2, 2, 2, 2, 2, 2, 1, 0, 0, 0),
    (0, 1, 0, 0, 1, 0, 0, 0, 1, 1, 0, 0),
)
ORDER = (
    -1, -1, 0, -1, 8, -1, 16, -1, 24, -1, 1, 9, -1, -1, 17, -1, 32, -1, 40, 25, -1, 48, -1, 56, 33, 41, 49, 2,
    57, 18, -1, 10, 26, -1, -1, 64, -1, -1, 65, 34, 42, -1, -1, 50, 11, 3, -1, -1, -1, 35, 58, 19, -1, -1, -1,
    12, 27, 4, -1, -1, -1, 72, -1, 80, -1, 88, 36, 20, 73, 81, 89, 66, 13, 43, 28, -1, 90, 82, 5, -1, 51, 37,
    -1, -1, 21, 59, 67, 44, 74, 52, 91, 60, -1, 38, 45, 6, 14, 29, -1, 75, 83, -1, -1, 22, -1, -1, 39, 128,
    129, -1, 68, 7, 96, 97, 15, 104, 105, 53, -1, -1, 23, 112, 113, 92, -1, 130, 98, 106, -1, -1, 114, -1, 46,
    84, 61, -1, -1, 47, 136, 137, 30, -1, 131, 69, 138, -1, 93, 54, 31, 120, 121, -1, 99, -1, 122, 55, 144,
    145, 76, 85, 62, -1, -1, 107, 146, 132, 63, 152, 153, -1, 1000, 70, 94, -1, 154, -1, 100, 115, -1, 71,
    160, -1, -1, 95, 184, 86, 161, 77, 139, 185, 1001, 87, 176, 1002, 133, 177, 108, 123, 101, 186, 78, -1,
    147, 155, 116, 140, 1003, 79, 168, 134, 109, 169, 124, 135, 178, 117, 102, 141, 103, 148, 162, 110, 125,
    111, 156, 187, 170, 149, 1004, 163, 179, 188, 1005, 171, 180, 118, 157, 119, 142, 189, 143, 1006, 126,
    127, 172, 181, 150, 151, 164, 158, 173, 159, 190, 191, 165, 182, 183, 174, 166, 175, 167,
)


def pieces_of(width, columns, hidden, layer):
    names = [DOWN] * DOWN_PIECES + [UP] * UP_PIECES + [OUTPUT] + [PROJECTION] * 3
    rows = {DOWN: hidden // DOWN_PIECES, UP: 2 * width // UP_PIECES, OUTPUT: width, PROJECTION: width}
    return [(name, rows[name], kind) for name, kind in zip(names, PIECE_KINDS[layer])]


def slots_of(name, rows, long, width, columns, hidden):
    across = {DOWN: width, UP: hidden // 2, OUTPUT: columns, PROJECTION: columns}[name]

    def room(count):
        return pltpu.VMEM((count, across), BF16)

    return Slots(
        core=room(rows // 2),
        x=room(rows // 4),
        near=room(rows // 2 if long else rows // 4),
        mid=room(rows // 4),
    )


def fused_body(tokens, lengths, cotangent, projection, conv_taps, output_weight, norm_gains, norm_shifts, up_weight, down_weight):
    rows, width = tokens.shape
    columns, hidden = projection.shape[3], up_weight.shape[2]
    heads, reach = conv_taps.shape[1:]
    size_h = width // heads
    pairs = columns // (2 * size_h)
    by_kind = jnp.transpose(projection, (0, 2, 1, 3))
    by_head = jnp.transpose(conv_taps, (1, 0, 2))
    vmem = pl.BlockSpec(memory_space=pltpu.VMEM)
    hbm = pl.BlockSpec(memory_space=pl.ANY)
    two = 2 * M
    pieces = pieces_of(width, columns, hidden, 0)
    scratch = (
        Weights(
            projection=pltpu.VMEM((LAYERS, 3, width, columns), BF16),
            output=pltpu.VMEM((LAYERS, 2, columns, width), BF16),
            up=pltpu.VMEM((LAYERS, width, hidden), BF16),
            down=pltpu.VMEM((LAYERS, hidden, width), BF16),
        ),
        Stored(
            attention=Kept(
                ql=pltpu.VMEM((LAYERS, M, columns), F32),
                kl=pltpu.VMEM((LAYERS, M, columns), F32),
                second=pltpu.VMEM((LAYERS, pairs, two, two), F32),
                inverse=pltpu.VMEM((LAYERS, NEWTON + 1, pairs, M, two), F32),
                first=pltpu.VMEM((LAYERS, rows, columns), BF16),
                third=pltpu.VMEM((LAYERS, pairs, two, rows), BF16),
                summary=pltpu.VMEM((LAYERS, pairs, two, two), F32),
                carried=pltpu.VMEM((LAYERS, pairs, two, two), F32),
            ),
            qkv=pltpu.VMEM((LAYERS, 3, rows, columns), BF16),
            normed=pltpu.VMEM((LAYERS, 2, rows, width), BF16),
            spread=pltpu.VMEM((LAYERS, 2, rows, 1), F32),
            slope=pltpu.VMEM((LAYERS, rows, hidden), BF16),
            x_t=pltpu.VMEM((LAYERS, width, rows), BF16),
            mixed_t=pltpu.VMEM((LAYERS, columns, rows), BF16),
            y_t=pltpu.VMEM((LAYERS, width, rows), BF16),
            active_t=pltpu.VMEM((LAYERS, hidden, rows), BF16),
        ),
        Work(
            x=pltpu.VMEM((rows, width), F32),
            x_low=pltpu.VMEM((rows, width), BF16),
            y=pltpu.VMEM((rows, width), F32),
            y_low=pltpu.VMEM((rows, width), BF16),
            mixed=pltpu.VMEM((2, rows, columns), BF16),
            active=pltpu.VMEM((rows, hidden), BF16),
            dmixed=pltpu.VMEM((rows, columns), F32),
            dqkv=pltpu.VMEM((3, rows, columns), BF16),
            taps=pltpu.VMEM((LAYERS, 16, rows), F32),
            turned=pltpu.VMEM((LAYERS, 16, rows), F32),
        ),
        Shared(
            active_t=pltpu.VMEM((hidden // 2, rows), BF16),
            slope=pltpu.VMEM((rows, hidden // 2), BF16),
            y_t=pltpu.VMEM((width, rows), BF16),
            e=pltpu.VMEM((rows, width), BF16),
        ),
        Wire(
            send=pltpu.VMEM((rows, width), BF16),
            receive=pltpu.VMEM((2, rows, width), BF16),
            small=pltpu.VMEM((6, 8 + LAYERS * heads, width), F32),
        ),
        [
            slots_of(name, count, 1 in kinds, width, columns, hidden)
            for (name, count, _), kinds in zip(pieces, zip(*PIECE_KINDS))
        ],
        Sems(
            load=pltpu.SemaphoreType.DMA((4 * LAYERS,)),
            ring_send=pltpu.SemaphoreType.DMA((SENDS * len(pieces),)),
            ring_receive=pltpu.SemaphoreType.DMA((RECEIVES * len(pieces),)),
            small_send=pltpu.SemaphoreType.DMA((6,)),
            small_receive=pltpu.SemaphoreType.DMA((6,)),
            credit=pltpu.SemaphoreType.REGULAR((4 * len(pieces),)),
            ready=pltpu.SemaphoreType.REGULAR((4 * len(pieces),)),
            factor_send=pltpu.SemaphoreType.DMA((4,)),
            factor_receive=pltpu.SemaphoreType.DMA((4,)),
            share_send=pltpu.SemaphoreType.DMA((2 * LAYERS,)),
            share_receive=pltpu.SemaphoreType.DMA((2 * LAYERS,)),
            gather_send=pltpu.SemaphoreType.DMA((2,)),
            gather_receive=pltpu.SemaphoreType.DMA((2,)),
            send=pltpu.SemaphoreType.DMA((4,)),
            receive=pltpu.SemaphoreType.DMA((4,)),
        ),
    )
    own = pltpu.VMEM
    results = pl.pallas_call(
        whole_step,
        out_shape=[
            own((rows, width), BF16),
            own((rows, width), F32),
            own((8 + LAYERS * heads, width), F32),
            own((LAYERS, hidden, width), BF16),
            own((LAYERS, 2 * width, hidden // 2), BF16),
            own((LAYERS, 4, width, columns), BF16),
        ],
        in_specs=[pl.BlockSpec(memory_space=pltpu.SMEM)] + [vmem] * 5 + [hbm] * 4,
        out_specs=[vmem] * 6,
        scratch_shapes=scratch,
        compiler_params=pltpu.CompilerParams(
            collective_id=0, has_side_effects=True, vmem_limit_bytes=VMEM_ROOM
        ),
    )(
        lengths,
        tokens,
        cotangent,
        by_head,
        norm_gains,
        norm_shifts,
        by_kind,
        output_weight,
        up_weight,
        down_weight,
    )
    shape = jax.ShapeDtypeStruct
    held = [pltpu.with_memory_space_constraint(result, pltpu.VMEM) for result in results]
    wide = [
        (LAYERS, hidden, width),
        (LAYERS, width, hidden),
        (LAYERS, 3, width, columns),
        (LAYERS, columns, width),
    ]
    outputs = pl.pallas_call(
        widen,
        out_shape=[shape(size, F32) for size in wide]
        + [
            shape((rows, width), BF16),
            shape((rows, width), F32),
            shape((heads, LAYERS, reach), F32),
            shape((LAYERS, 2, width), F32),
            shape((LAYERS, 2, width), F32),
        ],
        in_specs=[vmem] * 6,
        out_specs=[hbm] * 4 + [vmem] * 5,
        scratch_shapes=[pltpu.VMEM(size, F32) for size in wide] + [pltpu.SemaphoreType.DMA((LAYERS * (2 * WIDE_PARTS + 4),))],
        compiler_params=pltpu.CompilerParams(vmem_limit_bytes=WIDE_ROOM),
    )(*held)
    down_grad, up_grad, projection_grad, output_grad = outputs[:4]
    activations, token_grad, taps_grad, gains_grad, shifts_grad = outputs[4:]
    return (
        activations,
        token_grad,
        jnp.transpose(projection_grad, (0, 2, 1, 3)),
        jnp.transpose(taps_grad, (1, 0, 2)),
        output_grad,
        gains_grad,
        shifts_grad,
        up_grad,
        down_grad,
    )


VMEM_ROOM = 97 * 2**19
WIDE_ROOM = 32 * 2**20
WIDE_PARTS = 4


def widen(
    activations_ref,
    token_grad_ref,
    small_ref,
    down_ref,
    up_ref,
    other_ref,
    down_hbm,
    up_hbm,
    projection_hbm,
    output_hbm,
    activations_out,
    token_grad_out,
    taps_out,
    gains_out,
    shifts_out,
    down_wide,
    up_wide,
    projection_wide,
    output_wide,
    sems,
):
    heads, _, reach = taps_out.shape
    columns = output_wide.shape[1]
    copies = []

    def send(source, target):
        copies.append(pltpu.make_async_copy(source, target, sems.at[len(copies)]))
        copies[-1].start()

    def cast(target, source):
        def step(i, unused):
            span = pl.ds(pl.multiple_of(i * 32, 32), 32)
            target[span, :] = source[span, :].astype(F32)
            return unused

        lax.fori_loop(0, source.shape[0] // 32, step, 0)

    for layer in range(LAYERS):
        count = down_ref.shape[1] // WIDE_PARTS
        for part in range(WIDE_PARTS):
            span = pl.ds(part * count, count)
            cast(down_wide.at[layer, span], down_ref.at[layer, span])
            send(down_wide.at[layer, span], down_hbm.at[layer, span])
        count, side = up_wide.shape[1] // WIDE_PARTS, up_wide.shape[2] // 2
        for part in range(WIDE_PARTS):
            span = pl.ds(part * count, count)
            for i in range(2):
                cast(
                    up_wide.at[layer, span, pl.ds(i * side, side)],
                    up_ref.at[layer, pl.ds(i * up_wide.shape[1] + part * count, count)],
                )
            send(up_wide.at[layer, span], up_hbm.at[layer, span])
        for i in range(3):
            cast(projection_wide.at[layer, i], other_ref.at[layer, 1 + i])
            send(projection_wide.at[layer, i], projection_hbm.at[layer, i])
        for i in range(2):
            side = slice(i * columns, (i + 1) * columns)
            output_wide[layer, :, side] = other_ref[layer, 0, side, :].astype(F32)
        send(output_wide.at[layer], output_hbm.at[layer])
    activations_out[...] = activations_ref[...]
    token_grad_out[...] = token_grad_ref[...]
    for layer in range(LAYERS):
        gains_out[layer] = small_ref[2 * layer : 2 * layer + 2, :]
        shifts_out[layer] = small_ref[4 + 2 * layer : 6 + 2 * layer, :]
        first = 8 + layer * heads
        taps_out[:, layer, :] = small_ref[first : first + heads, :reach]
    for copy in copies:
        copy.wait()


def solution(mesh):
    fused = mesh.shape["mp"] == 2 and mesh.shape["dp"] == 16

    def step(*arrays):
        return (fused_body if fused else body)(*arrays)

    return jax.shard_map(
        step,
        mesh=mesh,
        in_specs=(
            P("dp", None),
            P("dp"),
            P("dp", None),
            P(None, None, None, "mp"),
            P(),
            P(None, "mp", None),
            P(),
            P(),
            P(None, None, "mp"),
            P(None, "mp", None),
        ),
        out_specs=(
            P("dp", None),
            P("dp", None),
            P(None, None, None, "mp"),
            P(),
            P(None, "mp", None),
            P(),
            P(),
            P(None, None, "mp"),
            P(None, "mp", None),
        ),
        check_vma=False,
    )
```

```python
from typing import Any, NamedTuple

import jax
import jax.numpy as jnp
from jax import lax
from jax.experimental import pallas as pl
from jax.experimental.pallas import tpu as pltpu
from jax.sharding import PartitionSpec as P

M = 64
NEWTON = 6
LAYERS = 2


highest_value = lax.Precision.HIGHEST


def merged(array, axis, join):
    gathered = jax.tree.map(
        lambda a, kind: lax.all_gather(a.astype(kind), axis),
        array,
        (jnp.bfloat16, jnp.bfloat16, jnp.bfloat16),
    )

    def take(source):
        return jax.tree.map(
            lambda a, own: lax.dynamic_index_in_dim(a, source, 0, False).astype(own.dtype),
            gathered,
            array,
        )

    return lax.fori_loop(
        1, lax.axis_size(axis), lambda source, state: join(state, take(source)), take(0)
    )


def for_sending(array):
    return jax.tree.map(lambda a: a.astype(jnp.bfloat16) if a.dtype == jnp.float32 else a, array)


def softmax_row_block(scores):
    top = jnp.max(scores, axis=-1, keepdims=True)
    matrix_powers = jnp.exp(scores - top)
    return matrix_powers / jnp.sum(matrix_powers, axis=-1, keepdims=True)


def slot_masks(length, count, marks):
    position = jnp.arange(count, dtype=jnp.int32)
    inside = position < length
    segment = position * marks // length
    member = (segment[None, :] == jnp.arange(marks, dtype=jnp.int32)[:, None]) & inside[None, :]
    member = member.astype(jnp.float32)
    pooling = member / jnp.sum(member, axis=1, keepdims=True)
    return (pooling, inside.astype(jnp.float32))


def inverse_head(query_landmarks, key_landmarks, summary):
    scale_factor = query_landmarks.shape[-1] ** (-0.5)
    second = softmax_row_block(
        jnp.dot(query_landmarks, key_landmarks.T, precision=highest_value) * scale_factor
    )
    identity = jnp.eye(second.shape[0], dtype=jnp.float32)
    inverse = second.T / jnp.sum(second * second)
    for sweep in range(NEWTON):
        product = jnp.dot(second, inverse, precision=highest_value)
        inner = 7.0 * identity - product
        inner = 15.0 * identity - jnp.dot(product, inner, precision=highest_value)
        inner = 13.0 * identity - jnp.dot(product, inner, precision=highest_value)
        inverse = 0.25 * jnp.dot(inverse, inner, precision=highest_value)
    return jnp.dot(inverse, summary, precision=highest_value)


def inverse_section(query_landmarks, key_landmarks, summary):
    return jax.vmap(inverse_head)(query_landmarks, key_landmarks, summary)


def near_section(query_matrix, key_landmarks, carried_over):
    scale_factor = query_matrix.shape[-1] ** (-0.5)
    first_entry = softmax_row_block(
        jnp.einsum("nlv,lgv->lng", query_matrix, key_landmarks, precision=highest_value)
        * scale_factor
    )
    return jnp.einsum("xtz,xzb->txb", first_entry, carried_over, precision=highest_value)


def far_scores(query_landmarks, key_matrix, valid_own):
    scale_factor = query_landmarks.shape[-1] ** (-0.5)
    distant_scores = (
        jnp.einsum("owz,toz->owt", query_landmarks, key_matrix, precision=highest_value)
        * scale_factor
    )
    live = valid_own[None, None, :] > 0
    return (jnp.where(live, distant_scores, -1e30), live)


def join_softmax(left, right):
    peak = jnp.maximum(left[0], right[0])
    left_factor = jnp.exp(left[0] - peak)
    right_factor = jnp.exp(right[0] - peak)
    return (
        peak,
        left[1] * left_factor + right[1] * right_factor,
        left[2] * left_factor[..., None] + right[2] * right_factor[..., None],
    )


def attend(query_matrix, key_matrix, value_matrix, pooled_local, valid_own):
    query_portion = jnp.einsum("ji,ilk->ljk", pooled_local, query_matrix, precision=highest_value)
    key_portion = jnp.einsum("ji,ilk->ljk", pooled_local, key_matrix, precision=highest_value)
    query_landmarks, key_landmarks = (
        lax.psum(query_portion.astype(jnp.bfloat16), "mp").astype(jnp.float32),
        lax.psum(key_portion.astype(jnp.bfloat16), "mp").astype(jnp.float32),
    )
    distant_scores, live = far_scores(query_landmarks, key_matrix, valid_own)
    peak = jnp.max(distant_scores, axis=-1)
    matrix_powers = jnp.where(live, jnp.exp(distant_scores - peak[..., None]), 0.0)
    totals = jnp.sum(matrix_powers, axis=-1)
    weighted_values = jnp.einsum(
        "naw,wno->nao", matrix_powers, value_matrix, precision=highest_value
    )
    peak, totals, weighted_values = merged((peak, totals, weighted_values), "mp", join_softmax)
    summary = weighted_values / totals[..., None]
    carried_over = inverse_section(query_landmarks, key_landmarks, summary)
    mixed = near_section(query_matrix, key_landmarks, carried_over)
    return (mixed, (query_landmarks, key_landmarks, peak, totals, summary))


def attend_back(
    grad_rows, query_matrix, key_matrix, value_matrix, pooled_local, valid_own, saved, tap_part
):
    query_landmarks, key_landmarks, peak, totals, summary = saved
    scale_factor = query_matrix.shape[-1] ** (-0.5)
    carried_over, inverse_back = jax.vjp(inverse_section, query_landmarks, key_landmarks, summary)
    unused, near_back = jax.vjp(near_section, query_matrix, key_landmarks, carried_over)
    query_grad, kland_part, carried_part = near_back(grad_rows)
    key_landmark_nearby, carried_grad, tap_grad = (
        lax.psum(kland_part.astype(jnp.bfloat16), "mp").astype(jnp.float32),
        lax.psum(carried_part.astype(jnp.bfloat16), "mp").astype(jnp.float32),
        lax.psum(tap_part.astype(jnp.bfloat16), "mp").astype(jnp.float32),
    )
    query_landmark_gradient, key_landmark_gradient, summary_gradient = inverse_back(carried_grad)
    distant_scores, live = far_scores(query_landmarks, key_matrix, valid_own)
    weight_spread = jnp.where(
        live, jnp.exp(distant_scores - peak[..., None]) / totals[..., None], 0.0
    )
    moving_along = jnp.einsum(
        "owz,toz->owt", summary_gradient, value_matrix, precision=highest_value
    )
    agreed = jnp.sum(summary_gradient * summary, axis=-1)
    slope_values = weight_spread * (moving_along - agreed[..., None])
    value_gradient = jnp.einsum(
        "ofq,ofn->qon", weight_spread, summary_gradient, precision=highest_value
    )
    query_landmark_remote = (
        jnp.einsum("naw,wno->nao", slope_values, key_matrix, precision=highest_value) * scale_factor
    )
    key_gradient = (
        jnp.einsum("ofq,ofn->qon", slope_values, query_landmarks, precision=highest_value)
        * scale_factor
    )
    query_landmark_remote = lax.psum(query_landmark_remote.astype(jnp.bfloat16), "mp").astype(
        jnp.float32
    )
    query_grad = query_grad + jnp.einsum(
        "ge,xgl->exl",
        pooled_local,
        query_landmark_gradient + query_landmark_remote,
        precision=highest_value,
    )
    key_gradient = key_gradient + jnp.einsum(
        "ge,xgl->exl",
        pooled_local,
        key_landmark_gradient + key_landmark_nearby,
        precision=highest_value,
    )
    return (query_grad, key_gradient, value_gradient, tap_grad)


def head_table(columns, heads, size_h):
    begin = lax.axis_index("mp") * columns
    owner = (begin + jnp.arange(columns, dtype=jnp.int32)) // size_h
    return (owner[None, :] == jnp.arange(heads, dtype=jnp.int32)[:, None]).astype(jnp.float32)


def convolve(value_cols, taps, table, valid):
    tap_cols = jnp.dot(taps.T, table, precision=highest_value)
    masked = value_cols * valid[:, None]
    reach = taps.shape[1] // 2
    padded = jnp.pad(masked, ((reach, reach), (0, 0)))
    length_rows = masked.shape[0]
    convolved = jnp.zeros_like(masked)
    for offset in range(taps.shape[1]):
        convolved = convolved + tap_cols[offset] * padded[offset : offset + length_rows]
    return convolved


def contract(left, right, left_dim, right_dim):
    return lax.dot_general(
        left, right, (((left_dim,), (right_dim,)), ((), ())), preferred_element_type=jnp.float32
    )


def normalize(resid, gain, shift):
    centre = resid - jnp.mean(resid, axis=-1, keepdims=True)
    spread = lax.rsqrt(jnp.mean(centre * centre, axis=-1, keepdims=True) + 1e-05)
    normed = centre * spread
    return (normed * gain + shift, normed, spread)


def normalize_back(upstream, normed, spread, gain):
    scaled = upstream * gain
    result = spread * (
        scaled
        - jnp.mean(scaled, axis=-1, keepdims=True)
        - normed * jnp.mean(scaled * normed, axis=-1, keepdims=True)
    )
    return (result, jnp.sum(upstream * normed, axis=0), jnp.sum(upstream, axis=0))


def own_rows(whole):
    count = whole.shape[0] // lax.axis_size("mp")
    return lax.dynamic_slice_in_dim(whole, lax.axis_index("mp") * count, count, 0)


def whole_rows(share):
    return lax.all_gather(share.astype(jnp.bfloat16), "mp", axis=0, tiled=True).astype(share.dtype)


def row_sums(partial_value):
    return lax.psum_scatter(
        partial_value.astype(jnp.bfloat16), "mp", scatter_dimension=0, tiled=True
    ).astype(jnp.float32)


def add_norm(partial_value, resid, gain, shift):
    summed = row_sums(partial_value)
    output, normed, spread = normalize(own_rows(resid) + summed, gain, shift)
    output = whole_rows(output)
    return (output, normed, spread)


def norm_step_back(upstream, normed, spread, gain):
    result, gain_part, shift_part = normalize_back(upstream, normed, spread, gain)
    whole = whole_rows(result)
    return (result, whole, gain_part, shift_part)


def add_input_grad(result, partial_value):
    total = result + row_sums(partial_value)
    return total


def forward_layer(hidden, weights, pooling_own, valid, valid_own):
    projection, taps, output_weight, gains, shifts, up_weight, down_weight = weights
    count, width = hidden.shape
    heads = taps.shape[0]
    size_h = width // heads
    columns = projection.shape[2]
    entering = hidden.astype(jnp.bfloat16)
    mixed = jnp.einsum(
        "td,dsc->tsc", entering, projection, preferred_element_type=jnp.float32
    ).astype(jnp.bfloat16)
    gathered = lax.all_to_all(mixed, "mp", split_axis=0, concat_axis=2, tiled=True)
    rows = gathered.shape[0]
    split_rows = gathered.astype(jnp.float32).reshape(rows, 3, heads, size_h)
    attended, saved = attend(
        split_rows[:, 0], split_rows[:, 1], split_rows[:, 2], pooling_own, valid_own
    )
    attended_cols = lax.all_to_all(
        for_sending(attended.reshape(rows, width)), "mp", split_axis=1, concat_axis=0, tiled=True
    )
    table = head_table(columns, heads, size_h)
    value_cols = mixed[:, 2].astype(jnp.float32)
    convolved = convolve(value_cols, taps, table, valid)
    joined = ((attended_cols + convolved) * valid[:, None]).astype(jnp.bfloat16)
    partial_value = jnp.dot(joined, output_weight, preferred_element_type=jnp.float32)
    middle, normed_first, spread_first = add_norm(partial_value, hidden, gains[0], shifts[0])
    entering_ffn = middle.astype(jnp.bfloat16)
    upward = jnp.dot(entering_ffn, up_weight, preferred_element_type=jnp.float32)
    active = jax.nn.gelu(upward, approximate=True).astype(jnp.bfloat16)
    partial_value = jnp.dot(active, down_weight, preferred_element_type=jnp.float32)
    output, normed_second, spread_second = add_norm(partial_value, middle, gains[1], shifts[1])
    kept = (
        entering,
        value_cols,
        split_rows,
        saved,
        joined,
        table,
        normed_first,
        spread_first,
        entering_ffn,
        upward,
        active,
        normed_second,
        spread_second,
    )
    return (output, kept)


def backward_layer(upstream, weights, kept, pooling_own, valid, valid_own):
    projection, taps, output_weight, gains, shifts, up_weight, down_weight = weights
    (
        entering,
        value_cols,
        split_rows,
        saved,
        joined,
        table,
        normed_first,
        spread_first,
        entering_ffn,
        upward,
        active,
        normed_second,
        spread_second,
    ) = kept
    count, width = entering.shape
    rows = split_rows.shape[0]
    heads = taps.shape[0]
    size_h = width // heads
    result_second, whole_second, gain_second, shift_second = norm_step_back(
        upstream, normed_second, spread_second, gains[1]
    )
    sent_second = whole_second.astype(jnp.bfloat16)
    down_grad = contract(active, sent_second, 0, 0)
    hidden_grad = contract(sent_second, down_weight, 1, 1)
    unused, gelu_back = jax.vjp(lambda value: jax.nn.gelu(value, approximate=True), upward)
    upward_sent = gelu_back(hidden_grad)[0].astype(jnp.bfloat16)
    up_grad = contract(entering_ffn, upward_sent, 0, 0)
    middle_grad = add_input_grad(result_second, contract(upward_sent, up_weight, 1, 1))
    result_first, whole_first, gain_first, shift_first = norm_step_back(
        middle_grad, normed_first, spread_first, gains[0]
    )
    sent_first = whole_first.astype(jnp.bfloat16)
    out_grad = contract(joined, sent_first, 0, 0)
    joined_grad = contract(sent_first, output_weight, 1, 1)
    masked_grad = joined_grad * valid[:, None]
    unused, conv_back = jax.vjp(
        lambda values, tap_rows: convolve(values, tap_rows, table, valid), value_cols, taps
    )
    conv_value_grad, tap_part = conv_back(masked_grad)
    row_grad = (
        lax.all_to_all(
            masked_grad.astype(jnp.bfloat16), "mp", split_axis=0, concat_axis=1, tiled=True
        )
        .astype(masked_grad.dtype)
        .reshape(rows, heads, size_h)
    )
    query_grad, key_gradient, value_gradient, tap_grad = attend_back(
        row_grad,
        split_rows[:, 0],
        split_rows[:, 1],
        split_rows[:, 2],
        pooling_own,
        valid_own,
        saved,
        tap_part,
    )
    stacked_rows = jnp.stack([query_grad, key_gradient, value_gradient], axis=1).reshape(
        rows, 3, width
    )
    column_grad = lax.all_to_all(
        for_sending(stacked_rows), "mp", split_axis=2, concat_axis=0, tiled=True
    ).astype(stacked_rows.dtype)
    column_grad = jnp.concatenate(
        [column_grad[:, :2], (column_grad[:, 2] + conv_value_grad)[:, None]], axis=1
    )
    mixed_sent = column_grad.astype(jnp.bfloat16)
    proj_grad = jnp.einsum("td,tsc->dsc", entering, mixed_sent, preferred_element_type=jnp.float32)
    below = add_input_grad(
        result_first,
        jnp.einsum("tsc,dsc->td", mixed_sent, projection, preferred_element_type=jnp.float32),
    )
    gain_grad = jnp.stack([gain_first, gain_second])
    shift_grad = jnp.stack([shift_first, shift_second])
    gain_grad, shift_grad = lax.psum((gain_grad, shift_grad), "mp")
    return (below, (proj_grad, tap_grad, out_grad, gain_grad, shift_grad, up_grad, down_grad))


def sum_layer(parts):
    return (
        lax.psum(parts[0].astype(jnp.bfloat16), "dp").astype(jnp.float32),
        lax.psum(parts[1].astype(jnp.bfloat16), "dp").astype(jnp.float32),
        lax.psum(parts[2].astype(jnp.bfloat16), "dp").astype(jnp.float32),
        lax.psum(parts[3].astype(jnp.bfloat16), "dp").astype(jnp.float32),
        lax.psum(parts[4].astype(jnp.bfloat16), "dp").astype(jnp.float32),
        lax.psum(parts[5].astype(jnp.bfloat16), "dp").astype(jnp.float32),
        lax.psum(parts[6].astype(jnp.bfloat16), "dp").astype(jnp.float32),
    )


def body(
    tokens,
    lengths,
    cotangent,
    projection,
    conv_taps,
    output_weight,
    norm_gains,
    norm_shifts,
    up_weight,
    down_weight,
):
    count = tokens.shape[0]
    pooling, valid = slot_masks(lengths[0], count, M)
    rows = count // lax.axis_size("mp")
    begin = lax.axis_index("mp") * rows
    pooling_own = lax.dynamic_slice_in_dim(pooling, begin, rows, 1)
    valid_own = lax.dynamic_slice_in_dim(valid, begin, rows, 0)
    weights = (
        projection,
        conv_taps,
        output_weight,
        norm_gains,
        norm_shifts,
        up_weight,
        down_weight,
    )
    hidden = tokens.astype(jnp.float32)
    keeping = []
    for layer_index in range(LAYERS):
        hidden, kept = forward_layer(
            hidden, tuple((item[layer_index] for item in weights)), pooling_own, valid, valid_own
        )
        keeping.append(kept)
    activations = (hidden * valid[:, None]).astype(jnp.bfloat16)
    upstream = cotangent.astype(jnp.float32) * valid[:, None]
    upstream = own_rows(upstream)
    collected = [None] * LAYERS
    for layer_index in reversed(range(LAYERS)):
        upstream, parts = backward_layer(
            upstream,
            tuple((item[layer_index] for item in weights)),
            keeping[layer_index],
            pooling_own,
            valid,
            valid_own,
        )
        collected[layer_index] = sum_layer(parts)
    stacked = tuple(
        (
            jnp.stack([collected[layer_index][member] for layer_index in range(LAYERS)])
            for member in range(7)
        )
    )
    upstream = whole_rows(upstream)
    return (
        activations,
        upstream,
        stacked[0],
        stacked[1],
        stacked[2],
        stacked[3],
        stacked[4],
        stacked[5],
        stacked[6],
    )


class Weights(NamedTuple):
    projection: Any
    output: Any
    up: Any
    down: Any


class Kept(NamedTuple):
    ql: Any
    kl: Any
    second: Any
    inverse: Any
    first: Any
    third: Any
    summary: Any
    carried: Any


class Stored(NamedTuple):
    attention: Any
    qkv: Any
    normed: Any
    spread: Any
    slope: Any
    x_t: Any
    mixed_t: Any
    y_t: Any
    active_t: Any


class Work(NamedTuple):
    x: Any
    x_low: Any
    y: Any
    y_low: Any
    mixed: Any
    active: Any
    e_second: Any
    dmixed: Any
    dqkv: Any
    taps: Any
    turned: Any


class Shared(NamedTuple):
    active_t: Any
    slope: Any
    y_t: Any
    e: Any


class Wire(NamedTuple):
    send: Any
    receive: Any
    small: Any


class Sems(NamedTuple):
    load: Any
    ring_send: Any
    ring_receive: Any
    small_send: Any
    small_receive: Any
    credit: Any
    ready: Any
    factor_send: Any
    factor_receive: Any
    share_send: Any
    share_receive: Any
    gather_send: Any
    gather_receive: Any
    send: Any
    receive: Any


class Slots(NamedTuple):
    core: Any
    x: Any
    near: Any
    mid: Any


class Grads(NamedTuple):
    down: Any
    up: Any
    other: Any


DOWN, UP, OUTPUT, PROJECTION = range(4)


MESH = pl.DeviceIdType.MESH
F32 = jnp.float32
BF16 = jnp.bfloat16


def nn(a, b):
    return lax.dot_general(a, b, (((1,), (0,)), ((), ())), preferred_element_type=F32)


def nt(a, b):
    return lax.dot_general(a, b, (((1,), (1,)), ((), ())), preferred_element_type=F32)


def parts_of(x):
    high = x.astype(BF16)
    return high, (x - high.astype(F32)).astype(BF16)


def nn3(a, b):
    return nn(jnp.concatenate([a[0], a[1]], 1), jnp.concatenate([b[0], b[0]], 0)) + nn(a[0], b[1])


def nt3(a, b):
    return nt(jnp.concatenate([a[0], a[1]], 1), jnp.concatenate([b[0], b[0]], 1)) + nt(a[0], b[1])


def iota(shape, axis):
    return lax.broadcasted_iota(jnp.int32, shape, axis)


class Frame:
    def __init__(self, length, rows, size_h):
        self.length = length
        self.rows = rows
        self.lane0 = iota((1, 2 * size_h), 1) < size_h
        self.keep = [self.lane0.astype(F32).astype(BF16), (~self.lane0).astype(F32).astype(BF16)]
        self.diag = (iota((2 * M, 2 * M), 0) < M) == (iota((2 * M, 2 * M), 1) < M)
        self.ones = self.diag.astype(F32).astype(BF16)
        self.ones2 = jnp.concatenate([self.ones, self.ones], 0)
        j, t = iota((M, rows), 0), iota((M, rows), 1)
        member = (t * M >= j * length) & (t * M < (j + 1) * length)
        member = member.astype(F32)
        self.member = member.astype(BF16)
        self.inv = 1.0 / jnp.sum(member, axis=1, keepdims=True)
        t, j = iota((rows, M), 0), iota((rows, M), 1)
        self.member_t = ((t * M >= j * length) & (t * M < (j + 1) * length)).astype(F32).astype(BF16)
        self.valid = (iota((rows, 1), 0) < length).astype(F32)
        self.valid_lane = iota((1, rows), 1) < length
        self.band = jnp.abs(iota((rows, rows), 0) - iota((rows, rows), 1)) <= KREACH

    def stack(self, x):
        return jnp.where(self.diag, jnp.concatenate([x, x], 0), 0.0)

    def block(self, x):
        return jnp.where(self.diag, x, 0.0)

    def pack(self, x):
        return x[:M] + x[M:]

    def spread(self, x):
        return jnp.concatenate([x * self.keep[0], x * self.keep[1]], 0)

    def times(self, a, b):
        high, low = b
        left = jnp.concatenate([a[0], a[1]], 1)
        return nn(left, jnp.concatenate([high, high], 0)) + nn(a[0], low)

    def spread_parts(self, x):
        return tuple(self.spread(half) for half in parts_of(x))

    def half_sums(self, x):
        high, low = parts_of(x)
        return nn(jnp.concatenate([high, low], 1), self.ones2)

    def toeplitz(self, row):
        spread = jnp.broadcast_to(row, (self.rows, self.rows))
        turned = pltpu.roll(spread, self.rows - KREACH, 1, stride=1, stride_axis=0)
        return jnp.where(self.band, turned, 0.0).astype(BF16)

    def conv(self, rows_pair, value):
        both = jnp.concatenate([self.toeplitz(rows_pair[0]), self.toeplitz(rows_pair[1])], 1)
        stacked = jnp.concatenate([value * self.keep[0], value * self.keep[1]], 0)
        return nn(both, stacked)

    def diagonals(self, product):
        banded = jnp.where(self.band, product, 0.0)
        total = banded[:8]
        for group in range(1, self.rows // 8):
            part = banded[8 * group : 8 * group + 8]
            total = total + pltpu.roll(part, self.rows - 8 * group, 1)
        total = pltpu.roll(total, KREACH, 1)
        result = total[:1]
        for row in range(1, 8):
            result = result + pltpu.roll(total[row : row + 1], self.rows - row, 1)
        return result


KREACH = 16


def softmax_masked(scores, live):
    scores = jnp.where(live, scores, -1e30)
    top = jnp.max(scores, axis=-1, keepdims=True)
    powers = jnp.where(live, jnp.exp(scores - top), 0.0)
    return powers / jnp.sum(powers, axis=-1, keepdims=True)


def attention(frame, qkv, taps, head0, size_h, keep, out_ref):
    scale = size_h ** (-0.5)
    pairs = qkv.shape[2] // (2 * size_h)
    ql = nn(frame.member, qkv[0]) * frame.inv
    kl = nn(frame.member, qkv[1]) * frame.inv
    keep.ql[...] = ql
    keep.kl[...] = kl
    cols = [slice(p * 2 * size_h, (p + 1) * 2 * size_h) for p in range(pairs)]
    qs = [parts_of(frame.stack(ql[:, c])) for c in cols]
    ks = [parts_of(frame.stack(kl[:, c])) for c in cols]
    second = [softmax_masked(nt3(qs[p], ks[p]) * scale, frame.diag) for p in range(pairs)]
    inverse = []
    halves = iota((2 * M, 1), 0) < M
    for p in range(pairs):
        keep.second[p] = second[p]
        squares = jnp.sum(second[p] * second[p], axis=1, keepdims=True)
        first_total = jnp.sum(jnp.where(halves, squares, 0.0), axis=0, keepdims=True)
        other_total = jnp.sum(jnp.where(halves, 0.0, squares), axis=0, keepdims=True)
        inverse.append(second[p].T * (1.0 / jnp.where(halves, first_total, other_total)))
    second_parts = [parts_of(frame.pack(s)) for s in second]
    summaries, firsts, convolved = [None] * pairs, [None] * pairs, [None] * pairs

    def far(p):
        key, value = qkv[1, :, cols[p]], qkv[2, :, cols[p]]
        scores = nt(jnp.concatenate(qs[p], 1), jnp.concatenate([key, key], 1)) * scale
        third = softmax_masked(scores, frame.valid_lane).astype(BF16)
        keep.third[p] = third
        summaries[p] = frame.block(nn(third, value))
        keep.summary[p] = summaries[p]

    def near(p):
        query = qkv[0, :, cols[p]]
        scores = nt(jnp.concatenate([query, query], 1), jnp.concatenate(ks[p], 1)) * scale
        top0 = jnp.max(jnp.where(frame.lane0, scores, -1e30), axis=-1, keepdims=True)
        top1 = jnp.max(jnp.where(frame.lane0, -1e30, scores), axis=-1, keepdims=True)
        powers = jnp.exp(scores - jnp.where(frame.lane0, top0, top1))
        firsts[p] = (powers / frame.half_sums(powers)).astype(BF16)
        keep.first[:, cols[p]] = firsts[p]

    def local(p):
        inside = (qkv[2, :, cols[p]].astype(F32) * frame.valid).astype(BF16)
        rows_pair = [taps[pl.ds(head0 + 2 * p + i, 1), :] for i in range(2)]
        convolved[p] = frame.conv(rows_pair, inside)

    beside = [(task, p) for p in range(pairs) for task in (far, near, local)]
    inverse = [frame.pack(z) for z in inverse]
    product = [frame.times(second_parts[p], frame.spread_parts(inverse[p])) for p in range(pairs)]
    for sweep in range(NEWTON):
        for p in range(pairs):
            keep.inverse[sweep, p] = inverse[p]
        zp = [parts_of(z) for z in inverse]
        pp = [parts_of(x) for x in product]
        right = [tuple(frame.spread(half) for half in pp[p]) for p in range(pairs)]
        square = [frame.times(pp[p], right[p]) for p in range(pairs)]
        forward = [frame.times(zp[p], right[p]) for p in range(pairs)]
        for task, p in beside[sweep * len(beside) // NEWTON : (sweep + 1) * len(beside) // NEWTON]:
            task(p)
        inner = [frame.spread_parts(7.0 * product[p] - square[p]) for p in range(pairs)]
        if sweep + 1 < NEWTON:
            product = [0.25 * (13.0 * product[p] - 15.0 * square[p] + frame.times(parts_of(square[p]), inner[p])) for p in range(pairs)]
        inverse = [0.25 * (13.0 * inverse[p] - 15.0 * forward[p] + frame.times(parts_of(forward[p]), inner[p])) for p in range(pairs)]
    for p in range(pairs):
        keep.inverse[NEWTON, p] = inverse[p]
        carried = frame.stack(frame.times(parts_of(inverse[p]), parts_of(summaries[p])))
        keep.carried[p] = carried
        mixed = nn(firsts[p], carried.astype(BF16))
        out_ref[:, cols[p]] = ((mixed + convolved[p]) * frame.valid).astype(BF16)


def attention_back(frame, grad, qkv, taps_turned, head0, size_h, keep, out_ref, taps_out):
    scale = size_h ** (-0.5)
    pairs = qkv.shape[2] // (2 * size_h)
    cols = [slice(p * 2 * size_h, (p + 1) * 2 * size_h) for p in range(pairs)]
    each = range(pairs)
    ql, kl = keep.ql[...], keep.kl[...]
    qs = [parts_of(frame.stack(ql[:, c])) for c in cols]
    ks = [parts_of(frame.stack(kl[:, c])) for c in cols]
    summary = [keep.summary[p] for p in each]
    second = [keep.second[p] for p in each]
    dq, dk_landmark, dcarried, grad_low = [], [], [], []
    for p in each:
        c = cols[p]
        g = grad[:, c].astype(BF16)
        grad_low.append(g)
        first = keep.first[:, c].astype(F32)
        dfirst = nt(g, keep.carried[p].astype(BF16))
        slope = first * dfirst
        slope = (slope - first * frame.half_sums(slope)) * scale
        dq.append(nn(slope.astype(BF16), ks[p][0]))
        dk_landmark.append(frame.block(nn(slope.T.astype(BF16), qkv[0, :, c])))
        dcarried.append(frame.block(nn(first.T.astype(BF16), g)))
    yield
    dcp = [parts_of(x) for x in dcarried]
    up = [nt3(dcp[p], parts_of(summary[p])) for p in each]
    dsummary = [nn3(parts_of(frame.stack(keep.inverse[NEWTON, p]).T), dcp[p]) for p in each]
    second_parts = [parts_of(s) for s in second]
    second_turned = [parts_of(s.T) for s in second]
    dsecond = [jnp.zeros_like(s) for s in second]
    for sweep in reversed(range(NEWTON)):
        inverse = [frame.stack(keep.inverse[sweep, p]) for p in each]
        zp = [parts_of(z) for z in inverse]
        product = [nn3(second_parts[p], zp[p]) for p in each]
        pp = [parts_of(x) for x in product]
        inner = [parts_of(7.0 * product[p] - nn3(pp[p], pp[p])) for p in each]
        forward_turned = [parts_of(nn3(zp[p], pp[p]).T) for p in each]
        product_turned = [parts_of(x.T) for x in product]
        inverse_turned = [parts_of(z.T) for z in inverse]
        upp = [parts_of(x) for x in up]
        dforward = [parts_of(0.25 * (nt3(upp[p], inner[p]) - 15.0 * up[p])) for p in each]
        dinner_full = [0.25 * nn3(forward_turned[p], upp[p]) for p in each]
        dinner = [parts_of(x) for x in dinner_full]
        dproduct = [
            parts_of(
                7.0 * dinner_full[p]
                - nt3(dinner[p], pp[p])
                - nn3(product_turned[p], dinner[p])
                + nn3(inverse_turned[p], dforward[p])
            )
            for p in each
        ]
        up = [
            3.25 * up[p] + nt3(dforward[p], pp[p]) + nn3(second_turned[p], dproduct[p])
            for p in each
        ]
        dsecond = [dsecond[p] + nt3(dproduct[p], zp[p]) for p in each]
        yield
    halves = iota((2 * M, 1), 0) < M
    for p in each:
        c = cols[p]
        query, key, value = qkv[0, :, c], qkv[1, :, c], qkv[2, :, c]
        squares = jnp.sum(second[p] * second[p], axis=1, keepdims=True)
        total0 = jnp.sum(jnp.where(halves, squares, 0.0), axis=0, keepdims=True)
        total1 = jnp.sum(jnp.where(halves, 0.0, squares), axis=0, keepdims=True)
        inverse_total = 1.0 / jnp.where(halves, total0, total1)
        start_agree = jnp.sum(up[p] * frame.stack(keep.inverse[0, p]), axis=1, keepdims=True)
        agree0 = jnp.sum(jnp.where(halves, start_agree, 0.0), axis=0, keepdims=True)
        agree1 = jnp.sum(jnp.where(halves, 0.0, start_agree), axis=0, keepdims=True)
        agree = jnp.where(halves, agree0, agree1)
        dsec = dsecond[p] + (up[p].T - 2.0 * agree * second[p]) * inverse_total
        slope = second[p] * dsec
        slope = (slope - second[p] * jnp.sum(slope, axis=-1, keepdims=True)) * scale
        dql = nn(slope.astype(BF16), ks[p][0])
        dkl = nn(slope.T.astype(BF16), qs[p][0]) + dk_landmark[p]
        third = keep.third[p].astype(F32)
        ds = dsummary[p].astype(BF16)
        dthird = nt(ds, value)
        agreed = jnp.sum(dsummary[p] * summary[p], axis=-1, keepdims=True)
        slope = third * (dthird - agreed) * scale
        dv = nn(third.T.astype(BF16), ds)
        dql = dql + frame.block(nn(slope.astype(BF16), key))
        dk = nn(slope.T.astype(BF16), qs[p][0])
        dql = ((dql[:M] + dql[M:]) * frame.inv).astype(BF16)
        dkl = ((dkl[:M] + dkl[M:]) * frame.inv).astype(BF16)
        out_ref[0, :, c] = (dq[p] + nn(frame.member_t, dql)).astype(BF16)
        out_ref[1, :, c] = (dk + nn(frame.member_t, dkl)).astype(BF16)
        inside = (value.astype(F32) * frame.valid).astype(BF16)
        rows_pair = [taps_turned[pl.ds(head0 + 2 * p + i, 1), :] for i in range(2)]
        dv = dv + frame.valid * frame.conv(rows_pair, grad_low[p])
        out_ref[2, :, c] = dv.astype(BF16)
        for i in range(2):
            product = nt(grad_low[p] * frame.keep[i], inside)
            taps_out(2 * p + i, frame.diagonals(product))
        yield


def norm_rows(r, gain, shift):
    centre = r - jnp.mean(r, axis=-1, keepdims=True)
    spread = lax.rsqrt(jnp.mean(centre * centre, axis=-1, keepdims=True) + 1e-05)
    normed = centre * spread
    return normed * gain + shift, normed, spread


def norm_rows_back(dy, normed, spread, gain):
    scaled = dy * gain
    result = spread * (
        scaled
        - jnp.mean(scaled, axis=-1, keepdims=True)
        - normed * jnp.mean(scaled * normed, axis=-1, keepdims=True)
    )
    return (
        result,
        jnp.sum(dy * normed, axis=0, keepdims=True),
        jnp.sum(dy, axis=0, keepdims=True),
    )


GELU_A = 0.7978845608028654
GELU_B = 0.044715


def gelu_both(u):
    square = u * u
    t = jnp.tanh(GELU_A * (u + GELU_B * u * square))
    half = 0.5 * (1.0 + t)
    slope = half + 0.5 * u * (1.0 - t * t) * (GELU_A + (3.0 * GELU_A * GELU_B) * square)
    return u * half, slope


SEND_SEM = ((0, 1, 2, 2, 0, 1, 2, 3), (0, 1, 2, 2, 0, 3, 2, 4, 1), (0, 1, 2, 2, 0, 1, 2, 3))
RECEIVE_SEM = ((0, 1, 2, 3, 2, 6, 5, 4), (0, 1, 2, 3, 6, 6, 5, 4, 2), (0, 1, 2, 3, 2, 6, 5, 4))
SENDS, RECEIVES = 5, 7


class Reduction:
    def __init__(self, sems):
        dp, self.mp = lax.axis_index("dp"), lax.axis_index("mp")
        z = dp // 4
        self.x = (dp // 2) % 2
        self.core = dp % 2
        self.upper = z // 2
        self.inner = (z == 1) | (z == 2)
        self.outer = (z == 0) | (z == 3)
        self.to_core = dp + 1 - 2 * self.core
        self.to_x = dp + 2 - 4 * self.x
        self.to_near = dp + 4 - 8 * (z % 2)
        self.to_mid = (3 - z) * 4 + dp % 4
        self.sems = sems
        self.pieces = []

    def greet(self, barrier):
        for other in (self.to_core, self.to_x, self.to_near, self.to_mid):
            pl.semaphore_signal(barrier, inc=1, device_id=(other, self.mp), device_id_type=MESH)

    def add(self, rows, kind, view, slots, credit, gives, takes, other_kind):
        self.pieces.append((rows // 4, kind, view, slots, credit, gives, takes, other_kind))

    def copy(self, index, slot, source, target, to):
        kind, place = self.pieces[index][1], self.pieces[index][4]
        return pltpu.make_async_remote_copy(
            src_ref=source,
            dst_ref=target,
            send_sem=self.sems.ring_send.at[place * SENDS + SEND_SEM[kind][slot]],
            recv_sem=self.sems.ring_receive.at[place * RECEIVES + RECEIVE_SEM[kind][slot]],
            device_id=(to, self.mp),
            device_id_type=MESH,
        )

    def event(self, index, step):
        quarter, kind, view, slots, credit, gives, takes, other_kind = self.pieces[index]
        x, core, upper = self.x, self.core, self.upper
        side = upper if kind == 1 else x

        def region(half, which, count=1):
            return view(half, which, count * quarter)

        def arrived(slot, ref):
            self.copy(index, slot, ref, ref, self.to_core).wait_recv()

        def sent(slot, ref):
            self.copy(index, slot, ref, ref, self.to_core).wait_send()

        def send(slot, source, destination, to, need=None):
            if takes and need is not None:
                pl.semaphore_wait(self.sems.credit.at[credit * 4 + need], 1)
            self.copy(index, slot, source, destination, to).start()

        def free(which, to):
            if gives:
                pl.semaphore_signal(
                    self.sems.credit.at[credit * 4 + which],
                    inc=1,
                    device_id=(to, self.mp),
                    device_id_type=MESH,
                )

        def ready(which, slot, ref, to):
            sent(slot, ref)
            pl.semaphore_signal(
                self.sems.ready.at[credit * 4 + which],
                inc=1,
                device_id=(to, self.mp),
                device_id_type=MESH,
            )

        def await_ready(which):
            pl.semaphore_wait(self.sems.ready.at[credit * 4 + which], 1)

        def slot_part(ref, which):
            return ref.at[pl.ds(pl.multiple_of(which * quarter, 16), quarter)]

        def sum_into(ref, others):
            block = 48 if quarter % 48 == 0 else 16

            def step_rows(i, unused):
                span = pl.ds(pl.multiple_of(i * block, 16), block)
                total = ref[span, :].astype(F32)
                for other in others:
                    total = total + other[span, :].astype(F32)
                ref[span, :] = total.astype(BF16)
                return unused

            lax.fori_loop(0, quarter // block, step_rows, 0)

        mine, other = region(core, side), region(core, 1 - side)
        if step == 0:
            if kind == 2:
                send(0, region(1 - core, x), slot_part(slots.core, 0), self.to_core, need=0)
            else:
                send(0, region(1 - core, 0, 2), slots.core, self.to_core, need=0)
        elif step == 7:
            for slot, which in ((6, side), (7, 1 - side)):
                arrived(slot, region(1 - core, which))
            sent(6, mine)
            sent(7, other)
            if kind != 1:
                sent(5, mine)

                @pl.when(self.inner)
                def _():
                    sent(4, mine)

            else:

                @pl.when(self.inner)
                def _():
                    for slot in (4, 5, 8):
                        sent(slot, mine)

        elif kind == 2 and step < 4:
            if step > 1:

                @pl.when(self.outer if step == 2 else self.inner)
                def _():
                    arrived(0, slot_part(slots.core, 0))
                    if step == 2:
                        sum_into(mine, [slot_part(slots.core, 0)])
                        send(2, mine, slot_part(slots.near, 0), self.to_near, need=2)
                    else:
                        arrived(2, slot_part(slots.near, 0))
                        sum_into(mine, [slot_part(slots.core, 0), slot_part(slots.near, 0)])
                        send(3, mine, slots.mid, self.to_mid, need=3)
                    ready(0, 0, region(1 - core, x), self.to_core)

            if step == 3:

                @pl.when(self.outer)
                def _():
                    ready(2, 2, mine, self.to_near)

        elif kind != 1:
            if step == 1:
                arrived(0, slots.core)
                sum_into(other, [slot_part(slots.core, 1 - x)])
                if other_kind == 0:
                    send(1, other, slots.x, self.to_x, need=1)
                else:
                    if takes:

                        @pl.when(self.inner)
                        def _():
                            pl.semaphore_wait(self.sems.credit.at[credit * 4 + 1], 1)

                    send(1, other, slots.x, self.to_x)
                ready(0, 0, region(1 - core, 0, 2), self.to_core)
            elif step == 2:

                @pl.when(self.outer)
                def _():
                    arrived(1, slots.x)
                    sum_into(mine, [slot_part(slots.core, x), slots.x])
                    free(0, self.to_core)
                    if other_kind == 0:
                        free(1, self.to_x)
                    send(2, mine, slot_part(slots.near, 0), self.to_near, need=2)
                    ready(1, 1, other, self.to_x)

            elif step == 3:

                @pl.when(self.inner)
                def _():
                    arrived(1, slots.x)
                    arrived(2, slot_part(slots.near, 0))
                    sum_into(mine, [slot_part(slots.core, x), slots.x, slot_part(slots.near, 0)])
                    free(0, self.to_core)
                    if other_kind != 2:
                        free(1, self.to_x)
                    free(2, self.to_near)
                    send(3, mine, slots.mid, self.to_mid, need=3)
                    ready(1, 1, other, self.to_x)

                @pl.when(self.outer)
                def _():
                    ready(2, 2, mine, self.to_near)

            elif step == 4:

                @pl.when(self.inner)
                def _():
                    arrived(3, slots.mid)
                    sent(3, mine)
                    sum_into(mine, [slots.mid])
                    free(3, self.to_mid)
                    await_ready(2)
                    send(4, mine, mine, self.to_near)
                    if kind == 0:
                        await_ready(1)
                    send(5, mine, mine, self.to_x)
                    await_ready(0)
                    send(6, mine, mine, self.to_core)

            elif step == 5:

                @pl.when(self.outer)
                def _():
                    arrived(4, mine)
                    if kind == 0:
                        await_ready(1)
                    send(5, mine, mine, self.to_x)
                    await_ready(0)
                    send(6, mine, mine, self.to_core)

            elif step == 6:
                arrived(5, other)
                send(7, other, other, self.to_core)
        else:
            if step == 1:

                @pl.when(self.outer)
                def _():
                    arrived(0, slots.core)
                    sum_into(region(core, 0), [slot_part(slots.core, 0)])
                    sum_into(region(core, 1), [slot_part(slots.core, 1)])
                    free(0, self.to_core)
                    send(2, region(core, 0, 2), slots.near, self.to_near, need=2)
                    ready(0, 0, region(1 - core, 0, 2), self.to_core)

            elif step == 2:

                @pl.when(self.outer)
                def _():
                    ready(2, 2, region(core, 0, 2), self.to_near)

                @pl.when(self.inner)
                def _():
                    arrived(0, slots.core)
                    arrived(2, slots.near)
                    sum_into(other, [slot_part(slots.core, 1 - side), slot_part(slots.near, 1 - side)])
                    send(3, other, slots.mid, self.to_mid, need=3)
                    ready(0, 0, region(1 - core, 0, 2), self.to_core)

            elif step == 3:

                @pl.when(self.inner)
                def _():
                    arrived(3, slots.mid)
                    sum_into(mine, [slot_part(slots.core, side), slot_part(slots.near, side), slots.mid])
                    free(0, self.to_core)
                    free(2, self.to_near)
                    free(3, self.to_mid)
                    send(1, mine, slots.x, self.to_x, need=1)
                    ready(3, 3, other, self.to_mid)

            elif step == 4:

                @pl.when(self.inner)
                def _():
                    arrived(1, slots.x)
                    sent(1, mine)
                    sum_into(mine, [slots.x])
                    if other_kind != 2:
                        free(1, self.to_x)
                    await_ready(3)
                    send(4, mine, mine, self.to_mid)
                    await_ready(2)
                    send(8, mine, mine, self.to_near)
                    await_ready(0)
                    send(6, mine, mine, self.to_core)

            elif step == 5:

                @pl.when(self.inner)
                def _():
                    arrived(4, other)
                    send(5, other, other, self.to_near)
                    send(7, other, other, self.to_core)

                @pl.when(self.outer)
                def _():
                    arrived(8, mine)
                    await_ready(0)
                    send(6, mine, mine, self.to_core)

            elif step == 6:

                @pl.when(self.outer)
                def _():
                    arrived(5, other)
                    send(7, other, other, self.to_core)


class SmallSum:
    def __init__(self, ring, total, slots, sems, first_tap):
        self.ring, self.total, self.slots, self.sems, self.first_tap = ring, total, slots, sems, first_tap

    def copy(self, slot, target, to, mp):
        return pltpu.make_async_remote_copy(
            src_ref=self.total,
            dst_ref=target,
            send_sem=self.sems.small_send.at[slot],
            recv_sem=self.sems.small_receive.at[slot],
            device_id=(to, mp),
            device_id_type=MESH,
        )

    def event(self, step):
        ring, total, slots = self.ring, self.total, self.slots
        dp = ring.to_core + 2 * ring.core - 1

        def start(slot, to, mp=None):
            self.copy(slot, slots.at[slot], to, ring.mp if mp is None else mp).start()

        def take(slot):
            self.copy(slot, slots.at[slot], dp, ring.mp).wait_recv()

        def sent(slot):
            self.copy(slot, slots.at[slot], dp, ring.mp).wait_send()

        if step == 0:
            start(0, dp, 1 - ring.mp)
        elif step == 1:
            take(0)
            sent(0)
            total[self.first_tap :, :] += slots[0, self.first_tap :, :]
            start(1, ring.to_core)
        elif step == 2:
            take(1)
            sent(1)
            total[...] += slots[1]
            start(2, ring.to_x)
        elif step == 3:
            take(2)
            sent(2)
            total[...] += slots[2]

            @pl.when(ring.outer)
            def _():
                start(3, ring.to_near)

        elif step == 4:

            @pl.when(ring.inner)
            def _():
                take(3)
                total[...] += slots[3]
                start(4, ring.to_mid)

        elif step == 5:

            @pl.when(ring.inner)
            def _():
                take(4)
                sent(4)
                total[...] += slots[4]
                start(5, ring.to_near)

        elif step == 6:

            @pl.when(ring.outer)
            def _():
                take(5)
                sent(3)
                total[...] = slots[5]

            @pl.when(ring.inner)
            def _():
                sent(5)


def whole_step(
    length_ref,
    tokens_ref,
    cotangent_ref,
    raw_taps_ref,
    gains_ref,
    shifts_ref,
    projection_hbm,
    output_hbm,
    up_hbm,
    down_hbm,
    activations_ref,
    token_grad_ref,
    small_ref,
    down_grad_ref,
    up_grad_ref,
    other_grad_ref,
    weights,
    kept,
    work,
    shared,
    wire,
    slots,
    sems,
):
    rows, width = tokens_ref.shape
    columns = projection_hbm.shape[3]
    hidden = up_hbm.shape[2]
    heads, _, reach = raw_taps_ref.shape
    grads = Grads(down_grad_ref, up_grad_ref, other_grad_ref)
    size_h = width // heads
    half = rows // 2
    tile = hidden // 2
    dp, mp = lax.axis_index("dp"), lax.axis_index("mp")
    head0 = mp * (columns // size_h)
    partner = (dp, 1 - mp)

    def own_half(layer):
        return weights.output.at[layer, mp]

    loads = []
    order = [
        (projection_hbm, weights.projection),
        (output_hbm, weights.output),
        (up_hbm, weights.up),
        (down_hbm, weights.down),
    ]
    for layer in range(LAYERS):
        for index, (source, place) in enumerate(order):
            load = pltpu.make_async_copy(
                source.at[layer],
                own_half(layer) if index == 1 else place.at[layer],
                sems.load.at[layer * 4 + index],
            )
            load.start()
            loads.append(load)

    barrier = pltpu.get_barrier_semaphore()
    pl.semaphore_signal(barrier, inc=1, device_id=partner, device_id_type=MESH)
    ring = Reduction(sems)
    ring.greet(barrier)

    frame = Frame(length_ref[0], rows, size_h)
    taps_ref, turned_ref = work.taps, work.turned
    taps_ref[...] = jnp.zeros_like(taps_ref)
    mirror = iota((rows, rows), 0) + iota((rows, rows), 1) == reach - 1
    mirror = mirror.astype(F32).astype(BF16)
    for layer in range(LAYERS):
        taps_ref[layer, :heads, :reach] = raw_taps_ref[:, layer, :]
        turned_ref[layer] = nn(taps_ref[layer].astype(BF16), mirror)
    flights = {}

    def send(slot, piece, partial_value):
        span = pl.ds(piece * half, half)
        wire.send[span, :] = partial_value.astype(BF16)
        copy = pltpu.make_async_remote_copy(
            src_ref=wire.send.at[span],
            dst_ref=wire.receive.at[slot % 2, span],
            send_sem=sems.send.at[slot % 2 * 2 + piece],
            recv_sem=sems.receive.at[slot % 2 * 2 + piece],
            device_id=partner,
            device_id_type=MESH,
        )
        copy.start()
        flights[slot, piece] = copy

    def arrived(slot, piece):
        span = pl.ds(piece * half, half)
        flights[slot, piece].wait()
        return wire.send[span, :].astype(F32) + wire.receive[
            slot % 2, span, :
        ].astype(F32)

    def share_copy(layer, hop):
        part = columns // 2
        which, first = (mp, ring.core) if hop == 0 else (1 - mp, ring.core)
        place = weights.output.at[layer, which, pl.ds(pl.multiple_of(first * part, 16), part)]
        return pltpu.make_async_remote_copy(
            src_ref=place,
            dst_ref=place,
            send_sem=sems.share_send.at[layer * 2 + hop],
            recv_sem=sems.share_receive.at[layer * 2 + hop],
            device_id=partner if hop == 0 else (ring.to_core, mp),
            device_id_type=MESH,
        )

    def gather_copy(layer, piece):
        place = work.mixed.at[mp, pl.ds(piece * half, half)]
        return pltpu.make_async_remote_copy(
            src_ref=place,
            dst_ref=place,
            send_sem=sems.gather_send.at[piece],
            recv_sem=sems.gather_receive.at[piece],
            device_id=partner,
            device_id_type=MESH,
        )

    side = hidden // 2
    near_rows = pl.ds(pl.multiple_of(ring.x * side, 128), side)
    far_rows = pl.ds(pl.multiple_of((1 - ring.x) * side, 128), side)
    factors = []

    def factor_copy(index, source, target, to=None):
        return pltpu.make_async_remote_copy(
            src_ref=source,
            dst_ref=target,
            send_sem=sems.factor_send.at[index],
            recv_sem=sems.factor_receive.at[index],
            device_id=(ring.to_x, mp) if to is None else to,
            device_id_type=MESH,
        )

    halves = [slice(0, half), slice(half, rows)]

    def project(layer, c):
        for i in range(3):
            kept.qkv[layer, i, c, :] = nn(
                work.x_low[c, :], weights.projection[layer, i]
            ).astype(BF16)

    def keep_of(layer):
        return Kept(*(ref.at[layer] for ref in kept.attention))

    work.x[...] = tokens_ref[...].astype(F32)
    work.x_low[...] = tokens_ref[...]
    loads[0].wait()
    project(0, halves[0])
    loads[1].wait()
    pl.semaphore_wait(barrier, 5)
    share_copy(0, 0).start()
    project(0, halves[1])
    for layer in range(LAYERS):
        attention(
            frame,
            kept.qkv.at[layer],
            taps_ref.at[layer],
            head0,
            size_h,
            keep_of(layer),
            work.mixed.at[mp],
        )
        slot = layer * 2
        for piece in range(len(halves)):
            gather_copy(layer, piece).start()
        share_copy(layer, 0).wait()
        share_copy(layer, 1).start()
        kept.mixed_t[layer] = work.mixed[mp].T
        kept.x_t[layer] = work.x_low[...].T
        loads[layer * 4 + 2].wait()
        loads[layer * 4 + 3].wait()
        share_copy(layer, 1).wait()
        for piece, c in enumerate(halves):
            gather_copy(layer, piece).wait()
            summed = work.x[c, :] + nn(
                jnp.concatenate([work.mixed[0, c, :], work.mixed[1, c, :]], 1),
                weights.output[layer].reshape(2 * columns, width),
            )
            y, normed, spread = norm_rows(summed, gains_ref[layer, 0:1], shifts_ref[layer, 0:1])
            kept.normed[layer, 0, c, :] = normed.astype(BF16)
            kept.spread[layer, 0, c, :] = spread
            work.y[c, :] = y
            work.y_low[c, :] = y.astype(BF16)
            for j in range(hidden // tile):
                span = slice(j * tile, (j + 1) * tile)
                u = nn(work.y_low[c, :], weights.up[layer, :, span])
                active, slope = gelu_both(u)
                work.active[c, span] = active.astype(BF16)
                kept.slope[layer, c, span] = slope.astype(BF16)
            send(slot + 1, piece, nn(work.active[c, :], weights.down[layer]))
        if layer + 1 < LAYERS:
            loads[layer * 4 + 5].wait()
            share_copy(layer + 1, 0).start()
        kept.active_t[layer] = work.active[...].T
        kept.y_t[layer] = work.y_low[...].T
        if FACTORED[layer]:
            factors.append(factor_copy(0, kept.active_t.at[layer, far_rows], shared.active_t))
            factors.append(factor_copy(1, kept.slope.at[layer, :, far_rows], shared.slope))
            factors.append(factor_copy(2, kept.y_t.at[layer], shared.y_t))
            for copy in factors:
                copy.start()
        if layer + 1 < LAYERS:
            loads[layer * 4 + 4].wait()
        for piece, c in enumerate(halves):
            summed = work.y[c, :] + arrived(slot + 1, piece)
            y, normed, spread = norm_rows(summed, gains_ref[layer, 1:2], shifts_ref[layer, 1:2])
            kept.normed[layer, 1, c, :] = normed.astype(BF16)
            kept.spread[layer, 1, c, :] = spread
            if layer + 1 < LAYERS:
                work.x[c, :] = y
                work.x_low[c, :] = y.astype(BF16)
                project(layer + 1, c)
            else:
                activations_ref[c, :] = (y * frame.valid[c]).astype(BF16)

    def add_pieces(layer):
        listed = pieces_of(width, columns, hidden, layer)
        listed_rows = {DOWN: hidden, UP: 2 * width}
        for k, (name, rows_of, kind) in enumerate(listed):
            before = sum(item[1] for item in listed[:k] if item[0] == name)
            index = sum(1 for item in listed[:k] if item[0] == name)

            quarter = rows_of // 4
            if kind == 2:
                before, high, wide = before // 2, quarter, listed_rows[name] // 2
            else:
                high, wide = 2 * quarter, quarter
            if name in (DOWN, UP):
                ref = (grads.down if name == DOWN else grads.up).at[layer]
            else:
                ref = grads.other.at[layer, 0 if name == OUTPUT else 1 + index]
                before = 0

            def view(half, which, count, ref=ref, before=before, high=high, wide=wide):
                return ref.at[pl.ds(pl.multiple_of(before + half * high + which * wide, 16), count)]

            ring.add(rows_of, kind, view, slots[k], k, layer > 0, layer + 1 < LAYERS, PIECE_KINDS[1 - layer][k])

    for layer in reversed(range(LAYERS)):
        add_pieces(layer)
    small = SmallSum(ring, small_ref, wire.small, sems, 8)
    dy_ref, dr_ref, e_ref, du_ref = work.x, work.y, work.y_low, work.active

    def norm_back(layer, which):
        gain = gains_ref[layer, which : which + 1]
        gain_sum = shift_sum = 0.0
        for c in halves:
            result, gain_part, shift_part = norm_rows_back(
                dy_ref[c, :],
                kept.normed[layer, which, c, :].astype(F32),
                kept.spread[layer, which, c, :],
                gain,
            )
            dr_ref[c, :] = result
            (e_ref, e_second)[which][c, :] = result.astype(BF16)
            gain_sum, shift_sum = gain_sum + gain_part, shift_sum + shift_part
        row = layer * 2 + which
        small_ref[row : row + 1, :] = gain_sum
        small_ref[row + 4 : row + 5, :] = shift_sum

    du_other, e_second = work.x_low, work.e_second

    def down_grads(layer):
        block = hidden // DOWN_PIECES
        for j in range(DOWN_PIECES):
            if FACTORED[layer]:
                low = slice(j * block // 2, (j + 1) * block // 2)
                span = pl.ds(pl.multiple_of(ring.x * side + low.start, 16), block // 2)
                value = nn(kept.active_t[layer, span, :], e_second[...]) + nn(
                    shared.active_t[low, :], shared.e[...]
                )
            else:
                span = slice(j * block, (j + 1) * block)
                value = nn(kept.active_t[layer, span, :], e_second[...])
            grads.down[layer, span, :] = value.astype(BF16)
            yield

    def up_grads(layer):
        block = 2 * width // UP_PIECES
        for j in range(UP_PIECES):
            if FACTORED[layer]:
                low = slice(j * block // 2, (j + 1) * block // 2)
                span = pl.ds(pl.multiple_of(ring.x * width + low.start, 16), block // 2)
                value = nn(kept.y_t[layer, low, :], du_ref[:, near_rows]) + nn(
                    shared.y_t[low, :], du_other[...]
                )
            else:
                span = slice(j * block, (j + 1) * block)
                at, first = divmod(j * block, width)
                value = nn(
                    kept.y_t[layer, first : first + block, :],
                    du_ref[:, at * side : (at + 1) * side],
                )
            grads.up[layer, span, :] = value.astype(BF16)
            yield

    def backward():
        small_ref[...] = jnp.zeros_like(small_ref)
        for piece, c in enumerate(halves):
            dy_ref[c, :] = cotangent_ref[c, :].astype(F32) * frame.valid[c]
        for layer in reversed(range(LAYERS)):
            slot = 4 + (LAYERS - 1 - layer) * 2
            norm_back(layer, 1)
            if FACTORED[layer]:
                own = pl.ds(pl.multiple_of(mp * half, 16), half)
                factors.append(factor_copy(3, e_second.at[own], shared.e.at[own]))
                factors[3].start()
            yield
            if not FACTORED[layer]:
                yield from down_grads(layer)
            for j in range(hidden // tile):
                span = slice(j * tile, (j + 1) * tile)
                dh = nt(e_second[...], weights.down[layer, span, :])
                du_ref[:, span] = (dh * kept.slope[layer, :, span].astype(F32)).astype(BF16)
            yield
            for piece, c in enumerate(halves):
                send(slot, piece, nt(du_ref[c, :], weights.up[layer]))
                yield
            if FACTORED[layer]:
                for copy in factors:
                    copy.wait()
                passing = factor_copy(4, shared.e.at[own], shared.e.at[own], partner)
                passing.start()
                yield
            else:
                yield from up_grads(layer)
            for piece, c in enumerate(halves):
                dy_ref[c, :] = dr_ref[c, :] + arrived(slot, piece)
            norm_back(layer, 0)
            yield
            for piece, c in enumerate(halves):
                work.dmixed[c, :] = nt(e_ref[c, :], weights.output[layer, mp]) * frame.valid[c]
            yield
            for j in range(2):
                span = slice(j * columns, (j + 1) * columns)
                grads.other[layer, 0, span, :] = nn(
                    kept.mixed_t[layer], e_ref[:, span]
                ).astype(BF16)
            yield
            if FACTORED[layer]:
                passing.wait()
                for j in range(side // tile):
                    span = slice(j * tile, (j + 1) * tile)
                    near = pl.ds(pl.multiple_of(ring.x * side + j * tile, 128), tile)
                    dh = nt(shared.e[...], weights.down[layer, near, :])
                    du_other[:, span] = (dh * shared.slope[:, span].astype(F32)).astype(BF16)
                yield
                yield from down_grads(layer)
                yield from up_grads(layer)

            def taps_out(head, row, layer=layer):
                lanes = slice(head * 128, (head + 1) * 128)
                for side in range(2):
                    at = 8 + 2 * layer + side
                    small_ref[at : at + 1, lanes] = jnp.where(mp == side, row[:, :128], 0.0)

            yield from attention_back(
                frame,
                work.dmixed,
                kept.qkv.at[layer],
                turned_ref.at[layer],
                head0,
                size_h,
                keep_of(layer),
                work.dqkv,
                taps_out,
            )
            for piece, c in enumerate(halves):
                total = 0.0
                for i in range(3):
                    total = total + nt(work.dqkv[i, c, :], weights.projection[layer, i])
                send(slot + 1, piece, total)
                yield
            for i in range(3):
                grads.other[layer, 1 + i] = nn(kept.x_t[layer], work.dqkv[i]).astype(BF16)
                yield
            target = dy_ref if layer > 0 else token_grad_ref
            for piece, c in enumerate(halves):
                target[c, :] = dr_ref[c, :] + arrived(slot + 1, piece)
        yield

    items = backward()
    for code in ORDER:
        if code < 0:
            next(items)
        elif code >= 1000:
            small.event(code - 1000)
        else:
            ring.event(code // 8, code % 8)


FACTORED = (True, False)
DOWN_PIECES = 4
UP_PIECES = 4
PIECE_KINDS = (
    (2, 2, 2, 2, 2, 2, 2, 2, 1, 0, 0, 0),
    (0, 0, 1, 0, 0, 0, 1, 0, 1, 0, 1, 0),
)
ORDER = (
    -1, -1, 0, -1, 8, -1, 16, -1, 24, -1, 1, 9, -1, -1, 17, -1, 32, -1, 40, 25, -1, 48, -1, 56, 33, 41, 49, 2,
    57, 10, -1, 18, 26, -1, -1, 64, -1, -1, 34, 65, -1, 50, -1, 42, 19, -1, -1, 3, -1, 58, -1, -1, 51, 11, -1,
    -1, 20, -1, -1, 72, -1, 80, 4, 27, -1, 88, 73, 81, 52, 35, 12, 89, 21, 74, 5, -1, 66, 90, 28, -1, -1, -1,
    43, 53, 6, 13, 59, 36, 67, -1, 22, 29, 14, 82, 44, -1, 54, -1, -1, -1, -1, 75, 60, 7, 96, 97, -1, 15, 104,
    105, 30, -1, 23, 112, 37, 113, -1, 98, -1, 106, -1, -1, 55, 144, 145, 114, 31, 120, 121, -1, 83, 91, -1,
    146, 45, 68, 122, -1, 76, -1, 61, 38, 99, -1, -1, 39, 128, 129, 92, -1, 107, 46, -1, 130, 69, -1, 47, 136,
    137, 84, 115, -1, 77, 62, -1, 1000, 138, 100, -1, 147, 63, 152, 153, -1, 93, -1, -1, -1, 154, 108, 123,
    1001, 78, 70, 1002, 79, 168, 71, 160, 131, 94, 85, 169, 161, 116, 95, 184, 139, 101, 185, 1003, 148, -1,
    155, 170, 109, 124, 102, 86, 87, 176, 186, 117, 103, 177, 132, 162, 1004, 140, 110, 149, 111, 171, 156,
    118, 125, 119, 187, 163, 178, 133, 1005, 150, 141, 151, 172, 179, 188, 126, 157, 127, 1006, 134, 135, 180,
    173, 142, 143, 189, 158, 164, 159, 181, 174, 175, 165, 190, 191, 182, 166, 183, 167,
)


def pieces_of(width, columns, hidden, layer):
    names = [DOWN] * DOWN_PIECES + [UP] * UP_PIECES + [OUTPUT] + [PROJECTION] * 3
    rows = {DOWN: hidden // DOWN_PIECES, UP: 2 * width // UP_PIECES, OUTPUT: width, PROJECTION: width}
    return [(name, rows[name], kind) for name, kind in zip(names, PIECE_KINDS[layer])]


def slots_of(name, rows, long, width, columns, hidden):
    across = {DOWN: width, UP: hidden // 2, OUTPUT: columns, PROJECTION: columns}[name]

    def room(count):
        return pltpu.VMEM((count, across), BF16)

    return Slots(
        core=room(rows // 2),
        x=room(rows // 4),
        near=room(rows // 2 if long else rows // 4),
        mid=room(rows // 4),
    )


def fused_body(tokens, lengths, cotangent, projection, conv_taps, output_weight, norm_gains, norm_shifts, up_weight, down_weight):
    rows, width = tokens.shape
    columns, hidden = projection.shape[3], up_weight.shape[2]
    heads, reach = conv_taps.shape[1:]
    size_h = width // heads
    pairs = columns // (2 * size_h)
    by_kind = jnp.transpose(projection, (0, 2, 1, 3))
    by_head = jnp.transpose(conv_taps, (1, 0, 2))
    vmem = pl.BlockSpec(memory_space=pltpu.VMEM)
    hbm = pl.BlockSpec(memory_space=pl.ANY)
    two = 2 * M
    pieces = pieces_of(width, columns, hidden, 0)
    scratch = (
        Weights(
            projection=pltpu.VMEM((LAYERS, 3, width, columns), BF16),
            output=pltpu.VMEM((LAYERS, 2, columns, width), BF16),
            up=pltpu.VMEM((LAYERS, width, hidden), BF16),
            down=pltpu.VMEM((LAYERS, hidden, width), BF16),
        ),
        Stored(
            attention=Kept(
                ql=pltpu.VMEM((LAYERS, M, columns), F32),
                kl=pltpu.VMEM((LAYERS, M, columns), F32),
                second=pltpu.VMEM((LAYERS, pairs, two, two), F32),
                inverse=pltpu.VMEM((LAYERS, NEWTON + 1, pairs, M, two), F32),
                first=pltpu.VMEM((LAYERS, rows, columns), BF16),
                third=pltpu.VMEM((LAYERS, pairs, two, rows), BF16),
                summary=pltpu.VMEM((LAYERS, pairs, two, two), F32),
                carried=pltpu.VMEM((LAYERS, pairs, two, two), F32),
            ),
            qkv=pltpu.VMEM((LAYERS, 3, rows, columns), BF16),
            normed=pltpu.VMEM((LAYERS, 2, rows, width), BF16),
            spread=pltpu.VMEM((LAYERS, 2, rows, 1), F32),
            slope=pltpu.VMEM((LAYERS, rows, hidden), BF16),
            x_t=pltpu.VMEM((LAYERS, width, rows), BF16),
            mixed_t=pltpu.VMEM((LAYERS, columns, rows), BF16),
            y_t=pltpu.VMEM((LAYERS, width, rows), BF16),
            active_t=pltpu.VMEM((LAYERS, hidden, rows), BF16),
        ),
        Work(
            x=pltpu.VMEM((rows, width), F32),
            x_low=pltpu.VMEM((rows, width), BF16),
            y=pltpu.VMEM((rows, width), F32),
            y_low=pltpu.VMEM((rows, width), BF16),
            mixed=pltpu.VMEM((2, rows, columns), BF16),
            active=pltpu.VMEM((rows, hidden), BF16),
            e_second=pltpu.VMEM((rows, width), BF16),
            dmixed=pltpu.VMEM((rows, columns), F32),
            dqkv=pltpu.VMEM((3, rows, columns), BF16),
            taps=pltpu.VMEM((LAYERS, 16, rows), F32),
            turned=pltpu.VMEM((LAYERS, 16, rows), F32),
        ),
        Shared(
            active_t=pltpu.VMEM((hidden // 2, rows), BF16),
            slope=pltpu.VMEM((rows, hidden // 2), BF16),
            y_t=pltpu.VMEM((width, rows), BF16),
            e=pltpu.VMEM((rows, width), BF16),
        ),
        Wire(
            send=pltpu.VMEM((rows, width), BF16),
            receive=pltpu.VMEM((2, rows, width), BF16),
            small=pltpu.VMEM((6, 8 + 2 * LAYERS, width), F32),
        ),
        [
            slots_of(name, count, 1 in kinds, width, columns, hidden)
            for (name, count, _), kinds in zip(pieces, zip(*PIECE_KINDS))
        ],
        Sems(
            load=pltpu.SemaphoreType.DMA((4 * LAYERS,)),
            ring_send=pltpu.SemaphoreType.DMA((SENDS * len(pieces),)),
            ring_receive=pltpu.SemaphoreType.DMA((RECEIVES * len(pieces),)),
            small_send=pltpu.SemaphoreType.DMA((6,)),
            small_receive=pltpu.SemaphoreType.DMA((6,)),
            credit=pltpu.SemaphoreType.REGULAR((4 * len(pieces),)),
            ready=pltpu.SemaphoreType.REGULAR((4 * len(pieces),)),
            factor_send=pltpu.SemaphoreType.DMA((5,)),
            factor_receive=pltpu.SemaphoreType.DMA((5,)),
            share_send=pltpu.SemaphoreType.DMA((2 * LAYERS,)),
            share_receive=pltpu.SemaphoreType.DMA((2 * LAYERS,)),
            gather_send=pltpu.SemaphoreType.DMA((2,)),
            gather_receive=pltpu.SemaphoreType.DMA((2,)),
            send=pltpu.SemaphoreType.DMA((4,)),
            receive=pltpu.SemaphoreType.DMA((4,)),
        ),
    )
    own = pltpu.VMEM
    results = pl.pallas_call(
        whole_step,
        out_shape=[
            own((rows, width), BF16),
            own((rows, width), F32),
            own((8 + 2 * LAYERS, width), F32),
            own((LAYERS, hidden, width), BF16),
            own((LAYERS, 2 * width, hidden // 2), BF16),
            own((LAYERS, 4, width, columns), BF16),
        ],
        in_specs=[pl.BlockSpec(memory_space=pltpu.SMEM)] + [vmem] * 5 + [hbm] * 4,
        out_specs=[vmem] * 6,
        scratch_shapes=scratch,
        compiler_params=pltpu.CompilerParams(
            collective_id=0, has_side_effects=True, vmem_limit_bytes=VMEM_ROOM
        ),
    )(
        lengths,
        tokens,
        cotangent,
        by_head,
        norm_gains,
        norm_shifts,
        by_kind,
        output_weight,
        up_weight,
        down_weight,
    )
    shape = jax.ShapeDtypeStruct
    held = [pltpu.with_memory_space_constraint(result, pltpu.VMEM) for result in results]
    wide = [
        (LAYERS, hidden, width),
        (LAYERS, width, hidden),
        (LAYERS, 3, width, columns),
        (LAYERS, columns, width),
    ]
    outputs = pl.pallas_call(
        widen,
        out_shape=[shape(size, F32) for size in wide]
        + [
            shape((rows, width), BF16),
            shape((rows, width), F32),
            shape((heads, LAYERS, reach), F32),
            shape((LAYERS, 2, width), F32),
            shape((LAYERS, 2, width), F32),
        ],
        in_specs=[vmem] * 6,
        out_specs=[hbm] * 6 + [vmem] * 3,
        scratch_shapes=[pltpu.VMEM(size, F32) for size in wide] + [pltpu.SemaphoreType.DMA((6,))],
        compiler_params=pltpu.CompilerParams(vmem_limit_bytes=WIDE_ROOM),
    )(*held)
    down_grad, up_grad, projection_grad, output_grad = outputs[:4]
    activations, token_grad, taps_grad, gains_grad, shifts_grad = outputs[4:]
    return (
        activations,
        token_grad,
        jnp.transpose(projection_grad, (0, 2, 1, 3)),
        jnp.transpose(taps_grad, (1, 0, 2)),
        output_grad,
        gains_grad,
        shifts_grad,
        up_grad,
        down_grad,
    )


VMEM_ROOM = 97 * 2**19
WIDE_ROOM = 32 * 2**20
WIDE_PARTS = 4


def widen(
    activations_ref,
    token_grad_ref,
    small_ref,
    down_ref,
    up_ref,
    other_ref,
    down_hbm,
    up_hbm,
    projection_hbm,
    output_hbm,
    activations_out,
    token_grad_out,
    taps_out,
    gains_out,
    shifts_out,
    down_wide,
    up_wide,
    projection_wide,
    output_wide,
    sems,
):
    heads, _, reach = taps_out.shape
    columns = output_wide.shape[1]

    def send(source, target, index):
        pltpu.make_async_copy(source, target, sems.at[index]).start()

    send(activations_ref, activations_out, 4)
    send(token_grad_ref, token_grad_out, 5)

    def cast(target, source):
        def step(i, unused):
            span = pl.ds(pl.multiple_of(i * 32, 32), 32)
            target[span, :] = source[span, :].astype(F32)
            return unused

        lax.fori_loop(0, source.shape[0] // 32, step, 0)

    for layer in range(LAYERS):
        count = down_ref.shape[1] // WIDE_PARTS
        for part in range(WIDE_PARTS):
            span = pl.ds(part * count, count)
            cast(down_wide.at[layer, span], down_ref.at[layer, span])
            send(down_wide.at[layer, span], down_hbm.at[layer, span], 0)
        count, side = up_wide.shape[1] // WIDE_PARTS, up_wide.shape[2] // 2
        for part in range(WIDE_PARTS):
            span = pl.ds(part * count, count)
            for i in range(2):
                cast(
                    up_wide.at[layer, span, pl.ds(i * side, side)],
                    up_ref.at[layer, pl.ds(i * up_wide.shape[1] + part * count, count)],
                )
            send(up_wide.at[layer, span], up_hbm.at[layer, span], 1)
        for i in range(3):
            cast(projection_wide.at[layer, i], other_ref.at[layer, 1 + i])
            send(projection_wide.at[layer, i], projection_hbm.at[layer, i], 2)
        for i in range(2):
            side = slice(i * columns, (i + 1) * columns)
            output_wide[layer, :, side] = other_ref[layer, 0, side, :].astype(F32)
        send(output_wide.at[layer], output_hbm.at[layer], 3)
    for layer in range(LAYERS):
        gains_out[layer] = small_ref[2 * layer : 2 * layer + 2, :]
        shifts_out[layer] = small_ref[4 + 2 * layer : 6 + 2 * layer, :]
        for head in range(heads):
            side, place = divmod(head, heads // 2)
            row = 8 + 2 * layer + side
            taps_out[head, layer : layer + 1, :] = small_ref[
                row : row + 1, place * 128 : place * 128 + reach
            ]
    whole = [
        (down_wide, down_hbm),
        (up_wide, up_hbm),
        (projection_wide, projection_hbm),
        (output_wide, output_hbm),
        (activations_ref, activations_out),
        (token_grad_ref, token_grad_out),
    ]
    for index, (source, target) in enumerate(whole):
        pltpu.make_async_copy(source, target, sems.at[index]).wait()


def solution(mesh):
    fused = mesh.shape["mp"] == 2 and mesh.shape["dp"] == 16

    def step(*arrays):
        return (fused_body if fused else body)(*arrays)

    return jax.shard_map(
        step,
        mesh=mesh,
        in_specs=(
            P("dp", None),
            P("dp"),
            P("dp", None),
            P(None, None, None, "mp"),
            P(),
            P(None, "mp", None),
            P(),
            P(),
            P(None, None, "mp"),
            P(None, "mp", None),
        ),
        out_specs=(
            P("dp", None),
            P("dp", None),
            P(None, None, None, "mp"),
            P(),
            P(None, "mp", None),
            P(),
            P(),
            P(None, None, "mp"),
            P(None, "mp", None),
        ),
        check_vma=False,
    )
```

```python
from typing import Any, NamedTuple

import jax
import jax.numpy as jnp
from jax import lax
from jax.experimental import pallas as pl
from jax.experimental.pallas import tpu as pltpu
from jax.sharding import PartitionSpec as P

M = 64
NEWTON = 6
LAYERS = 2


highest_value = lax.Precision.HIGHEST


def merged(array, axis, join):
    gathered = jax.tree.map(
        lambda a, kind: lax.all_gather(a.astype(kind), axis),
        array,
        (jnp.bfloat16, jnp.bfloat16, jnp.bfloat16),
    )

    def take(source):
        return jax.tree.map(
            lambda a, own: lax.dynamic_index_in_dim(a, source, 0, False).astype(own.dtype),
            gathered,
            array,
        )

    return lax.fori_loop(
        1, lax.axis_size(axis), lambda source, state: join(state, take(source)), take(0)
    )


def for_sending(array):
    return jax.tree.map(lambda a: a.astype(jnp.bfloat16) if a.dtype == jnp.float32 else a, array)


def softmax_row_block(scores):
    top = jnp.max(scores, axis=-1, keepdims=True)
    matrix_powers = jnp.exp(scores - top)
    return matrix_powers / jnp.sum(matrix_powers, axis=-1, keepdims=True)


def slot_masks(length, count, marks):
    position = jnp.arange(count, dtype=jnp.int32)
    inside = position < length
    segment = position * marks // length
    member = (segment[None, :] == jnp.arange(marks, dtype=jnp.int32)[:, None]) & inside[None, :]
    member = member.astype(jnp.float32)
    pooling = member / jnp.sum(member, axis=1, keepdims=True)
    return (pooling, inside.astype(jnp.float32))


def inverse_head(query_landmarks, key_landmarks, summary):
    scale_factor = query_landmarks.shape[-1] ** (-0.5)
    second = softmax_row_block(
        jnp.dot(query_landmarks, key_landmarks.T, precision=highest_value) * scale_factor
    )
    identity = jnp.eye(second.shape[0], dtype=jnp.float32)
    inverse = second.T / jnp.sum(second * second)
    for sweep in range(NEWTON):
        product = jnp.dot(second, inverse, precision=highest_value)
        inner = 7.0 * identity - product
        inner = 15.0 * identity - jnp.dot(product, inner, precision=highest_value)
        inner = 13.0 * identity - jnp.dot(product, inner, precision=highest_value)
        inverse = 0.25 * jnp.dot(inverse, inner, precision=highest_value)
    return jnp.dot(inverse, summary, precision=highest_value)


def inverse_section(query_landmarks, key_landmarks, summary):
    return jax.vmap(inverse_head)(query_landmarks, key_landmarks, summary)


def near_section(query_matrix, key_landmarks, carried_over):
    scale_factor = query_matrix.shape[-1] ** (-0.5)
    first_entry = softmax_row_block(
        jnp.einsum("nlv,lgv->lng", query_matrix, key_landmarks, precision=highest_value)
        * scale_factor
    )
    return jnp.einsum("xtz,xzb->txb", first_entry, carried_over, precision=highest_value)


def far_scores(query_landmarks, key_matrix, valid_own):
    scale_factor = query_landmarks.shape[-1] ** (-0.5)
    distant_scores = (
        jnp.einsum("owz,toz->owt", query_landmarks, key_matrix, precision=highest_value)
        * scale_factor
    )
    live = valid_own[None, None, :] > 0
    return (jnp.where(live, distant_scores, -1e30), live)


def join_softmax(left, right):
    peak = jnp.maximum(left[0], right[0])
    left_factor = jnp.exp(left[0] - peak)
    right_factor = jnp.exp(right[0] - peak)
    return (
        peak,
        left[1] * left_factor + right[1] * right_factor,
        left[2] * left_factor[..., None] + right[2] * right_factor[..., None],
    )


def attend(query_matrix, key_matrix, value_matrix, pooled_local, valid_own):
    query_portion = jnp.einsum("ji,ilk->ljk", pooled_local, query_matrix, precision=highest_value)
    key_portion = jnp.einsum("ji,ilk->ljk", pooled_local, key_matrix, precision=highest_value)
    query_landmarks, key_landmarks = (
        lax.psum(query_portion.astype(jnp.bfloat16), "mp").astype(jnp.float32),
        lax.psum(key_portion.astype(jnp.bfloat16), "mp").astype(jnp.float32),
    )
    distant_scores, live = far_scores(query_landmarks, key_matrix, valid_own)
    peak = jnp.max(distant_scores, axis=-1)
    matrix_powers = jnp.where(live, jnp.exp(distant_scores - peak[..., None]), 0.0)
    totals = jnp.sum(matrix_powers, axis=-1)
    weighted_values = jnp.einsum(
        "naw,wno->nao", matrix_powers, value_matrix, precision=highest_value
    )
    peak, totals, weighted_values = merged((peak, totals, weighted_values), "mp", join_softmax)
    summary = weighted_values / totals[..., None]
    carried_over = inverse_section(query_landmarks, key_landmarks, summary)
    mixed = near_section(query_matrix, key_landmarks, carried_over)
    return (mixed, (query_landmarks, key_landmarks, peak, totals, summary))


def attend_back(
    grad_rows, query_matrix, key_matrix, value_matrix, pooled_local, valid_own, saved, tap_part
):
    query_landmarks, key_landmarks, peak, totals, summary = saved
    scale_factor = query_matrix.shape[-1] ** (-0.5)
    carried_over, inverse_back = jax.vjp(inverse_section, query_landmarks, key_landmarks, summary)
    unused, near_back = jax.vjp(near_section, query_matrix, key_landmarks, carried_over)
    query_grad, kland_part, carried_part = near_back(grad_rows)
    key_landmark_nearby, carried_grad, tap_grad = (
        lax.psum(kland_part.astype(jnp.bfloat16), "mp").astype(jnp.float32),
        lax.psum(carried_part.astype(jnp.bfloat16), "mp").astype(jnp.float32),
        lax.psum(tap_part.astype(jnp.bfloat16), "mp").astype(jnp.float32),
    )
    query_landmark_gradient, key_landmark_gradient, summary_gradient = inverse_back(carried_grad)
    distant_scores, live = far_scores(query_landmarks, key_matrix, valid_own)
    weight_spread = jnp.where(
        live, jnp.exp(distant_scores - peak[..., None]) / totals[..., None], 0.0
    )
    moving_along = jnp.einsum(
        "owz,toz->owt", summary_gradient, value_matrix, precision=highest_value
    )
    agreed = jnp.sum(summary_gradient * summary, axis=-1)
    slope_values = weight_spread * (moving_along - agreed[..., None])
    value_gradient = jnp.einsum(
        "ofq,ofn->qon", weight_spread, summary_gradient, precision=highest_value
    )
    query_landmark_remote = (
        jnp.einsum("naw,wno->nao", slope_values, key_matrix, precision=highest_value) * scale_factor
    )
    key_gradient = (
        jnp.einsum("ofq,ofn->qon", slope_values, query_landmarks, precision=highest_value)
        * scale_factor
    )
    query_landmark_remote = lax.psum(query_landmark_remote.astype(jnp.bfloat16), "mp").astype(
        jnp.float32
    )
    query_grad = query_grad + jnp.einsum(
        "ge,xgl->exl",
        pooled_local,
        query_landmark_gradient + query_landmark_remote,
        precision=highest_value,
    )
    key_gradient = key_gradient + jnp.einsum(
        "ge,xgl->exl",
        pooled_local,
        key_landmark_gradient + key_landmark_nearby,
        precision=highest_value,
    )
    return (query_grad, key_gradient, value_gradient, tap_grad)


def head_table(columns, heads, size_h):
    begin = lax.axis_index("mp") * columns
    owner = (begin + jnp.arange(columns, dtype=jnp.int32)) // size_h
    return (owner[None, :] == jnp.arange(heads, dtype=jnp.int32)[:, None]).astype(jnp.float32)


def convolve(value_cols, taps, table, valid):
    tap_cols = jnp.dot(taps.T, table, precision=highest_value)
    masked = value_cols * valid[:, None]
    reach = taps.shape[1] // 2
    padded = jnp.pad(masked, ((reach, reach), (0, 0)))
    length_rows = masked.shape[0]
    convolved = jnp.zeros_like(masked)
    for offset in range(taps.shape[1]):
        convolved = convolved + tap_cols[offset] * padded[offset : offset + length_rows]
    return convolved


def contract(left, right, left_dim, right_dim):
    return lax.dot_general(
        left, right, (((left_dim,), (right_dim,)), ((), ())), preferred_element_type=jnp.float32
    )


def normalize(resid, gain, shift):
    centre = resid - jnp.mean(resid, axis=-1, keepdims=True)
    spread = lax.rsqrt(jnp.mean(centre * centre, axis=-1, keepdims=True) + 1e-05)
    normed = centre * spread
    return (normed * gain + shift, normed, spread)


def normalize_back(upstream, normed, spread, gain):
    scaled = upstream * gain
    result = spread * (
        scaled
        - jnp.mean(scaled, axis=-1, keepdims=True)
        - normed * jnp.mean(scaled * normed, axis=-1, keepdims=True)
    )
    return (result, jnp.sum(upstream * normed, axis=0), jnp.sum(upstream, axis=0))


def own_rows(whole):
    count = whole.shape[0] // lax.axis_size("mp")
    return lax.dynamic_slice_in_dim(whole, lax.axis_index("mp") * count, count, 0)


def whole_rows(share):
    return lax.all_gather(share.astype(jnp.bfloat16), "mp", axis=0, tiled=True).astype(share.dtype)


def row_sums(partial_value):
    return lax.psum_scatter(
        partial_value.astype(jnp.bfloat16), "mp", scatter_dimension=0, tiled=True
    ).astype(jnp.float32)


def add_norm(partial_value, resid, gain, shift):
    summed = row_sums(partial_value)
    output, normed, spread = normalize(own_rows(resid) + summed, gain, shift)
    output = whole_rows(output)
    return (output, normed, spread)


def norm_step_back(upstream, normed, spread, gain):
    result, gain_part, shift_part = normalize_back(upstream, normed, spread, gain)
    whole = whole_rows(result)
    return (result, whole, gain_part, shift_part)


def add_input_grad(result, partial_value):
    total = result + row_sums(partial_value)
    return total


def forward_layer(hidden, weights, pooling_own, valid, valid_own):
    projection, taps, output_weight, gains, shifts, up_weight, down_weight = weights
    count, width = hidden.shape
    heads = taps.shape[0]
    size_h = width // heads
    columns = projection.shape[2]
    entering = hidden.astype(jnp.bfloat16)
    mixed = jnp.einsum(
        "td,dsc->tsc", entering, projection, preferred_element_type=jnp.float32
    ).astype(jnp.bfloat16)
    gathered = lax.all_to_all(mixed, "mp", split_axis=0, concat_axis=2, tiled=True)
    rows = gathered.shape[0]
    split_rows = gathered.astype(jnp.float32).reshape(rows, 3, heads, size_h)
    attended, saved = attend(
        split_rows[:, 0], split_rows[:, 1], split_rows[:, 2], pooling_own, valid_own
    )
    attended_cols = lax.all_to_all(
        for_sending(attended.reshape(rows, width)), "mp", split_axis=1, concat_axis=0, tiled=True
    )
    table = head_table(columns, heads, size_h)
    value_cols = mixed[:, 2].astype(jnp.float32)
    convolved = convolve(value_cols, taps, table, valid)
    joined = ((attended_cols + convolved) * valid[:, None]).astype(jnp.bfloat16)
    partial_value = jnp.dot(joined, output_weight, preferred_element_type=jnp.float32)
    middle, normed_first, spread_first = add_norm(partial_value, hidden, gains[0], shifts[0])
    entering_ffn = middle.astype(jnp.bfloat16)
    upward = jnp.dot(entering_ffn, up_weight, preferred_element_type=jnp.float32)
    active = jax.nn.gelu(upward, approximate=True).astype(jnp.bfloat16)
    partial_value = jnp.dot(active, down_weight, preferred_element_type=jnp.float32)
    output, normed_second, spread_second = add_norm(partial_value, middle, gains[1], shifts[1])
    kept = (
        entering,
        value_cols,
        split_rows,
        saved,
        joined,
        table,
        normed_first,
        spread_first,
        entering_ffn,
        upward,
        active,
        normed_second,
        spread_second,
    )
    return (output, kept)


def backward_layer(upstream, weights, kept, pooling_own, valid, valid_own):
    projection, taps, output_weight, gains, shifts, up_weight, down_weight = weights
    (
        entering,
        value_cols,
        split_rows,
        saved,
        joined,
        table,
        normed_first,
        spread_first,
        entering_ffn,
        upward,
        active,
        normed_second,
        spread_second,
    ) = kept
    count, width = entering.shape
    rows = split_rows.shape[0]
    heads = taps.shape[0]
    size_h = width // heads
    result_second, whole_second, gain_second, shift_second = norm_step_back(
        upstream, normed_second, spread_second, gains[1]
    )
    sent_second = whole_second.astype(jnp.bfloat16)
    down_grad = contract(active, sent_second, 0, 0)
    hidden_grad = contract(sent_second, down_weight, 1, 1)
    unused, gelu_back = jax.vjp(lambda value: jax.nn.gelu(value, approximate=True), upward)
    upward_sent = gelu_back(hidden_grad)[0].astype(jnp.bfloat16)
    up_grad = contract(entering_ffn, upward_sent, 0, 0)
    middle_grad = add_input_grad(result_second, contract(upward_sent, up_weight, 1, 1))
    result_first, whole_first, gain_first, shift_first = norm_step_back(
        middle_grad, normed_first, spread_first, gains[0]
    )
    sent_first = whole_first.astype(jnp.bfloat16)
    out_grad = contract(joined, sent_first, 0, 0)
    joined_grad = contract(sent_first, output_weight, 1, 1)
    masked_grad = joined_grad * valid[:, None]
    unused, conv_back = jax.vjp(
        lambda values, tap_rows: convolve(values, tap_rows, table, valid), value_cols, taps
    )
    conv_value_grad, tap_part = conv_back(masked_grad)
    row_grad = (
        lax.all_to_all(
            masked_grad.astype(jnp.bfloat16), "mp", split_axis=0, concat_axis=1, tiled=True
        )
        .astype(masked_grad.dtype)
        .reshape(rows, heads, size_h)
    )
    query_grad, key_gradient, value_gradient, tap_grad = attend_back(
        row_grad,
        split_rows[:, 0],
        split_rows[:, 1],
        split_rows[:, 2],
        pooling_own,
        valid_own,
        saved,
        tap_part,
    )
    stacked_rows = jnp.stack([query_grad, key_gradient, value_gradient], axis=1).reshape(
        rows, 3, width
    )
    column_grad = lax.all_to_all(
        for_sending(stacked_rows), "mp", split_axis=2, concat_axis=0, tiled=True
    ).astype(stacked_rows.dtype)
    column_grad = jnp.concatenate(
        [column_grad[:, :2], (column_grad[:, 2] + conv_value_grad)[:, None]], axis=1
    )
    mixed_sent = column_grad.astype(jnp.bfloat16)
    proj_grad = jnp.einsum("td,tsc->dsc", entering, mixed_sent, preferred_element_type=jnp.float32)
    below = add_input_grad(
        result_first,
        jnp.einsum("tsc,dsc->td", mixed_sent, projection, preferred_element_type=jnp.float32),
    )
    gain_grad = jnp.stack([gain_first, gain_second])
    shift_grad = jnp.stack([shift_first, shift_second])
    gain_grad, shift_grad = lax.psum((gain_grad, shift_grad), "mp")
    return (below, (proj_grad, tap_grad, out_grad, gain_grad, shift_grad, up_grad, down_grad))


def sum_layer(parts):
    return (
        lax.psum(parts[0].astype(jnp.bfloat16), "dp").astype(jnp.float32),
        lax.psum(parts[1].astype(jnp.bfloat16), "dp").astype(jnp.float32),
        lax.psum(parts[2].astype(jnp.bfloat16), "dp").astype(jnp.float32),
        lax.psum(parts[3].astype(jnp.bfloat16), "dp").astype(jnp.float32),
        lax.psum(parts[4].astype(jnp.bfloat16), "dp").astype(jnp.float32),
        lax.psum(parts[5].astype(jnp.bfloat16), "dp").astype(jnp.float32),
        lax.psum(parts[6].astype(jnp.bfloat16), "dp").astype(jnp.float32),
    )


def body(
    tokens,
    lengths,
    cotangent,
    projection,
    conv_taps,
    output_weight,
    norm_gains,
    norm_shifts,
    up_weight,
    down_weight,
):
    count = tokens.shape[0]
    pooling, valid = slot_masks(lengths[0], count, M)
    rows = count // lax.axis_size("mp")
    begin = lax.axis_index("mp") * rows
    pooling_own = lax.dynamic_slice_in_dim(pooling, begin, rows, 1)
    valid_own = lax.dynamic_slice_in_dim(valid, begin, rows, 0)
    weights = (
        projection,
        conv_taps,
        output_weight,
        norm_gains,
        norm_shifts,
        up_weight,
        down_weight,
    )
    hidden = tokens.astype(jnp.float32)
    keeping = []
    for layer_index in range(LAYERS):
        hidden, kept = forward_layer(
            hidden, tuple((item[layer_index] for item in weights)), pooling_own, valid, valid_own
        )
        keeping.append(kept)
    activations = (hidden * valid[:, None]).astype(jnp.bfloat16)
    upstream = cotangent.astype(jnp.float32) * valid[:, None]
    upstream = own_rows(upstream)
    collected = [None] * LAYERS
    for layer_index in reversed(range(LAYERS)):
        upstream, parts = backward_layer(
            upstream,
            tuple((item[layer_index] for item in weights)),
            keeping[layer_index],
            pooling_own,
            valid,
            valid_own,
        )
        collected[layer_index] = sum_layer(parts)
    stacked = tuple(
        (
            jnp.stack([collected[layer_index][member] for layer_index in range(LAYERS)])
            for member in range(7)
        )
    )
    upstream = whole_rows(upstream)
    return (
        activations,
        upstream,
        stacked[0],
        stacked[1],
        stacked[2],
        stacked[3],
        stacked[4],
        stacked[5],
        stacked[6],
    )


class Weights(NamedTuple):
    projection: Any
    output: Any
    up: Any
    down: Any


class Kept(NamedTuple):
    ql: Any
    kl: Any
    second: Any
    inverse: Any
    first: Any
    third: Any
    summary: Any
    carried: Any


class Stored(NamedTuple):
    attention: Any
    qkv: Any
    normed: Any
    spread: Any
    slope: Any
    x_t: Any
    mixed_t: Any
    y_t: Any
    active_t: Any


class Work(NamedTuple):
    x: Any
    x_low: Any
    y: Any
    y_low: Any
    mixed: Any
    active: Any
    e_second: Any
    dmixed: Any
    dqkv: Any
    taps: Any
    turned: Any


class Shared(NamedTuple):
    active_t: Any
    slope: Any
    y_t: Any
    e: Any


class Wire(NamedTuple):
    send: Any
    receive: Any
    small: Any


class Sems(NamedTuple):
    load: Any
    ring_send: Any
    ring_receive: Any
    small_send: Any
    small_receive: Any
    credit: Any
    ready: Any
    factor_send: Any
    factor_receive: Any
    share_send: Any
    share_receive: Any
    gather_send: Any
    gather_receive: Any
    send: Any
    receive: Any


class Slots(NamedTuple):
    core: Any
    x: Any
    near: Any
    mid: Any


class Grads(NamedTuple):
    down: Any
    up: Any
    other: Any


DOWN, UP, OUTPUT, PROJECTION = range(4)


MESH = pl.DeviceIdType.MESH
F32 = jnp.float32
BF16 = jnp.bfloat16


def nn(a, b):
    return lax.dot_general(a, b, (((1,), (0,)), ((), ())), preferred_element_type=F32)


def nt(a, b):
    return lax.dot_general(a, b, (((1,), (1,)), ((), ())), preferred_element_type=F32)


def parts_of(x):
    high = x.astype(BF16)
    return high, (x - high.astype(F32)).astype(BF16)


def nn3(a, b):
    return nn(jnp.concatenate([a[0], a[1]], 1), jnp.concatenate([b[0], b[0]], 0)) + nn(a[0], b[1])


def nt3(a, b):
    return nt(jnp.concatenate([a[0], a[1]], 1), jnp.concatenate([b[0], b[0]], 1)) + nt(a[0], b[1])


def iota(shape, axis):
    return lax.broadcasted_iota(jnp.int32, shape, axis)


class Frame:
    def __init__(self, length, rows, size_h):
        self.length = length
        self.rows = rows
        self.lane0 = iota((1, 2 * size_h), 1) < size_h
        self.keep = [self.lane0.astype(F32).astype(BF16), (~self.lane0).astype(F32).astype(BF16)]
        self.diag = (iota((2 * M, 2 * M), 0) < M) == (iota((2 * M, 2 * M), 1) < M)
        self.ones = self.diag.astype(F32).astype(BF16)
        self.ones2 = jnp.concatenate([self.ones, self.ones], 0)
        j, t = iota((M, rows), 0), iota((M, rows), 1)
        member = (t * M >= j * length) & (t * M < (j + 1) * length)
        member = member.astype(F32)
        self.member = member.astype(BF16)
        self.inv = 1.0 / jnp.sum(member, axis=1, keepdims=True)
        t, j = iota((rows, M), 0), iota((rows, M), 1)
        self.member_t = ((t * M >= j * length) & (t * M < (j + 1) * length)).astype(F32).astype(BF16)
        self.valid = (iota((rows, 1), 0) < length).astype(F32)
        self.valid_lane = iota((1, rows), 1) < length
        self.band = jnp.abs(iota((rows, rows), 0) - iota((rows, rows), 1)) <= KREACH

    def stack(self, x):
        return jnp.where(self.diag, jnp.concatenate([x, x], 0), 0.0)

    def block(self, x):
        return jnp.where(self.diag, x, 0.0)

    def pack(self, x):
        return x[:M] + x[M:]

    def spread(self, x):
        return jnp.concatenate([x * self.keep[0], x * self.keep[1]], 0)

    def times(self, a, b):
        high, low = b
        left = jnp.concatenate([a[0], a[1]], 1)
        return nn(left, jnp.concatenate([high, high], 0)) + nn(a[0], low)

    def spread_parts(self, x):
        return tuple(self.spread(half) for half in parts_of(x))

    def half_sums(self, x):
        high, low = parts_of(x)
        return nn(jnp.concatenate([high, low], 1), self.ones2)

    def toeplitz(self, row):
        spread = jnp.broadcast_to(row, (self.rows, self.rows))
        turned = pltpu.roll(spread, self.rows - KREACH, 1, stride=1, stride_axis=0)
        return jnp.where(self.band, turned, 0.0).astype(BF16)

    def conv(self, rows_pair, value):
        both = jnp.concatenate([self.toeplitz(rows_pair[0]), self.toeplitz(rows_pair[1])], 1)
        stacked = jnp.concatenate([value * self.keep[0], value * self.keep[1]], 0)
        return nn(both, stacked)

    def diagonals(self, product):
        banded = jnp.where(self.band, product, 0.0)
        total = banded[:8]
        for group in range(1, self.rows // 8):
            part = banded[8 * group : 8 * group + 8]
            total = total + pltpu.roll(part, self.rows - 8 * group, 1)
        total = pltpu.roll(total, KREACH, 1)
        result = total[:1]
        for row in range(1, 8):
            result = result + pltpu.roll(total[row : row + 1], self.rows - row, 1)
        return result


KREACH = 16


def softmax_masked(scores, live):
    scores = jnp.where(live, scores, -1e30)
    top = jnp.max(scores, axis=-1, keepdims=True)
    powers = jnp.where(live, jnp.exp(scores - top), 0.0)
    return powers / jnp.sum(powers, axis=-1, keepdims=True)


def attention(frame, qkv, taps, head0, size_h, keep, out_ref):
    scale = size_h ** (-0.5)
    pairs = qkv.shape[2] // (2 * size_h)
    ql = nn(frame.member, qkv[0]) * frame.inv
    kl = nn(frame.member, qkv[1]) * frame.inv
    keep.ql[...] = ql
    keep.kl[...] = kl
    cols = [slice(p * 2 * size_h, (p + 1) * 2 * size_h) for p in range(pairs)]
    qs = [parts_of(frame.stack(ql[:, c])) for c in cols]
    ks = [parts_of(frame.stack(kl[:, c])) for c in cols]
    second = [softmax_masked(nt3(qs[p], ks[p]) * scale, frame.diag) for p in range(pairs)]
    inverse = []
    halves = iota((2 * M, 1), 0) < M
    for p in range(pairs):
        keep.second[p] = second[p]
        squares = jnp.sum(second[p] * second[p], axis=1, keepdims=True)
        first_total = jnp.sum(jnp.where(halves, squares, 0.0), axis=0, keepdims=True)
        other_total = jnp.sum(jnp.where(halves, 0.0, squares), axis=0, keepdims=True)
        inverse.append(second[p].T * (1.0 / jnp.where(halves, first_total, other_total)))
    second_parts = [parts_of(frame.pack(s)) for s in second]
    summaries, firsts, convolved = [None] * pairs, [None] * pairs, [None] * pairs

    def far(p):
        key, value = qkv[1, :, cols[p]], qkv[2, :, cols[p]]
        scores = nt(jnp.concatenate(qs[p], 1), jnp.concatenate([key, key], 1)) * scale
        third = softmax_masked(scores, frame.valid_lane).astype(BF16)
        keep.third[p] = third
        summaries[p] = frame.block(nn(third, value))
        keep.summary[p] = summaries[p]

    def near(p):
        query = qkv[0, :, cols[p]]
        scores = nt(jnp.concatenate([query, query], 1), jnp.concatenate(ks[p], 1)) * scale
        top0 = jnp.max(jnp.where(frame.lane0, scores, -1e30), axis=-1, keepdims=True)
        top1 = jnp.max(jnp.where(frame.lane0, -1e30, scores), axis=-1, keepdims=True)
        powers = jnp.exp(scores - jnp.where(frame.lane0, top0, top1))
        firsts[p] = (powers / frame.half_sums(powers)).astype(BF16)
        keep.first[:, cols[p]] = firsts[p]

    def local(p):
        inside = (qkv[2, :, cols[p]].astype(F32) * frame.valid).astype(BF16)
        rows_pair = [taps[pl.ds(head0 + 2 * p + i, 1), :] for i in range(2)]
        convolved[p] = frame.conv(rows_pair, inside)

    beside = [(task, p) for p in range(pairs) for task in (far, near, local)]
    inverse = [frame.pack(z) for z in inverse]
    product = [frame.times(second_parts[p], frame.spread_parts(inverse[p])) for p in range(pairs)]
    for sweep in range(NEWTON):
        for p in range(pairs):
            keep.inverse[sweep, p] = inverse[p]
        zp = [parts_of(z) for z in inverse]
        pp = [parts_of(x) for x in product]
        right = [tuple(frame.spread(half) for half in pp[p]) for p in range(pairs)]
        square = [frame.times(pp[p], right[p]) for p in range(pairs)]
        forward = [frame.times(zp[p], right[p]) for p in range(pairs)]
        for task, p in beside[sweep * len(beside) // NEWTON : (sweep + 1) * len(beside) // NEWTON]:
            task(p)
        inner = [frame.spread_parts(7.0 * product[p] - square[p]) for p in range(pairs)]
        if sweep + 1 < NEWTON:
            product = [0.25 * (13.0 * product[p] - 15.0 * square[p] + frame.times(parts_of(square[p]), inner[p])) for p in range(pairs)]
        inverse = [0.25 * (13.0 * inverse[p] - 15.0 * forward[p] + frame.times(parts_of(forward[p]), inner[p])) for p in range(pairs)]
    for p in range(pairs):
        keep.inverse[NEWTON, p] = inverse[p]
        carried = frame.stack(frame.times(parts_of(inverse[p]), parts_of(summaries[p])))
        keep.carried[p] = carried
        mixed = nn(firsts[p], carried.astype(BF16))
        out_ref[:, cols[p]] = ((mixed + convolved[p]) * frame.valid).astype(BF16)


def attention_back(frame, grad, qkv, taps_turned, head0, size_h, keep, out_ref, taps_out):
    scale = size_h ** (-0.5)
    pairs = qkv.shape[2] // (2 * size_h)
    cols = [slice(p * 2 * size_h, (p + 1) * 2 * size_h) for p in range(pairs)]
    each = range(pairs)
    ql, kl = keep.ql[...], keep.kl[...]
    qs = [parts_of(frame.stack(ql[:, c])) for c in cols]
    ks = [parts_of(frame.stack(kl[:, c])) for c in cols]
    summary = [keep.summary[p] for p in each]
    second = [keep.second[p] for p in each]
    dq, dk_landmark, dcarried, grad_low = [], [], [], []
    for p in each:
        c = cols[p]
        g = grad[:, c].astype(BF16)
        grad_low.append(g)
        first = keep.first[:, c].astype(F32)
        dfirst = nt(g, keep.carried[p].astype(BF16))
        slope = first * dfirst
        slope = (slope - first * frame.half_sums(slope)) * scale
        dq.append(nn(slope.astype(BF16), ks[p][0]))
        dk_landmark.append(frame.block(nn(slope.T.astype(BF16), qkv[0, :, c])))
        dcarried.append(frame.block(nn(first.T.astype(BF16), g)))
    yield
    dcp = [parts_of(x) for x in dcarried]
    up = [nt3(dcp[p], parts_of(summary[p])) for p in each]
    dsummary = [nn3(parts_of(frame.stack(keep.inverse[NEWTON, p]).T), dcp[p]) for p in each]
    second_parts = [parts_of(s) for s in second]
    second_turned = [parts_of(s.T) for s in second]
    dsecond = [jnp.zeros_like(s) for s in second]
    for sweep in reversed(range(NEWTON)):
        inverse = [frame.stack(keep.inverse[sweep, p]) for p in each]
        zp = [parts_of(z) for z in inverse]
        product = [nn3(second_parts[p], zp[p]) for p in each]
        pp = [parts_of(x) for x in product]
        inner = [parts_of(7.0 * product[p] - nn3(pp[p], pp[p])) for p in each]
        forward_turned = [parts_of(nn3(zp[p], pp[p]).T) for p in each]
        product_turned = [parts_of(x.T) for x in product]
        inverse_turned = [parts_of(z.T) for z in inverse]
        upp = [parts_of(x) for x in up]
        dforward = [parts_of(0.25 * (nt3(upp[p], inner[p]) - 15.0 * up[p])) for p in each]
        dinner_full = [0.25 * nn3(forward_turned[p], upp[p]) for p in each]
        dinner = [parts_of(x) for x in dinner_full]
        dproduct = [
            parts_of(
                7.0 * dinner_full[p]
                - nt3(dinner[p], pp[p])
                - nn3(product_turned[p], dinner[p])
                + nn3(inverse_turned[p], dforward[p])
            )
            for p in each
        ]
        up = [
            3.25 * up[p] + nt3(dforward[p], pp[p]) + nn3(second_turned[p], dproduct[p])
            for p in each
        ]
        dsecond = [dsecond[p] + nt3(dproduct[p], zp[p]) for p in each]
        yield
    halves = iota((2 * M, 1), 0) < M
    for p in each:
        c = cols[p]
        query, key, value = qkv[0, :, c], qkv[1, :, c], qkv[2, :, c]
        squares = jnp.sum(second[p] * second[p], axis=1, keepdims=True)
        total0 = jnp.sum(jnp.where(halves, squares, 0.0), axis=0, keepdims=True)
        total1 = jnp.sum(jnp.where(halves, 0.0, squares), axis=0, keepdims=True)
        inverse_total = 1.0 / jnp.where(halves, total0, total1)
        start_agree = jnp.sum(up[p] * frame.stack(keep.inverse[0, p]), axis=1, keepdims=True)
        agree0 = jnp.sum(jnp.where(halves, start_agree, 0.0), axis=0, keepdims=True)
        agree1 = jnp.sum(jnp.where(halves, 0.0, start_agree), axis=0, keepdims=True)
        agree = jnp.where(halves, agree0, agree1)
        dsec = dsecond[p] + (up[p].T - 2.0 * agree * second[p]) * inverse_total
        slope = second[p] * dsec
        slope = (slope - second[p] * jnp.sum(slope, axis=-1, keepdims=True)) * scale
        dql = nn(slope.astype(BF16), ks[p][0])
        dkl = nn(slope.T.astype(BF16), qs[p][0]) + dk_landmark[p]
        third = keep.third[p].astype(F32)
        ds = dsummary[p].astype(BF16)
        dthird = nt(ds, value)
        agreed = jnp.sum(dsummary[p] * summary[p], axis=-1, keepdims=True)
        slope = third * (dthird - agreed) * scale
        dv = nn(third.T.astype(BF16), ds)
        dql = dql + frame.block(nn(slope.astype(BF16), key))
        dk = nn(slope.T.astype(BF16), qs[p][0])
        dql = ((dql[:M] + dql[M:]) * frame.inv).astype(BF16)
        dkl = ((dkl[:M] + dkl[M:]) * frame.inv).astype(BF16)
        out_ref[0, :, c] = (dq[p] + nn(frame.member_t, dql)).astype(BF16)
        out_ref[1, :, c] = (dk + nn(frame.member_t, dkl)).astype(BF16)
        inside = (value.astype(F32) * frame.valid).astype(BF16)
        rows_pair = [taps_turned[pl.ds(head0 + 2 * p + i, 1), :] for i in range(2)]
        dv = dv + frame.valid * frame.conv(rows_pair, grad_low[p])
        out_ref[2, :, c] = dv.astype(BF16)
        for i in range(2):
            product = nt(grad_low[p] * frame.keep[i], inside)
            taps_out(2 * p + i, frame.diagonals(product))
        yield


def norm_rows(r, gain, shift):
    centre = r - jnp.mean(r, axis=-1, keepdims=True)
    spread = lax.rsqrt(jnp.mean(centre * centre, axis=-1, keepdims=True) + 1e-05)
    normed = centre * spread
    return normed * gain + shift, normed, spread


def norm_rows_back(dy, normed, spread, gain):
    scaled = dy * gain
    result = spread * (
        scaled
        - jnp.mean(scaled, axis=-1, keepdims=True)
        - normed * jnp.mean(scaled * normed, axis=-1, keepdims=True)
    )
    return (
        result,
        jnp.sum(dy * normed, axis=0, keepdims=True),
        jnp.sum(dy, axis=0, keepdims=True),
    )


GELU_A = 0.7978845608028654
GELU_B = 0.044715


def gelu_both(u):
    square = u * u
    t = jnp.tanh(GELU_A * (u + GELU_B * u * square))
    half = 0.5 * (1.0 + t)
    slope = half + 0.5 * u * (1.0 - t * t) * (GELU_A + (3.0 * GELU_A * GELU_B) * square)
    return u * half, slope


SEND_SEM = (
    (0, 1, 2, 2, 0, 1, 2, 3),
    (0, 1, 2, 2, 0, 3, 2, 4, 1),
    (0, 1, 2, 2, 0, 1, 2, 3),
    (0, 1, 2, 2, 0, 1, 2, 3, 4, 4),
    (0, 1, 2, 2, 0, 1, 2, 3, 4, 4),
)
RECEIVE_SEM = (
    (0, 1, 2, 3, 2, 6, 5, 4),
    (0, 1, 2, 3, 6, 6, 5, 4, 2),
    (0, 1, 2, 3, 2, 7, 5, 4),
    (0, 1, 2, 3, 2, 6, 5, 4, 6, 6),
    (0, 1, 2, 3, 2, 7, 5, 4, 7, 7),
)
SENDS, RECEIVES = 5, 8
ROUTE = (0, 1, 2, 0, 2)


class Reduction:
    def __init__(self, sems):
        dp, self.mp = lax.axis_index("dp"), lax.axis_index("mp")
        z = dp // 4
        self.x = (dp // 2) % 2
        self.core = dp % 2
        self.upper = z // 2
        self.inner = (z == 1) | (z == 2)
        self.outer = (z == 0) | (z == 3)
        self.to_core = dp + 1 - 2 * self.core
        self.to_x = dp + 2 - 4 * self.x
        self.to_near = dp + 4 - 8 * (z % 2)
        self.to_mid = (3 - z) * 4 + dp % 4
        self.sems = sems
        self.pieces = []

    def greet(self, barrier):
        for other in (self.to_core, self.to_x, self.to_near, self.to_mid):
            pl.semaphore_signal(barrier, inc=1, device_id=(other, self.mp), device_id_type=MESH)

    def add(self, rows, kind, view, slots, credit, gives, takes, other_kind):
        self.pieces.append((rows // 4, kind, view, slots, credit, gives, takes, other_kind))

    def copy(self, index, slot, source, target, to):
        kind, place = self.pieces[index][1], self.pieces[index][4]
        return pltpu.make_async_remote_copy(
            src_ref=source,
            dst_ref=target,
            send_sem=self.sems.ring_send.at[place * SENDS + SEND_SEM[kind][slot]],
            recv_sem=self.sems.ring_receive.at[place * RECEIVES + RECEIVE_SEM[kind][slot]],
            device_id=(to, self.mp),
            device_id_type=MESH,
        )

    def event(self, index, step):
        quarter, kind, view, slots, credit, gives, takes, other_kind = self.pieces[index]
        by_outer, kind, other_kind = kind > 2, ROUTE[kind], ROUTE[other_kind]
        x, core, upper = self.x, self.core, self.upper
        side = upper if kind == 1 else x

        def region(half, which, count=1):
            return view(half, which, count * quarter)

        def arrived(slot, ref):
            self.copy(index, slot, ref, ref, self.to_core).wait_recv()

        def sent(slot, ref):
            self.copy(index, slot, ref, ref, self.to_core).wait_send()

        def send(slot, source, destination, to, need=None):
            if takes and need is not None:
                pl.semaphore_wait(self.sems.credit.at[credit * 4 + need], 1)
            self.copy(index, slot, source, destination, to).start()

        def free(which, to):
            if gives:
                pl.semaphore_signal(
                    self.sems.credit.at[credit * 4 + which],
                    inc=1,
                    device_id=(to, self.mp),
                    device_id_type=MESH,
                )

        def ready(which, slot, ref, to):
            sent(slot, ref)
            pl.semaphore_signal(
                self.sems.ready.at[credit * 4 + which],
                inc=1,
                device_id=(to, self.mp),
                device_id_type=MESH,
            )

        def await_ready(which):
            pl.semaphore_wait(self.sems.ready.at[credit * 4 + which], 1)

        def slot_part(ref, which):
            return ref.at[pl.ds(pl.multiple_of(which * quarter, 16), quarter)]

        def sum_into(ref, others):
            block = 48 if quarter % 48 == 0 else 16

            def step_rows(i, unused):
                span = pl.ds(pl.multiple_of(i * block, 16), block)
                total = ref[span, :].astype(F32)
                for other in others:
                    total = total + other[span, :].astype(F32)
                ref[span, :] = total.astype(BF16)
                return unused

            lax.fori_loop(0, quarter // block, step_rows, 0)

        mine, other = region(core, side), region(core, 1 - side)
        if step == 0:
            if kind == 2:
                send(0, region(1 - core, x), slot_part(slots.core, 0), self.to_core, need=0)
            else:
                send(0, region(1 - core, 0, 2), slots.core, self.to_core, need=0)
        elif step == 7 + by_outer:
            for slot, which in ((6, side), (7, 1 - side)):
                arrived(slot, region(1 - core, which))
            sent(6, mine)
            sent(7, other)
            if by_outer:

                @pl.when(self.outer)
                def _():
                    sent(5, mine)
                    sent(9, mine)

            elif kind != 1:
                sent(5, mine)

            if kind != 1:

                @pl.when(self.inner)
                def _():
                    sent(4, mine)

            else:

                @pl.when(self.inner)
                def _():
                    for slot in (4, 5, 8):
                        sent(slot, mine)

        elif kind == 2 and step < 4:
            if step > 1:

                @pl.when(self.outer if step == 2 else self.inner)
                def _():
                    arrived(0, slot_part(slots.core, 0))
                    if step == 2:
                        sum_into(mine, [slot_part(slots.core, 0)])
                        send(2, mine, slot_part(slots.near, 0), self.to_near, need=2)
                    else:
                        arrived(2, slot_part(slots.near, 0))
                        sum_into(mine, [slot_part(slots.core, 0), slot_part(slots.near, 0)])
                        send(3, mine, slots.mid, self.to_mid, need=3)
                    ready(0, 0, region(1 - core, x), self.to_core)

            if step == 3:

                @pl.when(self.outer)
                def _():
                    ready(2, 2, mine, self.to_near)

        elif kind != 1:
            if step == 1:
                arrived(0, slots.core)
                sum_into(other, [slot_part(slots.core, 1 - x)])
                if other_kind == 0:
                    send(1, other, slots.x, self.to_x, need=1)
                else:
                    if takes:

                        @pl.when(self.inner)
                        def _():
                            pl.semaphore_wait(self.sems.credit.at[credit * 4 + 1], 1)

                    send(1, other, slots.x, self.to_x)
                ready(0, 0, region(1 - core, 0, 2), self.to_core)
            elif step == 2:

                @pl.when(self.outer)
                def _():
                    arrived(1, slots.x)
                    sum_into(mine, [slot_part(slots.core, x), slots.x])
                    free(0, self.to_core)
                    if other_kind == 0:
                        free(1, self.to_x)
                    send(2, mine, slot_part(slots.near, 0), self.to_near, need=2)
                    ready(1, 1, other, self.to_x)

            elif step == 3:

                @pl.when(self.inner)
                def _():
                    arrived(1, slots.x)
                    arrived(2, slot_part(slots.near, 0))
                    sum_into(mine, [slot_part(slots.core, x), slots.x, slot_part(slots.near, 0)])
                    free(0, self.to_core)
                    if other_kind != 2:
                        free(1, self.to_x)
                    free(2, self.to_near)
                    send(3, mine, slots.mid, self.to_mid, need=3)
                    if by_outer:
                        ready(3, 1, other, self.to_near)
                    else:
                        ready(1, 1, other, self.to_x)

                @pl.when(self.outer)
                def _():
                    ready(2, 2, mine, self.to_near)

            elif step == 4:

                @pl.when(self.inner)
                def _():
                    arrived(3, slots.mid)
                    sent(3, mine)
                    sum_into(mine, [slots.mid])
                    free(3, self.to_mid)
                    await_ready(2)
                    send(4, mine, mine, self.to_near)
                    if not by_outer:
                        if kind == 0:
                            await_ready(1)
                        send(5, mine, mine, self.to_x)
                    await_ready(0)
                    send(6, mine, mine, self.to_core)

            elif step == 5:

                @pl.when(self.outer)
                def _():
                    arrived(4, mine)
                    if kind == 0:
                        await_ready(1)
                    send(5, mine, mine, self.to_x)
                    await_ready(0)
                    send(6, mine, mine, self.to_core)

            elif step == 6 and not by_outer:
                arrived(5, other)
                send(7, other, other, self.to_core)
            elif step == 6:

                @pl.when(self.outer)
                def _():
                    arrived(5, other)
                    if kind == 0:
                        await_ready(3)
                    send(9, other, other, self.to_near)
                    send(7, other, other, self.to_core)

            elif step == 7:

                @pl.when(self.inner)
                def _():
                    arrived(9, other)
                    send(7, other, other, self.to_core)

        else:
            if step == 1:

                @pl.when(self.outer)
                def _():
                    arrived(0, slots.core)
                    sum_into(region(core, 0), [slot_part(slots.core, 0)])
                    sum_into(region(core, 1), [slot_part(slots.core, 1)])
                    free(0, self.to_core)
                    send(2, region(core, 0, 2), slots.near, self.to_near, need=2)
                    ready(0, 0, region(1 - core, 0, 2), self.to_core)

            elif step == 2:

                @pl.when(self.outer)
                def _():
                    ready(2, 2, region(core, 0, 2), self.to_near)

                @pl.when(self.inner)
                def _():
                    arrived(0, slots.core)
                    arrived(2, slots.near)
                    sum_into(other, [slot_part(slots.core, 1 - side), slot_part(slots.near, 1 - side)])
                    send(3, other, slots.mid, self.to_mid, need=3)
                    ready(0, 0, region(1 - core, 0, 2), self.to_core)

            elif step == 3:

                @pl.when(self.inner)
                def _():
                    arrived(3, slots.mid)
                    sum_into(mine, [slot_part(slots.core, side), slot_part(slots.near, side), slots.mid])
                    free(0, self.to_core)
                    free(2, self.to_near)
                    free(3, self.to_mid)
                    send(1, mine, slots.x, self.to_x, need=1)
                    ready(3, 3, other, self.to_mid)

            elif step == 4:

                @pl.when(self.inner)
                def _():
                    arrived(1, slots.x)
                    sent(1, mine)
                    sum_into(mine, [slots.x])
                    if other_kind != 2:
                        free(1, self.to_x)
                    await_ready(3)
                    send(4, mine, mine, self.to_mid)
                    await_ready(2)
                    send(8, mine, mine, self.to_near)
                    await_ready(0)
                    send(6, mine, mine, self.to_core)

            elif step == 5:

                @pl.when(self.inner)
                def _():
                    arrived(4, other)
                    send(5, other, other, self.to_near)
                    send(7, other, other, self.to_core)

                @pl.when(self.outer)
                def _():
                    arrived(8, mine)
                    await_ready(0)
                    send(6, mine, mine, self.to_core)

            elif step == 6:

                @pl.when(self.outer)
                def _():
                    arrived(5, other)
                    send(7, other, other, self.to_core)


class SmallSum:
    def __init__(self, ring, total, slots, sems, first_tap):
        self.ring, self.total, self.slots, self.sems, self.first_tap = ring, total, slots, sems, first_tap

    def copy(self, slot, target, to, mp):
        return pltpu.make_async_remote_copy(
            src_ref=self.total,
            dst_ref=target,
            send_sem=self.sems.small_send.at[slot],
            recv_sem=self.sems.small_receive.at[slot],
            device_id=(to, mp),
            device_id_type=MESH,
        )

    def event(self, step):
        ring, total, slots = self.ring, self.total, self.slots
        dp = ring.to_core + 2 * ring.core - 1

        def start(slot, to, mp=None):
            self.copy(slot, slots.at[slot], to, ring.mp if mp is None else mp).start()

        def take(slot):
            self.copy(slot, slots.at[slot], dp, ring.mp).wait_recv()

        def sent(slot):
            self.copy(slot, slots.at[slot], dp, ring.mp).wait_send()

        if step == 0:
            start(0, dp, 1 - ring.mp)
        elif step == 1:
            take(0)
            sent(0)
            total[self.first_tap :, :] += slots[0, self.first_tap :, :]
            start(1, ring.to_core)
        elif step == 2:
            take(1)
            sent(1)
            total[...] += slots[1]
            start(2, ring.to_x)
        elif step == 3:
            take(2)
            sent(2)
            total[...] += slots[2]

            @pl.when(ring.outer)
            def _():
                start(3, ring.to_near)

        elif step == 4:

            @pl.when(ring.inner)
            def _():
                take(3)
                total[...] += slots[3]
                start(4, ring.to_mid)

        elif step == 5:

            @pl.when(ring.inner)
            def _():
                take(4)
                sent(4)
                total[...] += slots[4]
                start(5, ring.to_near)

        elif step == 6:

            @pl.when(ring.outer)
            def _():
                take(5)
                sent(3)
                total[...] = slots[5]

            @pl.when(ring.inner)
            def _():
                sent(5)


def whole_step(
    length_ref,
    tokens_ref,
    cotangent_ref,
    raw_taps_ref,
    gains_ref,
    shifts_ref,
    projection_hbm,
    output_hbm,
    up_hbm,
    down_hbm,
    activations_ref,
    token_grad_ref,
    small_ref,
    down_grad_ref,
    up_grad_ref,
    other_grad_ref,
    weights,
    kept,
    work,
    shared,
    wire,
    slots,
    sems,
):
    rows, width = tokens_ref.shape
    columns = projection_hbm.shape[3]
    hidden = up_hbm.shape[2]
    heads, _, reach = raw_taps_ref.shape
    grads = Grads(down_grad_ref, up_grad_ref, other_grad_ref)
    size_h = width // heads
    half = rows // 2
    tile = hidden // 2
    dp, mp = lax.axis_index("dp"), lax.axis_index("mp")
    head0 = mp * (columns // size_h)
    partner = (dp, 1 - mp)

    def own_half(layer):
        return weights.output.at[layer, mp]

    loads = []
    order = [
        (projection_hbm, weights.projection),
        (output_hbm, weights.output),
        (up_hbm, weights.up),
        (down_hbm, weights.down),
    ]
    for layer in range(LAYERS):
        for index, (source, place) in enumerate(order):
            load = pltpu.make_async_copy(
                source.at[layer],
                own_half(layer) if index == 1 else place.at[layer],
                sems.load.at[layer * 4 + index],
            )
            load.start()
            loads.append(load)

    barrier = pltpu.get_barrier_semaphore()
    pl.semaphore_signal(barrier, inc=1, device_id=partner, device_id_type=MESH)
    ring = Reduction(sems)
    ring.greet(barrier)

    frame = Frame(length_ref[0], rows, size_h)
    taps_ref, turned_ref = work.taps, work.turned
    taps_ref[...] = jnp.zeros_like(taps_ref)
    mirror = iota((rows, rows), 0) + iota((rows, rows), 1) == reach - 1
    mirror = mirror.astype(F32).astype(BF16)
    for layer in range(LAYERS):
        taps_ref[layer, :heads, :reach] = raw_taps_ref[:, layer, :]
        turned_ref[layer] = nn(taps_ref[layer].astype(BF16), mirror)
    flights = {}

    def send(slot, piece, partial_value):
        span = pl.ds(piece * half, half)
        wire.send[span, :] = partial_value.astype(BF16)
        copy = pltpu.make_async_remote_copy(
            src_ref=wire.send.at[span],
            dst_ref=wire.receive.at[slot % 2, span],
            send_sem=sems.send.at[slot % 2 * 2 + piece],
            recv_sem=sems.receive.at[slot % 2 * 2 + piece],
            device_id=partner,
            device_id_type=MESH,
        )
        copy.start()
        flights[slot, piece] = copy

    def arrived(slot, piece):
        span = pl.ds(piece * half, half)
        flights[slot, piece].wait()
        return wire.send[span, :].astype(F32) + wire.receive[
            slot % 2, span, :
        ].astype(F32)

    def share_copy(layer, hop):
        part = columns // 2
        which, first = (mp, ring.core) if hop == 0 else (1 - mp, ring.core)
        place = weights.output.at[layer, which, pl.ds(pl.multiple_of(first * part, 16), part)]
        return pltpu.make_async_remote_copy(
            src_ref=place,
            dst_ref=place,
            send_sem=sems.share_send.at[layer * 2 + hop],
            recv_sem=sems.share_receive.at[layer * 2 + hop],
            device_id=partner if hop == 0 else (ring.to_core, mp),
            device_id_type=MESH,
        )

    def gather_copy(layer, piece):
        place = work.mixed.at[mp, pl.ds(piece * half, half)]
        return pltpu.make_async_remote_copy(
            src_ref=place,
            dst_ref=place,
            send_sem=sems.gather_send.at[piece],
            recv_sem=sems.gather_receive.at[piece],
            device_id=partner,
            device_id_type=MESH,
        )

    side = hidden // 2
    near_rows = pl.ds(pl.multiple_of(ring.x * side, 128), side)
    far_rows = pl.ds(pl.multiple_of((1 - ring.x) * side, 128), side)
    factors = []

    def factor_copy(index, source, target, to=None):
        return pltpu.make_async_remote_copy(
            src_ref=source,
            dst_ref=target,
            send_sem=sems.factor_send.at[index],
            recv_sem=sems.factor_receive.at[index],
            device_id=(ring.to_x, mp) if to is None else to,
            device_id_type=MESH,
        )

    halves = [slice(0, half), slice(half, rows)]

    def project(layer, c):
        for i in range(3):
            kept.qkv[layer, i, c, :] = nn(
                work.x_low[c, :], weights.projection[layer, i]
            ).astype(BF16)

    def keep_of(layer):
        return Kept(*(ref.at[layer] for ref in kept.attention))

    work.x[...] = tokens_ref[...].astype(F32)
    work.x_low[...] = tokens_ref[...]
    loads[0].wait()
    project(0, halves[0])
    loads[1].wait()
    pl.semaphore_wait(barrier, 5)
    share_copy(0, 0).start()
    project(0, halves[1])
    for layer in range(LAYERS):
        attention(
            frame,
            kept.qkv.at[layer],
            taps_ref.at[layer],
            head0,
            size_h,
            keep_of(layer),
            work.mixed.at[mp],
        )
        slot = layer * 2
        for piece in range(len(halves)):
            gather_copy(layer, piece).start()
        share_copy(layer, 0).wait()
        share_copy(layer, 1).start()
        kept.mixed_t[layer] = work.mixed[mp].T
        kept.x_t[layer] = work.x_low[...].T
        loads[layer * 4 + 2].wait()
        loads[layer * 4 + 3].wait()
        share_copy(layer, 1).wait()
        for piece, c in enumerate(halves):
            gather_copy(layer, piece).wait()
            summed = work.x[c, :] + nn(
                jnp.concatenate([work.mixed[0, c, :], work.mixed[1, c, :]], 1),
                weights.output[layer].reshape(2 * columns, width),
            )
            y, normed, spread = norm_rows(summed, gains_ref[layer, 0:1], shifts_ref[layer, 0:1])
            kept.normed[layer, 0, c, :] = normed.astype(BF16)
            kept.spread[layer, 0, c, :] = spread
            work.y[c, :] = y
            work.y_low[c, :] = y.astype(BF16)
            for j in range(hidden // tile):
                span = slice(j * tile, (j + 1) * tile)
                u = nn(work.y_low[c, :], weights.up[layer, :, span])
                active, slope = gelu_both(u)
                work.active[c, span] = active.astype(BF16)
                kept.slope[layer, c, span] = slope.astype(BF16)
            send(slot + 1, piece, nn(work.active[c, :], weights.down[layer]))
        if layer + 1 < LAYERS:
            loads[layer * 4 + 5].wait()
            share_copy(layer + 1, 0).start()
        kept.active_t[layer] = work.active[...].T
        kept.y_t[layer] = work.y_low[...].T
        if FACTORED[layer]:
            factors.append(factor_copy(0, kept.active_t.at[layer, far_rows], shared.active_t))
            factors.append(factor_copy(1, kept.slope.at[layer, :, far_rows], shared.slope))
            factors.append(factor_copy(2, kept.y_t.at[layer], shared.y_t))
            for copy in factors:
                copy.start()
        if layer + 1 < LAYERS:
            loads[layer * 4 + 4].wait()
        for piece, c in enumerate(halves):
            summed = work.y[c, :] + arrived(slot + 1, piece)
            y, normed, spread = norm_rows(summed, gains_ref[layer, 1:2], shifts_ref[layer, 1:2])
            kept.normed[layer, 1, c, :] = normed.astype(BF16)
            kept.spread[layer, 1, c, :] = spread
            if layer + 1 < LAYERS:
                work.x[c, :] = y
                work.x_low[c, :] = y.astype(BF16)
                project(layer + 1, c)
            else:
                activations_ref[c, :] = (y * frame.valid[c]).astype(BF16)

    def add_pieces(layer):
        listed = pieces_of(width, columns, hidden, layer)
        listed_rows = {DOWN: hidden, UP: 2 * width}
        for k, (name, rows_of, kind) in enumerate(listed):
            before = sum(item[1] for item in listed[:k] if item[0] == name)
            index = sum(1 for item in listed[:k] if item[0] == name)

            quarter = rows_of // 4
            if ROUTE[kind] == 2:
                before, high, wide = before // 2, quarter, listed_rows[name] // 2
            else:
                high, wide = 2 * quarter, quarter
            if name in (DOWN, UP):
                ref = (grads.down if name == DOWN else grads.up).at[layer]
            else:
                ref = grads.other.at[layer, 0 if name == OUTPUT else 1 + index]
                before = 0

            def view(half, which, count, ref=ref, before=before, high=high, wide=wide):
                return ref.at[pl.ds(pl.multiple_of(before + half * high + which * wide, 16), count)]

            ring.add(rows_of, kind, view, slots[k], k, layer > 0, layer + 1 < LAYERS, PIECE_KINDS[1 - layer][k])

    for layer in reversed(range(LAYERS)):
        add_pieces(layer)
    small = SmallSum(ring, small_ref, wire.small, sems, 8)
    dy_ref, dr_ref, e_ref, du_ref = work.x, work.y, work.y_low, work.active

    def norm_back(layer, which):
        gain = gains_ref[layer, which : which + 1]
        gain_sum = shift_sum = 0.0
        for c in halves:
            result, gain_part, shift_part = norm_rows_back(
                dy_ref[c, :],
                kept.normed[layer, which, c, :].astype(F32),
                kept.spread[layer, which, c, :],
                gain,
            )
            dr_ref[c, :] = result
            (e_ref, e_second)[which][c, :] = result.astype(BF16)
            gain_sum, shift_sum = gain_sum + gain_part, shift_sum + shift_part
        row = layer * 2 + which
        small_ref[row : row + 1, :] = gain_sum
        small_ref[row + 4 : row + 5, :] = shift_sum

    du_other, e_second = work.x_low, work.e_second

    def down_grads(layer):
        block = hidden // DOWN_PIECES
        for j in range(DOWN_PIECES):
            if FACTORED[layer]:
                low = slice(j * block // 2, (j + 1) * block // 2)
                span = pl.ds(pl.multiple_of(ring.x * side + low.start, 16), block // 2)
                value = nn(kept.active_t[layer, span, :], e_second[...]) + nn(
                    shared.active_t[low, :], shared.e[...]
                )
            else:
                span = slice(j * block, (j + 1) * block)
                value = nn(kept.active_t[layer, span, :], e_second[...])
            grads.down[layer, span, :] = value.astype(BF16)
            yield

    def up_grads(layer):
        block = 2 * width // UP_PIECES
        for j in range(UP_PIECES):
            if FACTORED[layer]:
                low = slice(j * block // 2, (j + 1) * block // 2)
                span = pl.ds(pl.multiple_of(ring.x * width + low.start, 16), block // 2)
                value = nn(kept.y_t[layer, low, :], du_ref[:, near_rows]) + nn(
                    shared.y_t[low, :], du_other[...]
                )
            else:
                span = slice(j * block, (j + 1) * block)
                at, first = divmod(j * block, width)
                value = nn(
                    kept.y_t[layer, first : first + block, :],
                    du_ref[:, at * side : (at + 1) * side],
                )
            grads.up[layer, span, :] = value.astype(BF16)
            yield

    def backward():
        small_ref[...] = jnp.zeros_like(small_ref)
        for piece, c in enumerate(halves):
            dy_ref[c, :] = cotangent_ref[c, :].astype(F32) * frame.valid[c]
        for layer in reversed(range(LAYERS)):
            slot = 4 + (LAYERS - 1 - layer) * 2
            norm_back(layer, 1)
            if FACTORED[layer]:
                own = pl.ds(pl.multiple_of(mp * half, 16), half)
                factors.append(factor_copy(3, e_second.at[own], shared.e.at[own]))
                factors[3].start()
            yield
            if not FACTORED[layer]:
                yield from down_grads(layer)
            for j in range(hidden // tile):
                span = slice(j * tile, (j + 1) * tile)
                dh = nt(e_second[...], weights.down[layer, span, :])
                du_ref[:, span] = (dh * kept.slope[layer, :, span].astype(F32)).astype(BF16)
            yield
            for piece, c in enumerate(halves):
                send(slot, piece, nt(du_ref[c, :], weights.up[layer]))
                yield
            if FACTORED[layer]:
                for copy in factors:
                    copy.wait()
                passing = factor_copy(4, shared.e.at[own], shared.e.at[own], partner)
                passing.start()
                yield
            else:
                yield from up_grads(layer)
            for piece, c in enumerate(halves):
                dy_ref[c, :] = dr_ref[c, :] + arrived(slot, piece)
            norm_back(layer, 0)
            yield
            for piece, c in enumerate(halves):
                work.dmixed[c, :] = nt(e_ref[c, :], weights.output[layer, mp]) * frame.valid[c]
            yield
            for j in range(2):
                span = slice(j * columns, (j + 1) * columns)
                grads.other[layer, 0, span, :] = nn(
                    kept.mixed_t[layer], e_ref[:, span]
                ).astype(BF16)
            yield
            if FACTORED[layer]:
                passing.wait()
                for j in range(side // tile):
                    span = slice(j * tile, (j + 1) * tile)
                    near = pl.ds(pl.multiple_of(ring.x * side + j * tile, 128), tile)
                    dh = nt(shared.e[...], weights.down[layer, near, :])
                    du_other[:, span] = (dh * shared.slope[:, span].astype(F32)).astype(BF16)
                yield
                yield from down_grads(layer)
                yield from up_grads(layer)

            def taps_out(head, row, layer=layer):
                lanes = slice(head * 128, (head + 1) * 128)
                for side in range(2):
                    at = 8 + 2 * layer + side
                    small_ref[at : at + 1, lanes] = jnp.where(mp == side, row[:, :128], 0.0)

            yield from attention_back(
                frame,
                work.dmixed,
                kept.qkv.at[layer],
                turned_ref.at[layer],
                head0,
                size_h,
                keep_of(layer),
                work.dqkv,
                taps_out,
            )
            for piece, c in enumerate(halves):
                total = 0.0
                for i in range(3):
                    total = total + nt(work.dqkv[i, c, :], weights.projection[layer, i])
                send(slot + 1, piece, total)
                yield
            for i in range(3):
                grads.other[layer, 1 + i] = nn(kept.x_t[layer], work.dqkv[i]).astype(BF16)
                yield
            target = dy_ref if layer > 0 else token_grad_ref
            for piece, c in enumerate(halves):
                target[c, :] = dr_ref[c, :] + arrived(slot + 1, piece)
        yield

    items = backward()
    for code in ORDER:
        if code < 0:
            next(items)
        elif code >= 1000:
            small.event(code - 1000)
        else:
            ring.event(code // 16, code % 16)


FACTORED = (True, False)
DOWN_PIECES = 4
UP_PIECES = 4
PIECE_KINDS = (
    (2, 2, 4, 2, 2, 2, 2, 4, 0, 0, 1, 0),
    (3, 1, 3, 3, 0, 0, 0, 0, 0, 0, 1, 0),
)
ORDER = (
    -1, -1, 0, -1, 16, -1, 32, -1, 48, -1, 1, 17, -1, -1, 33, -1, 64, -1, 49, 80, -1, 96, -1, 112, 65, 81, 97,
    2, 113, 34, -1, 3, 18, 50, -1, -1, 128, -1, -1, 66, 35, 129, -1, -1, 51, 82, 4, -1, -1, 19, -1, 67, 98,
    -1, -1, -1, 83, 36, -1, 114, 5, -1, -1, 144, -1, 160, -1, 176, 52, 99, 145, 130, 161, 177, 68, 20, 115,
    37, 6, 84, 131, -1, 146, 178, 69, 100, 53, -1, -1, -1, 38, 21, 162, 116, 7, 132, 147, -1, 70, 101, 85, 22,
    -1, 179, 163, -1, 54, -1, -1, -1, 8, 192, 193, 148, -1, 23, 208, 209, 39, 117, -1, -1, -1, 194, 71, 256,
    257, 210, 102, -1, -1, -1, 40, 224, 258, 225, -1, 226, 180, 133, 103, 288, 289, 55, 86, -1, -1, 290, 195,
    149, 56, 240, 241, 118, 87, 272, 273, 164, -1, 242, -1, 274, 211, 181, 134, 119, 304, 305, -1, -1, 306,
    196, 135, 320, -1, 259, 150, -1, 321, -1, 1000, 165, -1, 227, 182, -1, -1, 151, 336, -1, 197, -1, 183,
    368, 212, 291, 337, 1001, 369, 322, 166, 1002, 260, 243, 167, 352, 198, 213, 353, 199, 228, 275, 338, 261,
    -1, 307, 292, 370, 229, 244, 323, 1003, 276, 293, 214, 215, 308, 354, 245, 262, 263, 324, 339, 277, 230,
    355, 371, 1004, 340, 231, 372, 232, 356, 1005, 309, 294, 295, 325, 246, 247, 278, 279, 341, 310, 373, 326,
    327, 357, 311, 312, 342, 343, 374, 358, 375, 359, 1006,
)


def pieces_of(width, columns, hidden, layer):
    names = [DOWN] * DOWN_PIECES + [UP] * UP_PIECES + [OUTPUT] + [PROJECTION] * 3
    rows = {DOWN: hidden // DOWN_PIECES, UP: 2 * width // UP_PIECES, OUTPUT: width, PROJECTION: width}
    return [(name, rows[name], kind) for name, kind in zip(names, PIECE_KINDS[layer])]


def slots_of(name, rows, long, width, columns, hidden):
    across = {DOWN: width, UP: hidden // 2, OUTPUT: columns, PROJECTION: columns}[name]

    def room(count):
        return pltpu.VMEM((count, across), BF16)

    return Slots(
        core=room(rows // 2),
        x=room(rows // 4),
        near=room(rows // 2 if long else rows // 4),
        mid=room(rows // 4),
    )


def fused_body(tokens, lengths, cotangent, projection, conv_taps, output_weight, norm_gains, norm_shifts, up_weight, down_weight):
    rows, width = tokens.shape
    columns, hidden = projection.shape[3], up_weight.shape[2]
    heads, reach = conv_taps.shape[1:]
    size_h = width // heads
    pairs = columns // (2 * size_h)
    by_kind = jnp.transpose(projection, (0, 2, 1, 3))
    by_head = jnp.transpose(conv_taps, (1, 0, 2))
    vmem = pl.BlockSpec(memory_space=pltpu.VMEM)
    hbm = pl.BlockSpec(memory_space=pl.ANY)
    two = 2 * M
    pieces = pieces_of(width, columns, hidden, 0)
    scratch = (
        Weights(
            projection=pltpu.VMEM((LAYERS, 3, width, columns), BF16),
            output=pltpu.VMEM((LAYERS, 2, columns, width), BF16),
            up=pltpu.VMEM((LAYERS, width, hidden), BF16),
            down=pltpu.VMEM((LAYERS, hidden, width), BF16),
        ),
        Stored(
            attention=Kept(
                ql=pltpu.VMEM((LAYERS, M, columns), F32),
                kl=pltpu.VMEM((LAYERS, M, columns), F32),
                second=pltpu.VMEM((LAYERS, pairs, two, two), F32),
                inverse=pltpu.VMEM((LAYERS, NEWTON + 1, pairs, M, two), F32),
                first=pltpu.VMEM((LAYERS, rows, columns), BF16),
                third=pltpu.VMEM((LAYERS, pairs, two, rows), BF16),
                summary=pltpu.VMEM((LAYERS, pairs, two, two), F32),
                carried=pltpu.VMEM((LAYERS, pairs, two, two), F32),
            ),
            qkv=pltpu.VMEM((LAYERS, 3, rows, columns), BF16),
            normed=pltpu.VMEM((LAYERS, 2, rows, width), BF16),
            spread=pltpu.VMEM((LAYERS, 2, rows, 1), F32),
            slope=pltpu.VMEM((LAYERS, rows, hidden), BF16),
            x_t=pltpu.VMEM((LAYERS, width, rows), BF16),
            mixed_t=pltpu.VMEM((LAYERS, columns, rows), BF16),
            y_t=pltpu.VMEM((LAYERS, width, rows), BF16),
            active_t=pltpu.VMEM((LAYERS, hidden, rows), BF16),
        ),
        Work(
            x=pltpu.VMEM((rows, width), F32),
            x_low=pltpu.VMEM((rows, width), BF16),
            y=pltpu.VMEM((rows, width), F32),
            y_low=pltpu.VMEM((rows, width), BF16),
            mixed=pltpu.VMEM((2, rows, columns), BF16),
            active=pltpu.VMEM((rows, hidden), BF16),
            e_second=pltpu.VMEM((rows, width), BF16),
            dmixed=pltpu.VMEM((rows, columns), F32),
            dqkv=pltpu.VMEM((3, rows, columns), BF16),
            taps=pltpu.VMEM((LAYERS, 16, rows), F32),
            turned=pltpu.VMEM((LAYERS, 16, rows), F32),
        ),
        Shared(
            active_t=pltpu.VMEM((hidden // 2, rows), BF16),
            slope=pltpu.VMEM((rows, hidden // 2), BF16),
            y_t=pltpu.VMEM((width, rows), BF16),
            e=pltpu.VMEM((rows, width), BF16),
        ),
        Wire(
            send=pltpu.VMEM((rows, width), BF16),
            receive=pltpu.VMEM((2, rows, width), BF16),
            small=pltpu.VMEM((6, 8 + 2 * LAYERS, width), F32),
        ),
        [
            slots_of(name, count, 1 in kinds, width, columns, hidden)
            for (name, count, _), kinds in zip(pieces, zip(*PIECE_KINDS))
        ],
        Sems(
            load=pltpu.SemaphoreType.DMA((4 * LAYERS,)),
            ring_send=pltpu.SemaphoreType.DMA((SENDS * len(pieces),)),
            ring_receive=pltpu.SemaphoreType.DMA((RECEIVES * len(pieces),)),
            small_send=pltpu.SemaphoreType.DMA((6,)),
            small_receive=pltpu.SemaphoreType.DMA((6,)),
            credit=pltpu.SemaphoreType.REGULAR((4 * len(pieces),)),
            ready=pltpu.SemaphoreType.REGULAR((4 * len(pieces),)),
            factor_send=pltpu.SemaphoreType.DMA((5,)),
            factor_receive=pltpu.SemaphoreType.DMA((5,)),
            share_send=pltpu.SemaphoreType.DMA((2 * LAYERS,)),
            share_receive=pltpu.SemaphoreType.DMA((2 * LAYERS,)),
            gather_send=pltpu.SemaphoreType.DMA((2,)),
            gather_receive=pltpu.SemaphoreType.DMA((2,)),
            send=pltpu.SemaphoreType.DMA((4,)),
            receive=pltpu.SemaphoreType.DMA((4,)),
        ),
    )
    own = pltpu.VMEM
    results = pl.pallas_call(
        whole_step,
        out_shape=[
            own((rows, width), BF16),
            own((rows, width), F32),
            own((8 + 2 * LAYERS, width), F32),
            own((LAYERS, hidden, width), BF16),
            own((LAYERS, 2 * width, hidden // 2), BF16),
            own((LAYERS, 4, width, columns), BF16),
        ],
        in_specs=[pl.BlockSpec(memory_space=pltpu.SMEM)] + [vmem] * 5 + [hbm] * 4,
        out_specs=[vmem] * 6,
        scratch_shapes=scratch,
        compiler_params=pltpu.CompilerParams(
            collective_id=0, has_side_effects=True, vmem_limit_bytes=VMEM_ROOM
        ),
    )(
        lengths,
        tokens,
        cotangent,
        by_head,
        norm_gains,
        norm_shifts,
        by_kind,
        output_weight,
        up_weight,
        down_weight,
    )
    shape = jax.ShapeDtypeStruct
    held = [pltpu.with_memory_space_constraint(result, pltpu.VMEM) for result in results]
    wide = [
        (LAYERS, hidden, width),
        (LAYERS, width, hidden),
        (LAYERS, 3, width, columns),
        (LAYERS, columns, width),
    ]
    outputs = pl.pallas_call(
        widen,
        out_shape=[shape(size, F32) for size in wide]
        + [
            shape((rows, width), BF16),
            shape((rows, width), F32),
            shape((heads, LAYERS, reach), F32),
            shape((LAYERS, 2, width), F32),
            shape((LAYERS, 2, width), F32),
        ],
        in_specs=[vmem] * 6,
        out_specs=[hbm] * 6 + [vmem] * 3,
        scratch_shapes=[pltpu.VMEM(size, F32) for size in wide] + [pltpu.SemaphoreType.DMA((6,))],
        compiler_params=pltpu.CompilerParams(vmem_limit_bytes=WIDE_ROOM),
    )(*held)
    down_grad, up_grad, projection_grad, output_grad = outputs[:4]
    activations, token_grad, taps_grad, gains_grad, shifts_grad = outputs[4:]
    return (
        activations,
        token_grad,
        jnp.transpose(projection_grad, (0, 2, 1, 3)),
        jnp.transpose(taps_grad, (1, 0, 2)),
        output_grad,
        gains_grad,
        shifts_grad,
        up_grad,
        down_grad,
    )


VMEM_ROOM = 97 * 2**19
WIDE_ROOM = 32 * 2**20
WIDE_PARTS = 4


def widen(
    activations_ref,
    token_grad_ref,
    small_ref,
    down_ref,
    up_ref,
    other_ref,
    down_hbm,
    up_hbm,
    projection_hbm,
    output_hbm,
    activations_out,
    token_grad_out,
    taps_out,
    gains_out,
    shifts_out,
    down_wide,
    up_wide,
    projection_wide,
    output_wide,
    sems,
):
    heads, _, reach = taps_out.shape
    columns = output_wide.shape[1]

    def send(source, target, index):
        pltpu.make_async_copy(source, target, sems.at[index]).start()

    send(activations_ref, activations_out, 4)
    send(token_grad_ref, token_grad_out, 5)

    def cast(target, source):
        def step(i, unused):
            span = pl.ds(pl.multiple_of(i * 32, 32), 32)
            target[span, :] = source[span, :].astype(F32)
            return unused

        lax.fori_loop(0, source.shape[0] // 32, step, 0)

    for layer in range(LAYERS):
        count = down_ref.shape[1] // WIDE_PARTS
        for part in range(WIDE_PARTS):
            span = pl.ds(part * count, count)
            cast(down_wide.at[layer, span], down_ref.at[layer, span])
            send(down_wide.at[layer, span], down_hbm.at[layer, span], 0)
        count, side = up_wide.shape[1] // WIDE_PARTS, up_wide.shape[2] // 2
        for part in range(WIDE_PARTS):
            span = pl.ds(part * count, count)
            for i in range(2):
                cast(
                    up_wide.at[layer, span, pl.ds(i * side, side)],
                    up_ref.at[layer, pl.ds(i * up_wide.shape[1] + part * count, count)],
                )
            send(up_wide.at[layer, span], up_hbm.at[layer, span], 1)
        for i in range(3):
            cast(projection_wide.at[layer, i], other_ref.at[layer, 1 + i])
            send(projection_wide.at[layer, i], projection_hbm.at[layer, i], 2)
        for i in range(2):
            side = slice(i * columns, (i + 1) * columns)
            output_wide[layer, :, side] = other_ref[layer, 0, side, :].astype(F32)
        send(output_wide.at[layer], output_hbm.at[layer], 3)
    for layer in range(LAYERS):
        gains_out[layer] = small_ref[2 * layer : 2 * layer + 2, :]
        shifts_out[layer] = small_ref[4 + 2 * layer : 6 + 2 * layer, :]
        for head in range(heads):
            side, place = divmod(head, heads // 2)
            row = 8 + 2 * layer + side
            taps_out[head, layer : layer + 1, :] = small_ref[
                row : row + 1, place * 128 : place * 128 + reach
            ]
    whole = [
        (down_wide, down_hbm),
        (up_wide, up_hbm),
        (projection_wide, projection_hbm),
        (output_wide, output_hbm),
        (activations_ref, activations_out),
        (token_grad_ref, token_grad_out),
    ]
    for index, (source, target) in enumerate(whole):
        pltpu.make_async_copy(source, target, sems.at[index]).wait()


def solution(mesh):
    fused = mesh.shape["mp"] == 2 and mesh.shape["dp"] == 16

    def step(*arrays):
        return (fused_body if fused else body)(*arrays)

    return jax.shard_map(
        step,
        mesh=mesh,
        in_specs=(
            P("dp", None),
            P("dp"),
            P("dp", None),
            P(None, None, None, "mp"),
            P(),
            P(None, "mp", None),
            P(),
            P(),
            P(None, None, "mp"),
            P(None, "mp", None),
        ),
        out_specs=(
            P("dp", None),
            P("dp", None),
            P(None, None, None, "mp"),
            P(),
            P(None, "mp", None),
            P(),
            P(),
            P(None, None, "mp"),
            P(None, "mp", None),
        ),
        check_vma=False,
    )
```

```python
from typing import Any, NamedTuple

import jax
import jax.numpy as jnp
from jax import lax
from jax.experimental import pallas as pl
from jax.experimental.pallas import tpu as pltpu
from jax.sharding import PartitionSpec as P

M = 64
NEWTON = 6
LAYERS = 2


highest_value = lax.Precision.HIGHEST


def merged(array, axis, join):
    gathered = jax.tree.map(
        lambda a, kind: lax.all_gather(a.astype(kind), axis),
        array,
        (jnp.bfloat16, jnp.bfloat16, jnp.bfloat16),
    )

    def take(source):
        return jax.tree.map(
            lambda a, own: lax.dynamic_index_in_dim(a, source, 0, False).astype(own.dtype),
            gathered,
            array,
        )

    return lax.fori_loop(
        1, lax.axis_size(axis), lambda source, state: join(state, take(source)), take(0)
    )


def for_sending(array):
    return jax.tree.map(lambda a: a.astype(jnp.bfloat16) if a.dtype == jnp.float32 else a, array)


def softmax_row_block(scores):
    top = jnp.max(scores, axis=-1, keepdims=True)
    matrix_powers = jnp.exp(scores - top)
    return matrix_powers / jnp.sum(matrix_powers, axis=-1, keepdims=True)


def slot_masks(length, count, marks):
    position = jnp.arange(count, dtype=jnp.int32)
    inside = position < length
    segment = position * marks // length
    member = (segment[None, :] == jnp.arange(marks, dtype=jnp.int32)[:, None]) & inside[None, :]
    member = member.astype(jnp.float32)
    pooling = member / jnp.sum(member, axis=1, keepdims=True)
    return (pooling, inside.astype(jnp.float32))


def inverse_head(query_landmarks, key_landmarks, summary):
    scale_factor = query_landmarks.shape[-1] ** (-0.5)
    second = softmax_row_block(
        jnp.dot(query_landmarks, key_landmarks.T, precision=highest_value) * scale_factor
    )
    identity = jnp.eye(second.shape[0], dtype=jnp.float32)
    inverse = second.T / jnp.sum(second * second)
    for sweep in range(NEWTON):
        product = jnp.dot(second, inverse, precision=highest_value)
        inner = 7.0 * identity - product
        inner = 15.0 * identity - jnp.dot(product, inner, precision=highest_value)
        inner = 13.0 * identity - jnp.dot(product, inner, precision=highest_value)
        inverse = 0.25 * jnp.dot(inverse, inner, precision=highest_value)
    return jnp.dot(inverse, summary, precision=highest_value)


def inverse_section(query_landmarks, key_landmarks, summary):
    return jax.vmap(inverse_head)(query_landmarks, key_landmarks, summary)


def near_section(query_matrix, key_landmarks, carried_over):
    scale_factor = query_matrix.shape[-1] ** (-0.5)
    first_entry = softmax_row_block(
        jnp.einsum("nlv,lgv->lng", query_matrix, key_landmarks, precision=highest_value)
        * scale_factor
    )
    return jnp.einsum("xtz,xzb->txb", first_entry, carried_over, precision=highest_value)


def far_scores(query_landmarks, key_matrix, valid_own):
    scale_factor = query_landmarks.shape[-1] ** (-0.5)
    distant_scores = (
        jnp.einsum("owz,toz->owt", query_landmarks, key_matrix, precision=highest_value)
        * scale_factor
    )
    live = valid_own[None, None, :] > 0
    return (jnp.where(live, distant_scores, -1e30), live)


def join_softmax(left, right):
    peak = jnp.maximum(left[0], right[0])
    left_factor = jnp.exp(left[0] - peak)
    right_factor = jnp.exp(right[0] - peak)
    return (
        peak,
        left[1] * left_factor + right[1] * right_factor,
        left[2] * left_factor[..., None] + right[2] * right_factor[..., None],
    )


def attend(query_matrix, key_matrix, value_matrix, pooled_local, valid_own):
    query_portion = jnp.einsum("ji,ilk->ljk", pooled_local, query_matrix, precision=highest_value)
    key_portion = jnp.einsum("ji,ilk->ljk", pooled_local, key_matrix, precision=highest_value)
    query_landmarks, key_landmarks = (
        lax.psum(query_portion.astype(jnp.bfloat16), "mp").astype(jnp.float32),
        lax.psum(key_portion.astype(jnp.bfloat16), "mp").astype(jnp.float32),
    )
    distant_scores, live = far_scores(query_landmarks, key_matrix, valid_own)
    peak = jnp.max(distant_scores, axis=-1)
    matrix_powers = jnp.where(live, jnp.exp(distant_scores - peak[..., None]), 0.0)
    totals = jnp.sum(matrix_powers, axis=-1)
    weighted_values = jnp.einsum(
        "naw,wno->nao", matrix_powers, value_matrix, precision=highest_value
    )
    peak, totals, weighted_values = merged((peak, totals, weighted_values), "mp", join_softmax)
    summary = weighted_values / totals[..., None]
    carried_over = inverse_section(query_landmarks, key_landmarks, summary)
    mixed = near_section(query_matrix, key_landmarks, carried_over)
    return (mixed, (query_landmarks, key_landmarks, peak, totals, summary))


def attend_back(
    grad_rows, query_matrix, key_matrix, value_matrix, pooled_local, valid_own, saved, tap_part
):
    query_landmarks, key_landmarks, peak, totals, summary = saved
    scale_factor = query_matrix.shape[-1] ** (-0.5)
    carried_over, inverse_back = jax.vjp(inverse_section, query_landmarks, key_landmarks, summary)
    unused, near_back = jax.vjp(near_section, query_matrix, key_landmarks, carried_over)
    query_grad, kland_part, carried_part = near_back(grad_rows)
    key_landmark_nearby, carried_grad, tap_grad = (
        lax.psum(kland_part.astype(jnp.bfloat16), "mp").astype(jnp.float32),
        lax.psum(carried_part.astype(jnp.bfloat16), "mp").astype(jnp.float32),
        lax.psum(tap_part.astype(jnp.bfloat16), "mp").astype(jnp.float32),
    )
    query_landmark_gradient, key_landmark_gradient, summary_gradient = inverse_back(carried_grad)
    distant_scores, live = far_scores(query_landmarks, key_matrix, valid_own)
    weight_spread = jnp.where(
        live, jnp.exp(distant_scores - peak[..., None]) / totals[..., None], 0.0
    )
    moving_along = jnp.einsum(
        "owz,toz->owt", summary_gradient, value_matrix, precision=highest_value
    )
    agreed = jnp.sum(summary_gradient * summary, axis=-1)
    slope_values = weight_spread * (moving_along - agreed[..., None])
    value_gradient = jnp.einsum(
        "ofq,ofn->qon", weight_spread, summary_gradient, precision=highest_value
    )
    query_landmark_remote = (
        jnp.einsum("naw,wno->nao", slope_values, key_matrix, precision=highest_value) * scale_factor
    )
    key_gradient = (
        jnp.einsum("ofq,ofn->qon", slope_values, query_landmarks, precision=highest_value)
        * scale_factor
    )
    query_landmark_remote = lax.psum(query_landmark_remote.astype(jnp.bfloat16), "mp").astype(
        jnp.float32
    )
    query_grad = query_grad + jnp.einsum(
        "ge,xgl->exl",
        pooled_local,
        query_landmark_gradient + query_landmark_remote,
        precision=highest_value,
    )
    key_gradient = key_gradient + jnp.einsum(
        "ge,xgl->exl",
        pooled_local,
        key_landmark_gradient + key_landmark_nearby,
        precision=highest_value,
    )
    return (query_grad, key_gradient, value_gradient, tap_grad)


def head_table(columns, heads, size_h):
    begin = lax.axis_index("mp") * columns
    owner = (begin + jnp.arange(columns, dtype=jnp.int32)) // size_h
    return (owner[None, :] == jnp.arange(heads, dtype=jnp.int32)[:, None]).astype(jnp.float32)


def convolve(value_cols, taps, table, valid):
    tap_cols = jnp.dot(taps.T, table, precision=highest_value)
    masked = value_cols * valid[:, None]
    reach = taps.shape[1] // 2
    padded = jnp.pad(masked, ((reach, reach), (0, 0)))
    length_rows = masked.shape[0]
    convolved = jnp.zeros_like(masked)
    for offset in range(taps.shape[1]):
        convolved = convolved + tap_cols[offset] * padded[offset : offset + length_rows]
    return convolved


def contract(left, right, left_dim, right_dim):
    return lax.dot_general(
        left, right, (((left_dim,), (right_dim,)), ((), ())), preferred_element_type=jnp.float32
    )


def normalize(resid, gain, shift):
    centre = resid - jnp.mean(resid, axis=-1, keepdims=True)
    spread = lax.rsqrt(jnp.mean(centre * centre, axis=-1, keepdims=True) + 1e-05)
    normed = centre * spread
    return (normed * gain + shift, normed, spread)


def normalize_back(upstream, normed, spread, gain):
    scaled = upstream * gain
    result = spread * (
        scaled
        - jnp.mean(scaled, axis=-1, keepdims=True)
        - normed * jnp.mean(scaled * normed, axis=-1, keepdims=True)
    )
    return (result, jnp.sum(upstream * normed, axis=0), jnp.sum(upstream, axis=0))


def own_rows(whole):
    count = whole.shape[0] // lax.axis_size("mp")
    return lax.dynamic_slice_in_dim(whole, lax.axis_index("mp") * count, count, 0)


def whole_rows(share):
    return lax.all_gather(share.astype(jnp.bfloat16), "mp", axis=0, tiled=True).astype(share.dtype)


def row_sums(partial_value):
    return lax.psum_scatter(
        partial_value.astype(jnp.bfloat16), "mp", scatter_dimension=0, tiled=True
    ).astype(jnp.float32)


def add_norm(partial_value, resid, gain, shift):
    summed = row_sums(partial_value)
    output, normed, spread = normalize(own_rows(resid) + summed, gain, shift)
    output = whole_rows(output)
    return (output, normed, spread)


def norm_step_back(upstream, normed, spread, gain):
    result, gain_part, shift_part = normalize_back(upstream, normed, spread, gain)
    whole = whole_rows(result)
    return (result, whole, gain_part, shift_part)


def add_input_grad(result, partial_value):
    total = result + row_sums(partial_value)
    return total


def forward_layer(hidden, weights, pooling_own, valid, valid_own):
    projection, taps, output_weight, gains, shifts, up_weight, down_weight = weights
    count, width = hidden.shape
    heads = taps.shape[0]
    size_h = width // heads
    columns = projection.shape[2]
    entering = hidden.astype(jnp.bfloat16)
    mixed = jnp.einsum(
        "td,dsc->tsc", entering, projection, preferred_element_type=jnp.float32
    ).astype(jnp.bfloat16)
    gathered = lax.all_to_all(mixed, "mp", split_axis=0, concat_axis=2, tiled=True)
    rows = gathered.shape[0]
    split_rows = gathered.astype(jnp.float32).reshape(rows, 3, heads, size_h)
    attended, saved = attend(
        split_rows[:, 0], split_rows[:, 1], split_rows[:, 2], pooling_own, valid_own
    )
    attended_cols = lax.all_to_all(
        for_sending(attended.reshape(rows, width)), "mp", split_axis=1, concat_axis=0, tiled=True
    )
    table = head_table(columns, heads, size_h)
    value_cols = mixed[:, 2].astype(jnp.float32)
    convolved = convolve(value_cols, taps, table, valid)
    joined = ((attended_cols + convolved) * valid[:, None]).astype(jnp.bfloat16)
    partial_value = jnp.dot(joined, output_weight, preferred_element_type=jnp.float32)
    middle, normed_first, spread_first = add_norm(partial_value, hidden, gains[0], shifts[0])
    entering_ffn = middle.astype(jnp.bfloat16)
    upward = jnp.dot(entering_ffn, up_weight, preferred_element_type=jnp.float32)
    active = jax.nn.gelu(upward, approximate=True).astype(jnp.bfloat16)
    partial_value = jnp.dot(active, down_weight, preferred_element_type=jnp.float32)
    output, normed_second, spread_second = add_norm(partial_value, middle, gains[1], shifts[1])
    kept = (
        entering,
        value_cols,
        split_rows,
        saved,
        joined,
        table,
        normed_first,
        spread_first,
        entering_ffn,
        upward,
        active,
        normed_second,
        spread_second,
    )
    return (output, kept)


def backward_layer(upstream, weights, kept, pooling_own, valid, valid_own):
    projection, taps, output_weight, gains, shifts, up_weight, down_weight = weights
    (
        entering,
        value_cols,
        split_rows,
        saved,
        joined,
        table,
        normed_first,
        spread_first,
        entering_ffn,
        upward,
        active,
        normed_second,
        spread_second,
    ) = kept
    count, width = entering.shape
    rows = split_rows.shape[0]
    heads = taps.shape[0]
    size_h = width // heads
    result_second, whole_second, gain_second, shift_second = norm_step_back(
        upstream, normed_second, spread_second, gains[1]
    )
    sent_second = whole_second.astype(jnp.bfloat16)
    down_grad = contract(active, sent_second, 0, 0)
    hidden_grad = contract(sent_second, down_weight, 1, 1)
    unused, gelu_back = jax.vjp(lambda value: jax.nn.gelu(value, approximate=True), upward)
    upward_sent = gelu_back(hidden_grad)[0].astype(jnp.bfloat16)
    up_grad = contract(entering_ffn, upward_sent, 0, 0)
    middle_grad = add_input_grad(result_second, contract(upward_sent, up_weight, 1, 1))
    result_first, whole_first, gain_first, shift_first = norm_step_back(
        middle_grad, normed_first, spread_first, gains[0]
    )
    sent_first = whole_first.astype(jnp.bfloat16)
    out_grad = contract(joined, sent_first, 0, 0)
    joined_grad = contract(sent_first, output_weight, 1, 1)
    masked_grad = joined_grad * valid[:, None]
    unused, conv_back = jax.vjp(
        lambda values, tap_rows: convolve(values, tap_rows, table, valid), value_cols, taps
    )
    conv_value_grad, tap_part = conv_back(masked_grad)
    row_grad = (
        lax.all_to_all(
            masked_grad.astype(jnp.bfloat16), "mp", split_axis=0, concat_axis=1, tiled=True
        )
        .astype(masked_grad.dtype)
        .reshape(rows, heads, size_h)
    )
    query_grad, key_gradient, value_gradient, tap_grad = attend_back(
        row_grad,
        split_rows[:, 0],
        split_rows[:, 1],
        split_rows[:, 2],
        pooling_own,
        valid_own,
        saved,
        tap_part,
    )
    stacked_rows = jnp.stack([query_grad, key_gradient, value_gradient], axis=1).reshape(
        rows, 3, width
    )
    column_grad = lax.all_to_all(
        for_sending(stacked_rows), "mp", split_axis=2, concat_axis=0, tiled=True
    ).astype(stacked_rows.dtype)
    column_grad = jnp.concatenate(
        [column_grad[:, :2], (column_grad[:, 2] + conv_value_grad)[:, None]], axis=1
    )
    mixed_sent = column_grad.astype(jnp.bfloat16)
    proj_grad = jnp.einsum("td,tsc->dsc", entering, mixed_sent, preferred_element_type=jnp.float32)
    below = add_input_grad(
        result_first,
        jnp.einsum("tsc,dsc->td", mixed_sent, projection, preferred_element_type=jnp.float32),
    )
    gain_grad = jnp.stack([gain_first, gain_second])
    shift_grad = jnp.stack([shift_first, shift_second])
    gain_grad, shift_grad = lax.psum((gain_grad, shift_grad), "mp")
    return (below, (proj_grad, tap_grad, out_grad, gain_grad, shift_grad, up_grad, down_grad))


def sum_layer(parts):
    return (
        lax.psum(parts[0].astype(jnp.bfloat16), "dp").astype(jnp.float32),
        lax.psum(parts[1].astype(jnp.bfloat16), "dp").astype(jnp.float32),
        lax.psum(parts[2].astype(jnp.bfloat16), "dp").astype(jnp.float32),
        lax.psum(parts[3].astype(jnp.bfloat16), "dp").astype(jnp.float32),
        lax.psum(parts[4].astype(jnp.bfloat16), "dp").astype(jnp.float32),
        lax.psum(parts[5].astype(jnp.bfloat16), "dp").astype(jnp.float32),
        lax.psum(parts[6].astype(jnp.bfloat16), "dp").astype(jnp.float32),
    )


def body(
    tokens,
    lengths,
    cotangent,
    projection,
    conv_taps,
    output_weight,
    norm_gains,
    norm_shifts,
    up_weight,
    down_weight,
):
    count = tokens.shape[0]
    pooling, valid = slot_masks(lengths[0], count, M)
    rows = count // lax.axis_size("mp")
    begin = lax.axis_index("mp") * rows
    pooling_own = lax.dynamic_slice_in_dim(pooling, begin, rows, 1)
    valid_own = lax.dynamic_slice_in_dim(valid, begin, rows, 0)
    weights = (
        projection,
        conv_taps,
        output_weight,
        norm_gains,
        norm_shifts,
        up_weight,
        down_weight,
    )
    hidden = tokens.astype(jnp.float32)
    keeping = []
    for layer_index in range(LAYERS):
        hidden, kept = forward_layer(
            hidden, tuple((item[layer_index] for item in weights)), pooling_own, valid, valid_own
        )
        keeping.append(kept)
    activations = (hidden * valid[:, None]).astype(jnp.bfloat16)
    upstream = cotangent.astype(jnp.float32) * valid[:, None]
    upstream = own_rows(upstream)
    collected = [None] * LAYERS
    for layer_index in reversed(range(LAYERS)):
        upstream, parts = backward_layer(
            upstream,
            tuple((item[layer_index] for item in weights)),
            keeping[layer_index],
            pooling_own,
            valid,
            valid_own,
        )
        collected[layer_index] = sum_layer(parts)
    stacked = tuple(
        (
            jnp.stack([collected[layer_index][member] for layer_index in range(LAYERS)])
            for member in range(7)
        )
    )
    upstream = whole_rows(upstream)
    return (
        activations,
        upstream,
        stacked[0],
        stacked[1],
        stacked[2],
        stacked[3],
        stacked[4],
        stacked[5],
        stacked[6],
    )


class Weights(NamedTuple):
    projection: Any
    output: Any
    up: Any
    down: Any


class Kept(NamedTuple):
    ql: Any
    kl: Any
    second: Any
    inverse: Any
    first: Any
    third: Any
    summary: Any
    carried: Any


class Stored(NamedTuple):
    attention: Any
    qkv: Any
    normed: Any
    spread: Any
    slope: Any
    x_t: Any
    mixed_t: Any
    y_t: Any
    active_t: Any


class Work(NamedTuple):
    x: Any
    x_low: Any
    y: Any
    y_low: Any
    mixed: Any
    active: Any
    e_second: Any
    dmixed: Any
    dqkv: Any
    taps: Any
    turned: Any


class Shared(NamedTuple):
    active_t: Any
    slope: Any
    y_t: Any
    e: Any


class Wire(NamedTuple):
    send: Any
    receive: Any
    small: Any


class Sems(NamedTuple):
    load: Any
    ring_send: Any
    ring_receive: Any
    small_send: Any
    small_receive: Any
    credit: Any
    ready: Any
    factor_send: Any
    factor_receive: Any
    share_send: Any
    share_receive: Any
    gather_send: Any
    gather_receive: Any
    send: Any
    receive: Any


class Slots(NamedTuple):
    core: Any
    x: Any
    near: Any
    mid: Any


class Grads(NamedTuple):
    down: Any
    up: Any
    other: Any


DOWN, UP, OUTPUT, PROJECTION = range(4)


MESH = pl.DeviceIdType.MESH
F32 = jnp.float32
BF16 = jnp.bfloat16


def nn(a, b):
    return lax.dot_general(a, b, (((1,), (0,)), ((), ())), preferred_element_type=F32)


def nt(a, b):
    return lax.dot_general(a, b, (((1,), (1,)), ((), ())), preferred_element_type=F32)


def parts_of(x):
    high = x.astype(BF16)
    return high, (x - high.astype(F32)).astype(BF16)


def nn3(a, b):
    return nn(jnp.concatenate([a[0], a[1]], 1), jnp.concatenate([b[0], b[0]], 0)) + nn(a[0], b[1])


def nt3(a, b):
    return nt(jnp.concatenate([a[0], a[1]], 1), jnp.concatenate([b[0], b[0]], 1)) + nt(a[0], b[1])


def iota(shape, axis):
    return lax.broadcasted_iota(jnp.int32, shape, axis)


class Frame:
    def __init__(self, length, rows, size_h):
        self.length = length
        self.rows = rows
        self.lane0 = iota((1, 2 * size_h), 1) < size_h
        self.keep = [self.lane0.astype(F32).astype(BF16), (~self.lane0).astype(F32).astype(BF16)]
        self.diag = (iota((2 * M, 2 * M), 0) < M) == (iota((2 * M, 2 * M), 1) < M)
        self.ones = self.diag.astype(F32).astype(BF16)
        self.ones2 = jnp.concatenate([self.ones, self.ones], 0)
        j, t = iota((M, rows), 0), iota((M, rows), 1)
        member = (t * M >= j * length) & (t * M < (j + 1) * length)
        member = member.astype(F32)
        self.member = member.astype(BF16)
        self.inv = 1.0 / jnp.sum(member, axis=1, keepdims=True)
        t, j = iota((rows, M), 0), iota((rows, M), 1)
        self.member_t = ((t * M >= j * length) & (t * M < (j + 1) * length)).astype(F32).astype(BF16)
        self.valid = (iota((rows, 1), 0) < length).astype(F32)
        self.valid_lane = iota((1, rows), 1) < length
        self.band = jnp.abs(iota((rows, rows), 0) - iota((rows, rows), 1)) <= KREACH

    def stack(self, x):
        return jnp.where(self.diag, jnp.concatenate([x, x], 0), 0.0)

    def block(self, x):
        return jnp.where(self.diag, x, 0.0)

    def pack(self, x):
        return x[:M] + x[M:]

    def spread(self, x):
        return jnp.concatenate([x * self.keep[0], x * self.keep[1]], 0)

    def times(self, a, b):
        high, low = b
        left = jnp.concatenate([a[0], a[1]], 1)
        return nn(left, jnp.concatenate([high, high], 0)) + nn(a[0], low)

    def spread_parts(self, x):
        return tuple(self.spread(half) for half in parts_of(x))

    def half_sums(self, x):
        high, low = parts_of(x)
        return nn(jnp.concatenate([high, low], 1), self.ones2)

    def toeplitz(self, row):
        spread = jnp.broadcast_to(row, (self.rows, self.rows))
        turned = pltpu.roll(spread, self.rows - KREACH, 1, stride=1, stride_axis=0)
        return jnp.where(self.band, turned, 0.0).astype(BF16)

    def conv(self, rows_pair, value):
        both = jnp.concatenate([self.toeplitz(rows_pair[0]), self.toeplitz(rows_pair[1])], 1)
        stacked = jnp.concatenate([value * self.keep[0], value * self.keep[1]], 0)
        return nn(both, stacked)

    def diagonals(self, product):
        banded = jnp.where(self.band, product, 0.0)
        total = banded[:8]
        for group in range(1, self.rows // 8):
            part = banded[8 * group : 8 * group + 8]
            total = total + pltpu.roll(part, self.rows - 8 * group, 1)
        total = pltpu.roll(total, KREACH, 1)
        result = total[:1]
        for row in range(1, 8):
            result = result + pltpu.roll(total[row : row + 1], self.rows - row, 1)
        return result


KREACH = 16


def softmax_masked(scores, live):
    scores = jnp.where(live, scores, -1e30)
    top = jnp.max(scores, axis=-1, keepdims=True)
    powers = jnp.where(live, jnp.exp(scores - top), 0.0)
    return powers / jnp.sum(powers, axis=-1, keepdims=True)


def attention(frame, qkv, taps, head0, size_h, keep, out_ref):
    scale = size_h ** (-0.5)
    pairs = qkv.shape[2] // (2 * size_h)
    ql = nn(frame.member, qkv[0]) * frame.inv
    kl = nn(frame.member, qkv[1]) * frame.inv
    keep.ql[...] = ql
    keep.kl[...] = kl
    cols = [slice(p * 2 * size_h, (p + 1) * 2 * size_h) for p in range(pairs)]
    qs = [parts_of(frame.stack(ql[:, c])) for c in cols]
    ks = [parts_of(frame.stack(kl[:, c])) for c in cols]
    second = [softmax_masked(nt3(qs[p], ks[p]) * scale, frame.diag) for p in range(pairs)]
    inverse = []
    halves = iota((2 * M, 1), 0) < M
    for p in range(pairs):
        keep.second[p] = second[p]
        squares = jnp.sum(second[p] * second[p], axis=1, keepdims=True)
        first_total = jnp.sum(jnp.where(halves, squares, 0.0), axis=0, keepdims=True)
        other_total = jnp.sum(jnp.where(halves, 0.0, squares), axis=0, keepdims=True)
        inverse.append(second[p].T * (1.0 / jnp.where(halves, first_total, other_total)))
    second_parts = [parts_of(frame.pack(s)) for s in second]
    summaries, firsts, convolved = [None] * pairs, [None] * pairs, [None] * pairs

    def far(p):
        key, value = qkv[1, :, cols[p]], qkv[2, :, cols[p]]
        scores = nt(jnp.concatenate(qs[p], 1), jnp.concatenate([key, key], 1)) * scale
        third = softmax_masked(scores, frame.valid_lane).astype(BF16)
        keep.third[p] = third
        summaries[p] = frame.block(nn(third, value))
        keep.summary[p] = summaries[p]

    def near(p):
        query = qkv[0, :, cols[p]]
        scores = nt(jnp.concatenate([query, query], 1), jnp.concatenate(ks[p], 1)) * scale
        top0 = jnp.max(jnp.where(frame.lane0, scores, -1e30), axis=-1, keepdims=True)
        top1 = jnp.max(jnp.where(frame.lane0, -1e30, scores), axis=-1, keepdims=True)
        powers = jnp.exp(scores - jnp.where(frame.lane0, top0, top1))
        firsts[p] = (powers / frame.half_sums(powers)).astype(BF16)
        keep.first[:, cols[p]] = firsts[p]

    def local(p):
        inside = (qkv[2, :, cols[p]].astype(F32) * frame.valid).astype(BF16)
        rows_pair = [taps[pl.ds(head0 + 2 * p + i, 1), :] for i in range(2)]
        convolved[p] = frame.conv(rows_pair, inside)

    beside = [(task, p) for p in range(pairs) for task in (far, near, local)]
    inverse = [frame.pack(z) for z in inverse]
    product = [frame.times(second_parts[p], frame.spread_parts(inverse[p])) for p in range(pairs)]
    for sweep in range(NEWTON):
        for p in range(pairs):
            keep.inverse[sweep, p] = inverse[p]
        zp = [parts_of(z) for z in inverse]
        pp = [parts_of(x) for x in product]
        right = [tuple(frame.spread(half) for half in pp[p]) for p in range(pairs)]
        square = [frame.times(pp[p], right[p]) for p in range(pairs)]
        forward = [frame.times(zp[p], right[p]) for p in range(pairs)]
        for task, p in beside[sweep * len(beside) // NEWTON : (sweep + 1) * len(beside) // NEWTON]:
            task(p)
        inner = [frame.spread_parts(7.0 * product[p] - square[p]) for p in range(pairs)]
        if sweep + 1 < NEWTON:
            product = [0.25 * (13.0 * product[p] - 15.0 * square[p] + frame.times(parts_of(square[p]), inner[p])) for p in range(pairs)]
        inverse = [0.25 * (13.0 * inverse[p] - 15.0 * forward[p] + frame.times(parts_of(forward[p]), inner[p])) for p in range(pairs)]
    for p in range(pairs):
        keep.inverse[NEWTON, p] = inverse[p]
        carried = frame.stack(frame.times(parts_of(inverse[p]), parts_of(summaries[p])))
        keep.carried[p] = carried
        mixed = nn(firsts[p], carried.astype(BF16))
        out_ref[:, cols[p]] = ((mixed + convolved[p]) * frame.valid).astype(BF16)


def attention_back(frame, grad, qkv, taps_turned, head0, size_h, keep, out_ref, taps_out):
    scale = size_h ** (-0.5)
    pairs = qkv.shape[2] // (2 * size_h)
    cols = [slice(p * 2 * size_h, (p + 1) * 2 * size_h) for p in range(pairs)]
    each = range(pairs)
    ql, kl = keep.ql[...], keep.kl[...]
    qs = [parts_of(frame.stack(ql[:, c])) for c in cols]
    ks = [parts_of(frame.stack(kl[:, c])) for c in cols]
    summary = [keep.summary[p] for p in each]
    second = [keep.second[p] for p in each]
    dq, dk_landmark, dcarried, grad_low = [], [], [], []
    for p in each:
        c = cols[p]
        g = grad[:, c].astype(BF16)
        grad_low.append(g)
        first = keep.first[:, c].astype(F32)
        dfirst = nt(g, keep.carried[p].astype(BF16))
        slope = first * dfirst
        slope = (slope - first * frame.half_sums(slope)) * scale
        dq.append(nn(slope.astype(BF16), ks[p][0]))
        dk_landmark.append(frame.block(nn(slope.T.astype(BF16), qkv[0, :, c])))
        dcarried.append(frame.block(nn(first.T.astype(BF16), g)))
    yield
    dcp = [parts_of(x) for x in dcarried]
    up = [nt3(dcp[p], parts_of(summary[p])) for p in each]
    dsummary = [nn3(parts_of(frame.stack(keep.inverse[NEWTON, p]).T), dcp[p]) for p in each]
    second_parts = [parts_of(s) for s in second]
    second_turned = [parts_of(s.T) for s in second]
    dsecond = [jnp.zeros_like(s) for s in second]
    for sweep in reversed(range(NEWTON)):
        inverse = [frame.stack(keep.inverse[sweep, p]) for p in each]
        zp = [parts_of(z) for z in inverse]
        product = [nn3(second_parts[p], zp[p]) for p in each]
        pp = [parts_of(x) for x in product]
        inner = [parts_of(7.0 * product[p] - nn3(pp[p], pp[p])) for p in each]
        forward_turned = [parts_of(nn3(zp[p], pp[p]).T) for p in each]
        product_turned = [parts_of(x.T) for x in product]
        inverse_turned = [parts_of(z.T) for z in inverse]
        upp = [parts_of(x) for x in up]
        dforward = [parts_of(0.25 * (nt3(upp[p], inner[p]) - 15.0 * up[p])) for p in each]
        dinner_full = [0.25 * nn3(forward_turned[p], upp[p]) for p in each]
        dinner = [parts_of(x) for x in dinner_full]
        dproduct = [
            parts_of(
                7.0 * dinner_full[p]
                - nt3(dinner[p], pp[p])
                - nn3(product_turned[p], dinner[p])
                + nn3(inverse_turned[p], dforward[p])
            )
            for p in each
        ]
        up = [
            3.25 * up[p] + nt3(dforward[p], pp[p]) + nn3(second_turned[p], dproduct[p])
            for p in each
        ]
        dsecond = [dsecond[p] + nt3(dproduct[p], zp[p]) for p in each]
        yield
    halves = iota((2 * M, 1), 0) < M
    for p in each:
        c = cols[p]
        query, key, value = qkv[0, :, c], qkv[1, :, c], qkv[2, :, c]
        squares = jnp.sum(second[p] * second[p], axis=1, keepdims=True)
        total0 = jnp.sum(jnp.where(halves, squares, 0.0), axis=0, keepdims=True)
        total1 = jnp.sum(jnp.where(halves, 0.0, squares), axis=0, keepdims=True)
        inverse_total = 1.0 / jnp.where(halves, total0, total1)
        start_agree = jnp.sum(up[p] * frame.stack(keep.inverse[0, p]), axis=1, keepdims=True)
        agree0 = jnp.sum(jnp.where(halves, start_agree, 0.0), axis=0, keepdims=True)
        agree1 = jnp.sum(jnp.where(halves, 0.0, start_agree), axis=0, keepdims=True)
        agree = jnp.where(halves, agree0, agree1)
        dsec = dsecond[p] + (up[p].T - 2.0 * agree * second[p]) * inverse_total
        slope = second[p] * dsec
        slope = (slope - second[p] * jnp.sum(slope, axis=-1, keepdims=True)) * scale
        dql = nn(slope.astype(BF16), ks[p][0])
        dkl = nn(slope.T.astype(BF16), qs[p][0]) + dk_landmark[p]
        third = keep.third[p].astype(F32)
        ds = dsummary[p].astype(BF16)
        dthird = nt(ds, value)
        agreed = jnp.sum(dsummary[p] * summary[p], axis=-1, keepdims=True)
        slope = third * (dthird - agreed) * scale
        dv = nn(third.T.astype(BF16), ds)
        dql = dql + frame.block(nn(slope.astype(BF16), key))
        dk = nn(slope.T.astype(BF16), qs[p][0])
        dql = ((dql[:M] + dql[M:]) * frame.inv).astype(BF16)
        dkl = ((dkl[:M] + dkl[M:]) * frame.inv).astype(BF16)
        out_ref[0, :, c] = (dq[p] + nn(frame.member_t, dql)).astype(BF16)
        out_ref[1, :, c] = (dk + nn(frame.member_t, dkl)).astype(BF16)
        inside = (value.astype(F32) * frame.valid).astype(BF16)
        rows_pair = [taps_turned[pl.ds(head0 + 2 * p + i, 1), :] for i in range(2)]
        dv = dv + frame.valid * frame.conv(rows_pair, grad_low[p])
        out_ref[2, :, c] = dv.astype(BF16)
        for i in range(2):
            product = nt(grad_low[p] * frame.keep[i], inside)
            taps_out(2 * p + i, frame.diagonals(product))
        yield


def norm_rows(r, gain, shift):
    centre = r - jnp.mean(r, axis=-1, keepdims=True)
    spread = lax.rsqrt(jnp.mean(centre * centre, axis=-1, keepdims=True) + 1e-05)
    normed = centre * spread
    return normed * gain + shift, normed, spread


def norm_rows_back(dy, normed, spread, gain):
    scaled = dy * gain
    result = spread * (
        scaled
        - jnp.mean(scaled, axis=-1, keepdims=True)
        - normed * jnp.mean(scaled * normed, axis=-1, keepdims=True)
    )
    return (
        result,
        jnp.sum(dy * normed, axis=0, keepdims=True),
        jnp.sum(dy, axis=0, keepdims=True),
    )


GELU_A = 0.7978845608028654
GELU_B = 0.044715


def gelu_both(u):
    square = u * u
    t = jnp.tanh(GELU_A * (u + GELU_B * u * square))
    half = 0.5 * (1.0 + t)
    slope = half + 0.5 * u * (1.0 - t * t) * (GELU_A + (3.0 * GELU_A * GELU_B) * square)
    return u * half, slope


SEND_SEM = (
    (0, 1, 2, 2, 0, 1, 2, 3),
    (0, 1, 2, 2, 0, 3, 2, 4, 1),
    (0, 1, 2, 2, 0, 1, 2, 3),
    (0, 1, 2, 2, 0, 1, 2, 3, 4, 4),
    (0, 1, 2, 2, 0, 1, 2, 3, 4, 4),
)
RECEIVE_SEM = (
    (0, 1, 2, 3, 2, 6, 5, 4),
    (0, 1, 2, 3, 6, 6, 5, 4, 2),
    (0, 1, 2, 3, 2, 7, 5, 4),
    (0, 1, 2, 3, 2, 6, 5, 4, 6, 6),
    (0, 1, 2, 3, 2, 7, 5, 4, 7, 7),
)
SENDS, RECEIVES = 5, 8
ROUTE = (0, 1, 2, 0, 2)


class Reduction:
    def __init__(self, sems):
        dp, self.mp = lax.axis_index("dp"), lax.axis_index("mp")
        z = dp // 4
        self.x = (dp // 2) % 2
        self.core = dp % 2
        self.upper = z // 2
        self.inner = (z == 1) | (z == 2)
        self.outer = (z == 0) | (z == 3)
        self.to_core = dp + 1 - 2 * self.core
        self.to_x = dp + 2 - 4 * self.x
        self.to_near = dp + 4 - 8 * (z % 2)
        self.to_mid = (3 - z) * 4 + dp % 4
        self.sems = sems
        self.pieces = []

    def greet(self, barrier):
        for other in (self.to_core, self.to_x, self.to_near, self.to_mid):
            pl.semaphore_signal(barrier, inc=1, device_id=(other, self.mp), device_id_type=MESH)

    def add(self, rows, kind, view, slots, credit, gives, takes, other_kind):
        self.pieces.append((rows // 4, kind, view, slots, credit, gives, takes, other_kind))

    def copy(self, index, slot, source, target, to):
        kind, place = self.pieces[index][1], self.pieces[index][4]
        return pltpu.make_async_remote_copy(
            src_ref=source,
            dst_ref=target,
            send_sem=self.sems.ring_send.at[place * SENDS + SEND_SEM[kind][slot]],
            recv_sem=self.sems.ring_receive.at[place * RECEIVES + RECEIVE_SEM[kind][slot]],
            device_id=(to, self.mp),
            device_id_type=MESH,
        )

    def event(self, index, step):
        quarter, kind, view, slots, credit, gives, takes, other_kind = self.pieces[index]
        by_outer, kind, other_kind = kind > 2, ROUTE[kind], ROUTE[other_kind]
        x, core, upper = self.x, self.core, self.upper
        side = upper if kind == 1 else x

        def region(half, which, count=1):
            return view(half, which, count * quarter)

        def arrived(slot, ref):
            self.copy(index, slot, ref, ref, self.to_core).wait_recv()

        def sent(slot, ref):
            self.copy(index, slot, ref, ref, self.to_core).wait_send()

        def send(slot, source, destination, to, need=None):
            if takes and need is not None:
                pl.semaphore_wait(self.sems.credit.at[credit * 2 + need], 1)
            self.copy(index, slot, source, destination, to).start()

        def free(which, to):
            if gives:
                pl.semaphore_signal(
                    self.sems.credit.at[credit * 2 + which],
                    inc=1,
                    device_id=(to, self.mp),
                    device_id_type=MESH,
                )

        def ready(which, slot, ref, to):
            sent(slot, ref)
            pl.semaphore_signal(
                self.sems.ready.at[credit * 4 + which],
                inc=1,
                device_id=(to, self.mp),
                device_id_type=MESH,
            )

        def await_ready(which):
            pl.semaphore_wait(self.sems.ready.at[credit * 4 + which], 1)

        def slot_part(ref, which):
            return ref.at[pl.ds(pl.multiple_of(which * quarter, 16), quarter)]

        def sum_into(ref, others):
            block = 48 if quarter % 48 == 0 else 16

            def step_rows(i, unused):
                span = pl.ds(pl.multiple_of(i * block, 16), block)
                total = ref[span, :].astype(F32)
                for other in others:
                    total = total + other[span, :].astype(F32)
                ref[span, :] = total.astype(BF16)
                return unused

            lax.fori_loop(0, quarter // block, step_rows, 0)

        mine, other = region(core, side), region(core, 1 - side)
        if step == 0:
            if kind == 2:
                send(0, region(1 - core, x), slot_part(slots.core, 0), self.to_core)
            else:
                send(0, region(1 - core, 0, 2), slots.core, self.to_core)
        elif step == 7 + by_outer:
            for slot, which in ((6, side), (7, 1 - side)):
                arrived(slot, region(1 - core, which))
            sent(6, mine)
            sent(7, other)
            if by_outer:

                @pl.when(self.outer)
                def _():
                    sent(5, mine)
                    sent(9, mine)

            elif kind != 1:
                sent(5, mine)

            if kind != 1:

                @pl.when(self.inner)
                def _():
                    sent(4, mine)

            else:

                @pl.when(self.inner)
                def _():
                    for slot in (4, 5, 8):
                        sent(slot, mine)

        elif kind == 2 and step < 4:
            if step > 1:

                @pl.when(self.outer if step == 2 else self.inner)
                def _():
                    arrived(0, slot_part(slots.core, 0))
                    if step == 2:
                        sum_into(mine, [slot_part(slots.core, 0)])
                        send(2, mine, slot_part(slots.near, 0), self.to_near)
                    else:
                        arrived(2, slot_part(slots.near, 0))
                        sum_into(mine, [slot_part(slots.core, 0), slot_part(slots.near, 0)])
                        send(3, mine, slots.mid, self.to_mid, need=1)
                    ready(0, 0, region(1 - core, x), self.to_core)

            if step == 3:

                @pl.when(self.outer)
                def _():
                    ready(2, 2, mine, self.to_near)

        elif kind != 1:
            if step == 1:
                arrived(0, slots.core)
                sum_into(other, [slot_part(slots.core, 1 - x)])
                if other_kind == 0:
                    send(1, other, slots.x, self.to_x, need=0)
                else:
                    if takes:

                        @pl.when(self.inner)
                        def _():
                            pl.semaphore_wait(self.sems.credit.at[credit * 2], 1)

                    send(1, other, slots.x, self.to_x)
                ready(0, 0, region(1 - core, 0, 2), self.to_core)
            elif step == 2:

                @pl.when(self.outer)
                def _():
                    arrived(1, slots.x)
                    sum_into(mine, [slot_part(slots.core, x), slots.x])
                    if other_kind == 0:
                        free(0, self.to_x)
                    send(2, mine, slot_part(slots.near, 0), self.to_near)
                    ready(1, 1, other, self.to_x)

            elif step == 3:

                @pl.when(self.inner)
                def _():
                    arrived(1, slots.x)
                    arrived(2, slot_part(slots.near, 0))
                    sum_into(mine, [slot_part(slots.core, x), slots.x, slot_part(slots.near, 0)])
                    if other_kind != 2:
                        free(0, self.to_x)
                    send(3, mine, slots.mid, self.to_mid, need=1)
                    if by_outer:
                        ready(3, 1, other, self.to_near)
                    else:
                        ready(1, 1, other, self.to_x)

                @pl.when(self.outer)
                def _():
                    ready(2, 2, mine, self.to_near)

            elif step == 4:

                @pl.when(self.inner)
                def _():
                    arrived(3, slots.mid)
                    sent(3, mine)
                    sum_into(mine, [slots.mid])
                    free(1, self.to_mid)
                    await_ready(2)
                    send(4, mine, mine, self.to_near)
                    if not by_outer:
                        if kind == 0:
                            await_ready(1)
                        send(5, mine, mine, self.to_x)
                    await_ready(0)
                    send(6, mine, mine, self.to_core)

            elif step == 5:

                @pl.when(self.outer)
                def _():
                    arrived(4, mine)
                    if kind == 0:
                        await_ready(1)
                    send(5, mine, mine, self.to_x)
                    await_ready(0)
                    send(6, mine, mine, self.to_core)

            elif step == 6 and not by_outer:
                arrived(5, other)
                send(7, other, other, self.to_core)
            elif step == 6:

                @pl.when(self.outer)
                def _():
                    arrived(5, other)
                    if kind == 0:
                        await_ready(3)
                    send(9, other, other, self.to_near)
                    send(7, other, other, self.to_core)

            elif step == 7:

                @pl.when(self.inner)
                def _():
                    arrived(9, other)
                    send(7, other, other, self.to_core)

        else:
            if step == 1:

                @pl.when(self.outer)
                def _():
                    arrived(0, slots.core)
                    sum_into(region(core, 0), [slot_part(slots.core, 0)])
                    sum_into(region(core, 1), [slot_part(slots.core, 1)])
                    send(2, region(core, 0, 2), slots.near, self.to_near)
                    ready(0, 0, region(1 - core, 0, 2), self.to_core)

            elif step == 2:

                @pl.when(self.outer)
                def _():
                    ready(2, 2, region(core, 0, 2), self.to_near)

                @pl.when(self.inner)
                def _():
                    arrived(0, slots.core)
                    arrived(2, slots.near)
                    sum_into(other, [slot_part(slots.core, 1 - side), slot_part(slots.near, 1 - side)])
                    send(3, other, slots.mid, self.to_mid, need=1)
                    ready(0, 0, region(1 - core, 0, 2), self.to_core)

            elif step == 3:

                @pl.when(self.inner)
                def _():
                    arrived(3, slots.mid)
                    sum_into(mine, [slot_part(slots.core, side), slot_part(slots.near, side), slots.mid])
                    free(1, self.to_mid)
                    send(1, mine, slots.x, self.to_x, need=0)
                    ready(3, 3, other, self.to_mid)

            elif step == 4:

                @pl.when(self.inner)
                def _():
                    arrived(1, slots.x)
                    sent(1, mine)
                    sum_into(mine, [slots.x])
                    if other_kind != 2:
                        free(0, self.to_x)
                    await_ready(3)
                    send(4, mine, mine, self.to_mid)
                    await_ready(2)
                    send(8, mine, mine, self.to_near)
                    await_ready(0)
                    send(6, mine, mine, self.to_core)

            elif step == 5:

                @pl.when(self.inner)
                def _():
                    arrived(4, other)
                    send(5, other, other, self.to_near)
                    send(7, other, other, self.to_core)

                @pl.when(self.outer)
                def _():
                    arrived(8, mine)
                    await_ready(0)
                    send(6, mine, mine, self.to_core)

            elif step == 6:

                @pl.when(self.outer)
                def _():
                    arrived(5, other)
                    send(7, other, other, self.to_core)


class SmallSum:
    def __init__(self, ring, total, slots, sems, first_tap):
        self.ring, self.total, self.slots, self.sems, self.first_tap = ring, total, slots, sems, first_tap

    def copy(self, slot, target, to, mp):
        return pltpu.make_async_remote_copy(
            src_ref=self.total,
            dst_ref=target,
            send_sem=self.sems.small_send.at[slot],
            recv_sem=self.sems.small_receive.at[slot],
            device_id=(to, mp),
            device_id_type=MESH,
        )

    def event(self, step):
        ring, total, slots = self.ring, self.total, self.slots
        dp = ring.to_core + 2 * ring.core - 1

        def start(slot, to, mp=None):
            self.copy(slot, slots.at[slot], to, ring.mp if mp is None else mp).start()

        def take(slot):
            self.copy(slot, slots.at[slot], dp, ring.mp).wait_recv()

        def sent(slot):
            self.copy(slot, slots.at[slot], dp, ring.mp).wait_send()

        if step == 0:
            start(0, dp, 1 - ring.mp)
        elif step == 1:
            take(0)
            sent(0)
            total[self.first_tap :, :] += slots[0, self.first_tap :, :]
            start(1, ring.to_core)
        elif step == 2:
            take(1)
            sent(1)
            total[...] += slots[1]
            start(2, ring.to_x)
        elif step == 3:
            take(2)
            sent(2)
            total[...] += slots[2]

            @pl.when(ring.outer)
            def _():
                start(3, ring.to_near)

        elif step == 4:

            @pl.when(ring.inner)
            def _():
                take(3)
                total[...] += slots[3]
                start(4, ring.to_mid)

        elif step == 5:

            @pl.when(ring.inner)
            def _():
                take(4)
                sent(4)
                total[...] += slots[4]
                start(5, ring.to_near)

        elif step == 6:

            @pl.when(ring.outer)
            def _():
                take(5)
                sent(3)
                total[...] = slots[5]

            @pl.when(ring.inner)
            def _():
                sent(5)


def whole_step(
    length_ref,
    tokens_ref,
    cotangent_ref,
    raw_taps_ref,
    gains_ref,
    shifts_ref,
    projection_hbm,
    output_hbm,
    up_hbm,
    down_hbm,
    activations_ref,
    token_grad_ref,
    small_ref,
    down_grad_ref,
    up_grad_ref,
    other_grad_ref,
    weights,
    kept,
    work,
    shared,
    wire,
    slots,
    sems,
):
    rows, width = tokens_ref.shape
    columns = projection_hbm.shape[3]
    hidden = up_hbm.shape[2]
    heads, _, reach = raw_taps_ref.shape
    grads = Grads(down_grad_ref, up_grad_ref, other_grad_ref)
    size_h = width // heads
    half = rows // 2
    tile = hidden // 2
    dp, mp = lax.axis_index("dp"), lax.axis_index("mp")
    head0 = mp * (columns // size_h)
    partner = (dp, 1 - mp)

    def own_half(layer):
        return weights.output.at[layer, mp]

    loads = []
    order = [
        (projection_hbm, weights.projection),
        (output_hbm, weights.output),
        (up_hbm, weights.up),
        (down_hbm, weights.down),
    ]
    for layer in range(LAYERS):
        for index, (source, place) in enumerate(order):
            load = pltpu.make_async_copy(
                source.at[layer],
                own_half(layer) if index == 1 else place.at[layer],
                sems.load.at[layer * 4 + index],
            )
            load.start()
            loads.append(load)

    barrier = pltpu.get_barrier_semaphore()
    pl.semaphore_signal(barrier, inc=1, device_id=partner, device_id_type=MESH)
    ring = Reduction(sems)
    ring.greet(barrier)

    frame = Frame(length_ref[0], rows, size_h)
    taps_ref, turned_ref = work.taps, work.turned
    taps_ref[...] = jnp.zeros_like(taps_ref)
    mirror = iota((rows, rows), 0) + iota((rows, rows), 1) == reach - 1
    mirror = mirror.astype(F32).astype(BF16)
    for layer in range(LAYERS):
        taps_ref[layer, :heads, :reach] = raw_taps_ref[:, layer, :]
        turned_ref[layer] = nn(taps_ref[layer].astype(BF16), mirror)
    flights = {}

    def send(slot, piece, partial_value):
        span = pl.ds(piece * half, half)
        wire.send[span, :] = partial_value.astype(BF16)
        copy = pltpu.make_async_remote_copy(
            src_ref=wire.send.at[span],
            dst_ref=wire.receive.at[slot % 2, span],
            send_sem=sems.send.at[slot % 2 * 2 + piece],
            recv_sem=sems.receive.at[slot % 2 * 2 + piece],
            device_id=partner,
            device_id_type=MESH,
        )
        copy.start()
        flights[slot, piece] = copy

    def arrived(slot, piece):
        span = pl.ds(piece * half, half)
        flights[slot, piece].wait()
        return wire.send[span, :].astype(F32) + wire.receive[
            slot % 2, span, :
        ].astype(F32)

    def share_copy(layer, hop):
        part = columns // 2
        which, first = (mp, ring.core) if hop == 0 else (1 - mp, ring.core)
        place = weights.output.at[layer, which, pl.ds(pl.multiple_of(first * part, 16), part)]
        return pltpu.make_async_remote_copy(
            src_ref=place,
            dst_ref=place,
            send_sem=sems.share_send.at[layer * 2 + hop],
            recv_sem=sems.share_receive.at[layer * 2 + hop],
            device_id=partner if hop == 0 else (ring.to_core, mp),
            device_id_type=MESH,
        )

    def gather_copy(layer, piece):
        place = work.mixed.at[mp, pl.ds(piece * half, half)]
        return pltpu.make_async_remote_copy(
            src_ref=place,
            dst_ref=place,
            send_sem=sems.gather_send.at[piece],
            recv_sem=sems.gather_receive.at[piece],
            device_id=partner,
            device_id_type=MESH,
        )

    side = hidden // 2
    near_rows = pl.ds(pl.multiple_of(ring.x * side, 128), side)
    far_rows = pl.ds(pl.multiple_of((1 - ring.x) * side, 128), side)
    factors = []

    def factor_copy(index, source, target, to=None):
        return pltpu.make_async_remote_copy(
            src_ref=source,
            dst_ref=target,
            send_sem=sems.factor_send.at[index],
            recv_sem=sems.factor_receive.at[index],
            device_id=(ring.to_x, mp) if to is None else to,
            device_id_type=MESH,
        )

    halves = [slice(0, half), slice(half, rows)]

    def project(layer, c):
        for i in range(3):
            kept.qkv[layer, i, c, :] = nn(
                work.x_low[c, :], weights.projection[layer, i]
            ).astype(BF16)

    def keep_of(layer):
        return Kept(*(ref.at[layer] for ref in kept.attention))

    work.x[...] = tokens_ref[...].astype(F32)
    work.x_low[...] = tokens_ref[...]
    loads[0].wait()
    project(0, halves[0])
    loads[1].wait()
    pl.semaphore_wait(barrier, 5)
    share_copy(0, 0).start()
    project(0, halves[1])
    for layer in range(LAYERS):
        attention(
            frame,
            kept.qkv.at[layer],
            taps_ref.at[layer],
            head0,
            size_h,
            keep_of(layer),
            work.mixed.at[mp],
        )
        slot = layer * 2
        for piece in range(len(halves)):
            gather_copy(layer, piece).start()
        share_copy(layer, 0).wait()
        share_copy(layer, 1).start()
        kept.mixed_t[layer] = work.mixed[mp].T
        kept.x_t[layer] = work.x_low[...].T
        loads[layer * 4 + 2].wait()
        loads[layer * 4 + 3].wait()
        share_copy(layer, 1).wait()
        for piece, c in enumerate(halves):
            gather_copy(layer, piece).wait()
            summed = work.x[c, :] + nn(
                jnp.concatenate([work.mixed[0, c, :], work.mixed[1, c, :]], 1),
                weights.output[layer].reshape(2 * columns, width),
            )
            y, normed, spread = norm_rows(summed, gains_ref[layer, 0:1], shifts_ref[layer, 0:1])
            kept.normed[layer, 0, c, :] = normed.astype(BF16)
            kept.spread[layer, 0, c, :] = spread
            work.y[c, :] = y
            work.y_low[c, :] = y.astype(BF16)
            for j in range(hidden // tile):
                span = slice(j * tile, (j + 1) * tile)
                u = nn(work.y_low[c, :], weights.up[layer, :, span])
                active, slope = gelu_both(u)
                work.active[c, span] = active.astype(BF16)
                kept.slope[layer, c, span] = slope.astype(BF16)
            send(slot + 1, piece, nn(work.active[c, :], weights.down[layer]))
        if layer + 1 < LAYERS:
            loads[layer * 4 + 5].wait()
            share_copy(layer + 1, 0).start()
        kept.active_t[layer] = work.active[...].T
        kept.y_t[layer] = work.y_low[...].T
        if FACTORED[layer]:
            factors.append(factor_copy(0, kept.active_t.at[layer, far_rows], shared.active_t))
            factors.append(factor_copy(1, kept.slope.at[layer, :, far_rows], shared.slope))
            factors.append(factor_copy(2, kept.y_t.at[layer], shared.y_t))
            for copy in factors:
                copy.start()
        if layer + 1 < LAYERS:
            loads[layer * 4 + 4].wait()
        for piece, c in enumerate(halves):
            summed = work.y[c, :] + arrived(slot + 1, piece)
            y, normed, spread = norm_rows(summed, gains_ref[layer, 1:2], shifts_ref[layer, 1:2])
            kept.normed[layer, 1, c, :] = normed.astype(BF16)
            kept.spread[layer, 1, c, :] = spread
            if layer + 1 < LAYERS:
                work.x[c, :] = y
                work.x_low[c, :] = y.astype(BF16)
                project(layer + 1, c)
            else:
                activations_ref[c, :] = (y * frame.valid[c]).astype(BF16)

    def add_pieces(layer):
        listed = pieces_of(width, columns, hidden, layer)
        listed_rows = {DOWN: hidden, UP: 2 * width}
        for k, (name, rows_of, kind) in enumerate(listed):
            before = sum(item[1] for item in listed[:k] if item[0] == name)
            index = sum(1 for item in listed[:k] if item[0] == name)

            quarter = rows_of // 4
            if ROUTE[kind] == 2:
                before, high, wide = before // 2, quarter, listed_rows[name] // 2
            else:
                high, wide = 2 * quarter, quarter
            if name in (DOWN, UP):
                ref = (grads.down if name == DOWN else grads.up).at[layer]
            else:
                ref = grads.other.at[layer, 0 if name == OUTPUT else 1 + index]
                before = 0

            def view(half, which, count, ref=ref, before=before, high=high, wide=wide):
                return ref.at[pl.ds(pl.multiple_of(before + half * high + which * wide, 16), count)]

            ring.add(rows_of, kind, view, slots[k], k, layer > 0, layer + 1 < LAYERS, PIECE_KINDS[1 - layer][k])

    for layer in reversed(range(LAYERS)):
        add_pieces(layer)
    small = SmallSum(ring, small_ref, wire.small, sems, 8)
    dy_ref, dr_ref, e_ref, du_ref = work.x, work.y, work.y_low, work.active

    def norm_back(layer, which):
        gain = gains_ref[layer, which : which + 1]
        gain_sum = shift_sum = 0.0
        for c in halves:
            result, gain_part, shift_part = norm_rows_back(
                dy_ref[c, :],
                kept.normed[layer, which, c, :].astype(F32),
                kept.spread[layer, which, c, :],
                gain,
            )
            dr_ref[c, :] = result
            (e_ref, e_second)[which][c, :] = result.astype(BF16)
            gain_sum, shift_sum = gain_sum + gain_part, shift_sum + shift_part
        row = layer * 2 + which
        small_ref[row : row + 1, :] = gain_sum
        small_ref[row + 4 : row + 5, :] = shift_sum

    du_other, e_second = work.x_low, work.e_second

    def down_grads(layer):
        block = hidden // DOWN_PIECES
        for j in range(DOWN_PIECES):
            if FACTORED[layer]:
                low = slice(j * block // 2, (j + 1) * block // 2)
                span = pl.ds(pl.multiple_of(ring.x * side + low.start, 16), block // 2)
                value = nn(kept.active_t[layer, span, :], e_second[...]) + nn(
                    shared.active_t[low, :], shared.e[...]
                )
            else:
                span = slice(j * block, (j + 1) * block)
                value = nn(kept.active_t[layer, span, :], e_second[...])
            grads.down[layer, span, :] = value.astype(BF16)
            yield

    def up_grads(layer):
        block = 2 * width // UP_PIECES
        for j in range(UP_PIECES):
            if FACTORED[layer]:
                low = slice(j * block // 2, (j + 1) * block // 2)
                span = pl.ds(pl.multiple_of(ring.x * width + low.start, 16), block // 2)
                value = nn(kept.y_t[layer, low, :], du_ref[:, near_rows]) + nn(
                    shared.y_t[low, :], du_other[...]
                )
            else:
                span = slice(j * block, (j + 1) * block)
                at, first = divmod(j * block, width)
                value = nn(
                    kept.y_t[layer, first : first + block, :],
                    du_ref[:, at * side : (at + 1) * side],
                )
            grads.up[layer, span, :] = value.astype(BF16)
            yield

    def backward():
        small_ref[...] = jnp.zeros_like(small_ref)
        for piece, c in enumerate(halves):
            dy_ref[c, :] = cotangent_ref[c, :].astype(F32) * frame.valid[c]
        for layer in reversed(range(LAYERS)):
            slot = 4 + (LAYERS - 1 - layer) * 2
            norm_back(layer, 1)
            if FACTORED[layer]:
                own = pl.ds(pl.multiple_of(mp * half, 16), half)
                factors.append(factor_copy(3, e_second.at[own], shared.e.at[own]))
                factors[3].start()
            yield
            if not FACTORED[layer]:
                yield from down_grads(layer)
            for j in range(hidden // tile):
                span = slice(j * tile, (j + 1) * tile)
                dh = nt(e_second[...], weights.down[layer, span, :])
                du_ref[:, span] = (dh * kept.slope[layer, :, span].astype(F32)).astype(BF16)
            yield
            for piece, c in enumerate(halves):
                send(slot, piece, nt(du_ref[c, :], weights.up[layer]))
                yield
            if FACTORED[layer]:
                for copy in factors:
                    copy.wait()
                passing = factor_copy(4, shared.e.at[own], shared.e.at[own], partner)
                passing.start()
                yield
            else:
                yield from up_grads(layer)
            for piece, c in enumerate(halves):
                dy_ref[c, :] = dr_ref[c, :] + arrived(slot, piece)
            norm_back(layer, 0)
            yield
            for piece, c in enumerate(halves):
                work.dmixed[c, :] = nt(e_ref[c, :], weights.output[layer, mp]) * frame.valid[c]
            yield
            for j in range(2):
                span = slice(j * columns, (j + 1) * columns)
                grads.other[layer, 0, span, :] = nn(
                    kept.mixed_t[layer], e_ref[:, span]
                ).astype(BF16)
            yield
            if FACTORED[layer]:
                passing.wait()
                for j in range(side // tile):
                    span = slice(j * tile, (j + 1) * tile)
                    near = pl.ds(pl.multiple_of(ring.x * side + j * tile, 128), tile)
                    dh = nt(shared.e[...], weights.down[layer, near, :])
                    du_other[:, span] = (dh * shared.slope[:, span].astype(F32)).astype(BF16)
                yield
                yield from down_grads(layer)
                yield from up_grads(layer)

            def taps_out(head, row, layer=layer):
                lanes = slice(head * 128, (head + 1) * 128)
                for side in range(2):
                    at = 8 + 2 * layer + side
                    small_ref[at : at + 1, lanes] = jnp.where(mp == side, row[:, :128], 0.0)

            yield from attention_back(
                frame,
                work.dmixed,
                kept.qkv.at[layer],
                turned_ref.at[layer],
                head0,
                size_h,
                keep_of(layer),
                work.dqkv,
                taps_out,
            )
            for piece, c in enumerate(halves):
                total = 0.0
                for i in range(3):
                    total = total + nt(work.dqkv[i, c, :], weights.projection[layer, i])
                send(slot + 1, piece, total)
                yield
            for i in range(3):
                grads.other[layer, 1 + i] = nn(kept.x_t[layer], work.dqkv[i]).astype(BF16)
                yield
            target = dy_ref if layer > 0 else token_grad_ref
            for piece, c in enumerate(halves):
                target[c, :] = dr_ref[c, :] + arrived(slot + 1, piece)
        yield

    items = backward()
    for code in ORDER:
        if code < 0:
            next(items)
        elif code >= 1000:
            small.event(code - 1000)
        else:
            ring.event(code // 16, code % 16)


FACTORED = (True, False)
DOWN_PIECES = 4
UP_PIECES = 4
PIECE_KINDS = (
    (2, 2, 4, 2, 2, 2, 2, 4, 0, 0, 1, 0),
    (3, 1, 3, 3, 0, 0, 0, 0, 0, 0, 1, 0),
)
ORDER = (
    -1, -1, 0, -1, 16, -1, 32, -1, 48, -1, 1, 17, -1, -1, 33, -1, 64, -1, 49, 80, -1, 96, -1, 112, 65, 81, 97,
    2, 113, 34, -1, 3, 18, 50, -1, -1, 128, -1, -1, 66, 35, 129, -1, -1, 51, 82, 4, -1, -1, 19, -1, 67, 98,
    -1, -1, -1, 83, 36, -1, 114, 5, -1, -1, 144, -1, 160, -1, 176, 52, 99, 145, 130, 161, 177, 68, 20, 115,
    37, 6, 84, 131, -1, 146, 178, 69, 100, 53, -1, -1, -1, 38, 21, 162, 116, 7, 132, 147, -1, 70, 101, 85, 22,
    -1, 179, 163, -1, 54, -1, -1, -1, 8, 192, 193, 148, -1, 23, 208, 209, 39, 117, -1, -1, -1, 194, 71, 256,
    257, 210, 102, -1, -1, -1, 40, 224, 258, 225, -1, 226, 180, 133, 103, 288, 289, 55, 86, -1, -1, 290, 195,
    149, 56, 240, 241, 118, 87, 272, 273, 164, -1, 242, -1, 274, 211, 181, 134, 119, 304, 305, -1, -1, 306,
    196, 135, 320, -1, 259, 150, -1, 321, -1, 1000, 165, -1, 227, 182, -1, -1, 151, 336, -1, 197, -1, 183,
    368, 212, 291, 337, 1001, 369, 322, 166, 1002, 260, 243, 167, 352, 198, 213, 353, 199, 228, 275, 338, 261,
    -1, 307, 292, 370, 229, 244, 323, 1003, 276, 293, 214, 215, 308, 354, 245, 262, 263, 324, 339, 277, 230,
    355, 371, 1004, 340, 231, 372, 232, 356, 1005, 309, 294, 295, 325, 246, 247, 278, 279, 341, 310, 373, 326,
    327, 357, 311, 312, 342, 343, 374, 358, 375, 359, 1006,
)


def pieces_of(width, columns, hidden, layer):
    names = [DOWN] * DOWN_PIECES + [UP] * UP_PIECES + [OUTPUT] + [PROJECTION] * 3
    rows = {DOWN: hidden // DOWN_PIECES, UP: 2 * width // UP_PIECES, OUTPUT: width, PROJECTION: width}
    return [(name, rows[name], kind) for name, kind in zip(names, PIECE_KINDS[layer])]


def slots_of(name, rows, long, width, columns, hidden):
    across = {DOWN: width, UP: hidden // 2, OUTPUT: columns, PROJECTION: columns}[name]

    def room(count):
        return pltpu.VMEM((count, across), BF16)

    return Slots(
        core=room(rows // 2),
        x=room(rows // 4),
        near=room(rows // 2 if long else rows // 4),
        mid=room(rows // 4),
    )


def fused_body(tokens, lengths, cotangent, projection, conv_taps, output_weight, norm_gains, norm_shifts, up_weight, down_weight):
    rows, width = tokens.shape
    columns, hidden = projection.shape[3], up_weight.shape[2]
    heads, reach = conv_taps.shape[1:]
    size_h = width // heads
    pairs = columns // (2 * size_h)
    by_kind = jnp.transpose(projection, (0, 2, 1, 3))
    by_head = jnp.transpose(conv_taps, (1, 0, 2))
    vmem = pl.BlockSpec(memory_space=pltpu.VMEM)
    hbm = pl.BlockSpec(memory_space=pl.ANY)
    two = 2 * M
    pieces = pieces_of(width, columns, hidden, 0)
    scratch = (
        Weights(
            projection=pltpu.VMEM((LAYERS, 3, width, columns), BF16),
            output=pltpu.VMEM((LAYERS, 2, columns, width), BF16),
            up=pltpu.VMEM((LAYERS, width, hidden), BF16),
            down=pltpu.VMEM((LAYERS, hidden, width), BF16),
        ),
        Stored(
            attention=Kept(
                ql=pltpu.VMEM((LAYERS, M, columns), F32),
                kl=pltpu.VMEM((LAYERS, M, columns), F32),
                second=pltpu.VMEM((LAYERS, pairs, two, two), F32),
                inverse=pltpu.VMEM((LAYERS, NEWTON + 1, pairs, M, two), F32),
                first=pltpu.VMEM((LAYERS, rows, columns), BF16),
                third=pltpu.VMEM((LAYERS, pairs, two, rows), BF16),
                summary=pltpu.VMEM((LAYERS, pairs, two, two), F32),
                carried=pltpu.VMEM((LAYERS, pairs, two, two), F32),
            ),
            qkv=pltpu.VMEM((LAYERS, 3, rows, columns), BF16),
            normed=pltpu.VMEM((LAYERS, 2, rows, width), BF16),
            spread=pltpu.VMEM((LAYERS, 2, rows, 1), F32),
            slope=pltpu.VMEM((LAYERS, rows, hidden), BF16),
            x_t=pltpu.VMEM((LAYERS, width, rows), BF16),
            mixed_t=pltpu.VMEM((LAYERS, columns, rows), BF16),
            y_t=pltpu.VMEM((LAYERS, width, rows), BF16),
            active_t=pltpu.VMEM((LAYERS, hidden, rows), BF16),
        ),
        Work(
            x=pltpu.VMEM((rows, width), F32),
            x_low=pltpu.VMEM((rows, width), BF16),
            y=pltpu.VMEM((rows, width), F32),
            y_low=pltpu.VMEM((rows, width), BF16),
            mixed=pltpu.VMEM((2, rows, columns), BF16),
            active=pltpu.VMEM((rows, hidden), BF16),
            e_second=pltpu.VMEM((rows, width), BF16),
            dmixed=pltpu.VMEM((rows, columns), F32),
            dqkv=pltpu.VMEM((3, rows, columns), BF16),
            taps=pltpu.VMEM((LAYERS, 16, rows), F32),
            turned=pltpu.VMEM((LAYERS, 16, rows), F32),
        ),
        Shared(
            active_t=pltpu.VMEM((hidden // 2, rows), BF16),
            slope=pltpu.VMEM((rows, hidden // 2), BF16),
            y_t=pltpu.VMEM((width, rows), BF16),
            e=pltpu.VMEM((rows, width), BF16),
        ),
        Wire(
            send=pltpu.VMEM((rows, width), BF16),
            receive=pltpu.VMEM((2, rows, width), BF16),
            small=pltpu.VMEM((6, 8 + 2 * LAYERS, width), F32),
        ),
        [
            slots_of(name, count, 1 in kinds, width, columns, hidden)
            for (name, count, _), kinds in zip(pieces, zip(*PIECE_KINDS))
        ],
        Sems(
            load=pltpu.SemaphoreType.DMA((4 * LAYERS,)),
            ring_send=pltpu.SemaphoreType.DMA((SENDS * len(pieces),)),
            ring_receive=pltpu.SemaphoreType.DMA((RECEIVES * len(pieces),)),
            small_send=pltpu.SemaphoreType.DMA((6,)),
            small_receive=pltpu.SemaphoreType.DMA((6,)),
            credit=pltpu.SemaphoreType.REGULAR((2 * len(pieces),)),
            ready=pltpu.SemaphoreType.REGULAR((4 * len(pieces),)),
            factor_send=pltpu.SemaphoreType.DMA((5,)),
            factor_receive=pltpu.SemaphoreType.DMA((5,)),
            share_send=pltpu.SemaphoreType.DMA((2 * LAYERS,)),
            share_receive=pltpu.SemaphoreType.DMA((2 * LAYERS,)),
            gather_send=pltpu.SemaphoreType.DMA((2,)),
            gather_receive=pltpu.SemaphoreType.DMA((2,)),
            send=pltpu.SemaphoreType.DMA((4,)),
            receive=pltpu.SemaphoreType.DMA((4,)),
        ),
    )
    own = pltpu.VMEM
    results = pl.pallas_call(
        whole_step,
        out_shape=[
            own((rows, width), BF16),
            own((rows, width), F32),
            own((8 + 2 * LAYERS, width), F32),
            own((LAYERS, hidden, width), BF16),
            own((LAYERS, 2 * width, hidden // 2), BF16),
            own((LAYERS, 4, width, columns), BF16),
        ],
        in_specs=[pl.BlockSpec(memory_space=pltpu.SMEM)] + [vmem] * 5 + [hbm] * 4,
        out_specs=[vmem] * 6,
        scratch_shapes=scratch,
        compiler_params=pltpu.CompilerParams(
            collective_id=0, has_side_effects=True, vmem_limit_bytes=VMEM_ROOM
        ),
    )(
        lengths,
        tokens,
        cotangent,
        by_head,
        norm_gains,
        norm_shifts,
        by_kind,
        output_weight,
        up_weight,
        down_weight,
    )
    shape = jax.ShapeDtypeStruct
    held = [pltpu.with_memory_space_constraint(result, pltpu.VMEM) for result in results]
    wide = [
        (LAYERS, hidden, width),
        (LAYERS, width, hidden),
        (LAYERS, 3, width, columns),
        (LAYERS, columns, width),
    ]
    outputs = pl.pallas_call(
        widen,
        out_shape=[shape(size, F32) for size in wide]
        + [
            shape((rows, width), BF16),
            shape((rows, width), F32),
            shape((heads, LAYERS, reach), F32),
            shape((LAYERS, 2, width), F32),
            shape((LAYERS, 2, width), F32),
        ],
        in_specs=[vmem] * 6,
        out_specs=[hbm] * 6 + [vmem] * 3,
        scratch_shapes=[pltpu.VMEM(size, F32) for size in wide] + [pltpu.SemaphoreType.DMA((6,))],
        compiler_params=pltpu.CompilerParams(vmem_limit_bytes=WIDE_ROOM),
    )(*held)
    down_grad, up_grad, projection_grad, output_grad = outputs[:4]
    activations, token_grad, taps_grad, gains_grad, shifts_grad = outputs[4:]
    return (
        activations,
        token_grad,
        jnp.transpose(projection_grad, (0, 2, 1, 3)),
        jnp.transpose(taps_grad, (1, 0, 2)),
        output_grad,
        gains_grad,
        shifts_grad,
        up_grad,
        down_grad,
    )


VMEM_ROOM = 97 * 2**19
WIDE_ROOM = 32 * 2**20
WIDE_PARTS = 8


def widen(
    activations_ref,
    token_grad_ref,
    small_ref,
    down_ref,
    up_ref,
    other_ref,
    down_hbm,
    up_hbm,
    projection_hbm,
    output_hbm,
    activations_out,
    token_grad_out,
    taps_out,
    gains_out,
    shifts_out,
    down_wide,
    up_wide,
    projection_wide,
    output_wide,
    sems,
):
    heads, _, reach = taps_out.shape
    columns = output_wide.shape[1]

    def send(source, target, index):
        pltpu.make_async_copy(source, target, sems.at[index]).start()

    send(activations_ref, activations_out, 4)
    send(token_grad_ref, token_grad_out, 5)

    def cast(target, source):
        def step(i, unused):
            span = pl.ds(pl.multiple_of(i * 32, 32), 32)
            target[span, :] = source[span, :].astype(F32)
            return unused

        lax.fori_loop(0, source.shape[0] // 32, step, 0)

    for layer in range(LAYERS):
        count = down_ref.shape[1] // WIDE_PARTS
        for part in range(WIDE_PARTS):
            span = pl.ds(part * count, count)
            cast(down_wide.at[layer, span], down_ref.at[layer, span])
            send(down_wide.at[layer, span], down_hbm.at[layer, span], 0)
        count, side = up_wide.shape[1] // WIDE_PARTS, up_wide.shape[2] // 2
        for part in range(WIDE_PARTS):
            span = pl.ds(part * count, count)
            for i in range(2):
                cast(
                    up_wide.at[layer, span, pl.ds(i * side, side)],
                    up_ref.at[layer, pl.ds(i * up_wide.shape[1] + part * count, count)],
                )
            send(up_wide.at[layer, span], up_hbm.at[layer, span], 1)
        for i in range(3):
            cast(projection_wide.at[layer, i], other_ref.at[layer, 1 + i])
            send(projection_wide.at[layer, i], projection_hbm.at[layer, i], 2)
        for i in range(2):
            side = slice(i * columns, (i + 1) * columns)
            output_wide[layer, :, side] = other_ref[layer, 0, side, :].astype(F32)
        send(output_wide.at[layer], output_hbm.at[layer], 3)
    for layer in range(LAYERS):
        gains_out[layer] = small_ref[2 * layer : 2 * layer + 2, :]
        shifts_out[layer] = small_ref[4 + 2 * layer : 6 + 2 * layer, :]
        for head in range(heads):
            side, place = divmod(head, heads // 2)
            row = 8 + 2 * layer + side
            taps_out[head, layer : layer + 1, :] = small_ref[
                row : row + 1, place * 128 : place * 128 + reach
            ]
    whole = [
        (down_wide, down_hbm),
        (up_wide, up_hbm),
        (projection_wide, projection_hbm),
        (output_wide, output_hbm),
        (activations_ref, activations_out),
        (token_grad_ref, token_grad_out),
    ]
    for index, (source, target) in enumerate(whole):
        pltpu.make_async_copy(source, target, sems.at[index]).wait()


def solution(mesh):
    fused = mesh.shape["mp"] == 2 and mesh.shape["dp"] == 16

    def step(*arrays):
        return (fused_body if fused else body)(*arrays)

    return jax.shard_map(
        step,
        mesh=mesh,
        in_specs=(
            P("dp", None),
            P("dp"),
            P("dp", None),
            P(None, None, None, "mp"),
            P(),
            P(None, "mp", None),
            P(),
            P(),
            P(None, None, "mp"),
            P(None, "mp", None),
        ),
        out_specs=(
            P("dp", None),
            P("dp", None),
            P(None, None, None, "mp"),
            P(),
            P(None, "mp", None),
            P(),
            P(),
            P(None, None, "mp"),
            P(None, "mp", None),
        ),
        check_vma=False,
    )
```
